32 devices in a mesh: band: 2 (over y), row: 4 (over z), col: 4 (over x, core).
Axes of the slice: x: 2, y: 2, z: 4, core: 2. Of those that a mesh axis runs over, the one named last changes fastest.
Arguments:
- source: float32 [3, 512, 4096], P(None, ('band', 'row'), 'col'), parts along dimension 1, may hold values from -50 to 50
- weight: float32 [512, 4096], P(('band', 'row'), 'col'), parts along dimension 0, may hold values from 0.05 to 0.15
- seam_right: int32 [512, 4096], P(('band', 'row'), 'col'), parts along dimension 0, may hold values 0 or 1
- seam_down: int32 [512, 4096], P(('band', 'row'), 'col'), parts along dimension 0, may hold values 0 or 1
- offsets: int32 [2, 16, 3], P('band'), parts along dimension 0, may hold values from -64 to 64
Outputs:
- solution: float32 [3, 512, 4096], P(None, ('band', 'row'), 'col'), parts along dimension 1
- residual: float32 [3, 512, 4096], P(None, ('band', 'row'), 'col'), parts along dimension 1
- smoothed: float32 [3, 512, 4096], P(None, ('band', 'row'), 'col'), parts along dimension 1
The draws below stay inside these ranges and needn't reach their ends.
There are 2 independent parts, one for each index of `band`. The reference program is written for one: setup_inputs(seed, part) draws one part's arguments, and reference() takes and returns one part's arrays. A program takes and returns all parts, laid end to end along the dimension named above; each array names one. Nothing has to cross between parts.
All inputs are finite; a program needn't handle non-finite values. No bound on the sum of `seam_right` or of `seam_down` on one device may be relied on, other than what follows from the above.
Results may differ from the reference program's by a relative error of at most 0.0003.
Values sent between devices are 32-bit elements; how exact they have to be, the bound alone decides.
No kernel may reach another device: no remote copies, remote signals or barrier semaphores. Data moves between devices by JAX's collectives and lax.ppermute only.
A program may use at most 64 MiB of HBM per device.

```python
import math
import jax
import jax.numpy as jnp

CHANNELS = 3
ROW_DEV = 64
COL_DEV = 1024
TILE = 256
ITERS = 2
SWEEPS = 8
ROWS = 256
COLS = 4096
TILE_ROWS = 1
TILE_COLS = 16


def draw_source(key, part):
    key = jax.random.fold_in(key, 11)
    phase_key, factor_key, noise_key = jax.random.split(key, 3)
    rows_at = jnp.arange(ROWS, dtype=jnp.float32)
    cols_at = jnp.arange(COLS, dtype=jnp.float32)
    row_frac = rows_at / ROWS
    col_frac = cols_at / COLS
    row_scale = jnp.exp(1.1513 * (row_frac[:, None] + col_frac[None, :]))
    col_place = jnp.arange(COLS, dtype=jnp.int32) % COL_DEV
    row_place = jnp.arange(ROWS, dtype=jnp.int32) % ROW_DEV
    col_gap = jnp.minimum(col_place, COL_DEV - col_place).astype(jnp.float32)
    row_gap = jnp.minimum(row_place, ROW_DEV - row_place).astype(jnp.float32)
    envelope = 0.25 + 0.75 * jnp.maximum(jnp.exp(-col_gap / 24.0)[None, :], jnp.exp(-row_gap / 24.0)[:, None])
    phases = jax.random.uniform(phase_key, (CHANNELS, 2), jnp.float32, 0.0, 6.2832)
    factor = jax.random.uniform(factor_key, (CHANNELS, ROWS, COLS), jnp.float32, 0.6, 1.3)
    col_angle = phases[:, 0][:, None, None] + cols_at[None, None, :]
    row_angle = phases[:, 1][:, None, None] + rows_at[None, :, None]
    wave = 1.6 + 0.7 * jnp.sin(6.2832 * col_angle / 40.0) + 0.7 * jnp.sin(6.2832 * row_angle / 40.0)
    rough = 0.3 * jnp.clip(jax.random.normal(noise_key, (CHANNELS, ROWS, COLS), jnp.float32), -3.0, 3.0)
    values = row_scale[None, :, :] * (envelope[None, :, :] * wave * factor + rough)
    return jnp.clip(values, -49.0, 49.0).astype(jnp.float32)


def with_ends(drawn, stream_key, smallest, largest):
    shape = drawn.shape
    place = [jax.random.randint(jax.random.fold_in(stream_key, axis), (), 0, shape[axis]) for axis in range(len(shape))]
    drawn = drawn.at[tuple(place)].set(smallest)
    longest = shape.index(max(shape))
    place[longest] = (place[longest] + 1) % shape[longest]
    return drawn.at[tuple(place)].set(largest)


def level_of(key, shape, cuts, low, high):
    loudness = 1.0
    for dim, shards_of in cuts:
        draws = jax.random.uniform(jax.random.fold_in(jax.random.fold_in(key, 6), dim), (shards_of,), jnp.float32, low / len(cuts), high / len(cuts))
        loudness = loudness * jnp.repeat(jnp.exp(draws), shape[dim] // shards_of).reshape((-1,) + (1,) * (len(shape) - 1 - dim))
    return loudness


def setup_inputs(seed: int = 0, part: int = 0) -> dict:
    key_of = jax.random.split(jax.random.key(seed), 6)
    own_keys = jax.random.split(jax.random.fold_in(key_of[5], part), 6)
    return {
        "source": draw_source(jax.random.fold_in(jax.random.fold_in(key_of[5], part), 71), part),
        "weight": jnp.clip(jnp.exp(math.log(0.15) - 1.0986123 * jax.random.uniform(own_keys[1], (ROWS, COLS), jnp.float32) ** level_of(own_keys[1], (ROWS, COLS), ((0, 4), (1, 4)), -0.2, 0.2)), 0.05, 0.15),
        "seam_right": with_ends((jax.random.randint(own_keys[2], (ROWS, COLS), 0, 64) < 1).astype(jnp.int32), jax.random.fold_in(own_keys[2], 1), 0, 1),
        "seam_down": with_ends((jax.random.randint(own_keys[3], (ROWS, COLS), 0, 64) < 1).astype(jnp.int32), jax.random.fold_in(own_keys[3], 1), 0, 1),
        "offsets": with_ends(jax.random.randint(own_keys[4], (TILE_ROWS, TILE_COLS, CHANNELS), -64, 65), jax.random.fold_in(own_keys[4], 1), -64, 64).astype(jnp.int32),
    }


seam_damping = 0.8
offset_unit = 32.0
spectrum_low = 0.08
spectrum_high = 2.0


def apply_operator(values, coefficients):
    diagonal, cond_right, cond_left, cond_down, cond_up = coefficients
    padded = jnp.pad(values, ((0, 0), (1, 1), (1, 1)))
    neighbours = cond_right * padded[:, 1:-1, 2:] + cond_left * padded[:, 1:-1, :-2] + cond_down * padded[:, 2:, 1:-1] + cond_up * padded[:, :-2, 1:-1]
    return diagonal * values - neighbours


def chebyshev(residual, inverse, coefficients):
    centre = (spectrum_high + spectrum_low) / 2.0
    radius = (spectrum_high - spectrum_low) / 2.0
    sigma_ratio = centre / radius
    update = residual * inverse / centre
    smoothed = update
    recurrence = 1.0 / sigma_ratio
    for sweep_index in range(SWEEPS - 1):
        remainder = residual - apply_operator(smoothed, coefficients)
        following = 1.0 / (2.0 * sigma_ratio - recurrence)
        update = (following * recurrence) * update + (2.0 * following / radius) * inverse * remainder
        smoothed = smoothed + update
        recurrence = following
    return smoothed


def reference(source, weight, seam_right, seam_down, offsets):
    col_index = jnp.arange(COLS, dtype=jnp.int32)
    row_index = jnp.arange(ROWS, dtype=jnp.int32)
    cond_right = jnp.where(col_index[None, :] < COLS - 1, 1.0 - seam_damping * seam_right.astype(jnp.float32), 0.0).astype(jnp.float32)
    cond_down = jnp.where(row_index[:, None] < ROWS - 1, 1.0 - seam_damping * seam_down.astype(jnp.float32), 0.0).astype(jnp.float32)
    cond_left = jnp.pad(cond_right[:, :-1], ((0, 0), (1, 0)))
    cond_up = jnp.pad(cond_down[:-1, :], ((1, 0), (0, 0)))
    diagonal = weight + cond_right + cond_left + cond_down + cond_up
    inverse = 1.0 / diagonal
    coefficients = (diagonal, cond_right, cond_left, cond_down, cond_up)
    tiled = jnp.repeat(jnp.repeat(offsets, TILE, axis=0), TILE, axis=1).astype(jnp.float32)
    right_side = source + jnp.transpose(tiled, (2, 0, 1)) / offset_unit
    solution = jnp.zeros_like(right_side)
    residual = right_side
    smoothed = chebyshev(residual, inverse, coefficients)
    direction = smoothed
    inner_now = jnp.sum(residual * smoothed)
    for iteration in range(ITERS):
        applied = apply_operator(direction, coefficients)
        step_size = inner_now / jnp.sum(direction * applied)
        solution = solution + step_size * direction
        residual = residual - step_size * applied
        smoothed = chebyshev(residual, inverse, coefficients)
        inner_next = jnp.sum(residual * smoothed)
        direction = smoothed + (inner_next / inner_now) * direction
        inner_now = inner_next
    return (solution, residual, smoothed)
```

```python
import functools

import jax
import jax.numpy as jnp
from jax import lax
from jax.experimental import pallas as pl
from jax.experimental.pallas import tpu as pltpu
from jax.sharding import PartitionSpec as P

TILE = 256
SWEEPS = 8
LANES = 128
HALO = 24
PAD = 8

seam_damping = 0.8
offset_unit = 32.0
spectrum_low = 0.08
spectrum_high = 2.0
MIX = 2.4

VMEM_LIMIT = 48 * 1024 * 1024


def chebyshev_polynomial():
    centre = (spectrum_high + spectrum_low) / 2.0
    radius = (spectrum_high - spectrum_low) / 2.0
    sigma = centre / radius
    size = SWEEPS
    update = [1.0 / centre] + [0.0] * (size - 1)
    smoothed = list(update)
    rho = 1.0 / sigma
    for _ in range(SWEEPS - 1):
        remainder = [-s for s in smoothed]
        remainder[0] += 1.0
        for k in range(size - 1):
            remainder[k + 1] += smoothed[k]
        following = 1.0 / (2.0 * sigma - rho)
        update = [following * rho * u + 2.0 * following / radius * r for u, r in zip(update, remainder)]
        smoothed = [s + u for s, u in zip(smoothed, update)]
        rho = following
    return smoothed


def tile_range(application, rows):
    low = 1 + application
    high = rows + 2 * HALO - 1 - application
    return low // 8, -(-high // 8)


def stencil(z_ref, coefs, tile, chans, tiles):
    base = pl.multiple_of(PAD + 8 * tile, 8)
    lane = lax.broadcasted_iota(jnp.int32, (8, LANES), 1)
    first, last = (lane == 0, lane == LANES - 1)
    right_ref, left_ref, down_ref, up_ref = coefs
    centre = [[z_ref[c, j, pl.ds(base, 8), :] for j in range(tiles)] for c in range(chans)]
    ahead = [[pltpu.roll(v, LANES - 1, 1) for v in row] for row in centre]
    behind = [[pltpu.roll(v, 1, 1) for v in row] for row in centre]
    out = [[None] * tiles for _ in range(chans)]
    for j in range(tiles):
        a_right = right_ref[j, pl.ds(base, 8), :]
        a_left = left_ref[j, pl.ds(base, 8), :]
        a_down = down_ref[j, pl.ds(base, 8), :]
        a_up = up_ref[j, pl.ds(base, 8), :]
        for c in range(chans):
            to_right = jnp.where(last, ahead[c][(j + 1) % tiles], ahead[c][j])
            to_left = jnp.where(first, behind[c][(j - 1) % tiles], behind[c][j])
            below = z_ref[c, j, pl.ds(base + 1, 8), :]
            above = z_ref[c, j, pl.ds(base - 1, 8), :]
            out[c][j] = (a_right * to_right + a_left * to_left) + (a_down * below + a_up * above)
    return base, centre, out


def horner(g_ref, buffers, final_ref, coefs, first_application, rows, chans, tiles, count):
    poly = chebyshev_polynomial()
    degree = SWEEPS - 1
    source = g_ref
    for k in range(count):
        target = final_ref if k == degree - 1 else buffers[k % 2]
        low, high = tile_range(first_application + k, rows)
        scale = poly[degree] if k == 0 else None
        add = poly[degree - 1 - k]

        def body(tile, carry, source=source, target=target, scale=scale, add=add):
            base, _, moved = stencil(source, coefs, tile, chans, tiles)
            for c in range(chans):
                for j in range(tiles):
                    value = moved[c][j] if scale is None else scale * moved[c][j]
                    target[c, j, pl.ds(base, 8), :] = value + add * g_ref[c, j, pl.ds(base, 8), :]
            return carry

        lax.fori_loop(low, high, body, 0)
        source = target
    return source


def residual_step(g_ref, z_ref, next_ref, coefs, diag_ref, application, rows, chans, tiles, own_tiles):
    low, high = tile_range(application, rows)
    own_low = HALO // 8
    own_high = own_low + rows // 8

    def body(tile, carry, own):
        base, centre, moved = stencil(z_ref, coefs, tile, chans, tiles)
        for j in range(tiles):
            weigh = own and j < own_tiles
            diag = diag_ref[j, pl.ds(base, 8), :] if weigh else None
            for c in range(chans):
                g = g_ref[c, j, pl.ds(base, 8), :]
                z = centre[c][j]
                following = g - MIX * (z - moved[c][j])
                next_ref[c, j, pl.ds(base, 8), :] = following
                if weigh:
                    dz = diag * z
                    carry = (carry[0] + g * dz, carry[1] + following * dz)
        return carry

    zero = jnp.zeros((8, LANES), jnp.float32)
    lax.fori_loop(low, own_low, functools.partial(body, own=False), 0)
    lax.fori_loop(own_high, high, functools.partial(body, own=False), 0)
    return lax.fori_loop(own_low, own_high, functools.partial(body, own=True), (zero, zero))


def first_kernel(
    flags_ref, shift_ref, src_ref, weight_ref, seam_right_ref, seam_down_ref, top_ref, bottom_ref, before_ref, after_ref,
    right_ref, left_ref, down_ref, up_ref, diag_ref, g0_ref, z0_ref, g1_ref, f1_ref, g2_ref, sums_ref,
    cond_right, cond_down, work_a, work_b,
):
    chans, rows, cols = src_ref.shape
    own_tiles = cols // LANES
    tiles = own_tiles + 1
    total = rows + 2 * HALO
    lane = lax.broadcasted_iota(jnp.int32, (8, LANES), 1)
    sub = lax.broadcasted_iota(jnp.int32, (8, LANES), 0)
    zero = jnp.zeros((8, LANES), jnp.float32)

    for j in range(tiles):
        for at in (0, PAD + total):
            cond_down[j, pl.ds(at, 8), :] = zero
            for c in range(chans):
                for ref in (g0_ref, g1_ref, work_a, work_b, z0_ref, f1_ref):
                    ref[c, j, pl.ds(at, 8), :] = zero

    def put(base, j, planes):
        for c in range(chans):
            g0_ref[c, j, pl.ds(base, 8), :] = planes[c]
        diag_ref[j, pl.ds(base, 8), :] = planes[chans]
        cond_right[j, pl.ds(base, 8), :] = planes[chans + 1]
        cond_down[j, pl.ds(base, 8), :] = planes[chans + 2]

    def edge_rows(slab_ref, start):
        def body(t, carry):
            at = pl.multiple_of(8 * t, 8)
            base = pl.multiple_of(PAD + start + 8 * t, 8)
            for j in range(own_tiles):
                put(base, j, [slab_ref[p, pl.ds(at, 8), j * LANES:(j + 1) * LANES] for p in range(chans + 3)])
            return carry

        lax.fori_loop(0, HALO // 8, body, 0)

    edge_rows(top_ref, 0)
    edge_rows(bottom_ref, HALO + rows)

    def own_rows(t, carry):
        at = pl.multiple_of(8 * t, 8)
        base = pl.multiple_of(PAD + HALO + 8 * t, 8)
        bottom_row = (at + sub) == jnp.where(flags_ref[0] == 1, rows - 1, -1)
        for j in range(own_tiles):
            here = pl.ds(at, 8), pl.ds(j * LANES, LANES)
            planes = [src_ref[c, here[0], here[1]] + shift_ref[c, j * LANES // TILE] for c in range(chans)]
            planes.append(weight_ref[here[0], here[1]])
            to_right = 1.0 - seam_damping * seam_right_ref[here[0], here[1]].astype(jnp.float32)
            if j == own_tiles - 1:
                to_right = jnp.where(lane == jnp.where(flags_ref[1] == 1, LANES - 1, -1), 0.0, to_right)
            to_down = 1.0 - seam_damping * seam_down_ref[here[0], here[1]].astype(jnp.float32)
            planes.append(to_right)
            planes.append(jnp.where(bottom_row, 0.0, to_down))
            put(base, j, planes)
        return carry

    lax.fori_loop(0, rows // 8, own_rows, 0)

    def side_columns(t, carry):
        at = pl.multiple_of(8 * t, 8)
        base = pl.multiple_of(PAD + 8 * t, 8)
        put(
            base,
            own_tiles,
            [
                jnp.where(lane < LANES // 2, after_ref[p, pl.ds(at, 8), :], before_ref[p, pl.ds(at, 8), :])
                for p in range(chans + 3)
            ],
        )
        return carry

    lax.fori_loop(0, total // 8, side_columns, 0)

    def coefficients(t, carry):
        base = pl.multiple_of(PAD + 8 * t, 8)
        to_right = [cond_right[j, pl.ds(base, 8), :] for j in range(tiles)]
        behind = [pltpu.roll(v, 1, 1) for v in to_right]
        for j in range(tiles):
            to_left = jnp.where(lane == 0, behind[(j - 1) % tiles], behind[j])
            to_down = cond_down[j, pl.ds(base, 8), :]
            to_up = cond_down[j, pl.ds(base - 1, 8), :]
            diag = diag_ref[j, pl.ds(base, 8), :] + to_right[j] + to_left + to_down + to_up
            inverse = 1.0 / jnp.where(diag > 0.0, diag, 1.0)
            diag_ref[j, pl.ds(base, 8), :] = diag
            right_ref[j, pl.ds(base, 8), :] = to_right[j] * inverse
            left_ref[j, pl.ds(base, 8), :] = to_left * inverse
            down_ref[j, pl.ds(base, 8), :] = to_down * inverse
            up_ref[j, pl.ds(base, 8), :] = to_up * inverse
            for c in range(chans):
                g0_ref[c, j, pl.ds(base, 8), :] = g0_ref[c, j, pl.ds(base, 8), :] * inverse
        return carry

    lax.fori_loop(0, total // 8, coefficients, 0)

    coefs = (right_ref, left_ref, down_ref, up_ref)
    horner(g0_ref, (work_a, work_b), z0_ref, coefs, 1, rows, chans, tiles, SWEEPS - 1)
    sum0, sum1 = residual_step(g0_ref, z0_ref, g1_ref, coefs, diag_ref, SWEEPS, rows, chans, tiles, own_tiles)
    horner(g1_ref, (work_a, work_b), f1_ref, coefs, SWEEPS + 1, rows, chans, tiles, SWEEPS - 1)
    sum2, sum3 = residual_step(g1_ref, f1_ref, g2_ref, coefs, diag_ref, 2 * SWEEPS, rows, chans, tiles, own_tiles)
    row = lax.broadcasted_iota(jnp.int32, (8, LANES), 0)
    sums = zero
    for k, part in enumerate((sum0, sum1, sum2, sum3)):
        sums = jnp.where(row == k, jnp.sum(part), sums)
    sums_ref[...] = sums


def second_kernel(
    scalars_ref, right_ref, left_ref, down_ref, up_ref, diag_ref, g0_ref, z0_ref, g1_ref, f1_ref, g2_ref,
    solution_ref, residual_ref, smoothed_ref, work_a, work_b,
):
    chans, rows, cols = solution_ref.shape
    own_tiles = cols // LANES
    tiles = own_tiles + 1
    coefs = (right_ref, left_ref, down_ref, up_ref)
    degree = SWEEPS - 1
    source = horner(g2_ref, (work_a, work_b), None, coefs, 2 * SWEEPS + 1, rows, chans, tiles, degree - 1)
    add = chebyshev_polynomial()[0]
    x0, x1, r0, r1, r2, s0, s1, s2 = [scalars_ref[k] for k in range(8)]

    def body(t, carry):
        base, _, moved = stencil(source, coefs, t + HALO // 8, chans, tiles)
        at = pl.multiple_of(8 * t, 8)
        for j in range(own_tiles):
            diag = diag_ref[j, pl.ds(base, 8), :]
            for c in range(chans):
                g0 = g0_ref[c, j, pl.ds(base, 8), :]
                g1 = g1_ref[c, j, pl.ds(base, 8), :]
                g2 = g2_ref[c, j, pl.ds(base, 8), :]
                z0 = z0_ref[c, j, pl.ds(base, 8), :]
                f1 = f1_ref[c, j, pl.ds(base, 8), :]
                f2 = moved[c][j] + add * g2
                here = (c, pl.ds(at, 8), pl.ds(j * LANES, LANES))
                solution_ref[here] = x0 * z0 + x1 * f1
                residual_ref[here] = diag * (r0 * g0 + r1 * g1 + r2 * g2)
                smoothed_ref[here] = s0 * z0 + s1 * f1 + s2 * f2
        return carry

    lax.fori_loop(0, rows // 8, body, 0)


def combine(sums):
    n0, n1, n2, n3 = [sums[k] for k in range(4)]
    spread = n0 - n1
    keep = -n1 / spread
    step = n0 / spread
    beta = (n0 * n2 - n1 * n1) / (spread * spread)
    along = keep + beta
    curvature = along * along * spread + 2.0 * along * step * (n1 - n2) + step * step * (n2 - n3)
    scaled = n0 * beta / curvature
    first_size = step * MIX
    second_size = scaled * MIX
    x0 = first_size + second_size * along
    x1 = second_size * step
    r0 = keep - scaled * along
    r1 = step + scaled * (along - step)
    r2 = scaled * step
    return jnp.stack([x0, x1, r0, r1, r2, r0, r1, r2])


def per_device(source, weight, seam_right, seam_down, offsets):
    chans, rows, cols = source.shape
    row_axis, col_axis = lax.axis_size("row"), lax.axis_size("col")
    row_at, col_at = lax.axis_index("row"), lax.axis_index("col")
    last_row = row_at == row_axis - 1
    last_col = col_at == col_axis - 1
    per_tile = cols // TILE
    shift = lax.dynamic_slice(
        offsets, (row_at * rows // TILE, col_at * per_tile, 0), (1, per_tile, chans)
    )[0].T.astype(jnp.float32) / offset_unit
    shift_cols = jnp.repeat(shift, TILE, axis=1)[:, None, :]

    right_side = source + shift_cols
    row_number = lax.broadcasted_iota(jnp.int32, (rows, cols), 0)
    col_number = lax.broadcasted_iota(jnp.int32, (rows, cols), 1)
    cond_right = jnp.where(
        jnp.logical_and(last_col, col_number == cols - 1), 0.0, 1.0 - seam_damping * seam_right.astype(jnp.float32)
    )
    cond_down = jnp.where(
        jnp.logical_and(last_row, row_number == rows - 1), 0.0, 1.0 - seam_damping * seam_down.astype(jnp.float32)
    )

    def planes(at_rows, at_cols):
        return jnp.concatenate(
            [right_side[:, at_rows, at_cols]]
            + [v[None, at_rows, at_cols] for v in (weight, cond_right, cond_down)],
            axis=0,
        )

    every = slice(None)
    up = [(i, i + 1) for i in range(row_axis - 1)]
    down = [(j, i) for i, j in up]
    top = lax.ppermute(planes(slice(rows - HALO, rows), every), "row", up)
    bottom = lax.ppermute(planes(slice(0, HALO), every), "row", down)

    def side(at_cols):
        return jnp.concatenate([top[:, :, at_cols], planes(every, at_cols), bottom[:, :, at_cols]], axis=1)

    ahead = [(i, i + 1) for i in range(col_axis - 1)]
    back = [(j, i) for i, j in ahead]
    before = lax.ppermute(side(slice(cols - LANES, cols)), "col", ahead)
    after = lax.ppermute(side(slice(0, LANES)), "col", back)

    flags = jnp.stack([last_row, last_col]).astype(jnp.int32)
    tiles = cols // LANES + 1
    height = rows + 2 * HALO + 2 * PAD
    plane = jax.ShapeDtypeStruct((tiles, height, LANES), jnp.float32)
    field = jax.ShapeDtypeStruct((chans, tiles, height, LANES), jnp.float32)
    in_vmem = pl.BlockSpec(memory_space=pltpu.VMEM)
    in_smem = pl.BlockSpec(memory_space=pltpu.SMEM)
    work = [pltpu.VMEM(field.shape, jnp.float32)] * 2
    params = pltpu.CompilerParams(vmem_limit_bytes=VMEM_LIMIT)
    *basis, sums = pl.pallas_call(
        first_kernel,
        out_shape=[plane] * 5 + [field] * 5 + [jax.ShapeDtypeStruct((8, LANES), jnp.float32)],
        in_specs=[in_smem] * 2 + [in_vmem] * 8,
        out_specs=[in_vmem] * 11,
        scratch_shapes=[pltpu.VMEM(plane.shape, jnp.float32)] * 2 + work,
        compiler_params=params,
    )(flags, shift, source, weight, seam_right, seam_down, top, bottom, before, after)

    total = lax.psum(sums[:4, 0], ("row", "col"))
    outcome = jax.ShapeDtypeStruct(source.shape, jnp.float32)
    return pl.pallas_call(
        second_kernel,
        out_shape=[outcome] * 3,
        in_specs=[in_smem] + [in_vmem] * 10,
        out_specs=[in_vmem] * 3,
        scratch_shapes=work,
        compiler_params=params,
    )(combine(total), *basis)


def solution(mesh):
    placed = (
        P(None, ("band", "row"), "col"),
        P(("band", "row"), "col"),
        P(("band", "row"), "col"),
        P(("band", "row"), "col"),
        P("band", None, None),
    )
    return jax.shard_map(
        per_device,
        mesh=mesh,
        in_specs=placed,
        out_specs=(
            P(None, ("band", "row"), "col"),
            P(None, ("band", "row"), "col"),
            P(None, ("band", "row"), "col"),
        ),
        check_vma=False,
    )
```

```python
import functools

import jax
import jax.numpy as jnp
from jax import lax
from jax.experimental import pallas as pl
from jax.experimental.pallas import tpu as pltpu
from jax.sharding import PartitionSpec as P

TILE = 256
SWEEPS = 8
LANES = 128
HALO = 24
PAD = 8

seam_damping = 0.8
offset_unit = 32.0
spectrum_low = 0.08
spectrum_high = 2.0
MIX = 2.4

VMEM_LIMIT = 28 * 1024 * 1024


def chebyshev_polynomial():
    centre = (spectrum_high + spectrum_low) / 2.0
    radius = (spectrum_high - spectrum_low) / 2.0
    sigma = centre / radius
    size = SWEEPS
    update = [1.0 / centre] + [0.0] * (size - 1)
    smoothed = list(update)
    rho = 1.0 / sigma
    for _ in range(SWEEPS - 1):
        remainder = [-s for s in smoothed]
        remainder[0] += 1.0
        for k in range(size - 1):
            remainder[k + 1] += smoothed[k]
        following = 1.0 / (2.0 * sigma - rho)
        update = [following * rho * u + 2.0 * following / radius * r for u, r in zip(update, remainder)]
        smoothed = [s + u for s, u in zip(smoothed, update)]
        rho = following
    return smoothed


def tile_range(application, rows):
    low = 1 + application
    high = rows + 2 * HALO - 1 - application
    return low // 8, -(-high // 8)


def stencil(z_ref, coefs, tile, chans, tiles, emit):
    base = pl.multiple_of(PAD + 8 * tile, 8)
    lane = lax.broadcasted_iota(jnp.int32, (8, LANES), 1)
    first, last = (lane == 0, lane == LANES - 1)
    right_ref, left_ref, down_ref, up_ref = coefs
    every = range(chans)

    def here(j):
        return [z_ref[c, j, pl.ds(base, 8), :] for c in every]

    def ahead_of(values):
        return [pltpu.roll(v, LANES - 1, 1) for v in values]

    def behind_of(values):
        return [pltpu.roll(v, 1, 1) for v in values]

    behind_before = behind_of(here(tiles - 1))
    centre = here(0)
    ahead_first = ahead_now = ahead_of(centre)
    for j in range(tiles):
        behind_now = behind_of(centre)
        if j + 1 < tiles:
            centre_next = here(j + 1)
            ahead_next = ahead_of(centre_next)
        else:
            centre_next, ahead_next = None, ahead_first
        a_right = right_ref[j, pl.ds(base, 8), :]
        a_left = left_ref[j, pl.ds(base, 8), :]
        a_down = down_ref[j, pl.ds(base, 8), :]
        a_up = up_ref[j, pl.ds(base, 8), :]
        for c in every:
            to_right = jnp.where(last, ahead_next[c], ahead_now[c])
            to_left = jnp.where(first, behind_before[c], behind_now[c])
            below = z_ref[c, j, pl.ds(base + 1, 8), :]
            above = z_ref[c, j, pl.ds(base - 1, 8), :]
            moved = (a_right * to_right + a_left * to_left) + (a_down * below + a_up * above)
            emit(base, c, j, centre[c], moved)
        behind_before, centre, ahead_now = behind_now, centre_next, ahead_next


def over_tiles(low, high, body, carry):
    pairs = (high - low) // 2

    def pair(k, carry):
        return body(low + 2 * k + 1, body(low + 2 * k, carry))

    carry = lax.fori_loop(0, pairs, pair, carry)
    return body(high - 1, carry) if (high - low) % 2 else carry


def horner(g_ref, buffers, final_ref, coefs, first_application, rows, chans, tiles, count):
    poly = chebyshev_polynomial()
    degree = SWEEPS - 1
    source = g_ref
    for k in range(count):
        target = final_ref if k == degree - 1 else buffers[k % 2]
        low, high = tile_range(first_application + k, rows)
        scale = poly[degree] if k == 0 else None
        add = poly[degree - 1 - k]

        def body(tile, carry, source=source, target=target, scale=scale, add=add):
            def emit(base, c, j, centre, moved):
                g = centre if scale is not None else g_ref[c, j, pl.ds(base, 8), :]
                value = moved if scale is None else scale * moved
                target[c, j, pl.ds(base, 8), :] = value + add * g

            stencil(source, coefs, tile, chans, tiles, emit)
            return carry

        over_tiles(low, high, body, 0)
        source = target
    return source


def residual_step(g_ref, z_ref, next_ref, coefs, diag_ref, application, rows, chans, tiles, own_tiles):
    low, high = tile_range(application, rows)
    own_low = HALO // 8
    own_high = own_low + rows // 8

    def body(tile, carry, own):
        sums = list(carry)

        def emit(base, c, j, centre, moved):
            g = g_ref[c, j, pl.ds(base, 8), :]
            following = g - MIX * (centre - moved)
            next_ref[c, j, pl.ds(base, 8), :] = following
            if own and j < own_tiles:
                dz = diag_ref[j, pl.ds(base, 8), :] * centre
                sums[0] += g * dz
                sums[1] += following * dz

        stencil(z_ref, coefs, tile, chans, tiles, emit)
        return tuple(sums)

    zero = jnp.zeros((8, LANES), jnp.float32)
    over_tiles(low, own_low, functools.partial(body, own=False), (zero, zero))
    over_tiles(own_high, high, functools.partial(body, own=False), (zero, zero))
    return over_tiles(own_low, own_high, functools.partial(body, own=True), (zero, zero))


SLOT = 32
SLOTS = LANES // SLOT


def edges_kernel(flags_ref, shift_ref, src_ref, weight_ref, seam_right_ref, seam_down_ref, *outs):
    first_rows, last_rows, first_cols, last_cols, first_first, first_last, last_first, last_last = outs
    chans, rows, cols = src_ref.shape
    own_tiles = cols // LANES
    lane = lax.broadcasted_iota(jnp.int32, (8, LANES), 1)
    for t in range(rows // 8):
        packs = {}
        for j in range(own_tiles):
            edge_row = t < HALO // 8 or t >= (rows - HALO) // 8
            if not edge_row and j not in (0, own_tiles - 1):
                continue
            planes = own_planes(
                flags_ref, shift_ref, src_ref, weight_ref, seam_right_ref, seam_down_ref, 8 * t, j
            )
            if edge_row:
                for p, plane in enumerate(planes):
                    if t < HALO // 8:
                        first_rows[p, 8 * t:8 * t + 8, j * LANES:(j + 1) * LANES] = plane
                    if t >= (rows - HALO) // 8:
                        at = 8 * t - (rows - HALO)
                        last_rows[p, at:at + 8, j * LANES:(j + 1) * LANES] = plane
            for side, cols_ref in ((0, first_cols), (own_tiles - 1, last_cols)):
                if j != side:
                    continue
                start = 0 if side == 0 else LANES - SLOT
                packed = [None] * (-(-len(planes) // SLOTS))
                for p, plane in enumerate(planes):
                    slot = p % SLOTS
                    by = (slot * SLOT - start) % LANES
                    moved = pltpu.roll(plane, by, 1) if by else plane
                    at = p // SLOTS
                    packed[at] = moved if slot == 0 else jnp.where(lane < slot * SLOT, packed[at], moved)
                for q, value in enumerate(packed):
                    cols_ref[q, 8 * t:8 * t + 8, :] = value
                    if t < HALO // 8:
                        (first_first if side == 0 else first_last)[q, 8 * t:8 * t + 8, :] = value
                    if t >= (rows - HALO) // 8:
                        at = 8 * t - (rows - HALO)
                        (last_first if side == 0 else last_last)[q, at:at + 8, :] = value


def own_planes(flags_ref, shift_ref, src_ref, weight_ref, seam_right_ref, seam_down_ref, at, j):
    chans, rows, cols = src_ref.shape
    lane = lax.broadcasted_iota(jnp.int32, (8, LANES), 1)
    sub = lax.broadcasted_iota(jnp.int32, (8, LANES), 0)
    here = pl.ds(at, 8), pl.ds(j * LANES, LANES)
    planes = [src_ref[c, here[0], here[1]] + shift_ref[c, j * LANES // TILE] for c in range(chans)]
    planes.append(weight_ref[here[0], here[1]])
    to_right = 1.0 - seam_damping * seam_right_ref[here[0], here[1]].astype(jnp.float32)
    if j == cols // LANES - 1:
        to_right = jnp.where(lane == jnp.where(flags_ref[1] == 1, LANES - 1, -1), 0.0, to_right)
    to_down = 1.0 - seam_damping * seam_down_ref[here[0], here[1]].astype(jnp.float32)
    bottom = (at + sub) == jnp.where(flags_ref[0] == 1, rows - 1, -1)
    return planes + [to_right, jnp.where(bottom, 0.0, to_down)]


def first_kernel(
    flags_ref, shift_ref, src_ref, weight_ref, seam_right_ref, seam_down_ref,
    top_ref, bottom_ref, before_ref, after_ref, top_before_ref, top_after_ref, bottom_before_ref, bottom_after_ref,
    right_ref, left_ref, down_ref, up_ref, diag_ref, g0_ref, z0_ref, g1_ref, f1_ref, g2_ref, sums_ref,
    cond_right, cond_down, work_a, work_b,
):
    chans, rows, cols = src_ref.shape
    own_tiles = cols // LANES
    tiles = own_tiles + 1
    total = rows + 2 * HALO
    lane = lax.broadcasted_iota(jnp.int32, (8, LANES), 1)
    zero = jnp.zeros((8, LANES), jnp.float32)

    for j in range(tiles):
        for at in (0, PAD + total):
            cond_down[j, pl.ds(at, 8), :] = zero
            for c in range(chans):
                for ref in (g0_ref, g1_ref, work_a, work_b, z0_ref, f1_ref):
                    ref[c, j, pl.ds(at, 8), :] = zero

    def put(base, j, planes):
        for c in range(chans):
            g0_ref[c, j, pl.ds(base, 8), :] = planes[c]
        diag_ref[j, pl.ds(base, 8), :] = planes[chans]
        cond_right[j, pl.ds(base, 8), :] = planes[chans + 1]
        cond_down[j, pl.ds(base, 8), :] = planes[chans + 2]

    def edge_rows(slab_ref, start):
        def body(t, carry):
            at = pl.multiple_of(8 * t, 8)
            base = pl.multiple_of(PAD + start + 8 * t, 8)
            for j in range(own_tiles):
                put(base, j, [slab_ref[p, pl.ds(at, 8), j * LANES:(j + 1) * LANES] for p in range(chans + 3)])
            return carry

        lax.fori_loop(0, HALO // 8, body, 0)

    edge_rows(top_ref, 0)
    edge_rows(bottom_ref, HALO + rows)

    def own_rows(t, carry):
        at = pl.multiple_of(8 * t, 8)
        base = pl.multiple_of(PAD + HALO + 8 * t, 8)
        for j in range(own_tiles):
            put(
                base, j,
                own_planes(flags_ref, shift_ref, src_ref, weight_ref, seam_right_ref, seam_down_ref, at, j),
            )
        return carry

    lax.fori_loop(0, rows // 8, own_rows, 0)

    def side_columns(left_from, right_from, start, count):
        def body(t, carry):
            at = pl.multiple_of(8 * t, 8)
            base = pl.multiple_of(PAD + start + 8 * t, 8)
            planes = []
            for p in range(chans + 3):
                lefts = left_from[p // SLOTS, pl.ds(at, 8), :]
                rights = right_from[p // SLOTS, pl.ds(at, 8), :]
                slot = p % SLOTS
                lefts = pltpu.roll(lefts, (LANES - SLOT - slot * SLOT) % LANES, 1) if slot != SLOTS - 1 else lefts
                rights = pltpu.roll(rights, (-slot * SLOT) % LANES, 1) if slot else rights
                planes.append(jnp.where(lane < SLOT, rights, jnp.where(lane >= LANES - SLOT, lefts, 0.0)))
            put(base, own_tiles, planes)
            return carry

        lax.fori_loop(0, count // 8, body, 0)

    side_columns(top_before_ref, top_after_ref, 0, HALO)
    side_columns(before_ref, after_ref, HALO, rows)
    side_columns(bottom_before_ref, bottom_after_ref, HALO + rows, HALO)

    def coefficients(t, carry):
        base = pl.multiple_of(PAD + 8 * t, 8)
        to_right = [cond_right[j, pl.ds(base, 8), :] for j in range(tiles)]
        behind = [pltpu.roll(v, 1, 1) for v in to_right]
        for j in range(tiles):
            to_left = jnp.where(lane == 0, behind[(j - 1) % tiles], behind[j])
            to_down = cond_down[j, pl.ds(base, 8), :]
            to_up = cond_down[j, pl.ds(base - 1, 8), :]
            diag = diag_ref[j, pl.ds(base, 8), :] + to_right[j] + to_left + to_down + to_up
            inverse = 1.0 / jnp.where(diag > 0.0, diag, 1.0)
            diag_ref[j, pl.ds(base, 8), :] = diag
            right_ref[j, pl.ds(base, 8), :] = to_right[j] * inverse
            left_ref[j, pl.ds(base, 8), :] = to_left * inverse
            down_ref[j, pl.ds(base, 8), :] = to_down * inverse
            up_ref[j, pl.ds(base, 8), :] = to_up * inverse
            for c in range(chans):
                g0_ref[c, j, pl.ds(base, 8), :] = g0_ref[c, j, pl.ds(base, 8), :] * inverse
        return carry

    lax.fori_loop(0, total // 8, coefficients, 0)

    coefs = (right_ref, left_ref, down_ref, up_ref)
    horner(g0_ref, (work_a, work_b), z0_ref, coefs, 1, rows, chans, tiles, SWEEPS - 1)
    sum0, sum1 = residual_step(g0_ref, z0_ref, g1_ref, coefs, diag_ref, SWEEPS, rows, chans, tiles, own_tiles)
    horner(g1_ref, (work_a, work_b), f1_ref, coefs, SWEEPS + 1, rows, chans, tiles, SWEEPS - 1)
    sum2, sum3 = residual_step(g1_ref, f1_ref, g2_ref, coefs, diag_ref, 2 * SWEEPS, rows, chans, tiles, own_tiles)
    row = lax.broadcasted_iota(jnp.int32, (8, LANES), 0)
    sums = zero
    for k, part in enumerate((sum0, sum1, sum2, sum3)):
        sums = jnp.where(row == k, jnp.sum(part), sums)
    sums_ref[...] = sums


def second_kernel(right_ref, left_ref, down_ref, up_ref, g2_ref, f2_ref, work_a, work_b):
    chans, tiles = g2_ref.shape[:2]
    rows = g2_ref.shape[2] - 2 * PAD - 2 * HALO
    coefs = (right_ref, left_ref, down_ref, up_ref)
    horner(g2_ref, (work_a, work_b), f2_ref, coefs, 2 * SWEEPS + 1, rows, chans, tiles, SWEEPS - 1)


def combine(n0, n1, n2, n3):
    spread = n0 - n1
    keep = -n1 / spread
    step = n0 / spread
    beta = (n0 * n2 - n1 * n1) / (spread * spread)
    along = keep + beta
    curvature = along * along * spread + 2.0 * along * step * (n1 - n2) + step * step * (n2 - n3)
    scaled = n0 * beta / curvature
    first_size = step * MIX
    second_size = scaled * MIX
    x0 = first_size + second_size * along
    x1 = second_size * step
    r0 = keep - scaled * along
    r1 = step + scaled * (along - step)
    r2 = scaled * step
    return x0, x1, r0, r1, r2


def third_kernel(
    sums_ref, diag_ref, g0_ref, z0_ref, g1_ref, f1_ref, g2_ref, f2_ref, solution_ref, residual_ref, smoothed_ref
):
    chans, rows, cols = solution_ref.shape
    own_tiles = cols // LANES
    total = jnp.sum(sums_ref[...], axis=0)
    x0, x1, r0, r1, r2 = combine(*[jnp.broadcast_to(total[k:k + 1, :], (8, LANES)) for k in range(4)])

    def body(t, carry):
        base = pl.multiple_of(PAD + HALO + 8 * t, 8)
        at = pl.multiple_of(8 * t, 8)
        for j in range(own_tiles):
            diag = diag_ref[j, pl.ds(base, 8), :]
            for c in range(chans):
                g0, g1, g2, z0, f1, f2 = [
                    ref[c, j, pl.ds(base, 8), :] for ref in (g0_ref, g1_ref, g2_ref, z0_ref, f1_ref, f2_ref)
                ]
                here = (c, pl.ds(at, 8), pl.ds(j * LANES, LANES))
                solution_ref[here] = x0 * z0 + x1 * f1
                residual_ref[here] = diag * (r0 * g0 + r1 * g1 + r2 * g2)
                smoothed_ref[here] = r0 * z0 + r1 * f1 + r2 * f2
        return carry

    lax.fori_loop(0, rows // 8, body, 0)


def per_device(source, weight, seam_right, seam_down, offsets):
    chans, rows, cols = source.shape
    row_axis, col_axis = lax.axis_size("row"), lax.axis_size("col")
    row_at, col_at = lax.axis_index("row"), lax.axis_index("col")
    flags = jnp.stack([row_at == row_axis - 1, col_at == col_axis - 1]).astype(jnp.int32)
    per_tile = cols // TILE
    shift = lax.dynamic_slice(
        offsets, (row_at * rows // TILE, col_at * per_tile, 0), (1, per_tile, chans)
    )[0].T.astype(jnp.float32) / offset_unit

    in_vmem = pl.BlockSpec(memory_space=pltpu.VMEM)
    in_smem = pl.BlockSpec(memory_space=pltpu.SMEM)
    params = pltpu.CompilerParams(vmem_limit_bytes=VMEM_LIMIT)
    own = (flags, shift, source, weight, seam_right, seam_down)
    own_specs = [in_smem] * 2 + [in_vmem] * 4

    def shaped(*shape):
        return jax.ShapeDtypeStruct(shape, jnp.float32)

    packs = -(-(chans + 3) // SLOTS)
    first_rows, last_rows, first_cols, last_cols, first_first, first_last, last_first, last_last = pl.pallas_call(
        edges_kernel,
        out_shape=[shaped(chans + 3, HALO, cols)] * 2
        + [shaped(packs, rows, LANES)] * 2
        + [shaped(packs, HALO, LANES)] * 4,
        in_specs=own_specs,
        out_specs=[in_vmem] * 8,
        compiler_params=params,
    )(*own)

    def moved(value, down, right):
        pairs = [
            (r * col_axis + c, (r + down) * col_axis + c + right)
            for r in range(row_axis)
            for c in range(col_axis)
            if 0 <= r + down < row_axis and 0 <= c + right < col_axis
        ]
        return lax.ppermute(value, ("row", "col"), pairs)

    halo = (
        moved(last_rows, 1, 0),
        moved(first_rows, -1, 0),
        moved(last_cols, 0, 1),
        moved(first_cols, 0, -1),
        moved(last_last, 1, 1),
        moved(last_first, 1, -1),
        moved(first_last, -1, 1),
        moved(first_first, -1, -1),
    )

    tiles = cols // LANES + 1
    height = rows + 2 * HALO + 2 * PAD
    plane = shaped(tiles, height, LANES)
    field = shaped(chans, tiles, height, LANES)
    work = [pltpu.VMEM(field.shape, jnp.float32)] * 2
    right, left, down, up, diag, g0, z0, g1, f1, g2, sums = pl.pallas_call(
        first_kernel,
        out_shape=[plane] * 5 + [field] * 5 + [shaped(8, LANES)],
        in_specs=own_specs + [in_vmem] * 8,
        out_specs=[in_vmem] * 11,
        scratch_shapes=[pltpu.VMEM(plane.shape, jnp.float32)] * 2 + work,
        compiler_params=params,
    )(*own, *halo)

    every_sum = lax.all_gather(sums, ("row", "col"))
    f2 = pl.pallas_call(
        second_kernel,
        out_shape=field,
        in_specs=[in_vmem] * 5,
        out_specs=in_vmem,
        scratch_shapes=work,
        compiler_params=params,
        cost_estimate=pl.CostEstimate(flops=10**9, bytes_accessed=10**7, transcendentals=0),
    )(right, left, down, up, g2)
    return pl.pallas_call(
        third_kernel,
        out_shape=[shaped(chans, rows, cols)] * 3,
        in_specs=[in_vmem] * 8,
        out_specs=[in_vmem] * 3,
        compiler_params=params,
    )(every_sum, diag, g0, z0, g1, f1, g2, f2)


def solution(mesh):
    placed = (
        P(None, ("band", "row"), "col"),
        P(("band", "row"), "col"),
        P(("band", "row"), "col"),
        P(("band", "row"), "col"),
        P("band", None, None),
    )
    return jax.shard_map(
        per_device,
        mesh=mesh,
        in_specs=placed,
        out_specs=(
            P(None, ("band", "row"), "col"),
            P(None, ("band", "row"), "col"),
            P(None, ("band", "row"), "col"),
        ),
        check_vma=False,
    )
```

```python
import jax
import jax.numpy as jnp
from jax import lax
from jax.experimental import pallas as pl
from jax.experimental.pallas import tpu as pltpu
from jax.sharding import PartitionSpec as P

TILE = 256
SWEEPS = 8
SUBS = 8
LANES = 128
HALO = 24
SLOT = 32
SLOTS = LANES // SLOT

seam_damping = 0.8
offset_unit = 32.0
spectrum_low = 0.08
spectrum_high = 2.0
MIX = 2.4

VMEM_LIMIT = 28 * 1024 * 1024


def chebyshev_polynomial():
    centre = (spectrum_high + spectrum_low) / 2.0
    radius = (spectrum_high - spectrum_low) / 2.0
    sigma = centre / radius
    size = SWEEPS
    update = [1.0 / centre] + [0.0] * (size - 1)
    smoothed = list(update)
    rho = 1.0 / sigma
    for _ in range(SWEEPS - 1):
        remainder = [-s for s in smoothed]
        remainder[0] += 1.0
        for k in range(size - 1):
            remainder[k + 1] += smoothed[k]
        following = 1.0 / (2.0 * sigma - rho)
        update = [following * rho * u + 2.0 * following / radius * r for u, r in zip(update, remainder)]
        smoothed = [s + u for s, u in zip(smoothed, update)]
        rho = following
    return smoothed


def lane_index():
    return lax.broadcasted_iota(jnp.int32, (SUBS, LANES), 1)


def own_kernel(
    flags_ref, shift_ref, src_hbm, weight_hbm, seam_right_hbm, seam_down_hbm,
    own_ref, first_ref, last_ref,
    src_ref, weight_ref, seam_right_ref, seam_down_ref, sems,
):
    chans, rows, cols = src_ref.shape
    own_tiles = cols // LANES
    copies = [pltpu.make_async_copy(src_hbm.at[c], src_ref.at[c], sems.at[c]) for c in range(chans)]
    for k, (there, here) in enumerate(
        ((weight_hbm, weight_ref), (seam_right_hbm, seam_right_ref), (seam_down_hbm, seam_down_ref))
    ):
        copies.append(pltpu.make_async_copy(there, here, sems.at[chans + k]))
    for copy in copies:
        copy.start()
    for copy in copies:
        copy.wait()
    lane = lane_index()
    sub = lax.broadcasted_iota(jnp.int32, (SUBS, LANES), 0)
    last_row = jnp.where(flags_ref[0] == 1, rows - 1, -1)
    last_lane = jnp.where(flags_ref[1] == 1, LANES - 1, -1)

    def body(t, carry):
        at = pl.multiple_of(SUBS * t, SUBS)
        here = pl.ds(at, SUBS)
        for j in range(own_tiles):
            there = pl.ds(j * LANES, LANES)
            planes = [src_ref[c, here, there] + shift_ref[c, j * LANES // TILE] for c in range(chans)]
            planes.append(weight_ref[here, there])
            to_right = 1.0 - seam_damping * seam_right_ref[here, there].astype(jnp.float32)
            if j == own_tiles - 1:
                to_right = jnp.where(lane == last_lane, 0.0, to_right)
            to_down = 1.0 - seam_damping * seam_down_ref[here, there].astype(jnp.float32)
            planes += [to_right, jnp.where(at + sub == last_row, 0.0, to_down)]
            for p, plane in enumerate(planes):
                own_ref[p, j, here, :] = plane
            for side, start, cols_ref in ((0, 0, first_ref), (own_tiles - 1, LANES - SLOT, last_ref)):
                if j != side:
                    continue
                packed = [None] * (-(-len(planes) // SLOTS))
                for p, plane in enumerate(planes):
                    slot = p % SLOTS
                    by = (slot * SLOT - start) % LANES
                    moved = pltpu.roll(plane, by, 1) if by else plane
                    k = p // SLOTS
                    packed[k] = moved if slot == 0 else jnp.where(lane < slot * SLOT, packed[k], moved)
                for k, value in enumerate(packed):
                    cols_ref[k, here, :] = value
        return carry

    lax.fori_loop(0, rows // SUBS, body, 0)


def spread(b_right_ref, b_down_ref, z_ref, c, emit):
    tiles, height = z_ref.shape[1:3]
    steps = height // SUBS
    lane = lane_index()
    first, last = (lane == 0, lane == LANES - 1)

    def at(i):
        return pl.ds(i * SUBS, SUBS)

    def z_at(i, j):
        return z_ref[c, j, at(i), :]

    from_above = [pltpu.roll(b_down_ref[j, at(steps - 1), :] * z_at(steps - 1, j), 1, 0) for j in range(tiles)]
    centre = [z_at(0, j) for j in range(tiles)]
    wrapped = [pltpu.roll(v, SUBS - 1, 0) for v in centre]
    for i in range(steps):
        below = [z_at(i + 1, j) for j in range(tiles)] if i + 1 < steps else wrapped
        ahead_first = ahead_now = pltpu.roll(centre[0], LANES - 1, 1)
        b_last = b_right_ref[tiles - 1, at(i), :]
        pushed_before = pltpu.roll(b_last * centre[tiles - 1], 1, 1)
        for j in range(tiles):
            b_right = b_right_ref[j, at(i), :] if j + 1 < tiles else b_last
            b_down = b_down_ref[j, at(i), :]
            ahead_next = pltpu.roll(centre[j + 1], LANES - 1, 1) if j + 1 < tiles else ahead_first
            pushed_now = pltpu.roll(b_right * centre[j], 1, 1)
            to_right = jnp.where(last, ahead_next, ahead_now)
            from_left = jnp.where(first, pushed_before, pushed_now)
            moved = (b_right * to_right + from_left) + (b_down * below[j] + from_above[j])
            from_above[j] = b_down * centre[j]
            emit(i, j, centre[j], moved)
            ahead_now, pushed_before = ahead_next, pushed_now
        centre = below


def precondition(b_right_ref, b_down_ref, g_ref, z_ref, work_ref, c):
    poly = chebyshev_polynomial()
    degree = SWEEPS - 1

    def at(i):
        return pl.ds(i * SUBS, SUBS)

    def first(i, j, centre, moved):
        z_ref[c, j, at(i), :] = poly[degree] * moved + poly[degree - 1] * centre

    spread(b_right_ref, b_down_ref, g_ref, c, first)

    def pair(k, carry):
        adds = []
        for half in range(2):
            value = jnp.float32(poly[half])
            for later in range(1, (degree - 1) // 2):
                value = jnp.where(k == (degree - 1) // 2 - 1 - later, jnp.float32(poly[2 * later + half]), value)
            adds.append(value)

        def one(target, add):
            def emit(i, j, centre, moved):
                target[c, j, at(i), :] = moved + add * g_ref[c, j, at(i), :]

            return emit

        spread(b_right_ref, b_down_ref, z_ref, c, one(work_ref, adds[1]))
        spread(b_right_ref, b_down_ref, work_ref, c, one(z_ref, adds[0]))
        return carry

    lax.fori_loop(0, (degree - 1) // 2, pair, 0)


def own_bounds(steps, rows, i):
    return -(-(HALO - i) // steps), (HALO + rows - 1 - i) // steps


def next_residual(b_right_ref, b_down_ref, g_ref, z_ref, next_ref, c, rows):
    tiles, height = g_ref.shape[1:3]
    steps = height // SUBS
    sums = {}

    def emit(i, j, centre, moved):
        at = pl.ds(i * SUBS, SUBS)
        g = g_ref[c, j, at, :]
        following = g - MIX * (centre - moved)
        next_ref[c, j, at, :] = following
        if j + 1 < tiles:
            bounds = own_bounds(steps, rows, i)
            now = (g * centre, following * centre)
            before = sums.get(bounds)
            sums[bounds] = now if before is None else (before[0] + now[0], before[1] + now[1])

    spread(b_right_ref, b_down_ref, z_ref, c, emit)
    sub = lax.broadcasted_iota(jnp.int32, (SUBS, LANES), 0)
    total = [jnp.zeros((SUBS, LANES), jnp.float32)] * 2
    for (low, high), parts in sums.items():
        inside = jnp.logical_and(sub >= low, sub <= high)
        total = [t + jnp.where(inside, p, 0.0) for t, p in zip(total, parts)]
    return total


def first_kernel(
    own_ref, top_ref, bottom_ref, before_ref, after_ref,
    b_right_ref, b_down_ref, scale_ref, root_ref, g0_ref, z0_ref, g1_ref, f1_ref, g2_ref, sums_ref,
    natural, work_ref,
):
    planes, own_tiles, rows = own_ref.shape[:3]
    chans = planes - 3
    tiles = own_tiles + 1
    height = rows + 2 * HALO
    steps = height // SUBS
    packs = before_ref.shape[0]
    lane = lane_index()

    def copy_own(t, carry):
        here = pl.ds(pl.multiple_of(SUBS * t, SUBS), SUBS)
        there = pl.ds(pl.multiple_of(HALO + SUBS * t, SUBS), SUBS)
        for p in range(planes):
            for j in range(own_tiles):
                natural[p, j, there, :] = own_ref[p, j, here, :]
        return carry

    lax.fori_loop(0, rows // SUBS, copy_own, 0)
    main = planes * own_tiles * HALO
    for slab, start in ((top_ref, 0), (bottom_ref, HALO + rows)):
        for p in range(planes):
            for j in range(own_tiles):
                at = (p * own_tiles + j) * HALO
                natural[p, j, start:start + HALO, :] = slab[at:at + HALO, :]

    def unpack(p, lefts, rights):
        slot = p % SLOTS
        if slot != SLOTS - 1:
            lefts = pltpu.roll(lefts, LANES - SLOT - slot * SLOT, 1)
        if slot:
            rights = pltpu.roll(rights, LANES - slot * SLOT, 1)
        return jnp.where(lane < SLOT, rights, jnp.where(lane >= LANES - SLOT, lefts, 0.0))

    def side_own(t, carry):
        here = pl.ds(pl.multiple_of(SUBS * t, SUBS), SUBS)
        there = pl.ds(pl.multiple_of(HALO + SUBS * t, SUBS), SUBS)
        for p in range(planes):
            natural[p, own_tiles, there, :] = unpack(p, before_ref[p // SLOTS, here, :], after_ref[p // SLOTS, here, :])
        return carry

    lax.fori_loop(0, rows // SUBS, side_own, 0)
    for slab, start in ((top_ref, 0), (bottom_ref, HALO + rows)):
        for t in range(HALO // SUBS):
            for p in range(planes):
                at = main + (p // SLOTS) * HALO + t * SUBS
                lefts = slab[at:at + SUBS, :]
                at += packs * HALO
                rights = slab[at:at + SUBS, :]
                natural[p, own_tiles, start + t * SUBS:start + (t + 1) * SUBS, :] = unpack(p, lefts, rights)

    def at(i):
        return pl.ds(i * SUBS, SUBS)

    def interleaved(p, i, j):
        return natural[p, j, pl.ds(i, SUBS, stride=steps), :]

    to_up = [pltpu.roll(interleaved(chans + 2, steps - 1, j), 1, 0) for j in range(tiles)]
    for i in range(steps):
        to_right = [interleaved(chans + 1, i, j) for j in range(tiles)]
        behind = [pltpu.roll(v, 1, 1) for v in to_right]
        for j in range(tiles):
            to_left = jnp.where(lane == 0, behind[(j - 1) % tiles], behind[j])
            to_down = interleaved(chans + 2, i, j)
            diag = interleaved(chans, i, j) + to_right[j] + to_left + to_down + to_up[j]
            inside = diag > 0.0
            safe = jnp.where(inside, diag, 1.0)
            guess = lax.rsqrt(safe)
            scale = guess * (1.5 - 0.5 * safe * guess * guess)
            scale_ref[j, at(i), :] = jnp.where(inside, scale, 0.0)
            root_ref[j, at(i), :] = safe * scale
            to_up[j] = to_down
    wrapped = [pltpu.roll(scale_ref[j, at(0), :], SUBS - 1, 0) for j in range(tiles)]
    for i in range(steps):
        scale = [scale_ref[j, at(i), :] for j in range(tiles)]
        ahead = [pltpu.roll(v, LANES - 1, 1) for v in scale]
        for j in range(tiles):
            right_scale = jnp.where(lane == LANES - 1, ahead[(j + 1) % tiles], ahead[j])
            b_right_ref[j, at(i), :] = interleaved(chans + 1, i, j) * scale[j] * right_scale
            down_scale = scale_ref[j, at(i + 1), :] if i + 1 < steps else wrapped[j]
            b_down_ref[j, at(i), :] = interleaved(chans + 2, i, j) * scale[j] * down_scale
            for c in range(chans):
                g0_ref[c, j, at(i), :] = interleaved(c, i, j) * scale[j]

    def channel(c, carry):
        precondition(b_right_ref, b_down_ref, g0_ref, z0_ref, work_ref, c)
        sum0, sum1 = next_residual(b_right_ref, b_down_ref, g0_ref, z0_ref, g1_ref, c, rows)
        precondition(b_right_ref, b_down_ref, g1_ref, f1_ref, work_ref, c)
        sum2, sum3 = next_residual(b_right_ref, b_down_ref, g1_ref, f1_ref, g2_ref, c, rows)
        return tuple(a + b for a, b in zip(carry, (sum0, sum1, sum2, sum3)))

    zero = jnp.zeros((SUBS, LANES), jnp.float32)
    parts = lax.fori_loop(0, chans, channel, (zero,) * 4)
    sub = lax.broadcasted_iota(jnp.int32, (SUBS, LANES), 0)
    sums = zero
    for k, part in enumerate(parts):
        sums = jnp.where(sub == k, jnp.sum(part), sums)
    sums_ref[...] = sums


def second_kernel(b_right_ref, b_down_ref, g2_ref, f2_ref, work_ref):
    def channel(c, carry):
        precondition(b_right_ref, b_down_ref, g2_ref, f2_ref, work_ref, c)
        return carry

    lax.fori_loop(0, g2_ref.shape[0], channel, 0)


def combine(n0, n1, n2, n3):
    gap = n0 - n1
    keep = -n1 / gap
    step = n0 / gap
    beta = (n0 * n2 - n1 * n1) / (gap * gap)
    along = keep + beta
    curvature = along * along * gap + 2.0 * along * step * (n1 - n2) + step * step * (n2 - n3)
    scaled = n0 * beta / curvature
    first_size = step * MIX
    second_size = scaled * MIX
    x0 = first_size + second_size * along
    x1 = second_size * step
    r0 = keep - scaled * along
    r1 = step + scaled * (along - step)
    r2 = scaled * step
    return x0, x1, r0, r1, r2


def third_kernel(
    sums_ref, scale_ref, root_ref, g0_ref, z0_ref, g1_ref, f1_ref, g2_ref, f2_ref,
    solution_ref, residual_ref, smoothed_ref,
    natural,
):
    chans, rows, cols = solution_ref.shape
    own_tiles = cols // LANES
    steps = scale_ref.shape[1] // SUBS
    x0, x1, r0, r1, r2 = combine(*[jnp.broadcast_to(sums_ref[k:k + 1, :], (SUBS, LANES)) for k in range(4)])
    outs = (solution_ref, residual_ref, smoothed_ref)

    def channel(c, carry):
        for j in range(own_tiles):
            for i in range(steps):
                at = pl.ds(i * SUBS, SUBS)
                scale = scale_ref[j, at, :]
                root = root_ref[j, at, :]
                g0, g1, g2, z0, f1, f2 = [
                    ref[c, j, at, :] for ref in (g0_ref, g1_ref, g2_ref, z0_ref, f1_ref, f2_ref)
                ]
                there = pl.ds(i, SUBS, stride=steps)
                natural[0, j, there, :] = scale * (x0 * z0 + x1 * f1)
                natural[1, j, there, :] = root * (r0 * g0 + r1 * g1 + r2 * g2)
                natural[2, j, there, :] = scale * (r0 * z0 + r1 * f1 + r2 * f2)
        for k, ref in enumerate(outs):
            for j in range(own_tiles):
                ref[c, :, j * LANES:(j + 1) * LANES] = natural[k, j, HALO:HALO + rows, :]
        return carry

    lax.fori_loop(0, chans, channel, 0)


def sum_over(value, axis):
    size = lax.axis_size(axis)
    if size & (size - 1):
        return lax.psum(value, axis)
    step = 1
    while step < size:
        value = value + lax.ppermute(value, axis, [(i, i ^ step) for i in range(size)])
        step *= 2
    return value


def per_device(source, weight, seam_right, seam_down, offsets):
    chans, rows, cols = source.shape
    row_axis, col_axis = lax.axis_size("row"), lax.axis_size("col")
    row_at, col_at = lax.axis_index("row"), lax.axis_index("col")
    flags = jnp.stack([row_at == row_axis - 1, col_at == col_axis - 1]).astype(jnp.int32)
    per_tile = cols // TILE
    shift = lax.dynamic_slice(
        offsets, (row_at * rows // TILE, col_at * per_tile, 0), (1, per_tile, chans)
    )[0].T.astype(jnp.float32) / offset_unit

    in_vmem = pl.BlockSpec(memory_space=pltpu.VMEM)
    in_smem = pl.BlockSpec(memory_space=pltpu.SMEM)
    anywhere = pl.BlockSpec(memory_space=pl.ANY)
    params = pltpu.CompilerParams(vmem_limit_bytes=VMEM_LIMIT)

    def shaped(*shape):
        return jax.ShapeDtypeStruct(shape, jnp.float32)

    planes = chans + 3
    own_tiles = cols // LANES
    packs = -(-planes // SLOTS)
    own, first_cols, last_cols = pl.pallas_call(
        own_kernel,
        out_shape=[shaped(planes, own_tiles, rows, LANES)] + [shaped(packs, rows, LANES)] * 2,
        in_specs=[in_smem] * 2 + [anywhere] * 4,
        out_specs=[in_vmem] * 3,
        scratch_shapes=[
            pltpu.VMEM(source.shape, jnp.float32),
            pltpu.VMEM(weight.shape, jnp.float32),
            pltpu.VMEM(weight.shape, jnp.int32),
            pltpu.VMEM(weight.shape, jnp.int32),
            pltpu.SemaphoreType.DMA((planes,)),
        ],
        compiler_params=params,
    )(flags, shift, source, weight, seam_right, seam_down)

    onward = [(i, i + 1) for i in range(col_axis - 1)]
    back = [(j, i) for i, j in onward]
    before = lax.ppermute(last_cols, "col", onward)
    after = lax.ppermute(first_cols, "col", back)

    def slab(low, high):
        parts = [own[:, :, low:high], before[:, low:high], after[:, low:high]]
        return jnp.concatenate([part.reshape(-1, LANES) for part in parts], axis=0)

    down = [(i, i + 1) for i in range(row_axis - 1)]
    up = [(j, i) for i, j in down]
    top = lax.ppermute(slab(rows - HALO, rows), "row", down)
    bottom = lax.ppermute(slab(0, HALO), "row", up)

    tiles = own_tiles + 1
    height = rows + 2 * HALO
    plane = shaped(tiles, height, LANES)
    field = shaped(chans, tiles, height, LANES)
    work = pltpu.VMEM(field.shape, jnp.float32)
    b_right, b_down, scale, root, g0, z0, g1, f1, g2, sums = pl.pallas_call(
        first_kernel,
        out_shape=[plane] * 4 + [field] * 5 + [shaped(SUBS, LANES)],
        in_specs=[in_vmem] * 5,
        out_specs=[in_vmem] * 10,
        scratch_shapes=[pltpu.VMEM((planes, tiles, height, LANES), jnp.float32), work],
        compiler_params=params,
    )(own, top, bottom, before, after)

    total = sum_over(sum_over(sums, "col"), "row")
    f2 = pl.pallas_call(
        second_kernel,
        out_shape=field,
        in_specs=[in_vmem] * 3,
        out_specs=in_vmem,
        scratch_shapes=[work],
        compiler_params=params,
        cost_estimate=pl.CostEstimate(flops=10**9, bytes_accessed=10**7, transcendentals=0),
    )(b_right, b_down, g2)
    return pl.pallas_call(
        third_kernel,
        out_shape=[shaped(chans, rows, cols)] * 3,
        in_specs=[in_vmem] * 9,
        out_specs=[in_vmem] * 3,
        scratch_shapes=[pltpu.VMEM((3, own_tiles, height, LANES), jnp.float32)],
        compiler_params=params,
    )(total, scale, root, g0, z0, g1, f1, g2, f2)


def solution(mesh):
    placed = (
        P(None, ("band", "row"), "col"),
        P(("band", "row"), "col"),
        P(("band", "row"), "col"),
        P(("band", "row"), "col"),
        P("band", None, None),
    )
    return jax.shard_map(
        per_device,
        mesh=mesh,
        in_specs=placed,
        out_specs=(
            P(None, ("band", "row"), "col"),
            P(None, ("band", "row"), "col"),
            P(None, ("band", "row"), "col"),
        ),
        check_vma=False,
    )
```

```python
import functools

import jax
import jax.numpy as jnp
from jax import lax
from jax.experimental import pallas as pl
from jax.experimental.pallas import tpu as pltpu
from jax.sharding import PartitionSpec as P

TILE = 256
SWEEPS = 8
SUBS = 8
LANES = 128
HALO = 24
SLOT = 32
SLOTS = LANES // SLOT
WAYS = 3

seam_damping = 0.8
offset_unit = 32.0
spectrum_low = 0.08
spectrum_high = 2.0
MIX = 2.4

VMEM_LIMIT = 28 * 1024 * 1024


def chebyshev_polynomial():
    centre = (spectrum_high + spectrum_low) / 2.0
    radius = (spectrum_high - spectrum_low) / 2.0
    sigma = centre / radius
    size = SWEEPS
    update = [1.0 / centre] + [0.0] * (size - 1)
    smoothed = list(update)
    rho = 1.0 / sigma
    for _ in range(SWEEPS - 1):
        remainder = [-s for s in smoothed]
        remainder[0] += 1.0
        for k in range(size - 1):
            remainder[k + 1] += smoothed[k]
        following = 1.0 / (2.0 * sigma - rho)
        update = [following * rho * u + 2.0 * following / radius * r for u, r in zip(update, remainder)]
        smoothed = [s + u for s, u in zip(smoothed, update)]
        rho = following
    return smoothed


def lane_index():
    return lax.broadcasted_iota(jnp.int32, (SUBS, LANES), 1)


def own_kernel(
    place_ref, offsets_ref, src_hbm, weight_hbm, seam_right_hbm, seam_down_hbm,
    own_ref, first_ref, last_ref,
    src_ref, weight_ref, seam_right_ref, seam_down_ref, sems,
):
    chans, rows, cols = src_ref.shape
    own_tiles = cols // LANES
    copies = [pltpu.make_async_copy(src_hbm.at[c], src_ref.at[c], sems.at[c]) for c in range(chans)]
    for k, (there, here) in enumerate(
        ((weight_hbm, weight_ref), (seam_right_hbm, seam_right_ref), (seam_down_hbm, seam_down_ref))
    ):
        copies.append(pltpu.make_async_copy(there, here, sems.at[chans + k]))
    for copy in copies:
        copy.start()
    lane = lane_index()
    sub = lax.broadcasted_iota(jnp.int32, (SUBS, LANES), 0)
    last_row, last_lane, tile_at = place_ref[0], place_ref[1], place_ref[2]
    shift = [
        [
            jnp.broadcast_to(offsets_ref[tile_at + k * chans + c], (SUBS, LANES)).astype(jnp.float32) / offset_unit
            for k in range(cols // TILE)
        ]
        for c in range(chans)
    ]
    for copy in copies:
        copy.wait()

    def body(t, carry):
        at = pl.multiple_of(SUBS * t, SUBS)
        here = pl.ds(at, SUBS)
        for j in range(own_tiles):
            there = pl.ds(j * LANES, LANES)
            planes = [src_ref[c, here, there] + shift[c][j * LANES // TILE] for c in range(chans)]
            planes.append(weight_ref[here, there])
            to_right = 1.0 - seam_damping * seam_right_ref[here, there].astype(jnp.float32)
            if j == own_tiles - 1:
                to_right = jnp.where(lane == last_lane, 0.0, to_right)
            to_down = 1.0 - seam_damping * seam_down_ref[here, there].astype(jnp.float32)
            planes += [to_right, jnp.where(at + sub == last_row, 0.0, to_down)]
            for p, plane in enumerate(planes):
                own_ref[p, j, here, :] = plane
            for side, start, cols_ref in ((0, 0, first_ref), (own_tiles - 1, LANES - SLOT, last_ref)):
                if j != side:
                    continue
                packed = [None] * (-(-len(planes) // SLOTS))
                for p, plane in enumerate(planes):
                    slot = p % SLOTS
                    by = (slot * SLOT - start) % LANES
                    moved = pltpu.roll(plane, by, 1) if by else plane
                    k = p // SLOTS
                    packed[k] = moved if slot == 0 else jnp.where(lane < slot * SLOT, packed[k], moved)
                for k, value in enumerate(packed):
                    cols_ref[k, here, :] = value
        return carry

    lax.fori_loop(0, rows // SUBS, body, 0)


def unpack(p, lefts, rights):
    lane = lane_index()
    slot = p % SLOTS
    if slot != SLOTS - 1:
        lefts = pltpu.roll(lefts, LANES - SLOT - slot * SLOT, 1)
    if slot:
        rights = pltpu.roll(rights, LANES - slot * SLOT, 1)
    return jnp.where(lane < SLOT, rights, jnp.where(lane >= LANES - SLOT, lefts, 0.0))


def ways_of(tiles):
    return WAYS if tiles % WAYS == 0 else 1


def take(value, index):
    return jnp.take_along_axis(value, index, axis=1)


def deal(values):
    ways = ways_of(len(values))
    lane = lane_index()
    out = []
    for g in range(0, len(values), ways):
        for m in range(ways):
            place = ways * lane + m
            result = None
            for t in range(ways):
                part = take(values[g + t], place % LANES) if ways > 1 else values[g + t]
                result = part if result is None else jnp.where(place >= t * LANES, part, result)
            out.append(result)
    return out


def gather_back(values, t):
    ways = ways_of(len(values))
    if ways == 1:
        return values[t]
    lane = lane_index()
    group = t // ways * ways
    place = (t % ways) * LANES + lane
    result = None
    for m in range(ways):
        part = take(values[group + m], place // ways)
        result = part if result is None else jnp.where(place % ways == m, part, result)
    return result


def own_dealt_kernel(own_ref, before_ref, after_ref, dealt_ref):
    planes, own_tiles, rows = own_ref.shape[:3]

    def body(t, carry):
        here = pl.ds(pl.multiple_of(SUBS * t, SUBS), SUBS)
        for p in range(planes):
            values = [own_ref[p, j, here, :] for j in range(own_tiles)]
            values.append(unpack(p, before_ref[p // SLOTS, here, :], after_ref[p // SLOTS, here, :]))
            for j, value in enumerate(deal(values)):
                dealt_ref[p, j, here, :] = value
        return carry

    lax.fori_loop(0, rows // SUBS, body, 0)


def rightward(values):
    tiles = len(values)
    ways = ways_of(tiles)
    last = lane_index() == LANES - 1
    ahead = {g: pltpu.roll(values[g], LANES - 1, 1) for g in range(0, tiles, ways)}
    out = []
    for j in range(tiles):
        if j % ways + 1 < ways:
            out.append(values[j + 1])
        else:
            g = j - ways + 1
            out.append(jnp.where(last, ahead[(g + ways) % tiles], ahead[g]))
    return out


def leftward(values):
    tiles = len(values)
    ways = ways_of(tiles)
    first = lane_index() == 0
    behind = {g: pltpu.roll(values[g + ways - 1], 1, 1) for g in range(0, tiles, ways)}
    out = []
    for j in range(tiles):
        if j % ways:
            out.append(values[j - 1])
        else:
            out.append(jnp.where(first, behind[(j - ways) % tiles], behind[j]))
    return out


def spread(b_right_ref, b_down_ref, z_ref, c, emit):
    tiles, height = z_ref.shape[1:3]
    steps = height // SUBS

    def at(i):
        return pl.ds(i * SUBS, SUBS)

    def z_at(i, j):
        return z_ref[c, j, at(i), :]

    from_above = [pltpu.roll(b_down_ref[j, at(steps - 1), :] * z_at(steps - 1, j), 1, 0) for j in range(tiles)]
    centre = [z_at(0, j) for j in range(tiles)]
    wrapped = [pltpu.roll(v, SUBS - 1, 0) for v in centre]
    for i in range(steps):
        below = [z_at(i + 1, j) for j in range(tiles)] if i + 1 < steps else wrapped
        b_right = [b_right_ref[j, at(i), :] for j in range(tiles)]
        to_right = rightward(centre)
        from_left = leftward([b * v for b, v in zip(b_right, centre)])
        for j in range(tiles):
            b_down = b_down_ref[j, at(i), :]
            moved = (b_right[j] * to_right[j] + from_left[j]) + (b_down * below[j] + from_above[j])
            from_above[j] = b_down * centre[j]
            emit(i, j, centre[j], moved)
        centre = below


def precondition(b_right_ref, b_down_ref, g_ref, z_ref, work_ref, c):
    poly = chebyshev_polynomial()
    degree = SWEEPS - 1

    def at(i):
        return pl.ds(i * SUBS, SUBS)

    def first(i, j, centre, moved):
        z_ref[c, j, at(i), :] = poly[degree] * moved + poly[degree - 1] * centre

    spread(b_right_ref, b_down_ref, g_ref, c, first)

    def pair(k, carry):
        adds = []
        for half in range(2):
            value = jnp.float32(poly[half])
            for later in range(1, (degree - 1) // 2):
                value = jnp.where(k == (degree - 1) // 2 - 1 - later, jnp.float32(poly[2 * later + half]), value)
            adds.append(value)

        def one(target, add):
            def emit(i, j, centre, moved):
                target[c, j, at(i), :] = moved + add * g_ref[c, j, at(i), :]

            return emit

        spread(b_right_ref, b_down_ref, z_ref, c, one(work_ref, adds[1]))
        spread(b_right_ref, b_down_ref, work_ref, c, one(z_ref, adds[0]))
        return carry

    lax.fori_loop(0, (degree - 1) // 2, pair, 0)


def next_residual(b_right_ref, b_down_ref, g_ref, z_ref, next_ref, c, own_of):
    height = g_ref.shape[2]
    steps = height // SUBS
    sums = {}

    def emit(i, j, centre, moved):
        at = pl.ds(i * SUBS, SUBS)
        g = g_ref[c, j, at, :]
        following = g - MIX * (centre - moved)
        next_ref[c, j, at, :] = following
        key = own_of(i, j)
        now = (g * centre, following * centre)
        before = sums.get(key)
        sums[key] = now if before is None else (before[0] + now[0], before[1] + now[1])

    spread(b_right_ref, b_down_ref, z_ref, c, emit)
    sub = lax.broadcasted_iota(jnp.int32, (SUBS, LANES), 0)
    lane = lane_index()
    total = [jnp.zeros((SUBS, LANES), jnp.float32)] * 2
    for (low, high, lanes), parts in sums.items():
        inside = jnp.logical_and(jnp.logical_and(sub >= low, sub <= high), lane < lanes)
        total = [t + jnp.where(inside, p, 0.0) for t, p in zip(total, parts)]
    return total


def first_kernel(
    dealt_ref, top_ref, bottom_ref, top_corners_ref, bottom_corners_ref,
    b_right_ref, b_down_ref, scale_ref, root_ref, g0_ref, z0_ref, g1_ref, f1_ref, g2_ref, sums_ref,
    natural, work_ref,
):
    planes, tiles, rows = dealt_ref.shape[:3]
    chans = planes - 3
    own_tiles = tiles - 1
    height = rows + 2 * HALO
    steps = height // SUBS
    packs = -(-planes // SLOTS)

    def copy_own(t, carry):
        here = pl.ds(pl.multiple_of(SUBS * t, SUBS), SUBS)
        there = pl.ds(pl.multiple_of(HALO + SUBS * t, SUBS), SUBS)
        for p in range(planes):
            for j in range(tiles):
                natural[p, j, there, :] = dealt_ref[p, j, here, :]
        return carry

    lax.fori_loop(0, rows // SUBS, copy_own, 0)

    def deal_edge(t, carry):
        for slab, corners, start in ((top_ref, top_corners_ref, 0), (bottom_ref, bottom_corners_ref, HALO + rows)):
            there = pl.ds(pl.multiple_of(start + SUBS * t, SUBS), SUBS)
            for p in range(planes):

                def rows_at(k):
                    return pl.ds(pl.multiple_of(k * HALO + SUBS * t, SUBS), SUBS)

                values = [slab[rows_at(p * own_tiles + j), :] for j in range(own_tiles)]
                values.append(
                    unpack(p, corners[rows_at(p // SLOTS), :], corners[rows_at(packs + p // SLOTS), :])
                )
                for j, value in enumerate(deal(values)):
                    natural[p, j, there, :] = value
        return carry

    lax.fori_loop(0, HALO // SUBS, deal_edge, 0)

    def at(i):
        return pl.ds(i * SUBS, SUBS)

    def interleaved(p, i, j):
        return natural[p, j, pl.ds(i, SUBS, stride=steps), :]

    to_up = [pltpu.roll(interleaved(chans + 2, steps - 1, j), 1, 0) for j in range(tiles)]
    for i in range(steps):
        to_right = [interleaved(chans + 1, i, j) for j in range(tiles)]
        to_left = leftward(to_right)
        for j in range(tiles):
            to_down = interleaved(chans + 2, i, j)
            diag = interleaved(chans, i, j) + to_right[j] + to_left[j] + to_down + to_up[j]
            inside = diag > 0.0
            safe = jnp.where(inside, diag, 1.0)
            guess = lax.rsqrt(safe)
            scale = guess * (1.5 - 0.5 * safe * guess * guess)
            scale_ref[j, at(i), :] = jnp.where(inside, scale, 0.0)
            root_ref[j, at(i), :] = safe * scale
            to_up[j] = to_down
    wrapped = [pltpu.roll(scale_ref[j, at(0), :], SUBS - 1, 0) for j in range(tiles)]
    for i in range(steps):
        scale = [scale_ref[j, at(i), :] for j in range(tiles)]
        right_scale = rightward(scale)
        for j in range(tiles):
            b_right_ref[j, at(i), :] = interleaved(chans + 1, i, j) * scale[j] * right_scale[j]
            down_scale = scale_ref[j, at(i + 1), :] if i + 1 < steps else wrapped[j]
            b_down_ref[j, at(i), :] = interleaved(chans + 2, i, j) * scale[j] * down_scale
            for c in range(chans):
                g0_ref[c, j, at(i), :] = interleaved(c, i, j) * scale[j]

    ways = ways_of(tiles)

    def own_of(i, j):
        low, high = -(-(HALO - i) // steps), (HALO + rows - 1 - i) // steps
        left = own_tiles * LANES - j // ways * ways * LANES - j % ways
        return low, high, min(LANES, max(0, -(-left // ways)))

    def channel(c, carry):
        precondition(b_right_ref, b_down_ref, g0_ref, z0_ref, work_ref, c)
        sum0, sum1 = next_residual(b_right_ref, b_down_ref, g0_ref, z0_ref, g1_ref, c, own_of)
        precondition(b_right_ref, b_down_ref, g1_ref, f1_ref, work_ref, c)
        sum2, sum3 = next_residual(b_right_ref, b_down_ref, g1_ref, f1_ref, g2_ref, c, own_of)
        return tuple(a + b for a, b in zip(carry, (sum0, sum1, sum2, sum3)))

    zero = jnp.zeros((SUBS, LANES), jnp.float32)
    parts = lax.fori_loop(0, chans, channel, (zero,) * 4)
    sub = lax.broadcasted_iota(jnp.int32, (SUBS, LANES), 0)
    sums = zero
    for k, part in enumerate(parts):
        sums = jnp.where(sub == k, jnp.sum(part), sums)
    sums_ref[...] = sums


def second_kernel(
    c, b_right_ref, b_down_ref, scale_ref, root_ref, g0_ref, z0_ref, g1_ref, f1_ref, g2_ref,
    fields_ref, f2_ref, work_ref, natural,
):
    rows, cols = fields_ref.shape[1:]
    tiles, height = scale_ref.shape[:2]
    steps = height // SUBS

    def at(i):
        return pl.ds(i * SUBS, SUBS)

    for j in range(tiles):
        for i in range(steps):
            work_ref[0, j, at(i), :] = g2_ref[c, j, at(i), :]
    precondition(b_right_ref, b_down_ref, work_ref.at[pl.ds(0, 1)], f2_ref, work_ref.at[pl.ds(1, 1)], 0)
    sources = ((g0_ref, c, root_ref), (g1_ref, c, root_ref), (g2_ref, c, root_ref),
               (z0_ref, c, scale_ref), (f1_ref, c, scale_ref), (f2_ref, 0, scale_ref))
    for k, (ref, channel, factor_ref) in enumerate(sources):
        for j in range(tiles):
            for i in range(steps):
                natural[j, pl.ds(i, SUBS, stride=steps), :] = ref[channel, j, at(i), :] * factor_ref[j, at(i), :]

        def body(t, carry, k=k):
            there = pl.ds(pl.multiple_of(HALO + SUBS * t, SUBS), SUBS)
            here = pl.ds(pl.multiple_of(SUBS * t, SUBS), SUBS)
            values = [natural[j, there, :] for j in range(tiles)]
            for j in range(cols // LANES):
                fields_ref[k, here, j * LANES:(j + 1) * LANES] = gather_back(values, j)
            return carry

        lax.fori_loop(0, rows // SUBS, body, 0)


def combine(n0, n1, n2, n3):
    gap = n0 - n1
    keep = -n1 / gap
    step = n0 / gap
    beta = (n0 * n2 - n1 * n1) / (gap * gap)
    along = keep + beta
    curvature = along * along * gap + 2.0 * along * step * (n1 - n2) + step * step * (n2 - n3)
    scaled = n0 * beta / curvature
    first_size = step * MIX
    second_size = scaled * MIX
    x0 = first_size + second_size * along
    x1 = second_size * step
    r0 = keep - scaled * along
    r1 = step + scaled * (along - step)
    r2 = scaled * step
    return x0, x1, r0, r1, r2


def third_kernel(sums_ref, *refs):
    *field_refs, solution_ref, residual_ref, smoothed_ref = refs
    rows, cols = solution_ref.shape[1:]
    x0, x1, r0, r1, r2 = combine(*[jnp.broadcast_to(sums_ref[k:k + 1, :], (SUBS, LANES)) for k in range(4)])

    def body(t, carry):
        here = pl.ds(pl.multiple_of(SUBS * t, SUBS), SUBS)
        for c, fields in enumerate(field_refs):
            for j in range(cols // LANES):
                there = pl.ds(j * LANES, LANES)
                e0, e1, e2, z0, f1, f2 = [fields[k, here, there] for k in range(6)]
                solution_ref[c, here, there] = x0 * z0 + x1 * f1
                residual_ref[c, here, there] = r0 * e0 + r1 * e1 + r2 * e2
                smoothed_ref[c, here, there] = r0 * z0 + r1 * f1 + r2 * f2
        return carry

    lax.fori_loop(0, rows // SUBS, body, 0)


def sum_over(value, axis):
    size = lax.axis_size(axis)
    if size & (size - 1):
        return lax.psum(value, axis)
    step = 1
    while step < size:
        value = value + lax.ppermute(value, axis, [(i, i ^ step) for i in range(size)])
        step *= 2
    return value


def per_device(source, weight, seam_right, seam_down, offsets):
    chans, rows, cols = source.shape
    row_axis, col_axis = lax.axis_size("row"), lax.axis_size("col")
    row_at, col_at = lax.axis_index("row"), lax.axis_index("col")
    tile_at = (row_at * rows // TILE * offsets.shape[1] + col_at * (cols // TILE)) * chans
    place = jnp.stack(
        [jnp.where(row_at == row_axis - 1, rows - 1, -1), jnp.where(col_at == col_axis - 1, LANES - 1, -1), tile_at]
    ).astype(jnp.int32)

    in_vmem = pl.BlockSpec(memory_space=pltpu.VMEM)
    in_smem = pl.BlockSpec(memory_space=pltpu.SMEM)
    in_hbm = pl.BlockSpec(memory_space=pltpu.HBM)
    params = pltpu.CompilerParams(vmem_limit_bytes=VMEM_LIMIT)

    def shaped(*shape):
        return jax.ShapeDtypeStruct(shape, jnp.float32)

    def scratch(*shape):
        return pltpu.VMEM(shape, jnp.float32)

    planes = chans + 3
    own_tiles = cols // LANES
    tiles = own_tiles + 1
    packs = -(-planes // SLOTS)
    own, first_cols, last_cols = pl.pallas_call(
        own_kernel,
        out_shape=[shaped(planes, own_tiles, rows, LANES)] + [shaped(packs, rows, LANES)] * 2,
        in_specs=[in_smem] * 2 + [in_hbm] * 4,
        out_specs=[in_vmem] * 3,
        scratch_shapes=[
            scratch(*source.shape),
            scratch(*weight.shape),
            pltpu.VMEM(weight.shape, jnp.int32),
            pltpu.VMEM(weight.shape, jnp.int32),
            pltpu.SemaphoreType.DMA((planes,)),
        ],
        compiler_params=params,
    )(place, offsets.reshape(-1), source, weight, seam_right, seam_down)

    down = [(i, i + 1) for i in range(row_axis - 1)]
    up = [(j, i) for i, j in down]
    onward = [(i, i + 1) for i in range(col_axis - 1)]
    back = [(j, i) for i, j in onward]
    top = lax.ppermute(own[:, :, rows - HALO:].reshape(-1, LANES), "row", down)
    bottom = lax.ppermute(own[:, :, :HALO].reshape(-1, LANES), "row", up)
    before = lax.ppermute(last_cols, "col", onward)
    after = lax.ppermute(first_cols, "col", back)

    def corners(low, high):
        parts = [before[:, low:high], after[:, low:high]]
        return jnp.concatenate([part.reshape(-1, LANES) for part in parts], axis=0)

    top_corners = lax.ppermute(corners(rows - HALO, rows), "row", down)
    bottom_corners = lax.ppermute(corners(0, HALO), "row", up)
    dealt = pl.pallas_call(
        own_dealt_kernel,
        out_shape=shaped(planes, tiles, rows, LANES),
        in_specs=[in_vmem] * 3,
        out_specs=in_vmem,
        compiler_params=params,
        cost_estimate=pl.CostEstimate(flops=10**8, bytes_accessed=5 * 10**6, transcendentals=0),
    )(own, before, after)

    height = rows + 2 * HALO
    plane = shaped(tiles, height, LANES)
    field = shaped(chans, tiles, height, LANES)
    *basis, sums = pl.pallas_call(
        first_kernel,
        out_shape=[plane] * 4 + [field] * 5 + [shaped(SUBS, LANES)],
        in_specs=[in_vmem] * 5,
        out_specs=[in_vmem] * 10,
        scratch_shapes=[scratch(planes, tiles, height, LANES), scratch(*field.shape)],
        compiler_params=params,
    )(dealt, top, bottom, top_corners, bottom_corners)

    total = sum_over(sum_over(sums, "col"), "row")
    fields = [
        pl.pallas_call(
            functools.partial(second_kernel, c),
            out_shape=shaped(6, rows, cols),
            in_specs=[in_vmem] * 9,
            out_specs=in_vmem,
            scratch_shapes=[
                scratch(1, tiles, height, LANES), scratch(2, tiles, height, LANES), scratch(tiles, height, LANES)
            ],
            compiler_params=params,
            cost_estimate=pl.CostEstimate(flops=10**8, bytes_accessed=10**7, transcendentals=0),
        )(*basis)
        for c in range(chans)
    ]
    return pl.pallas_call(
        third_kernel,
        out_shape=[shaped(chans, rows, cols)] * 3,
        in_specs=[in_vmem] * (1 + chans),
        out_specs=[in_vmem] * 3,
        compiler_params=params,
    )(total, *fields)


def solution(mesh):
    placed = (
        P(None, ("band", "row"), "col"),
        P(("band", "row"), "col"),
        P(("band", "row"), "col"),
        P(("band", "row"), "col"),
        P("band", None, None),
    )
    return jax.shard_map(
        per_device,
        mesh=mesh,
        in_specs=placed,
        out_specs=(
            P(None, ("band", "row"), "col"),
            P(None, ("band", "row"), "col"),
            P(None, ("band", "row"), "col"),
        ),
        check_vma=False,
    )
```

```python
import functools

import jax
import jax.numpy as jnp
from jax import lax
from jax.experimental import pallas as pl
from jax.experimental.pallas import tpu as pltpu
from jax.sharding import PartitionSpec as P

TILE = 256
SWEEPS = 8
SUBS = 8
LANES = 128
HALO = 24
SLOT = 32
SLOTS = LANES // SLOT
WAYS = 3

seam_damping = 0.8
offset_unit = 32.0
spectrum_low = 0.08
spectrum_high = 2.0
MIX = 2.4

VMEM_LIMIT = 28 * 1024 * 1024


def chebyshev_polynomial():
    centre = (spectrum_high + spectrum_low) / 2.0
    radius = (spectrum_high - spectrum_low) / 2.0
    sigma = centre / radius
    size = SWEEPS
    update = [1.0 / centre] + [0.0] * (size - 1)
    smoothed = list(update)
    rho = 1.0 / sigma
    for _ in range(SWEEPS - 1):
        remainder = [-s for s in smoothed]
        remainder[0] += 1.0
        for k in range(size - 1):
            remainder[k + 1] += smoothed[k]
        following = 1.0 / (2.0 * sigma - rho)
        update = [following * rho * u + 2.0 * following / radius * r for u, r in zip(update, remainder)]
        smoothed = [s + u for s, u in zip(smoothed, update)]
        rho = following
    return smoothed


def lane_index():
    return lax.broadcasted_iota(jnp.int32, (SUBS, LANES), 1)


def own_kernel(
    place_ref, offsets_ref, src_hbm, weight_hbm, seam_right_hbm, seam_down_hbm,
    own_ref, first_ref, last_ref,
    src_ref, weight_ref, seam_right_ref, seam_down_ref, sems,
):
    chans, rows, cols = src_ref.shape
    own_tiles = cols // LANES
    copies = [pltpu.make_async_copy(src_hbm.at[c], src_ref.at[c], sems.at[c]) for c in range(chans)]
    for k, (there, here) in enumerate(
        ((weight_hbm, weight_ref), (seam_right_hbm, seam_right_ref), (seam_down_hbm, seam_down_ref))
    ):
        copies.append(pltpu.make_async_copy(there, here, sems.at[chans + k]))
    for copy in copies:
        copy.start()
    lane = lane_index()
    sub = lax.broadcasted_iota(jnp.int32, (SUBS, LANES), 0)
    last_row, last_lane, tile_at = place_ref[0], place_ref[1], place_ref[2]
    tiles_all = offsets_ref.shape[0] // chans
    shift = [
        [
            jnp.broadcast_to(offsets_ref[c * tiles_all + tile_at + k], (SUBS, LANES)).astype(jnp.float32) / offset_unit
            for k in range(cols // TILE)
        ]
        for c in range(chans)
    ]
    for copy in copies:
        copy.wait()

    def body(t, carry):
        at = pl.multiple_of(SUBS * t, SUBS)
        here = pl.ds(at, SUBS)
        for j in range(own_tiles):
            there = pl.ds(j * LANES, LANES)
            planes = [src_ref[c, here, there] + shift[c][j * LANES // TILE] for c in range(chans)]
            planes.append(weight_ref[here, there])
            to_right = 1.0 - seam_damping * seam_right_ref[here, there].astype(jnp.float32)
            if j == own_tiles - 1:
                to_right = jnp.where(lane == last_lane, 0.0, to_right)
            to_down = 1.0 - seam_damping * seam_down_ref[here, there].astype(jnp.float32)
            planes += [to_right, jnp.where(at + sub == last_row, 0.0, to_down)]
            for p, plane in enumerate(planes):
                own_ref[p, j, here, :] = plane
            for side, start, cols_ref in ((0, 0, first_ref), (own_tiles - 1, LANES - SLOT, last_ref)):
                if j != side:
                    continue
                packed = [None] * (-(-len(planes) // SLOTS))
                for p, plane in enumerate(planes):
                    slot = p % SLOTS
                    by = (slot * SLOT - start) % LANES
                    moved = pltpu.roll(plane, by, 1) if by else plane
                    k = p // SLOTS
                    packed[k] = moved if slot == 0 else jnp.where(lane < slot * SLOT, packed[k], moved)
                for k, value in enumerate(packed):
                    cols_ref[k, here, :] = value
        return carry

    lax.fori_loop(0, rows // SUBS, body, 0)


def unpack(p, lefts, rights):
    lane = lax.broadcasted_iota(jnp.int32, lefts.shape, 1)
    slot = p % SLOTS
    if slot != SLOTS - 1:
        lefts = pltpu.roll(lefts, LANES - SLOT - slot * SLOT, 1)
    if slot:
        rights = pltpu.roll(rights, LANES - slot * SLOT, 1)
    return jnp.where(lane < SLOT, rights, jnp.where(lane >= LANES - SLOT, lefts, 0.0))


def ways_of(tiles):
    return WAYS if tiles % WAYS == 0 else 1


def exact_parts(value):
    high = value.astype(jnp.bfloat16)
    rest = value - high.astype(jnp.float32)
    middle = rest.astype(jnp.bfloat16)
    low = (rest - middle.astype(jnp.float32)).astype(jnp.bfloat16)
    return jnp.concatenate([high, middle, low], axis=0)


def permuted(value, index):
    rows = value.shape[0]
    out = jnp.dot(exact_parts(value), index, preferred_element_type=jnp.float32)
    return (out[:rows] + out[rows:2 * rows]) + out[2 * rows:]


def dealing(ways):
    size = ways * LANES
    column = lax.broadcasted_iota(jnp.int32, (size, size), 0)
    place = lax.broadcasted_iota(jnp.int32, (size, size), 1)
    return jnp.where(column == ways * (place % LANES) + place // LANES, 1.0, 0.0).astype(jnp.bfloat16)


def undealing(ways):
    size = ways * LANES
    column = lax.broadcasted_iota(jnp.int32, (size, size), 1)
    place = lax.broadcasted_iota(jnp.int32, (size, size), 0)
    return jnp.where(column == ways * (place % LANES) + place // LANES, 1.0, 0.0).astype(jnp.bfloat16)


def deal(tile_of, tiles, emit):
    ways = ways_of(tiles)
    matrix = dealing(ways) if ways > 1 else None
    for g in range(0, tiles, ways):
        if ways == 1:
            emit(g, tile_of(g))
            continue
        value = permuted(jnp.concatenate([tile_of(g + m) for m in range(ways)], axis=1), matrix)
        for m in range(ways):
            emit(g + m, value[:, m * LANES:(m + 1) * LANES])


def own_dealt_kernel(own_ref, before_ref, after_ref, dealt_ref):
    planes, own_tiles, rows = own_ref.shape[:3]

    def tile_of(j):
        if j < own_tiles:
            return own_ref[:, j].reshape(planes * rows, LANES)
        return jnp.concatenate([unpack(p, before_ref[p // SLOTS], after_ref[p // SLOTS]) for p in range(planes)], axis=0)

    def emit(j, value):
        dealt_ref[:, j] = value.reshape(planes, rows, LANES)

    deal(tile_of, own_tiles + 1, emit)


def rightward(values):
    tiles = len(values)
    ways = ways_of(tiles)
    last = lane_index() == LANES - 1
    ahead = {g: pltpu.roll(values[g], LANES - 1, 1) for g in range(0, tiles, ways)}
    out = []
    for j in range(tiles):
        if j % ways + 1 < ways:
            out.append(values[j + 1])
        else:
            g = j - ways + 1
            out.append(jnp.where(last, ahead[(g + ways) % tiles], ahead[g]))
    return out


def leftward(values):
    tiles = len(values)
    ways = ways_of(tiles)
    first = lane_index() == 0
    behind = {g: pltpu.roll(values[g + ways - 1], 1, 1) for g in range(0, tiles, ways)}
    out = []
    for j in range(tiles):
        if j % ways:
            out.append(values[j - 1])
        else:
            out.append(jnp.where(first, behind[(j - ways) % tiles], behind[j]))
    return out


def spread(b_right_ref, b_down_ref, z_ref, emit):
    tiles, height = z_ref.shape[:2]
    steps = height // SUBS
    ways = ways_of(tiles)
    lane = lane_index()
    first, last = (lane == 0, lane == LANES - 1)

    def at(i):
        return pl.ds(i * SUBS, SUBS)

    from_above = [pltpu.roll(b_down_ref[j, at(steps - 1), :] * z_ref[j, at(steps - 1), :], 1, 0) for j in range(tiles)]
    centre = [z_ref[j, at(0), :] for j in range(tiles)]
    wrapped = [pltpu.roll(v, SUBS - 1, 0) for v in centre]
    for i in range(steps):
        pushed_out = {
            g: pltpu.roll(b_right_ref[g + ways - 1, at(i), :] * centre[g + ways - 1], 1, 1)
            for g in range(0, tiles, ways)
        }
        ahead = {g: pltpu.roll(centre[g], LANES - 1, 1) for g in range(0, tiles, ways)}
        pushed = None
        below = []
        for j in range(tiles):
            g = j // ways * ways
            b_right = b_right_ref[j, at(i), :]
            b_down = b_down_ref[j, at(i), :]
            below.append(z_ref[j, at(i + 1), :] if i + 1 < steps else wrapped[j])
            if j == g:
                from_left = jnp.where(first, pushed_out[(g - ways) % tiles], pushed_out[g])
            else:
                from_left = pushed
            if j + 1 < g + ways:
                to_right = centre[j + 1]
                pushed = b_right * centre[j]
            else:
                to_right = jnp.where(last, ahead[(g + ways) % tiles], ahead[g])
            moved = (b_right * to_right + from_left) + (b_down * below[j] + from_above[j])
            from_above[j] = b_down * centre[j]
            emit(i, j, centre[j], moved)
        centre = below


def precondition(b_right_ref, b_down_ref, g_ref, z_ref, work_ref):
    poly = chebyshev_polynomial()
    degree = SWEEPS - 1

    def at(i):
        return pl.ds(i * SUBS, SUBS)

    def first(i, j, centre, moved):
        z_ref[j, at(i), :] = poly[degree] * moved + poly[degree - 1] * centre

    spread(b_right_ref, b_down_ref, g_ref, first)

    def pair(k, carry):
        adds = []
        for half in range(2):
            value = jnp.float32(poly[half])
            for later in range(1, (degree - 1) // 2):
                value = jnp.where(k == (degree - 1) // 2 - 1 - later, jnp.float32(poly[2 * later + half]), value)
            adds.append(value)

        def one(target, add):
            def emit(i, j, centre, moved):
                target[j, at(i), :] = moved + add * g_ref[j, at(i), :]

            return emit

        spread(b_right_ref, b_down_ref, z_ref, one(work_ref, adds[1]))
        spread(b_right_ref, b_down_ref, work_ref, one(z_ref, adds[0]))
        return carry

    lax.fori_loop(0, (degree - 1) // 2, pair, 0)


def next_residual(b_right_ref, b_down_ref, g_ref, z_ref, next_ref, own_of):
    height = g_ref.shape[1]
    steps = height // SUBS
    sums = {}

    def emit(i, j, centre, moved):
        at = pl.ds(i * SUBS, SUBS)
        g = g_ref[j, at, :]
        following = g - MIX * (centre - moved)
        next_ref[j, at, :] = following
        key = own_of(i, j)
        now = (g * centre, following * centre)
        before = sums.get(key)
        sums[key] = now if before is None else (before[0] + now[0], before[1] + now[1])

    spread(b_right_ref, b_down_ref, z_ref, emit)
    sub = lax.broadcasted_iota(jnp.int32, (SUBS, LANES), 0)
    lane = lane_index()
    total = [jnp.zeros((SUBS, LANES), jnp.float32)] * 2
    for (low, high, lanes), parts in sums.items():
        inside = jnp.logical_and(jnp.logical_and(sub >= low, sub <= high), lane < lanes)
        total = [t + jnp.where(inside, p, 0.0) for t, p in zip(total, parts)]
    return total


def first_kernel(
    dealt_ref, top_ref, bottom_ref, top_corners_ref, bottom_corners_ref,
    b_right_ref, b_down_ref, scale_ref, root_ref, g0_ref, z0_ref, g1_ref, f1_ref, g2_ref, sums_ref,
    natural, work_ref,
):
    planes, tiles, rows = dealt_ref.shape[:3]
    chans = planes - 3
    own_tiles = tiles - 1
    height = rows + 2 * HALO
    steps = height // SUBS

    def copy_own(t, carry):
        here = pl.ds(pl.multiple_of(SUBS * t, SUBS), SUBS)
        there = pl.ds(pl.multiple_of(HALO + SUBS * t, SUBS), SUBS)
        for p in range(planes):
            for j in range(tiles):
                natural[p, j, there, :] = dealt_ref[p, j, here, :]
        return carry

    lax.fori_loop(0, rows // SUBS, copy_own, 0)

    def edge_tile(j):
        parts = []
        for slab, corners in ((top_ref, top_corners_ref), (bottom_ref, bottom_corners_ref)):
            if j < own_tiles:
                parts.append(slab[:, j].reshape(planes * HALO, LANES))
                continue
            for p in range(planes):
                parts.append(unpack(p, corners[0, p // SLOTS], corners[1, p // SLOTS]))
        return jnp.concatenate(parts, axis=0)

    def put_edge(j, value):
        value = value.reshape(2, planes, HALO, LANES)
        natural[:, j, 0:HALO, :] = value[0]
        natural[:, j, HALO + rows:height, :] = value[1]

    deal(edge_tile, tiles, put_edge)

    def at(i):
        return pl.ds(i * SUBS, SUBS)

    def interleaved(p, i, j):
        return natural[p, j, pl.ds(i, SUBS, stride=steps), :]

    to_up = [pltpu.roll(interleaved(chans + 2, steps - 1, j), 1, 0) for j in range(tiles)]
    for i in range(steps):
        to_right = [interleaved(chans + 1, i, j) for j in range(tiles)]
        to_left = leftward(to_right)
        for j in range(tiles):
            to_down = interleaved(chans + 2, i, j)
            diag = interleaved(chans, i, j) + to_right[j] + to_left[j] + to_down + to_up[j]
            inside = diag > 0.0
            safe = jnp.where(inside, diag, 1.0)
            guess = lax.rsqrt(safe)
            scale = guess * (1.5 - 0.5 * safe * guess * guess)
            scale_ref[j, at(i), :] = jnp.where(inside, scale, 0.0)
            root_ref[j, at(i), :] = safe * scale
            to_up[j] = to_down
    wrapped = [pltpu.roll(scale_ref[j, at(0), :], SUBS - 1, 0) for j in range(tiles)]
    for i in range(steps):
        scale = [scale_ref[j, at(i), :] for j in range(tiles)]
        right_scale = rightward(scale)
        for j in range(tiles):
            b_right_ref[j, at(i), :] = interleaved(chans + 1, i, j) * scale[j] * right_scale[j]
            down_scale = scale_ref[j, at(i + 1), :] if i + 1 < steps else wrapped[j]
            b_down_ref[j, at(i), :] = interleaved(chans + 2, i, j) * scale[j] * down_scale
            for c in range(chans):
                g0_ref[c, j, at(i), :] = interleaved(c, i, j) * scale[j]

    ways = ways_of(tiles)

    def own_of(i, j):
        low, high = -(-(HALO - i) // steps), (HALO + rows - 1 - i) // steps
        left = own_tiles * LANES - j // ways * ways * LANES - j % ways
        return low, high, min(LANES, max(0, -(-left // ways)))

    def channel(c, carry):
        g0, z0, g1, f1, g2 = [ref.at[c] for ref in (g0_ref, z0_ref, g1_ref, f1_ref, g2_ref)]
        precondition(b_right_ref, b_down_ref, g0, z0, work_ref)
        sum0, sum1 = next_residual(b_right_ref, b_down_ref, g0, z0, g1, own_of)
        precondition(b_right_ref, b_down_ref, g1, f1, work_ref)
        sum2, sum3 = next_residual(b_right_ref, b_down_ref, g1, f1, g2, own_of)
        return tuple(a + b for a, b in zip(carry, (sum0, sum1, sum2, sum3)))

    zero = jnp.zeros((SUBS, LANES), jnp.float32)
    parts = lax.fori_loop(0, chans, channel, (zero,) * 4)
    sub = lax.broadcasted_iota(jnp.int32, (SUBS, LANES), 0)
    sums = zero
    for k, part in enumerate(parts):
        sums = jnp.where(sub == k, jnp.sum(part), sums)
    sums_ref[...] = sums


def second_kernel(c, b_right_ref, b_down_ref, g2_ref, f2_ref, work_ref):
    precondition(b_right_ref, b_down_ref, g2_ref.at[c], f2_ref, work_ref)


def combine(n0, n1, n2, n3):
    gap = n0 - n1
    keep = -n1 / gap
    step = n0 / gap
    beta = (n0 * n2 - n1 * n1) / (gap * gap)
    along = keep + beta
    curvature = along * along * gap + 2.0 * along * step * (n1 - n2) + step * step * (n2 - n3)
    scaled = n0 * beta / curvature
    first_size = step * MIX
    second_size = scaled * MIX
    x0 = first_size + second_size * along
    x1 = second_size * step
    r0 = keep - scaled * along
    r1 = step + scaled * (along - step)
    r2 = scaled * step
    return x0, x1, r0, r1, r2


def third_kernel(
    sums_ref, scale_ref, root_ref, g0_ref, z0_ref, g1_ref, f1_ref, g2_ref, *refs
):
    *f2_refs, solution_ref, residual_ref, smoothed_ref, natural = refs
    rows, cols = solution_ref.shape[1:]
    own_tiles = cols // LANES
    tiles, height = scale_ref.shape[:2]
    steps = height // SUBS
    ways = ways_of(tiles)
    x0, x1, r0, r1, r2 = combine(*[jnp.broadcast_to(sums_ref[k:k + 1, :], (SUBS, LANES)) for k in range(4)])
    matrix = undealing(ways) if ways > 1 else None
    outs = (solution_ref, residual_ref, smoothed_ref)
    for c, f2_ref in enumerate(f2_refs):
        for j in range(tiles):
            for i in range(steps):
                at = pl.ds(i * SUBS, SUBS)
                scale = scale_ref[j, at, :]
                root = root_ref[j, at, :]
                g0, g1, g2, z0, f1 = [ref[c, j, at, :] for ref in (g0_ref, g1_ref, g2_ref, z0_ref, f1_ref)]
                f2 = f2_ref[j, at, :]
                there = pl.ds(i, SUBS, stride=steps)
                natural[c, 0, j, there, :] = scale * (x0 * z0 + x1 * f1)
                natural[c, 1, j, there, :] = root * (r0 * g0 + r1 * g1 + r2 * g2)
                natural[c, 2, j, there, :] = scale * (r0 * z0 + r1 * f1 + r2 * f2)
        for g in range(0, own_tiles, ways):
            value = jnp.concatenate(
                [natural[c, :, g + m, HALO:HALO + rows, :].reshape(3 * rows, LANES) for m in range(ways)], axis=1
            )
            width = min(ways, own_tiles - g) * LANES
            if ways > 1:
                value = permuted(value, matrix[:, :width])
            for k, ref in enumerate(outs):
                ref[c, :, g * LANES:g * LANES + width] = value[k * rows:(k + 1) * rows]


def sum_over(value, axis):
    size = lax.axis_size(axis)
    if size & (size - 1):
        return lax.psum(value, axis)
    step = 1
    while step < size:
        value = value + lax.ppermute(value, axis, [(i, i ^ step) for i in range(size)])
        step *= 2
    return value


def per_device(source, weight, seam_right, seam_down, offsets):
    chans, rows, cols = source.shape
    row_axis, col_axis = lax.axis_size("row"), lax.axis_size("col")
    row_at, col_at = lax.axis_index("row"), lax.axis_index("col")
    tile_at = lax.div(row_at * rows, TILE) * offsets.shape[1] + col_at * (cols // TILE)
    place = jnp.stack(
        [jnp.where(row_at == row_axis - 1, rows - 1, -1), jnp.where(col_at == col_axis - 1, LANES - 1, -1), tile_at]
    ).astype(jnp.int32)

    in_vmem = pl.BlockSpec(memory_space=pltpu.VMEM)
    in_smem = pl.BlockSpec(memory_space=pltpu.SMEM)
    in_hbm = pl.BlockSpec(memory_space=pltpu.HBM)
    params = pltpu.CompilerParams(vmem_limit_bytes=VMEM_LIMIT)

    def shaped(*shape):
        return jax.ShapeDtypeStruct(shape, jnp.float32)

    def scratch(*shape):
        return pltpu.VMEM(shape, jnp.float32)

    planes = chans + 3
    own_tiles = cols // LANES
    tiles = own_tiles + 1
    packs = -(-planes // SLOTS)
    own, first_cols, last_cols = pl.pallas_call(
        own_kernel,
        out_shape=[shaped(planes, own_tiles, rows, LANES)] + [shaped(packs, rows, LANES)] * 2,
        in_specs=[in_smem] * 2 + [in_hbm] * 4,
        out_specs=[in_vmem] * 3,
        scratch_shapes=[
            scratch(*source.shape),
            scratch(*weight.shape),
            pltpu.VMEM(weight.shape, jnp.int32),
            pltpu.VMEM(weight.shape, jnp.int32),
            pltpu.SemaphoreType.DMA((planes,)),
        ],
        compiler_params=params,
    )(
        place,
        offsets.transpose(2, 0, 1).reshape(-1),
        *[pltpu.with_memory_space_constraint(v, pltpu.HBM) for v in (source, weight, seam_right, seam_down)],
    )

    down = [(i, i + 1) for i in range(row_axis - 1)]
    up = [(j, i) for i, j in down]
    onward = [(i, i + 1) for i in range(col_axis - 1)]
    back = [(j, i) for i, j in onward]
    top = lax.ppermute(own[:, :, rows - HALO:], "row", down)
    bottom = lax.ppermute(own[:, :, :HALO], "row", up)
    before = lax.ppermute(last_cols, "col", onward)
    after = lax.ppermute(first_cols, "col", back)

    def corners(low, high):
        return jnp.stack([before[:, low:high], after[:, low:high]])

    top_corners = lax.ppermute(corners(rows - HALO, rows), "row", down)
    bottom_corners = lax.ppermute(corners(0, HALO), "row", up)
    dealt = pl.pallas_call(
        own_dealt_kernel,
        out_shape=shaped(planes, tiles, rows, LANES),
        in_specs=[in_vmem] * 3,
        out_specs=in_vmem,
        compiler_params=params,
        cost_estimate=pl.CostEstimate(flops=10**8, bytes_accessed=5 * 10**6, transcendentals=0),
    )(own, before, after)

    height = rows + 2 * HALO
    plane = shaped(tiles, height, LANES)
    field = shaped(chans, tiles, height, LANES)
    *basis, sums = pl.pallas_call(
        first_kernel,
        out_shape=[plane] * 4 + [field] * 5 + [shaped(SUBS, LANES)],
        in_specs=[in_vmem] * 5,
        out_specs=[in_vmem] * 10,
        scratch_shapes=[scratch(planes, tiles, height, LANES), scratch(*plane.shape)],
        compiler_params=params,
    )(dealt, top, bottom, top_corners, bottom_corners)

    total = sum_over(sum_over(sums, "col"), "row")
    b_right, b_down, scale, root, g0, z0, g1, f1, g2 = basis
    f2 = [
        pl.pallas_call(
            functools.partial(second_kernel, c),
            out_shape=plane,
            in_specs=[in_vmem] * 3,
            out_specs=in_vmem,
            scratch_shapes=[scratch(*plane.shape)],
            compiler_params=params,
            cost_estimate=pl.CostEstimate(flops=10**8, bytes_accessed=10**7, transcendentals=0),
        )(b_right, b_down, g2)
        for c in range(chans)
    ]
    return pl.pallas_call(
        third_kernel,
        out_shape=[shaped(chans, rows, cols)] * 3,
        in_specs=[in_vmem] * (8 + chans),
        out_specs=[in_vmem] * 3,
        scratch_shapes=[scratch(chans, 3, tiles, height, LANES)],
        compiler_params=params,
    )(total, scale, root, g0, z0, g1, f1, g2, *f2)


def solution(mesh):
    placed = (
        P(None, ("band", "row"), "col"),
        P(("band", "row"), "col"),
        P(("band", "row"), "col"),
        P(("band", "row"), "col"),
        P("band", None, None),
    )
    return jax.shard_map(
        per_device,
        mesh=mesh,
        in_specs=placed,
        out_specs=(
            P(None, ("band", "row"), "col"),
            P(None, ("band", "row"), "col"),
            P(None, ("band", "row"), "col"),
        ),
        check_vma=False,
    )
```

```python
import functools

import jax
import jax.numpy as jnp
from jax import lax
from jax.experimental import pallas as pl
from jax.experimental.pallas import tpu as pltpu
from jax.sharding import PartitionSpec as P

TILE = 256
SWEEPS = 8
SUBS = 8
LANES = 128
HALO = 24
SLOT = 32
SLOTS = LANES // SLOT
WAYS = 3

seam_damping = 0.8
offset_unit = 32.0
spectrum_low = 0.08
spectrum_high = 2.0
MIX = 2.4

VMEM_LIMIT = 28 * 1024 * 1024


def chebyshev_polynomial():
    centre = (spectrum_high + spectrum_low) / 2.0
    radius = (spectrum_high - spectrum_low) / 2.0
    sigma = centre / radius
    size = SWEEPS
    update = [1.0 / centre] + [0.0] * (size - 1)
    smoothed = list(update)
    rho = 1.0 / sigma
    for _ in range(SWEEPS - 1):
        remainder = [-s for s in smoothed]
        remainder[0] += 1.0
        for k in range(size - 1):
            remainder[k + 1] += smoothed[k]
        following = 1.0 / (2.0 * sigma - rho)
        update = [following * rho * u + 2.0 * following / radius * r for u, r in zip(update, remainder)]
        smoothed = [s + u for s, u in zip(smoothed, update)]
        rho = following
    return smoothed


def lane_index():
    return lax.broadcasted_iota(jnp.int32, (SUBS, LANES), 1)


def own_kernel(
    place_ref, offsets_ref, src_hbm, weight_hbm, seam_right_hbm, seam_down_hbm,
    own_ref, first_swap_ref, second_swap_ref,
    src_ref, weight_ref, seam_right_ref, seam_down_ref, sems,
):
    chans, rows, cols = src_ref.shape
    own_tiles = cols // LANES
    copies = [pltpu.make_async_copy(src_hbm.at[c], src_ref.at[c], sems.at[c]) for c in range(chans)]
    for k, (there, here) in enumerate(
        ((weight_hbm, weight_ref), (seam_right_hbm, seam_right_ref), (seam_down_hbm, seam_down_ref))
    ):
        copies.append(pltpu.make_async_copy(there, here, sems.at[chans + k]))
    for copy in copies:
        copy.start()
    lane = lane_index()
    sub = lax.broadcasted_iota(jnp.int32, (SUBS, LANES), 0)
    last_row, last_lane, tile_row, tile_at = [place_ref[k] for k in range(4)]
    odd = place_ref[5] == 1
    shift = [
        [
            jnp.broadcast_to(offsets_ref[c, tile_row, tile_at + k], (SUBS, LANES)).astype(jnp.float32) / offset_unit
            for k in range(cols // TILE)
        ]
        for c in range(chans)
    ]
    for copy in copies:
        copy.wait()

    def body(t, carry):
        at = pl.multiple_of(SUBS * t, SUBS)
        here = pl.ds(at, SUBS)
        ends_of = {}
        for j in range(own_tiles):
            there = pl.ds(j * LANES, LANES)
            planes = [src_ref[c, here, there] + shift[c][j * LANES // TILE] for c in range(chans)]
            planes.append(weight_ref[here, there])
            to_right = 1.0 - seam_damping * seam_right_ref[here, there].astype(jnp.float32)
            if j == own_tiles - 1:
                to_right = jnp.where(lane == last_lane, 0.0, to_right)
            to_down = 1.0 - seam_damping * seam_down_ref[here, there].astype(jnp.float32)
            planes += [to_right, jnp.where(at + sub == last_row, 0.0, to_down)]
            for p, plane in enumerate(planes):
                own_ref[p, j, here, :] = plane
            if j in (0, own_tiles - 1):
                ends_of[j] = planes
        ends = []
        for start, planes in ((0, ends_of[0]), (LANES - SLOT, ends_of[own_tiles - 1])):
            packed = [None] * (-(-len(planes) // SLOTS))
            for p, plane in enumerate(planes):
                slot = p % SLOTS
                by = (slot * SLOT - start) % LANES
                moved = pltpu.roll(plane, by, 1) if by else plane
                k = p // SLOTS
                packed[k] = moved if slot == 0 else jnp.where(lane < slot * SLOT, packed[k], moved)
            ends.append(packed)
        for k, (low, high) in enumerate(zip(*ends)):
            first_swap_ref[k, here, :] = jnp.where(odd, low, high)
            second_swap_ref[k, here, :] = jnp.where(odd, high, low)
        return carry

    lax.fori_loop(0, rows // SUBS, body, 0)


def unpack(p, lefts, rights):
    lane = lax.broadcasted_iota(jnp.int32, lefts.shape, 1)
    slot = p % SLOTS
    if slot != SLOTS - 1:
        lefts = pltpu.roll(lefts, LANES - SLOT - slot * SLOT, 1)
    if slot:
        rights = pltpu.roll(rights, LANES - slot * SLOT, 1)
    return jnp.where(lane < SLOT, rights, jnp.where(lane >= LANES - SLOT, lefts, 0.0))


def ways_of(tiles):
    return WAYS if tiles % WAYS == 0 else 1


def exact_parts(value):
    high = value.astype(jnp.bfloat16)
    rest = value - high.astype(jnp.float32)
    middle = rest.astype(jnp.bfloat16)
    low = (rest - middle.astype(jnp.float32)).astype(jnp.bfloat16)
    return jnp.concatenate([high, middle, low], axis=0)


def permuted(value, index):
    rows = value.shape[0]
    out = jnp.dot(exact_parts(value), index, preferred_element_type=jnp.float32)
    return (out[:rows] + out[rows:2 * rows]) + out[2 * rows:]


def dealing(ways):
    size = ways * LANES
    column = lax.broadcasted_iota(jnp.int32, (size, size), 0)
    place = lax.broadcasted_iota(jnp.int32, (size, size), 1)
    return jnp.where(column == ways * (place % LANES) + place // LANES, 1.0, 0.0).astype(jnp.bfloat16)


def undealing(ways):
    size = ways * LANES
    column = lax.broadcasted_iota(jnp.int32, (size, size), 1)
    place = lax.broadcasted_iota(jnp.int32, (size, size), 0)
    return jnp.where(column == ways * (place % LANES) + place // LANES, 1.0, 0.0).astype(jnp.bfloat16)


def deal(tile_of, tiles, emit):
    ways = ways_of(tiles)
    matrix = dealing(ways) if ways > 1 else None
    for g in range(0, tiles, ways):
        if ways == 1:
            emit(g, tile_of(g))
            continue
        value = permuted(jnp.concatenate([tile_of(g + m) for m in range(ways)], axis=1), matrix)
        for m in range(ways):
            emit(g + m, value[:, m * LANES:(m + 1) * LANES])


def own_dealt_kernel(own_ref, before_ref, after_ref, dealt_ref):
    planes, own_tiles, rows = own_ref.shape[:3]

    def tile_of(j):
        if j < own_tiles:
            return own_ref[:, j].reshape(planes * rows, LANES)
        return jnp.concatenate([unpack(p, before_ref[p // SLOTS], after_ref[p // SLOTS]) for p in range(planes)], axis=0)

    def emit(j, value):
        dealt_ref[:, j] = value.reshape(planes, rows, LANES)

    deal(tile_of, own_tiles + 1, emit)


def rightward(values):
    tiles = len(values)
    ways = ways_of(tiles)
    last = lane_index() == LANES - 1
    ahead = {g: pltpu.roll(values[g], LANES - 1, 1) for g in range(0, tiles, ways)}
    out = []
    for j in range(tiles):
        if j % ways + 1 < ways:
            out.append(values[j + 1])
        else:
            g = j - ways + 1
            out.append(jnp.where(last, ahead[(g + ways) % tiles], ahead[g]))
    return out


def leftward(values):
    tiles = len(values)
    ways = ways_of(tiles)
    first = lane_index() == 0
    behind = {g: pltpu.roll(values[g + ways - 1], 1, 1) for g in range(0, tiles, ways)}
    out = []
    for j in range(tiles):
        if j % ways:
            out.append(values[j - 1])
        else:
            out.append(jnp.where(first, behind[(j - ways) % tiles], behind[j]))
    return out


def spread(b_right_ref, b_down_ref, z_ref, emit):
    tiles, height = z_ref.shape[:2]
    steps = height // SUBS
    ways = ways_of(tiles)
    lane = lane_index()
    first, last = (lane == 0, lane == LANES - 1)

    def at(i):
        return pl.ds(i * SUBS, SUBS)

    from_above = [pltpu.roll(b_down_ref[j, at(steps - 1), :] * z_ref[j, at(steps - 1), :], 1, 0) for j in range(tiles)]
    centre = [z_ref[j, at(0), :] for j in range(tiles)]
    wrapped = [pltpu.roll(v, SUBS - 1, 0) for v in centre]
    for i in range(steps):
        pushed_out = {
            g: pltpu.roll(b_right_ref[g + ways - 1, at(i), :] * centre[g + ways - 1], 1, 1)
            for g in range(0, tiles, ways)
        }
        ahead = {g: pltpu.roll(centre[g], LANES - 1, 1) for g in range(0, tiles, ways)}
        pushed = None
        below = []
        for j in range(tiles):
            g = j // ways * ways
            b_right = b_right_ref[j, at(i), :]
            b_down = b_down_ref[j, at(i), :]
            below.append(z_ref[j, at(i + 1), :] if i + 1 < steps else wrapped[j])
            if j == g:
                from_left = jnp.where(first, pushed_out[(g - ways) % tiles], pushed_out[g])
            else:
                from_left = pushed
            if j + 1 < g + ways:
                to_right = centre[j + 1]
                pushed = b_right * centre[j]
            else:
                to_right = jnp.where(last, ahead[(g + ways) % tiles], ahead[g])
            moved = (b_right * to_right + from_left) + (b_down * below[j] + from_above[j])
            from_above[j] = b_down * centre[j]
            emit(i, j, centre[j], moved)
        centre = below


def precondition(b_right_ref, b_down_ref, g_ref, z_ref, work_ref):
    poly = chebyshev_polynomial()
    degree = SWEEPS - 1

    def at(i):
        return pl.ds(i * SUBS, SUBS)

    def first(i, j, centre, moved):
        z_ref[j, at(i), :] = poly[degree] * moved + poly[degree - 1] * centre

    spread(b_right_ref, b_down_ref, g_ref, first)

    def pair(k, carry):
        adds = []
        for half in range(2):
            value = jnp.float32(poly[half])
            for later in range(1, (degree - 1) // 2):
                value = jnp.where(k == (degree - 1) // 2 - 1 - later, jnp.float32(poly[2 * later + half]), value)
            adds.append(value)

        def one(target, add):
            def emit(i, j, centre, moved):
                target[j, at(i), :] = moved + add * g_ref[j, at(i), :]

            return emit

        spread(b_right_ref, b_down_ref, z_ref, one(work_ref, adds[1]))
        spread(b_right_ref, b_down_ref, work_ref, one(z_ref, adds[0]))
        return carry

    lax.fori_loop(0, (degree - 1) // 2, pair, 0)


def next_residual(b_right_ref, b_down_ref, g_ref, z_ref, next_ref, own_of):
    height = g_ref.shape[1]
    steps = height // SUBS
    sums = {}

    def emit(i, j, centre, moved):
        at = pl.ds(i * SUBS, SUBS)
        g = g_ref[j, at, :]
        following = g - MIX * (centre - moved)
        next_ref[j, at, :] = following
        key = own_of(i, j)
        now = (g * centre, following * centre)
        before = sums.get(key)
        sums[key] = now if before is None else (before[0] + now[0], before[1] + now[1])

    spread(b_right_ref, b_down_ref, z_ref, emit)
    sub = lax.broadcasted_iota(jnp.int32, (SUBS, LANES), 0)
    lane = lane_index()
    total = [jnp.zeros((SUBS, LANES), jnp.float32)] * 2
    for (low, high, lanes), parts in sums.items():
        inside = jnp.logical_and(jnp.logical_and(sub >= low, sub <= high), lane < lanes)
        total = [t + jnp.where(inside, p, 0.0) for t, p in zip(total, parts)]
    return total


def first_kernel(
    place_ref, dealt_ref, first_rows_ref, second_rows_ref, first_corners_ref, second_corners_ref,
    b_right_ref, b_down_ref, scale_ref, root_ref, g0_ref, z0_ref, g1_ref, f1_ref, g2_ref, sums_ref,
    natural, work_ref,
):
    planes, tiles, rows = dealt_ref.shape[:3]
    chans = planes - 3
    own_tiles = tiles - 1
    height = rows + 2 * HALO
    steps = height // SUBS

    def copy_own(t, carry):
        here = pl.ds(pl.multiple_of(SUBS * t, SUBS), SUBS)
        there = pl.ds(pl.multiple_of(HALO + SUBS * t, SUBS), SUBS)
        for p in range(planes):
            for j in range(tiles):
                natural[p, j, there, :] = dealt_ref[p, j, here, :]
        return carry

    lax.fori_loop(0, rows // SUBS, copy_own, 0)

    odd = place_ref[4] == 1

    def edge_tile(j):
        if j < own_tiles:
            first, second = [ref[:, j].reshape(planes * HALO, LANES) for ref in (first_rows_ref, second_rows_ref)]
        else:
            first, second = [
                jnp.concatenate([unpack(p, ref[0, p // SLOTS], ref[1, p // SLOTS]) for p in range(planes)], axis=0)
                for ref in (first_corners_ref, second_corners_ref)
            ]
        return jnp.concatenate([jnp.where(odd, first, second), jnp.where(odd, second, first)], axis=0)

    def put_edge(j, value):
        value = value.reshape(2, planes, HALO, LANES)
        natural[:, j, 0:HALO, :] = value[0]
        natural[:, j, HALO + rows:height, :] = value[1]

    deal(edge_tile, tiles, put_edge)

    def at(i):
        return pl.ds(i * SUBS, SUBS)

    def interleaved(p, i, j):
        return natural[p, j, pl.ds(i, SUBS, stride=steps), :]

    to_up = [pltpu.roll(interleaved(chans + 2, steps - 1, j), 1, 0) for j in range(tiles)]
    for i in range(steps):
        to_right = [interleaved(chans + 1, i, j) for j in range(tiles)]
        to_left = leftward(to_right)
        for j in range(tiles):
            to_down = interleaved(chans + 2, i, j)
            diag = interleaved(chans, i, j) + to_right[j] + to_left[j] + to_down + to_up[j]
            inside = diag > 0.0
            safe = jnp.where(inside, diag, 1.0)
            guess = lax.rsqrt(safe)
            scale = guess * (1.5 - 0.5 * safe * guess * guess)
            scale_ref[j, at(i), :] = jnp.where(inside, scale, 0.0)
            root_ref[j, at(i), :] = safe * scale
            to_up[j] = to_down
    wrapped = [pltpu.roll(scale_ref[j, at(0), :], SUBS - 1, 0) for j in range(tiles)]
    for i in range(steps):
        scale = [scale_ref[j, at(i), :] for j in range(tiles)]
        right_scale = rightward(scale)
        for j in range(tiles):
            b_right_ref[j, at(i), :] = interleaved(chans + 1, i, j) * scale[j] * right_scale[j]
            down_scale = scale_ref[j, at(i + 1), :] if i + 1 < steps else wrapped[j]
            b_down_ref[j, at(i), :] = interleaved(chans + 2, i, j) * scale[j] * down_scale
            for c in range(chans):
                g0_ref[c, j, at(i), :] = interleaved(c, i, j) * scale[j]

    ways = ways_of(tiles)

    def own_of(i, j):
        low, high = -(-(HALO - i) // steps), (HALO + rows - 1 - i) // steps
        left = own_tiles * LANES - j // ways * ways * LANES - j % ways
        return low, high, min(LANES, max(0, -(-left // ways)))

    def channel(c, carry):
        g0, z0, g1, f1, g2 = [ref.at[c] for ref in (g0_ref, z0_ref, g1_ref, f1_ref, g2_ref)]
        precondition(b_right_ref, b_down_ref, g0, z0, work_ref)
        sum0, sum1 = next_residual(b_right_ref, b_down_ref, g0, z0, g1, own_of)
        precondition(b_right_ref, b_down_ref, g1, f1, work_ref)
        sum2, sum3 = next_residual(b_right_ref, b_down_ref, g1, f1, g2, own_of)
        return tuple(a + b for a, b in zip(carry, (sum0, sum1, sum2, sum3)))

    zero = jnp.zeros((SUBS, LANES), jnp.float32)
    parts = lax.fori_loop(0, chans, channel, (zero,) * 4)
    sub = lax.broadcasted_iota(jnp.int32, (SUBS, LANES), 0)
    sums = zero
    for k, part in enumerate(parts):
        sums = jnp.where(sub == k, jnp.sum(part), sums)
    sums_ref[...] = sums


def second_kernel(c, b_right_ref, b_down_ref, g2_ref, f2_ref, work_ref):
    precondition(b_right_ref, b_down_ref, g2_ref.at[c], f2_ref, work_ref)


def combine(n0, n1, n2, n3):
    gap = n0 - n1
    keep = -n1 / gap
    step = n0 / gap
    beta = (n0 * n2 - n1 * n1) / (gap * gap)
    along = keep + beta
    curvature = along * along * gap + 2.0 * along * step * (n1 - n2) + step * step * (n2 - n3)
    scaled = n0 * beta / curvature
    first_size = step * MIX
    second_size = scaled * MIX
    x0 = first_size + second_size * along
    x1 = second_size * step
    r0 = keep - scaled * along
    r1 = step + scaled * (along - step)
    r2 = scaled * step
    return x0, x1, r0, r1, r2


def third_kernel(
    sums_ref, scale_ref, root_ref, g0_ref, z0_ref, g1_ref, f1_ref, g2_ref, *refs
):
    *f2_refs, solution_hbm, residual_hbm, smoothed_hbm, natural, done, sems = refs
    rows, cols = solution_hbm.shape[1:]
    own_tiles = cols // LANES
    tiles, height = scale_ref.shape[:2]
    steps = height // SUBS
    ways = ways_of(tiles)
    x0, x1, r0, r1, r2 = combine(*[jnp.broadcast_to(sums_ref[k:k + 1, :], (SUBS, LANES)) for k in range(4)])
    matrix = undealing(ways) if ways > 1 else None
    outs = (solution_hbm, residual_hbm, smoothed_hbm)
    copies = []
    for c, f2_ref in enumerate(f2_refs):
        for j in range(tiles):
            for i in range(steps):
                at = pl.ds(i * SUBS, SUBS)
                scale = scale_ref[j, at, :]
                root = root_ref[j, at, :]
                g0, g1, g2, z0, f1 = [ref[c, j, at, :] for ref in (g0_ref, g1_ref, g2_ref, z0_ref, f1_ref)]
                f2 = f2_ref[j, at, :]
                there = pl.ds(i, SUBS, stride=steps)
                natural[c, 0, j, there, :] = scale * (x0 * z0 + x1 * f1)
                natural[c, 1, j, there, :] = root * (r0 * g0 + r1 * g1 + r2 * g2)
                natural[c, 2, j, there, :] = scale * (r0 * z0 + r1 * f1 + r2 * f2)
        for g in range(0, own_tiles, ways):
            value = jnp.concatenate(
                [natural[c, :, g + m, HALO:HALO + rows, :].reshape(3 * rows, LANES) for m in range(ways)], axis=1
            )
            width = min(ways, own_tiles - g) * LANES
            if ways > 1:
                value = permuted(value, matrix[:, :width])
            for k in range(len(outs)):
                done[c, k, :, g * LANES:g * LANES + width] = value[k * rows:(k + 1) * rows]
        for k, ref in enumerate(outs):
            copies.append(pltpu.make_async_copy(done.at[c, k], ref.at[c], sems.at[c, k]))
            copies[-1].start()
    for copy in copies:
        copy.wait()


def sum_over(value, axis):
    size = lax.axis_size(axis)
    if size & (size - 1):
        return lax.psum(value, axis)
    step = 1
    while step < size:
        value = value + lax.ppermute(value, axis, [(i, i ^ step) for i in range(size)])
        step *= 2
    return value


def per_device(source, weight, seam_right, seam_down, offsets):
    chans, rows, cols = source.shape
    row_axis, col_axis = lax.axis_size("row"), lax.axis_size("col")
    row_at, col_at = lax.axis_index("row"), lax.axis_index("col")
    odd_row, odd_col = lax.rem(row_at, 2), lax.rem(col_at, 2)
    place = jnp.stack(
        [
            jnp.where(row_at == row_axis - 1, rows - 1, -1),
            jnp.where(col_at == col_axis - 1, LANES - 1, -1),
            lax.div(row_at * rows, TILE),
            col_at * (cols // TILE),
            odd_row,
            odd_col,
        ]
    ).astype(jnp.int32)

    in_vmem = pl.BlockSpec(memory_space=pltpu.VMEM)
    in_smem = pl.BlockSpec(memory_space=pltpu.SMEM)
    in_hbm = pl.BlockSpec(memory_space=pltpu.HBM)
    params = pltpu.CompilerParams(vmem_limit_bytes=VMEM_LIMIT)

    def shaped(*shape):
        return jax.ShapeDtypeStruct(shape, jnp.float32)

    def scratch(*shape):
        return pltpu.VMEM(shape, jnp.float32)

    planes = chans + 3
    own_tiles = cols // LANES
    tiles = own_tiles + 1
    packs = -(-planes // SLOTS)
    own, first_cols, second_cols = pl.pallas_call(
        own_kernel,
        out_shape=[shaped(planes, own_tiles, rows, LANES)] + [shaped(packs, rows, LANES)] * 2,
        in_specs=[in_smem] * 2 + [in_hbm] * 4,
        out_specs=[in_vmem] * 3,
        scratch_shapes=[
            scratch(*source.shape),
            scratch(*weight.shape),
            pltpu.VMEM(weight.shape, jnp.int32),
            pltpu.VMEM(weight.shape, jnp.int32),
            pltpu.SemaphoreType.DMA((planes,)),
        ],
        compiler_params=params,
    )(
        place,
        offsets.transpose(2, 0, 1),
        *[pltpu.with_memory_space_constraint(v, pltpu.HBM) for v in (source, weight, seam_right, seam_down)],
    )

    def swap(first, second, axis):
        size = lax.axis_size(axis)
        pairs = [[(i, i + 1) for i in range(start, size - 1, 2)] for start in range(2)]
        pairs = [some + [(j, i) for i, j in some] for some in pairs]
        return [lax.ppermute(value, axis, some) for value, some in zip((first, second), pairs)]

    def ends_of_rows(value):
        high = (1 - odd_row) * (rows - HALO)
        return [lax.dynamic_slice_in_dim(value, at, HALO, axis=2) for at in (high, rows - HALO - high)]

    first_rows, second_rows = swap(*ends_of_rows(own), "row")
    first_cols, second_cols = swap(first_cols, second_cols, "col")
    before = jnp.where(odd_col == 1, first_cols, second_cols)
    after = jnp.where(odd_col == 1, second_cols, first_cols)
    first_corners, second_corners = swap(*ends_of_rows(jnp.stack([before, after])), "row")
    dealt = pl.pallas_call(
        own_dealt_kernel,
        out_shape=shaped(planes, tiles, rows, LANES),
        in_specs=[in_vmem] * 3,
        out_specs=in_vmem,
        compiler_params=params,
        cost_estimate=pl.CostEstimate(flops=10**8, bytes_accessed=5 * 10**6, transcendentals=0),
    )(own, before, after)

    height = rows + 2 * HALO
    plane = shaped(tiles, height, LANES)
    field = shaped(chans, tiles, height, LANES)
    *basis, sums = pl.pallas_call(
        first_kernel,
        out_shape=[plane] * 4 + [field] * 5 + [shaped(SUBS, LANES)],
        in_specs=[in_smem] + [in_vmem] * 5,
        out_specs=[in_vmem] * 10,
        scratch_shapes=[scratch(planes, tiles, height, LANES), scratch(*plane.shape)],
        compiler_params=params,
    )(place, dealt, first_rows, second_rows, first_corners, second_corners)

    total = sum_over(sum_over(sums, "col"), "row")
    b_right, b_down, scale, root, g0, z0, g1, f1, g2 = basis
    f2 = [
        pl.pallas_call(
            functools.partial(second_kernel, c),
            out_shape=plane,
            in_specs=[in_vmem] * 3,
            out_specs=in_vmem,
            scratch_shapes=[scratch(*plane.shape)],
            compiler_params=params,
            cost_estimate=pl.CostEstimate(flops=10**8, bytes_accessed=10**7, transcendentals=0),
        )(b_right, b_down, g2)
        for c in range(chans)
    ]
    return pl.pallas_call(
        third_kernel,
        out_shape=[shaped(chans, rows, cols)] * 3,
        in_specs=[in_vmem] * (8 + chans),
        out_specs=[pl.BlockSpec(memory_space=pltpu.HBM)] * 3,
        scratch_shapes=[
            scratch(chans, 3, tiles, height, LANES),
            scratch(chans, 3, rows, cols),
            pltpu.SemaphoreType.DMA((chans, 3)),
        ],
        compiler_params=params,
    )(total, scale, root, g0, z0, g1, f1, g2, *f2)


def solution(mesh):
    placed = (
        P(None, ("band", "row"), "col"),
        P(("band", "row"), "col"),
        P(("band", "row"), "col"),
        P(("band", "row"), "col"),
        P("band", None, None),
    )
    return jax.shard_map(
        per_device,
        mesh=mesh,
        in_specs=placed,
        out_specs=(
            P(None, ("band", "row"), "col"),
            P(None, ("band", "row"), "col"),
            P(None, ("band", "row"), "col"),
        ),
        check_vma=False,
    )
```

```python
import functools

import jax
import jax.numpy as jnp
from jax import lax
from jax.experimental import pallas as pl
from jax.experimental.pallas import tpu as pltpu
from jax.sharding import PartitionSpec as P

TILE = 256
SWEEPS = 8
SUBS = 8
LANES = 128
HALO = 24
SLOT = 32
SLOTS = LANES // SLOT
WAYS = 3

seam_damping = 0.8
offset_unit = 32.0
spectrum_low = 0.08
spectrum_high = 2.0
MIX = 2.4

VMEM_LIMIT = 28 * 1024 * 1024


def chebyshev_polynomial():
    centre = (spectrum_high + spectrum_low) / 2.0
    radius = (spectrum_high - spectrum_low) / 2.0
    sigma = centre / radius
    size = SWEEPS
    update = [1.0 / centre] + [0.0] * (size - 1)
    smoothed = list(update)
    rho = 1.0 / sigma
    for _ in range(SWEEPS - 1):
        remainder = [-s for s in smoothed]
        remainder[0] += 1.0
        for k in range(size - 1):
            remainder[k + 1] += smoothed[k]
        following = 1.0 / (2.0 * sigma - rho)
        update = [following * rho * u + 2.0 * following / radius * r for u, r in zip(update, remainder)]
        smoothed = [s + u for s, u in zip(smoothed, update)]
        rho = following
    return smoothed


def lane_index():
    return lax.broadcasted_iota(jnp.int32, (SUBS, LANES), 1)


def pack(planes, start):
    lane = lane_index()
    packed = [None] * (-(-len(planes) // SLOTS))
    for p, plane in enumerate(planes):
        slot = p % SLOTS
        by = (slot * SLOT - start) % LANES
        moved = pltpu.roll(plane, by, 1) if by else plane
        k = p // SLOTS
        packed[k] = moved if slot == 0 else jnp.where(lane < slot * SLOT, packed[k], moved)
    return packed


def own_kernel(
    place_ref, offsets_ref, src_hbm, weight_hbm, seam_right_hbm, seam_down_hbm,
    own_ref, first_rows_ref, second_rows_ref, first_cols_ref, second_cols_ref,
    src_ref, weight_ref, seam_right_ref, seam_down_ref, sems,
):
    chans, rows, cols = src_ref.shape
    own_tiles = cols // LANES
    moves = [(weight_hbm, weight_ref), (seam_right_hbm, seam_right_ref), (seam_down_hbm, seam_down_ref)]
    moves += [(src_hbm.at[c], src_ref.at[c]) for c in range(chans)]
    copies = [pltpu.make_async_copy(there, here, sems.at[k]) for k, (there, here) in enumerate(moves)]
    for copy in copies:
        copy.start()
    lane = lane_index()
    sub = lax.broadcasted_iota(jnp.int32, (SUBS, LANES), 0)
    last_row, last_lane, tile_row, tile_at = [place_ref[k] for k in range(4)]
    odd_row, odd_col = (place_ref[4] == 1, place_ref[5] == 1)

    def over_own(plane, value_of):
        def body(t, carry):
            at = pl.multiple_of(SUBS * t, SUBS)
            for j in range(own_tiles):
                own_ref[plane, j, pl.ds(at, SUBS), :] = value_of(at, j)
            return carry

        lax.fori_loop(0, rows // SUBS, body, 0)

    def tile(ref, at, j):
        return ref[pl.ds(at, SUBS), pl.ds(j * LANES, LANES)]

    def to_right(at, j):
        value = 1.0 - seam_damping * tile(seam_right_ref, at, j).astype(jnp.float32)
        return jnp.where(lane == last_lane, 0.0, value) if j == own_tiles - 1 else value

    def to_down(at, j):
        value = 1.0 - seam_damping * tile(seam_down_ref, at, j).astype(jnp.float32)
        return jnp.where(at + sub == last_row, 0.0, value)

    copies[0].wait()
    over_own(chans, lambda at, j: tile(weight_ref, at, j))
    copies[1].wait()
    over_own(chans + 1, to_right)
    copies[2].wait()
    over_own(chans + 2, to_down)
    for c in range(chans):
        shift = [
            jnp.broadcast_to(offsets_ref[c, tile_row, tile_at + k], (SUBS, LANES)).astype(jnp.float32) / offset_unit
            for k in range(cols // TILE)
        ]
        copies[3 + c].wait()
        over_own(c, lambda at, j, c=c, shift=shift: tile(src_ref.at[c], at, j) + shift[j * LANES // TILE])

    planes = range(chans + 3)
    low, high = pl.ds(0, HALO), pl.ds(rows - HALO, HALO)
    for ref, odd, even in ((first_rows_ref, low, high), (second_rows_ref, high, low)):

        @pl.when(odd_row)
        def _(ref=ref, odd=odd):
            for p in planes:
                ref[p] = own_ref[p, :, odd, :]

        @pl.when(jnp.logical_not(odd_row))
        def _(ref=ref, even=even):
            for p in planes:
                ref[p] = own_ref[p, :, even, :]

    def columns(t, carry):
        here = pl.ds(pl.multiple_of(SUBS * t, SUBS), SUBS)
        left = pack([own_ref[p, 0, here, :] for p in planes], 0)
        right = pack([own_ref[p, own_tiles - 1, here, :] for p in planes], LANES - SLOT)
        for k, (a, b) in enumerate(zip(left, right)):
            first_cols_ref[k, here, :] = jnp.where(odd_col, a, b)
            second_cols_ref[k, here, :] = jnp.where(odd_col, b, a)
        return carry

    lax.fori_loop(0, rows // SUBS, columns, 0)


def corners_kernel(place_ref, first_ref, second_ref, first_out, second_out):
    rows = first_ref.shape[1]
    odd_row, odd_col = (place_ref[4] == 1, place_ref[5] == 1)
    for k in range(first_ref.shape[0]):
        for low in range(0, HALO, SUBS):
            lows = [ref[k, low:low + SUBS, :] for ref in (first_ref, second_ref)]
            at = rows - HALO + low
            highs = [ref[k, at:at + SUBS, :] for ref in (first_ref, second_ref)]
            for side in range(2):
                near = jnp.where(odd_col, lows[side], lows[1 - side])
                far = jnp.where(odd_col, highs[side], highs[1 - side])
                first_out[side, k, low:low + SUBS, :] = jnp.where(odd_row, near, far)
                second_out[side, k, low:low + SUBS, :] = jnp.where(odd_row, far, near)


def unpack(p, lefts, rights):
    lane = lax.broadcasted_iota(jnp.int32, lefts.shape, 1)
    slot = p % SLOTS
    if slot != SLOTS - 1:
        lefts = pltpu.roll(lefts, LANES - SLOT - slot * SLOT, 1)
    if slot:
        rights = pltpu.roll(rights, LANES - slot * SLOT, 1)
    return jnp.where(lane < SLOT, rights, jnp.where(lane >= LANES - SLOT, lefts, 0.0))


def ways_of(tiles):
    return WAYS if tiles % WAYS == 0 else 1


def split(value, count):
    parts = []
    for k in range(count):
        part = value.astype(jnp.bfloat16)
        parts.append(part)
        if k + 1 < count:
            value = value - part.astype(jnp.float32)
    return jnp.concatenate(parts, axis=0)


def permuted(value, index, count):
    rows = value.shape[0]
    out = jnp.dot(split(value, count), index, preferred_element_type=jnp.float32)
    total = out[:rows]
    for k in range(1, count):
        total = total + out[k * rows:(k + 1) * rows]
    return total


def dealing(ways):
    size = ways * LANES
    column = lax.broadcasted_iota(jnp.int32, (size, size), 0)
    place = lax.broadcasted_iota(jnp.int32, (size, size), 1)
    return jnp.where(column == ways * (place % LANES) + place // LANES, 1.0, 0.0).astype(jnp.bfloat16)


def undealing(ways):
    size = ways * LANES
    column = lax.broadcasted_iota(jnp.int32, (size, size), 1)
    place = lax.broadcasted_iota(jnp.int32, (size, size), 0)
    return jnp.where(column == ways * (place % LANES) + place // LANES, 1.0, 0.0).astype(jnp.bfloat16)


def deal(tile_of, tiles, emit):
    ways = ways_of(tiles)
    matrix = dealing(ways) if ways > 1 else None
    for g in range(0, tiles, ways):
        if ways == 1:
            emit(g, tile_of(g))
            continue
        value = permuted(jnp.concatenate([tile_of(g + m) for m in range(ways)], axis=1), matrix, 3)
        for m in range(ways):
            emit(g + m, value[:, m * LANES:(m + 1) * LANES])


def own_dealt_kernel(place_ref, own_ref, first_ref, second_ref, dealt_ref):
    planes, own_tiles, rows = own_ref.shape[:3]
    odd = place_ref[5] == 1

    def tile_of(j):
        if j < own_tiles:
            return own_ref[:, j].reshape(planes * rows, LANES)
        parts = []
        for p in range(planes):
            first, second = first_ref[p // SLOTS], second_ref[p // SLOTS]
            parts.append(unpack(p, jnp.where(odd, first, second), jnp.where(odd, second, first)))
        return jnp.concatenate(parts, axis=0)

    def emit(j, value):
        dealt_ref[:, j] = value.reshape(planes, rows, LANES)

    deal(tile_of, own_tiles + 1, emit)


def rightward(values):
    tiles = len(values)
    ways = ways_of(tiles)
    last = lane_index() == LANES - 1
    ahead = {g: pltpu.roll(values[g], LANES - 1, 1) for g in range(0, tiles, ways)}
    out = []
    for j in range(tiles):
        if j % ways + 1 < ways:
            out.append(values[j + 1])
        else:
            g = j - ways + 1
            out.append(jnp.where(last, ahead[(g + ways) % tiles], ahead[g]))
    return out


def leftward(values):
    tiles = len(values)
    ways = ways_of(tiles)
    first = lane_index() == 0
    behind = {g: pltpu.roll(values[g + ways - 1], 1, 1) for g in range(0, tiles, ways)}
    out = []
    for j in range(tiles):
        if j % ways:
            out.append(values[j - 1])
        else:
            out.append(jnp.where(first, behind[(j - ways) % tiles], behind[j]))
    return out


def spread(b_right_ref, b_down_ref, z_ref, emit):
    tiles, height = z_ref.shape[:2]
    steps = height // SUBS
    ways = ways_of(tiles)
    lane = lane_index()
    first, last = (lane == 0, lane == LANES - 1)

    def at(i):
        return pl.ds(i * SUBS, SUBS)

    from_above = [pltpu.roll(b_down_ref[j, at(steps - 1), :] * z_ref[j, at(steps - 1), :], 1, 0) for j in range(tiles)]
    centre = [z_ref[j, at(0), :] for j in range(tiles)]
    wrapped = [pltpu.roll(v, SUBS - 1, 0) for v in centre]
    for i in range(steps):
        pushed_out = {
            g: pltpu.roll(b_right_ref[g + ways - 1, at(i), :] * centre[g + ways - 1], 1, 1)
            for g in range(0, tiles, ways)
        }
        ahead = {g: pltpu.roll(centre[g], LANES - 1, 1) for g in range(0, tiles, ways)}
        pushed = None
        below = []
        for j in range(tiles):
            g = j // ways * ways
            b_right = b_right_ref[j, at(i), :]
            b_down = b_down_ref[j, at(i), :]
            below.append(z_ref[j, at(i + 1), :] if i + 1 < steps else wrapped[j])
            if j == g:
                from_left = jnp.where(first, pushed_out[(g - ways) % tiles], pushed_out[g])
            else:
                from_left = pushed
            if j + 1 < g + ways:
                to_right = centre[j + 1]
                pushed = b_right * centre[j]
            else:
                to_right = jnp.where(last, ahead[(g + ways) % tiles], ahead[g])
            moved = (b_right * to_right + from_left) + (b_down * below[j] + from_above[j])
            from_above[j] = b_down * centre[j]
            emit(i, j, centre[j], moved)
        centre = below


def precondition(b_right_ref, b_down_ref, g_ref, z_ref, work_ref):
    poly = chebyshev_polynomial()
    degree = SWEEPS - 1

    def at(i):
        return pl.ds(i * SUBS, SUBS)

    def first(i, j, centre, moved):
        z_ref[j, at(i), :] = poly[degree] * moved + poly[degree - 1] * centre

    spread(b_right_ref, b_down_ref, g_ref, first)

    def pair(k, carry):
        adds = []
        for half in range(2):
            value = jnp.float32(poly[half])
            for later in range(1, (degree - 1) // 2):
                value = jnp.where(k == (degree - 1) // 2 - 1 - later, jnp.float32(poly[2 * later + half]), value)
            adds.append(value)

        def one(target, add):
            def emit(i, j, centre, moved):
                target[j, at(i), :] = moved + add * g_ref[j, at(i), :]

            return emit

        spread(b_right_ref, b_down_ref, z_ref, one(work_ref, adds[1]))
        spread(b_right_ref, b_down_ref, work_ref, one(z_ref, adds[0]))
        return carry

    lax.fori_loop(0, (degree - 1) // 2, pair, 0)


def next_residual(b_right_ref, b_down_ref, g_ref, z_ref, next_ref, own_of):
    height = g_ref.shape[1]
    steps = height // SUBS
    sums = {}

    def emit(i, j, centre, moved):
        at = pl.ds(i * SUBS, SUBS)
        g = g_ref[j, at, :]
        following = g - MIX * (centre - moved)
        next_ref[j, at, :] = following
        key = own_of(i, j)
        now = (g * centre, following * centre)
        before = sums.get(key)
        sums[key] = now if before is None else (before[0] + now[0], before[1] + now[1])

    spread(b_right_ref, b_down_ref, z_ref, emit)
    sub = lax.broadcasted_iota(jnp.int32, (SUBS, LANES), 0)
    lane = lane_index()
    total = [jnp.zeros((SUBS, LANES), jnp.float32)] * 2
    for (low, high, lanes), parts in sums.items():
        inside = jnp.logical_and(jnp.logical_and(sub >= low, sub <= high), lane < lanes)
        total = [t + jnp.where(inside, p, 0.0) for t, p in zip(total, parts)]
    return total


def first_kernel(
    place_ref, dealt_ref, first_rows_ref, second_rows_ref, first_corners_ref, second_corners_ref,
    b_right_ref, b_down_ref, scale_ref, root_ref, g0_ref, z0_ref, g1_ref, f1_ref, g2_ref, sums_ref,
    natural, work_ref,
):
    planes, tiles, rows = dealt_ref.shape[:3]
    chans = planes - 3
    own_tiles = tiles - 1
    height = rows + 2 * HALO
    steps = height // SUBS

    def copy_own(t, carry):
        here = pl.ds(pl.multiple_of(SUBS * t, SUBS), SUBS)
        there = pl.ds(pl.multiple_of(HALO + SUBS * t, SUBS), SUBS)
        for p in range(planes):
            for j in range(tiles):
                natural[p, j, there, :] = dealt_ref[p, j, here, :]
        return carry

    lax.fori_loop(0, rows // SUBS, copy_own, 0)

    odd = place_ref[4] == 1

    def edge_tile(j):
        if j < own_tiles:
            first, second = [ref[:, j].reshape(planes * HALO, LANES) for ref in (first_rows_ref, second_rows_ref)]
        else:
            first, second = [
                jnp.concatenate([unpack(p, ref[0, p // SLOTS], ref[1, p // SLOTS]) for p in range(planes)], axis=0)
                for ref in (first_corners_ref, second_corners_ref)
            ]
        return jnp.concatenate([jnp.where(odd, first, second), jnp.where(odd, second, first)], axis=0)

    def put_edge(j, value):
        value = value.reshape(2, planes, HALO, LANES)
        natural[:, j, 0:HALO, :] = value[0]
        natural[:, j, HALO + rows:height, :] = value[1]

    deal(edge_tile, tiles, put_edge)

    def at(i):
        return pl.ds(i * SUBS, SUBS)

    def interleaved(p, i, j):
        return natural[p, j, pl.ds(i, SUBS, stride=steps), :]

    to_up = [pltpu.roll(interleaved(chans + 2, steps - 1, j), 1, 0) for j in range(tiles)]
    for i in range(steps):
        to_right = [interleaved(chans + 1, i, j) for j in range(tiles)]
        to_left = leftward(to_right)
        for j in range(tiles):
            to_down = interleaved(chans + 2, i, j)
            diag = interleaved(chans, i, j) + to_right[j] + to_left[j] + to_down + to_up[j]
            inside = diag > 0.0
            safe = jnp.where(inside, diag, 1.0)
            guess = lax.rsqrt(safe)
            scale = guess * (1.5 - 0.5 * safe * guess * guess)
            scale_ref[j, at(i), :] = jnp.where(inside, scale, 0.0)
            root_ref[j, at(i), :] = safe * scale
            to_up[j] = to_down
    wrapped = [pltpu.roll(scale_ref[j, at(0), :], SUBS - 1, 0) for j in range(tiles)]
    for i in range(steps):
        scale = [scale_ref[j, at(i), :] for j in range(tiles)]
        right_scale = rightward(scale)
        for j in range(tiles):
            b_right_ref[j, at(i), :] = interleaved(chans + 1, i, j) * scale[j] * right_scale[j]
            down_scale = scale_ref[j, at(i + 1), :] if i + 1 < steps else wrapped[j]
            b_down_ref[j, at(i), :] = interleaved(chans + 2, i, j) * scale[j] * down_scale
            for c in range(chans):
                g0_ref[c, j, at(i), :] = interleaved(c, i, j) * scale[j]

    ways = ways_of(tiles)

    def own_of(i, j):
        low, high = -(-(HALO - i) // steps), (HALO + rows - 1 - i) // steps
        left = own_tiles * LANES - j // ways * ways * LANES - j % ways
        return low, high, min(LANES, max(0, -(-left // ways)))

    def channel(c, carry):
        g0, z0, g1, f1, g2 = [ref.at[c] for ref in (g0_ref, z0_ref, g1_ref, f1_ref, g2_ref)]
        precondition(b_right_ref, b_down_ref, g0, z0, work_ref)
        sum0, sum1 = next_residual(b_right_ref, b_down_ref, g0, z0, g1, own_of)
        precondition(b_right_ref, b_down_ref, g1, f1, work_ref)
        sum2, sum3 = next_residual(b_right_ref, b_down_ref, g1, f1, g2, own_of)
        return tuple(a + b for a, b in zip(carry, (sum0, sum1, sum2, sum3)))

    zero = jnp.zeros((SUBS, LANES), jnp.float32)
    parts = lax.fori_loop(0, chans, channel, (zero,) * 4)
    sub = lax.broadcasted_iota(jnp.int32, (SUBS, LANES), 0)
    sums = zero
    for k, part in enumerate(parts):
        sums = jnp.where(sub == k, jnp.sum(part), sums)
    sums_ref[...] = sums


def second_kernel(c, b_right_ref, b_down_ref, g2_ref, f2_ref, work_ref):
    precondition(b_right_ref, b_down_ref, g2_ref.at[c], f2_ref, work_ref)


def combine(n0, n1, n2, n3):
    gap = n0 - n1
    keep = -n1 / gap
    step = n0 / gap
    beta = (n0 * n2 - n1 * n1) / (gap * gap)
    along = keep + beta
    curvature = along * along * gap + 2.0 * along * step * (n1 - n2) + step * step * (n2 - n3)
    scaled = n0 * beta / curvature
    first_size = step * MIX
    second_size = scaled * MIX
    x0 = first_size + second_size * along
    x1 = second_size * step
    r0 = keep - scaled * along
    r1 = step + scaled * (along - step)
    r2 = scaled * step
    return x0, x1, r0, r1, r2


def third_kernel(
    sums_ref, scale_ref, root_ref, g0_ref, z0_ref, g1_ref, f1_ref, g2_ref, *refs
):
    *f2_refs, solution_hbm, residual_hbm, smoothed_hbm, natural, done, sems = refs
    rows, cols = solution_hbm.shape[1:]
    own_tiles = cols // LANES
    tiles, height = scale_ref.shape[:2]
    steps = height // SUBS
    ways = ways_of(tiles)
    x0, x1, r0, r1, r2 = combine(*[jnp.broadcast_to(sums_ref[k:k + 1, :], (SUBS, LANES)) for k in range(4)])
    matrix = undealing(ways) if ways > 1 else None
    outs = (solution_hbm, residual_hbm, smoothed_hbm)
    copies = []
    for c, f2_ref in enumerate(f2_refs):
        for j in range(tiles):
            for i in range(steps):
                at = pl.ds(i * SUBS, SUBS)
                scale = scale_ref[j, at, :]
                root = root_ref[j, at, :]
                g0, g1, g2, z0, f1 = [ref[c, j, at, :] for ref in (g0_ref, g1_ref, g2_ref, z0_ref, f1_ref)]
                f2 = f2_ref[j, at, :]
                there = pl.ds(i, SUBS, stride=steps)
                natural[c, 0, j, there, :] = scale * (x0 * z0 + x1 * f1)
                natural[c, 1, j, there, :] = root * (r0 * g0 + r1 * g1 + r2 * g2)
                natural[c, 2, j, there, :] = scale * (r0 * z0 + r1 * f1 + r2 * f2)
        for g in range(0, own_tiles, ways):
            value = jnp.concatenate(
                [natural[c, :, g + m, HALO:HALO + rows, :].reshape(3 * rows, LANES) for m in range(ways)], axis=1
            )
            width = min(ways, own_tiles - g) * LANES
            if ways > 1:
                value = permuted(value, matrix[:, :width], 2)
            for k in range(len(outs)):
                done[c, k, :, g * LANES:g * LANES + width] = value[k * rows:(k + 1) * rows]
        for k, ref in enumerate(outs):
            copies.append(pltpu.make_async_copy(done.at[c, k], ref.at[c], sems.at[c, k]))
            copies[-1].start()
    for copy in copies:
        copy.wait()


def sum_over(value, axis):
    size = lax.axis_size(axis)
    if size & (size - 1):
        return lax.psum(value, axis)
    step = 1
    while step < size:
        value = value + lax.ppermute(value, axis, [(i, i ^ step) for i in range(size)])
        step *= 2
    return value


def per_device(source, weight, seam_right, seam_down, offsets):
    chans, rows, cols = source.shape
    row_axis, col_axis = lax.axis_size("row"), lax.axis_size("col")
    row_at, col_at = lax.axis_index("row"), lax.axis_index("col")
    odd_row, odd_col = lax.rem(row_at, 2), lax.rem(col_at, 2)
    place = jnp.stack(
        [
            jnp.where(row_at == row_axis - 1, rows - 1, -1),
            jnp.where(col_at == col_axis - 1, LANES - 1, -1),
            lax.div(row_at * rows, TILE),
            col_at * (cols // TILE),
            odd_row,
            odd_col,
        ]
    ).astype(jnp.int32)

    in_vmem = pl.BlockSpec(memory_space=pltpu.VMEM)
    in_smem = pl.BlockSpec(memory_space=pltpu.SMEM)
    in_hbm = pl.BlockSpec(memory_space=pltpu.HBM)
    params = pltpu.CompilerParams(vmem_limit_bytes=VMEM_LIMIT)

    def shaped(*shape):
        return jax.ShapeDtypeStruct(shape, jnp.float32)

    def scratch(*shape):
        return pltpu.VMEM(shape, jnp.float32)

    planes = chans + 3
    own_tiles = cols // LANES
    tiles = own_tiles + 1
    packs = -(-planes // SLOTS)
    own, first_rows, second_rows, first_cols, second_cols = pl.pallas_call(
        own_kernel,
        out_shape=[shaped(planes, own_tiles, rows, LANES)]
        + [shaped(planes, own_tiles, HALO, LANES)] * 2
        + [shaped(packs, rows, LANES)] * 2,
        in_specs=[in_smem] * 2 + [in_hbm] * 4,
        out_specs=[in_vmem] * 5,
        scratch_shapes=[
            scratch(*source.shape),
            scratch(*weight.shape),
            pltpu.VMEM(weight.shape, jnp.int32),
            pltpu.VMEM(weight.shape, jnp.int32),
            pltpu.SemaphoreType.DMA((planes,)),
        ],
        compiler_params=params,
    )(
        place,
        offsets.transpose(2, 0, 1),
        *[pltpu.with_memory_space_constraint(v, pltpu.HBM) for v in (source, weight, seam_right, seam_down)],
    )

    def swap(first, second, axis):
        size = lax.axis_size(axis)
        pairs = [[(i, i + 1) for i in range(start, size - 1, 2)] for start in range(2)]
        pairs = [some + [(j, i) for i, j in some] for some in pairs]
        return [lax.ppermute(value, axis, some) for value, some in zip((first, second), pairs)]

    first_rows, second_rows = swap(first_rows, second_rows, "row")
    first_cols, second_cols = swap(first_cols, second_cols, "col")
    corners = pl.pallas_call(
        corners_kernel,
        out_shape=[shaped(2, packs, HALO, LANES)] * 2,
        in_specs=[in_smem] + [in_vmem] * 2,
        out_specs=[in_vmem] * 2,
        compiler_params=params,
    )(place, first_cols, second_cols)
    first_corners, second_corners = swap(*corners, "row")
    dealt = pl.pallas_call(
        own_dealt_kernel,
        out_shape=shaped(planes, tiles, rows, LANES),
        in_specs=[in_smem] + [in_vmem] * 3,
        out_specs=in_vmem,
        compiler_params=params,
        cost_estimate=pl.CostEstimate(flops=10**8, bytes_accessed=5 * 10**6, transcendentals=0),
    )(place, own, first_cols, second_cols)

    height = rows + 2 * HALO
    plane = shaped(tiles, height, LANES)
    field = shaped(chans, tiles, height, LANES)
    *basis, sums = pl.pallas_call(
        first_kernel,
        out_shape=[plane] * 4 + [field] * 5 + [shaped(SUBS, LANES)],
        in_specs=[in_smem] + [in_vmem] * 5,
        out_specs=[in_vmem] * 10,
        scratch_shapes=[scratch(planes, tiles, height, LANES), scratch(*plane.shape)],
        compiler_params=params,
    )(place, dealt, first_rows, second_rows, first_corners, second_corners)

    total = sum_over(sum_over(sums, "col"), "row")
    b_right, b_down, scale, root, g0, z0, g1, f1, g2 = basis
    f2 = [
        pl.pallas_call(
            functools.partial(second_kernel, c),
            out_shape=plane,
            in_specs=[in_vmem] * 3,
            out_specs=in_vmem,
            scratch_shapes=[scratch(*plane.shape)],
            compiler_params=params,
            cost_estimate=pl.CostEstimate(flops=10**8, bytes_accessed=10**7, transcendentals=0),
        )(b_right, b_down, g2)
        for c in range(chans)
    ]
    return pl.pallas_call(
        third_kernel,
        out_shape=[shaped(chans, rows, cols)] * 3,
        in_specs=[in_vmem] * (8 + chans),
        out_specs=[pl.BlockSpec(memory_space=pltpu.HBM)] * 3,
        scratch_shapes=[
            scratch(chans, 3, tiles, height, LANES),
            scratch(chans, 3, rows, cols),
            pltpu.SemaphoreType.DMA((chans, 3)),
        ],
        compiler_params=params,
    )(total, scale, root, g0, z0, g1, f1, g2, *f2)


def solution(mesh):
    placed = (
        P(None, ("band", "row"), "col"),
        P(("band", "row"), "col"),
        P(("band", "row"), "col"),
        P(("band", "row"), "col"),
        P("band", None, None),
    )
    return jax.shard_map(
        per_device,
        mesh=mesh,
        in_specs=placed,
        out_specs=(
            P(None, ("band", "row"), "col"),
            P(None, ("band", "row"), "col"),
            P(None, ("band", "row"), "col"),
        ),
        check_vma=False,
    )
```

```python
import functools

import jax
import jax.numpy as jnp
from jax import lax
from jax.experimental import pallas as pl
from jax.experimental.pallas import tpu as pltpu
from jax.sharding import PartitionSpec as P

TILE = 256
SWEEPS = 8
SUBS = 8
LANES = 128
HALO = 16
LATE = 8
SLOT = 32
SLOTS = LANES // SLOT
WAYS = 3

seam_damping = 0.8
offset_unit = 32.0
spectrum_low = 0.08
spectrum_high = 2.0
MIX = 2.4

VMEM_LIMIT = 28 * 1024 * 1024


def chebyshev_polynomial():
    centre = (spectrum_high + spectrum_low) / 2.0
    radius = (spectrum_high - spectrum_low) / 2.0
    sigma = centre / radius
    size = SWEEPS
    update = [1.0 / centre] + [0.0] * (size - 1)
    smoothed = list(update)
    rho = 1.0 / sigma
    for _ in range(SWEEPS - 1):
        remainder = [-s for s in smoothed]
        remainder[0] += 1.0
        for k in range(size - 1):
            remainder[k + 1] += smoothed[k]
        following = 1.0 / (2.0 * sigma - rho)
        update = [following * rho * u + 2.0 * following / radius * r for u, r in zip(update, remainder)]
        smoothed = [s + u for s, u in zip(smoothed, update)]
        rho = following
    return smoothed


def lane_index():
    return lax.broadcasted_iota(jnp.int32, (SUBS, LANES), 1)


def pack(planes, start):
    lane = lax.broadcasted_iota(jnp.int32, planes[0].shape, 1)
    packed = [None] * (-(-len(planes) // SLOTS))
    for p, plane in enumerate(planes):
        slot = p % SLOTS
        by = (slot * SLOT - start) % LANES
        moved = pltpu.roll(plane, by, 1) if by else plane
        k = p // SLOTS
        packed[k] = moved if slot == 0 else jnp.where(lane < slot * SLOT, packed[k], moved)
    return packed


def own_kernel(
    place_ref, offsets_ref, src_hbm, weight_hbm, seam_right_hbm, seam_down_hbm,
    own_ref, first_rows_ref, second_rows_ref, first_cols_ref, second_cols_ref,
    src_ref, weight_ref, seam_right_ref, seam_down_ref, sems,
):
    chans, rows, cols = src_ref.shape
    own_tiles = cols // LANES
    moves = [(weight_hbm, weight_ref), (seam_right_hbm, seam_right_ref), (seam_down_hbm, seam_down_ref)]
    moves += [(src_hbm.at[c], src_ref.at[c]) for c in range(chans)]
    copies = [pltpu.make_async_copy(there, here, sems.at[k]) for k, (there, here) in enumerate(moves)]
    for copy in copies:
        copy.start()
    row = lax.broadcasted_iota(jnp.int32, (rows, LANES), 0)
    lane = lax.broadcasted_iota(jnp.int32, (rows, LANES), 1)
    sub = lax.broadcasted_iota(jnp.int32, (SUBS, LANES), 0)
    last_row, last_lane, tile_row, tile_at = [place_ref[k] for k in range(4)]
    odd_row, odd_col = (place_ref[4] == 1, place_ref[5] == 1)

    def tile(ref, j):
        return ref[:, j * LANES:(j + 1) * LANES]

    copies[0].wait()
    for j in range(own_tiles):
        own_ref[chans, j] = tile(weight_ref, j)
    copies[1].wait()
    for j in range(own_tiles):
        value = 1.0 - seam_damping * tile(seam_right_ref, j).astype(jnp.float32)
        own_ref[chans + 1, j] = jnp.where(lane == last_lane, 0.0, value) if j == own_tiles - 1 else value
    copies[2].wait()
    for j in range(own_tiles):
        value = 1.0 - seam_damping * tile(seam_down_ref, j).astype(jnp.float32)
        own_ref[chans + 2, j] = jnp.where(row == last_row, 0.0, value)
    for c in range(chans):
        shift = [
            jnp.broadcast_to(offsets_ref[c, tile_row, tile_at + k], (rows, LANES)).astype(jnp.float32) / offset_unit
            for k in range(cols // TILE)
        ]
        copies[3 + c].wait()
        for j in range(own_tiles):
            own_ref[c, j] = tile(src_ref.at[c], j) + shift[j * LANES // TILE]

    planes = range(chans + 3)

    def low_rows(ref):
        for p in planes:
            ref[p] = own_ref[p, :, 0:HALO, :]

    def high_rows(ref):
        at = rows - HALO
        for p in planes:
            ref[p] = own_ref[p, :, at:rows, :]
        for j in range(own_tiles):
            above = jnp.where(sub == 0, own_ref[chans + 2, j, at - 1:at, :], 0.0)
            ref[chans, j, 0:SUBS, :] = own_ref[chans, j, at:at + SUBS, :] + above

    @pl.when(odd_row)
    def _():
        low_rows(first_rows_ref)
        high_rows(second_rows_ref)

    @pl.when(jnp.logical_not(odd_row))
    def _():
        high_rows(first_rows_ref)
        low_rows(second_rows_ref)

    left = pack([own_ref[p, 0] for p in planes], 0)
    right = pack([own_ref[p, own_tiles - 1] for p in planes], LANES - SLOT)
    for k, (a, b) in enumerate(zip(left, right)):
        first_cols_ref[k] = jnp.where(odd_col, a, b)
        second_cols_ref[k] = jnp.where(odd_col, b, a)


def corners_kernel(chans, place_ref, first_ref, second_ref, first_out, second_out):
    rows = first_ref.shape[1]
    odd_row, odd_col = (place_ref[4] == 1, place_ref[5] == 1)
    sub = lax.broadcasted_iota(jnp.int32, (SUBS, LANES), 0)
    lane = lane_index()
    weight, down = chans, chans + 2
    slot = weight % SLOTS
    at = rows - HALO
    for side, (odd, even) in enumerate(((first_ref, second_ref), (second_ref, first_ref))):

        def tile(k, low, count=SUBS, odd=odd, even=even):
            return jnp.where(odd_col, odd[k, low:low + count, :], even[k, low:low + count, :])

        above = jnp.broadcast_to(tile(down // SLOTS, at - 1, 1), (SUBS, LANES))
        above = pltpu.roll(above, (slot - down % SLOTS) % SLOTS * SLOT, 1)
        own_slot = jnp.logical_and(lane >= slot * SLOT, lane < (slot + 1) * SLOT)
        above = jnp.where(jnp.logical_and(sub == 0, own_slot), above, 0.0)
        for k in range(first_ref.shape[0]):
            for low in range(0, HALO, SUBS):
                near = tile(k, low)
                far = tile(k, at + low)
                if low == 0 and k == weight // SLOTS:
                    far = far + above
                first_out[side, k, low:low + SUBS, :] = jnp.where(odd_row, near, far)
                second_out[side, k, low:low + SUBS, :] = jnp.where(odd_row, far, near)


def unpack(p, lefts, rights):
    lane = lax.broadcasted_iota(jnp.int32, lefts.shape, 1)
    slot = p % SLOTS
    if slot != SLOTS - 1:
        lefts = pltpu.roll(lefts, LANES - SLOT - slot * SLOT, 1)
    if slot:
        rights = pltpu.roll(rights, LANES - slot * SLOT, 1)
    return jnp.where(lane < SLOT, rights, jnp.where(lane >= LANES - SLOT, lefts, 0.0))


def ways_of(tiles):
    return WAYS if tiles % WAYS == 0 else 1


def split(value, count):
    parts = []
    for k in range(count):
        part = value.astype(jnp.bfloat16)
        parts.append(part)
        if k + 1 < count:
            value = value - part.astype(jnp.float32)
    return jnp.concatenate(parts, axis=0)


def permuted(value, index, count):
    rows = value.shape[0]
    out = jnp.dot(split(value, count), index, preferred_element_type=jnp.float32)
    total = out[:rows]
    for k in range(1, count):
        total = total + out[k * rows:(k + 1) * rows]
    return total


def dealing(ways):
    size = ways * LANES
    column = lax.broadcasted_iota(jnp.int32, (size, size), 0)
    place = lax.broadcasted_iota(jnp.int32, (size, size), 1)
    return jnp.where(column == ways * (place % LANES) + place // LANES, 1.0, 0.0).astype(jnp.bfloat16)


def undealing(ways):
    size = ways * LANES
    column = lax.broadcasted_iota(jnp.int32, (size, size), 1)
    place = lax.broadcasted_iota(jnp.int32, (size, size), 0)
    return jnp.where(column == ways * (place % LANES) + place // LANES, 1.0, 0.0).astype(jnp.bfloat16)


def deal(tile_of, low, high, ways, emit):
    matrix = dealing(ways) if ways > 1 else None
    for g in range(low, high, ways):
        if ways == 1:
            emit(g, tile_of(g))
            continue
        value = permuted(jnp.concatenate([tile_of(g + m) for m in range(ways)], axis=1), matrix, 3)
        for m in range(ways):
            emit(g + m, value[:, m * LANES:(m + 1) * LANES])


def inner_dealt_kernel(own_ref, dealt_ref):
    planes, own_tiles, rows = own_ref.shape[:3]

    def emit(j, value):
        dealt_ref[:, j] = value.reshape(planes, rows, LANES)

    deal(lambda j: own_ref[:, j].reshape(planes * rows, LANES), 0, dealt_ref.shape[1], ways_of(own_tiles + 1), emit)


def outer_dealt_kernel(place_ref, own_ref, first_ref, second_ref, dealt_ref):
    planes, own_tiles, rows = own_ref.shape[:3]
    tiles = own_tiles + 1
    low = tiles - dealt_ref.shape[1]
    odd = place_ref[5] == 1

    def tile_of(j):
        if j < own_tiles:
            return own_ref[:, j].reshape(planes * rows, LANES)
        parts = []
        for p in range(planes):
            first, second = first_ref[p // SLOTS], second_ref[p // SLOTS]
            parts.append(unpack(p, jnp.where(odd, first, second), jnp.where(odd, second, first)))
        return jnp.concatenate(parts, axis=0)

    def emit(j, value):
        dealt_ref[:, j - low] = value.reshape(planes, rows, LANES)

    deal(tile_of, low, tiles, ways_of(tiles), emit)


def rightward(values):
    tiles = len(values)
    ways = ways_of(tiles)
    last = lane_index() == LANES - 1
    ahead = {g: pltpu.roll(values[g], LANES - 1, 1) for g in range(0, tiles, ways)}
    out = []
    for j in range(tiles):
        if j % ways + 1 < ways:
            out.append(values[j + 1])
        else:
            g = j - ways + 1
            out.append(jnp.where(last, ahead[(g + ways) % tiles], ahead[g]))
    return out


def leftward(values):
    tiles = len(values)
    ways = ways_of(tiles)
    first = lane_index() == 0
    behind = {g: pltpu.roll(values[g + ways - 1], 1, 1) for g in range(0, tiles, ways)}
    out = []
    for j in range(tiles):
        if j % ways:
            out.append(values[j - 1])
        else:
            out.append(jnp.where(first, behind[(j - ways) % tiles], behind[j]))
    return out


def spread(b_right_ref, b_down_ref, z_ref, emit):
    tiles, height = z_ref.shape[:2]
    steps = height // SUBS
    ways = ways_of(tiles)
    lane = lane_index()
    first, last = (lane == 0, lane == LANES - 1)

    def at(i):
        return pl.ds(i * SUBS, SUBS)

    from_above = [pltpu.roll(b_down_ref[j, at(steps - 1), :] * z_ref[j, at(steps - 1), :], 1, 0) for j in range(tiles)]
    centre = [z_ref[j, at(0), :] for j in range(tiles)]
    wrapped = [pltpu.roll(v, SUBS - 1, 0) for v in centre]
    for i in range(steps):
        pushed_out = {
            g: pltpu.roll(b_right_ref[g + ways - 1, at(i), :] * centre[g + ways - 1], 1, 1)
            for g in range(0, tiles, ways)
        }
        ahead = {g: pltpu.roll(centre[g], LANES - 1, 1) for g in range(0, tiles, ways)}
        pushed = None
        below = []
        for j in range(tiles):
            g = j // ways * ways
            b_right = b_right_ref[j, at(i), :]
            b_down = b_down_ref[j, at(i), :]
            below.append(z_ref[j, at(i + 1), :] if i + 1 < steps else wrapped[j])
            if j == g:
                from_left = jnp.where(first, pushed_out[(g - ways) % tiles], pushed_out[g])
            else:
                from_left = pushed
            if j + 1 < g + ways:
                to_right = centre[j + 1]
                pushed = b_right * centre[j]
            else:
                to_right = jnp.where(last, ahead[(g + ways) % tiles], ahead[g])
            moved = (b_right * to_right + from_left) + (b_down * below[j] + from_above[j])
            from_above[j] = b_down * centre[j]
            emit(i, j, centre[j], moved)
        centre = below


def precondition(b_right_ref, b_down_ref, g_ref, z_ref, work_ref):
    poly = chebyshev_polynomial()
    degree = SWEEPS - 1

    def at(i):
        return pl.ds(i * SUBS, SUBS)

    def first(i, j, centre, moved):
        z_ref[j, at(i), :] = poly[degree] * moved + poly[degree - 1] * centre

    spread(b_right_ref, b_down_ref, g_ref, first)

    def pair(k, carry):
        adds = []
        for half in range(2):
            value = jnp.float32(poly[half])
            for later in range(1, (degree - 1) // 2):
                value = jnp.where(k == (degree - 1) // 2 - 1 - later, jnp.float32(poly[2 * later + half]), value)
            adds.append(value)

        def one(target, add):
            def emit(i, j, centre, moved):
                target[j, at(i), :] = moved + add * g_ref[j, at(i), :]

            return emit

        spread(b_right_ref, b_down_ref, z_ref, one(work_ref, adds[1]))
        spread(b_right_ref, b_down_ref, work_ref, one(z_ref, adds[0]))
        return carry

    lax.fori_loop(0, (degree - 1) // 2, pair, 0)


def next_residual(b_right_ref, b_down_ref, g_ref, z_ref, next_ref, own_of):
    height = g_ref.shape[1]
    steps = height // SUBS
    sums = {}

    def emit(i, j, centre, moved):
        at = pl.ds(i * SUBS, SUBS)
        g = g_ref[j, at, :]
        following = g - MIX * (centre - moved)
        next_ref[j, at, :] = following
        key = own_of(i, j)
        now = (g * centre, following * centre)
        before = sums.get(key)
        sums[key] = now if before is None else (before[0] + now[0], before[1] + now[1])

    spread(b_right_ref, b_down_ref, z_ref, emit)
    sub = lax.broadcasted_iota(jnp.int32, (SUBS, LANES), 0)
    lane = lane_index()
    total = [jnp.zeros((SUBS, LANES), jnp.float32)] * 2
    for (low, high, lanes), parts in sums.items():
        inside = jnp.logical_and(jnp.logical_and(sub >= low, sub <= high), lane < lanes)
        total = [t + jnp.where(inside, p, 0.0) for t, p in zip(total, parts)]
    return total


def first_kernel(
    place_ref, inner_ref, outer_ref, first_rows_ref, second_rows_ref, first_corners_ref, second_corners_ref,
    b_right_ref, b_down_ref, scale_ref, root_ref, g0_ref, z0_ref, g1_ref, f1_ref, g2_ref, sums_ref,
    first_late_ref, second_late_ref,
    natural, work_ref,
):
    planes, inner, rows = inner_ref.shape[:3]
    tiles = inner + outer_ref.shape[1]
    chans = planes - 3
    own_tiles = tiles - 1
    height = rows + 2 * HALO
    steps = height // SUBS

    for p in range(planes):
        for j in range(tiles):
            natural[p, j, HALO:HALO + rows, :] = inner_ref[p, j] if j < inner else outer_ref[p, j - inner]
    odd = place_ref[4] == 1

    def edge_tile(j):
        if j < own_tiles:
            first, second = [ref[:, j].reshape(planes * HALO, LANES) for ref in (first_rows_ref, second_rows_ref)]
        else:
            first, second = [
                jnp.concatenate([unpack(p, ref[0, p // SLOTS], ref[1, p // SLOTS]) for p in range(planes)], axis=0)
                for ref in (first_corners_ref, second_corners_ref)
            ]
        return jnp.concatenate([jnp.where(odd, first, second), jnp.where(odd, second, first)], axis=0)

    def put_edge(j, value):
        value = value.reshape(2, planes, HALO, LANES)
        natural[:, j, 0:HALO, :] = value[0]
        natural[:, j, HALO + rows:height, :] = value[1]

    deal(edge_tile, 0, tiles, ways_of(tiles), put_edge)

    def at(i):
        return pl.ds(i * SUBS, SUBS)

    def interleaved(p, i, j):
        return natural[p, j, pl.ds(i, SUBS, stride=steps), :]

    sub = lax.broadcasted_iota(jnp.int32, (SUBS, LANES), 0)
    to_up = [
        jnp.where(sub == 0, 0.0, pltpu.roll(interleaved(chans + 2, steps - 1, j), 1, 0)) for j in range(tiles)
    ]
    for i in range(steps):
        to_right = [interleaved(chans + 1, i, j) for j in range(tiles)]
        to_left = leftward(to_right)
        for j in range(tiles):
            to_down = interleaved(chans + 2, i, j)
            diag = interleaved(chans, i, j) + to_right[j] + to_left[j] + to_down + to_up[j]
            inside = diag > 0.0
            safe = jnp.where(inside, diag, 1.0)
            guess = lax.rsqrt(safe)
            scale = guess * (1.5 - 0.5 * safe * guess * guess)
            scale_ref[j, at(i), :] = jnp.where(inside, scale, 0.0)
            root_ref[j, at(i), :] = safe * scale
            to_up[j] = to_down
    wrapped = [pltpu.roll(scale_ref[j, at(0), :], SUBS - 1, 0) for j in range(tiles)]
    for i in range(steps):
        scale = [scale_ref[j, at(i), :] for j in range(tiles)]
        right_scale = rightward(scale)
        for j in range(tiles):
            b_right_ref[j, at(i), :] = interleaved(chans + 1, i, j) * scale[j] * right_scale[j]
            down_scale = scale_ref[j, at(i + 1), :] if i + 1 < steps else wrapped[j]
            b_down_ref[j, at(i), :] = interleaved(chans + 2, i, j) * scale[j] * down_scale
            for c in range(chans):
                g0_ref[c, j, at(i), :] = interleaved(c, i, j) * scale[j]

    ways = ways_of(tiles)

    def own_of(i, j):
        low, high = -(-(HALO - i) // steps), (HALO + rows - 1 - i) // steps
        left = own_tiles * LANES - j // ways * ways * LANES - j % ways
        return low, high, min(LANES, max(0, -(-left // ways)))

    def channel(c, carry):
        g0, z0, g1, f1, g2 = [ref.at[c] for ref in (g0_ref, z0_ref, g1_ref, f1_ref, g2_ref)]
        precondition(b_right_ref, b_down_ref, g0, z0, work_ref)
        sum0, sum1 = next_residual(b_right_ref, b_down_ref, g0, z0, g1, own_of)
        precondition(b_right_ref, b_down_ref, g1, f1, work_ref)
        sum2, sum3 = next_residual(b_right_ref, b_down_ref, g1, f1, g2, own_of)
        return tuple(a + b for a, b in zip(carry, (sum0, sum1, sum2, sum3)))

    zero = jnp.zeros((SUBS, LANES), jnp.float32)
    parts = lax.fori_loop(0, chans, channel, (zero,) * 4)
    sums = zero
    for k, part in enumerate(parts):
        sums = jnp.where(sub == k, jnp.sum(part), sums)
    sums_ref[...] = sums

    def edge(c, j, at):
        s, i = divmod(HALO + at, steps)
        return g2_ref[c, j, pl.ds(i * SUBS + s, LATE, stride=SUBS), :]

    for c in range(chans):
        for j in range(tiles):
            low, high = edge(c, j, 0), edge(c, j, rows - LATE)
            first_late_ref[c, j] = jnp.where(odd, low, high)
            second_late_ref[c, j] = jnp.where(odd, high, low)


def second_kernel(
    c, place_ref, first_late_ref, second_late_ref, b_right_ref, b_down_ref, g2_ref, f2_ref, g_ref, work_ref
):
    tiles, height = b_right_ref.shape[:2]
    rows = height - 2 * HALO
    steps = height // SUBS
    odd = place_ref[4] == 1
    sub = lax.broadcasted_iota(jnp.int32, (SUBS, LANES), 0)
    halo = {i: [] for i in range(steps)}
    for k in range(LATE):
        for top, at in ((True, HALO - LATE + k), (False, HALO + rows + k)):
            s, i = divmod(at, steps)
            halo[i].append((s, top, k))
    for j in range(tiles):
        for i in range(steps):
            value = g2_ref[c, j, i * SUBS:(i + 1) * SUBS, :]
            for s, top, k in halo[i]:
                first, second = [ref[c, j, k:k + 1, :] for ref in (first_late_ref, second_late_ref)]
                row = jnp.where(odd, first, second) if top else jnp.where(odd, second, first)
                value = jnp.where(sub == s, row, value)
            g_ref[j, i * SUBS:(i + 1) * SUBS, :] = value
    precondition(b_right_ref, b_down_ref, g_ref, f2_ref, work_ref)


def combine(n0, n1, n2, n3):
    gap = n0 - n1
    keep = -n1 / gap
    step = n0 / gap
    beta = (n0 * n2 - n1 * n1) / (gap * gap)
    along = keep + beta
    curvature = along * along * gap + 2.0 * along * step * (n1 - n2) + step * step * (n2 - n3)
    scaled = n0 * beta / curvature
    first_size = step * MIX
    second_size = scaled * MIX
    x0 = first_size + second_size * along
    x1 = second_size * step
    r0 = keep - scaled * along
    r1 = step + scaled * (along - step)
    r2 = scaled * step
    return x0, x1, r0, r1, r2


def third_kernel(
    sums_ref, scale_ref, root_ref, g0_ref, z0_ref, g1_ref, f1_ref, g2_ref, *refs
):
    *f2_refs, solution_hbm, residual_hbm, smoothed_hbm, natural, done, sems = refs
    rows, cols = solution_hbm.shape[1:]
    own_tiles = cols // LANES
    tiles, height = scale_ref.shape[:2]
    steps = height // SUBS
    ways = ways_of(tiles)
    x0, x1, r0, r1, r2 = combine(*[jnp.broadcast_to(sums_ref[k:k + 1, :], (SUBS, LANES)) for k in range(4)])
    matrix = undealing(ways) if ways > 1 else None
    outs = (solution_hbm, residual_hbm, smoothed_hbm)
    copies = []
    for c, f2_ref in enumerate(f2_refs):
        for j in range(tiles):
            for i in range(steps):
                at = pl.ds(i * SUBS, SUBS)
                scale = scale_ref[j, at, :]
                root = root_ref[j, at, :]
                g0, g1, g2, z0, f1 = [ref[c, j, at, :] for ref in (g0_ref, g1_ref, g2_ref, z0_ref, f1_ref)]
                f2 = f2_ref[j, at, :]
                there = pl.ds(i, SUBS, stride=steps)
                natural[c, 0, j, there, :] = scale * (x0 * z0 + x1 * f1)
                natural[c, 1, j, there, :] = root * (r0 * g0 + r1 * g1 + r2 * g2)
                natural[c, 2, j, there, :] = scale * (r0 * z0 + r1 * f1 + r2 * f2)
        for g in range(0, own_tiles, ways):
            value = jnp.concatenate(
                [natural[c, :, g + m, HALO:HALO + rows, :].reshape(3 * rows, LANES) for m in range(ways)], axis=1
            )
            width = min(ways, own_tiles - g) * LANES
            if ways > 1:
                value = permuted(value, matrix[:, :width], 2)
            for k in range(len(outs)):
                done[c, k, :, g * LANES:g * LANES + width] = value[k * rows:(k + 1) * rows]
        for k, ref in enumerate(outs):
            copies.append(pltpu.make_async_copy(done.at[c, k], ref.at[c], sems.at[c, k]))
            copies[-1].start()
    for copy in copies:
        copy.wait()


def sum_over(value, axes, beside):
    steps = []
    for axis in axes:
        size = lax.axis_size(axis)
        if size & (size - 1):
            value = lax.psum(value, axis)
            continue
        steps += [(axis, [(i, i ^ (1 << k)) for i in range(size)]) for k in range(size.bit_length() - 1)]
    done = []
    for k, (axis, pairs) in enumerate(steps):
        other = lax.ppermute(value, axis, pairs)
        if len(steps) - k <= len(beside):
            value, array = lax.optimization_barrier((value, beside[len(done)]))
            done.append(array)
        value = value + other
    return value, done + list(beside[len(done):])


def per_device(source, weight, seam_right, seam_down, offsets):
    chans, rows, cols = source.shape
    row_axis, col_axis = lax.axis_size("row"), lax.axis_size("col")
    row_at, col_at = lax.axis_index("row"), lax.axis_index("col")
    odd_row, odd_col = lax.rem(row_at, 2), lax.rem(col_at, 2)
    place = jnp.stack(
        [
            jnp.where(row_at == row_axis - 1, rows - 1, -1),
            jnp.where(col_at == col_axis - 1, LANES - 1, -1),
            lax.div(row_at * rows, TILE),
            col_at * (cols // TILE),
            odd_row,
            odd_col,
        ]
    ).astype(jnp.int32)

    in_vmem = pl.BlockSpec(memory_space=pltpu.VMEM)
    in_smem = pl.BlockSpec(memory_space=pltpu.SMEM)
    in_hbm = pl.BlockSpec(memory_space=pltpu.HBM)
    params = pltpu.CompilerParams(vmem_limit_bytes=VMEM_LIMIT)

    def shaped(*shape):
        return jax.ShapeDtypeStruct(shape, jnp.float32)

    def scratch(*shape):
        return pltpu.VMEM(shape, jnp.float32)

    planes = chans + 3
    own_tiles = cols // LANES
    tiles = own_tiles + 1
    packs = -(-planes // SLOTS)
    own, first_rows, second_rows, first_cols, second_cols = pl.pallas_call(
        own_kernel,
        out_shape=[shaped(planes, own_tiles, rows, LANES)]
        + [shaped(planes, own_tiles, HALO, LANES)] * 2
        + [shaped(packs, rows, LANES)] * 2,
        in_specs=[in_smem] * 2 + [in_hbm] * 4,
        out_specs=[in_vmem] * 5,
        scratch_shapes=[
            scratch(*source.shape),
            scratch(*weight.shape),
            pltpu.VMEM(weight.shape, jnp.int32),
            pltpu.VMEM(weight.shape, jnp.int32),
            pltpu.SemaphoreType.DMA((planes,)),
        ],
        compiler_params=params,
    )(
        place,
        offsets.transpose(2, 0, 1),
        *[pltpu.with_memory_space_constraint(v, pltpu.HBM) for v in (source, weight, seam_right, seam_down)],
    )

    def swap(first, second, axis):
        size = lax.axis_size(axis)
        pairs = [[(i, i + 1) for i in range(start, size - 1, 2)] for start in range(2)]
        pairs = [some + [(j, i) for i, j in some] for some in pairs]
        return [lax.ppermute(value, axis, some) for value, some in zip((first, second), pairs)]

    first_rows, second_rows = swap(first_rows, second_rows, "row")
    first_cols, second_cols = swap(first_cols, second_cols, "col")
    corners = pl.pallas_call(
        functools.partial(corners_kernel, chans),
        out_shape=[shaped(2, packs, HALO, LANES)] * 2,
        in_specs=[in_smem] + [in_vmem] * 2,
        out_specs=[in_vmem] * 2,
        compiler_params=params,
    )(place, first_cols, second_cols)
    first_corners, second_corners = swap(*corners, "row")
    ways = ways_of(tiles)
    inner = pl.pallas_call(
        inner_dealt_kernel,
        out_shape=shaped(planes, tiles - ways, rows, LANES),
        in_specs=[in_vmem],
        out_specs=in_vmem,
        compiler_params=params,
        cost_estimate=pl.CostEstimate(flops=10**8, bytes_accessed=4 * 10**6, transcendentals=0),
    )(own)
    outer = pl.pallas_call(
        outer_dealt_kernel,
        out_shape=shaped(planes, ways, rows, LANES),
        in_specs=[in_smem] + [in_vmem] * 3,
        out_specs=in_vmem,
        compiler_params=params,
        cost_estimate=pl.CostEstimate(flops=10**8, bytes_accessed=2 * 10**6, transcendentals=0),
    )(place, own, first_cols, second_cols)

    height = rows + 2 * HALO
    plane = shaped(tiles, height, LANES)
    field = shaped(chans, tiles, height, LANES)
    late = shaped(chans, tiles, LATE, LANES)
    *basis, sums, first_late, second_late = pl.pallas_call(
        first_kernel,
        out_shape=[plane] * 4 + [field] * 5 + [shaped(SUBS, LANES)] + [late] * 2,
        in_specs=[in_smem] + [in_vmem] * 6,
        out_specs=[in_vmem] * 12,
        scratch_shapes=[scratch(planes, tiles, height, LANES), scratch(*plane.shape)],
        compiler_params=params,
    )(place, inner, outer, first_rows, second_rows, first_corners, second_corners)

    first_late, second_late = swap(first_late, second_late, "row")

    b_right, b_down, scale, root, g0, z0, g1, f1, g2 = basis
    f2 = [
        pl.pallas_call(
            functools.partial(second_kernel, c),
            out_shape=plane,
            in_specs=[in_smem] + [in_vmem] * 5,
            out_specs=in_vmem,
            scratch_shapes=[scratch(*plane.shape)] * 2,
            compiler_params=params,
            cost_estimate=pl.CostEstimate(flops=10**8, bytes_accessed=10**7, transcendentals=0),
        )(place, first_late, second_late, b_right, b_down, g2)
        for c in range(chans)
    ]
    total, f2 = sum_over(sums, ("col", "row"), f2)
    return pl.pallas_call(
        third_kernel,
        out_shape=[shaped(chans, rows, cols)] * 3,
        in_specs=[in_vmem] * (8 + chans),
        out_specs=[pl.BlockSpec(memory_space=pltpu.HBM)] * 3,
        scratch_shapes=[
            scratch(chans, 3, tiles, height, LANES),
            scratch(chans, 3, rows, cols),
            pltpu.SemaphoreType.DMA((chans, 3)),
        ],
        compiler_params=params,
    )(total, scale, root, g0, z0, g1, f1, g2, *f2)


def solution(mesh):
    placed = (
        P(None, ("band", "row"), "col"),
        P(("band", "row"), "col"),
        P(("band", "row"), "col"),
        P(("band", "row"), "col"),
        P("band", None, None),
    )
    return jax.shard_map(
        per_device,
        mesh=mesh,
        in_specs=placed,
        out_specs=(
            P(None, ("band", "row"), "col"),
            P(None, ("band", "row"), "col"),
            P(None, ("band", "row"), "col"),
        ),
        check_vma=False,
    )
```

```python
import functools

import jax
import jax.numpy as jnp
from jax import lax
from jax.experimental import pallas as pl
from jax.experimental.pallas import tpu as pltpu
from jax.sharding import PartitionSpec as P

TILE = 256
SWEEPS = 8
SUBS = 8
LANES = 128
HALO = 16
LATE = 8
SLOT = 32
SLOTS = LANES // SLOT
WAYS = 3

seam_damping = 0.8
offset_unit = 32.0
spectrum_low = 0.08
spectrum_high = 2.0
MIX = 2.4

VMEM_LIMIT = 28 * 1024 * 1024


def chebyshev_polynomial():
    centre = (spectrum_high + spectrum_low) / 2.0
    radius = (spectrum_high - spectrum_low) / 2.0
    sigma = centre / radius
    size = SWEEPS
    update = [1.0 / centre] + [0.0] * (size - 1)
    smoothed = list(update)
    rho = 1.0 / sigma
    for _ in range(SWEEPS - 1):
        remainder = [-s for s in smoothed]
        remainder[0] += 1.0
        for k in range(size - 1):
            remainder[k + 1] += smoothed[k]
        following = 1.0 / (2.0 * sigma - rho)
        update = [following * rho * u + 2.0 * following / radius * r for u, r in zip(update, remainder)]
        smoothed = [s + u for s, u in zip(smoothed, update)]
        rho = following
    return smoothed


def lane_index():
    return lax.broadcasted_iota(jnp.int32, (SUBS, LANES), 1)


def pack(planes, start):
    lane = lax.broadcasted_iota(jnp.int32, planes[0].shape, 1)
    packed = [None] * (-(-len(planes) // SLOTS))
    for p, plane in enumerate(planes):
        slot = p % SLOTS
        by = (slot * SLOT - start) % LANES
        moved = pltpu.roll(plane, by, 1) if by else plane
        k = p // SLOTS
        packed[k] = moved if slot == 0 else jnp.where(lane < slot * SLOT, packed[k], moved)
    return packed


def own_kernel(
    place_ref, offsets_hbm, src_hbm, weight_hbm, seam_right_hbm, seam_down_hbm,
    own_ref, first_rows_ref, second_rows_ref, first_cols_ref, second_cols_ref,
    offsets_ref, src_ref, weight_ref, seam_right_ref, seam_down_ref, sems,
):
    chans, rows, cols = src_ref.shape
    own_tiles = cols // LANES
    moves = [(weight_hbm, weight_ref), (seam_right_hbm, seam_right_ref), (seam_down_hbm, seam_down_ref)]
    moves += [(src_hbm.at[c], src_ref.at[c]) for c in range(chans)] + [(offsets_hbm, offsets_ref)]
    copies = [pltpu.make_async_copy(there, here, sems.at[k]) for k, (there, here) in enumerate(moves)]
    for copy in copies:
        copy.start()
    row = lax.broadcasted_iota(jnp.int32, (rows, LANES), 0)
    lane = lax.broadcasted_iota(jnp.int32, (rows, LANES), 1)
    sub = lax.broadcasted_iota(jnp.int32, (SUBS, LANES), 0)
    last_row, last_lane, tile_row, tile_at = [place_ref[k] for k in range(4)]
    odd_row, odd_col = (place_ref[4] == 1, place_ref[5] == 1)

    def tile(ref, j):
        return ref[:, j * LANES:(j + 1) * LANES]

    copies[0].wait()
    for j in range(own_tiles):
        own_ref[chans, j] = tile(weight_ref, j)
    copies[1].wait()
    for j in range(own_tiles):
        value = 1.0 - seam_damping * tile(seam_right_ref, j).astype(jnp.float32)
        own_ref[chans + 1, j] = jnp.where(lane == last_lane, 0.0, value) if j == own_tiles - 1 else value
    copies[2].wait()
    for j in range(own_tiles):
        value = 1.0 - seam_damping * tile(seam_down_ref, j).astype(jnp.float32)
        own_ref[chans + 2, j] = jnp.where(row == last_row, 0.0, value)
    copies[-1].wait()
    for c in range(chans):
        shift = [
            jnp.broadcast_to(offsets_ref[c, tile_row, tile_at + k], (rows, LANES)).astype(jnp.float32) / offset_unit
            for k in range(cols // TILE)
        ]
        copies[3 + c].wait()
        for j in range(own_tiles):
            own_ref[c, j] = tile(src_ref.at[c], j) + shift[j * LANES // TILE]

    planes = range(chans + 3)

    def low_rows(ref):
        for p in planes:
            ref[p] = own_ref[p, :, 0:HALO, :]

    def high_rows(ref):
        at = rows - HALO
        for p in planes:
            ref[p] = own_ref[p, :, at:rows, :]
        for j in range(own_tiles):
            above = jnp.where(sub == 0, own_ref[chans + 2, j, at - 1:at, :], 0.0)
            ref[chans, j, 0:SUBS, :] = own_ref[chans, j, at:at + SUBS, :] + above

    @pl.when(odd_row)
    def _():
        low_rows(first_rows_ref)
        high_rows(second_rows_ref)

    @pl.when(jnp.logical_not(odd_row))
    def _():
        high_rows(first_rows_ref)
        low_rows(second_rows_ref)

    left = pack([own_ref[p, 0] for p in planes], 0)
    right = pack([own_ref[p, own_tiles - 1] for p in planes], LANES - SLOT)
    for k, (a, b) in enumerate(zip(left, right)):
        first_cols_ref[k] = jnp.where(odd_col, a, b)
        second_cols_ref[k] = jnp.where(odd_col, b, a)


def corners_kernel(chans, place_ref, first_ref, second_ref, first_out, second_out):
    rows = first_ref.shape[1]
    odd_row, odd_col = (place_ref[4] == 1, place_ref[5] == 1)
    sub = lax.broadcasted_iota(jnp.int32, (SUBS, LANES), 0)
    lane = lane_index()
    weight, down = chans, chans + 2
    slot = weight % SLOTS
    at = rows - HALO
    for side, (odd, even) in enumerate(((first_ref, second_ref), (second_ref, first_ref))):

        def tile(k, low, count=SUBS, odd=odd, even=even):
            return jnp.where(odd_col, odd[k, low:low + count, :], even[k, low:low + count, :])

        above = jnp.broadcast_to(tile(down // SLOTS, at - 1, 1), (SUBS, LANES))
        above = pltpu.roll(above, (slot - down % SLOTS) % SLOTS * SLOT, 1)
        own_slot = jnp.logical_and(lane >= slot * SLOT, lane < (slot + 1) * SLOT)
        above = jnp.where(jnp.logical_and(sub == 0, own_slot), above, 0.0)
        for k in range(first_ref.shape[0]):
            for low in range(0, HALO, SUBS):
                near = tile(k, low)
                far = tile(k, at + low)
                if low == 0 and k == weight // SLOTS:
                    far = far + above
                first_out[side, k, low:low + SUBS, :] = jnp.where(odd_row, near, far)
                second_out[side, k, low:low + SUBS, :] = jnp.where(odd_row, far, near)


def unpack(p, lefts, rights):
    lane = lax.broadcasted_iota(jnp.int32, lefts.shape, 1)
    slot = p % SLOTS
    if slot != SLOTS - 1:
        lefts = pltpu.roll(lefts, LANES - SLOT - slot * SLOT, 1)
    if slot:
        rights = pltpu.roll(rights, LANES - slot * SLOT, 1)
    return jnp.where(lane < SLOT, rights, jnp.where(lane >= LANES - SLOT, lefts, 0.0))


def ways_of(tiles):
    return WAYS if tiles % WAYS == 0 else 1


def split(value, count):
    parts = []
    for k in range(count):
        part = value.astype(jnp.bfloat16)
        parts.append(part)
        if k + 1 < count:
            value = value - part.astype(jnp.float32)
    return jnp.concatenate(parts, axis=0)


def permuted(value, index, count):
    rows = value.shape[0]
    out = jnp.dot(split(value, count), index, preferred_element_type=jnp.float32)
    total = out[:rows]
    for k in range(1, count):
        total = total + out[k * rows:(k + 1) * rows]
    return total


def dealing(ways):
    size = ways * LANES
    column = lax.broadcasted_iota(jnp.int32, (size, size), 0)
    place = lax.broadcasted_iota(jnp.int32, (size, size), 1)
    return jnp.where(column == ways * (place % LANES) + place // LANES, 1.0, 0.0).astype(jnp.bfloat16)


def undealing(ways):
    size = ways * LANES
    column = lax.broadcasted_iota(jnp.int32, (size, size), 1)
    place = lax.broadcasted_iota(jnp.int32, (size, size), 0)
    return jnp.where(column == ways * (place % LANES) + place // LANES, 1.0, 0.0).astype(jnp.bfloat16)


def deal(tile_of, low, high, ways, emit):
    matrix = dealing(ways) if ways > 1 else None
    for g in range(low, high, ways):
        if ways == 1:
            emit(g, tile_of(g))
            continue
        value = permuted(jnp.concatenate([tile_of(g + m) for m in range(ways)], axis=1), matrix, 3)
        for m in range(ways):
            emit(g + m, value[:, m * LANES:(m + 1) * LANES])


def inner_dealt_kernel(own_ref, dealt_ref):
    planes, own_tiles, rows = own_ref.shape[:3]

    def emit(j, value):
        dealt_ref[:, j] = value.reshape(planes, rows, LANES)

    deal(lambda j: own_ref[:, j].reshape(planes * rows, LANES), 0, dealt_ref.shape[1], ways_of(own_tiles + 1), emit)


def outer_dealt_kernel(place_ref, own_ref, first_ref, second_ref, dealt_ref):
    planes, own_tiles, rows = own_ref.shape[:3]
    tiles = own_tiles + 1
    low = tiles - dealt_ref.shape[1]
    odd = place_ref[5] == 1

    def tile_of(j):
        if j < own_tiles:
            return own_ref[:, j].reshape(planes * rows, LANES)
        parts = []
        for p in range(planes):
            first, second = first_ref[p // SLOTS], second_ref[p // SLOTS]
            parts.append(unpack(p, jnp.where(odd, first, second), jnp.where(odd, second, first)))
        return jnp.concatenate(parts, axis=0)

    def emit(j, value):
        dealt_ref[:, j - low] = value.reshape(planes, rows, LANES)

    deal(tile_of, low, tiles, ways_of(tiles), emit)


def rightward(values):
    tiles = len(values)
    ways = ways_of(tiles)
    last = lane_index() == LANES - 1
    ahead = {g: pltpu.roll(values[g], LANES - 1, 1) for g in range(0, tiles, ways)}
    out = []
    for j in range(tiles):
        if j % ways + 1 < ways:
            out.append(values[j + 1])
        else:
            g = j - ways + 1
            out.append(jnp.where(last, ahead[(g + ways) % tiles], ahead[g]))
    return out


def leftward(values):
    tiles = len(values)
    ways = ways_of(tiles)
    first = lane_index() == 0
    behind = {g: pltpu.roll(values[g + ways - 1], 1, 1) for g in range(0, tiles, ways)}
    out = []
    for j in range(tiles):
        if j % ways:
            out.append(values[j - 1])
        else:
            out.append(jnp.where(first, behind[(j - ways) % tiles], behind[j]))
    return out


def spread(b_right_ref, b_down_ref, z_ref, emit):
    tiles, height = z_ref.shape[:2]
    steps = height // SUBS
    ways = ways_of(tiles)
    lane = lane_index()
    first, last = (lane == 0, lane == LANES - 1)

    def at(i):
        return pl.ds(i * SUBS, SUBS)

    from_above = [pltpu.roll(b_down_ref[j, at(steps - 1), :] * z_ref[j, at(steps - 1), :], 1, 0) for j in range(tiles)]
    centre = [z_ref[j, at(0), :] for j in range(tiles)]
    wrapped = [pltpu.roll(v, SUBS - 1, 0) for v in centre]
    for i in range(steps):
        pushed_out = {
            g: pltpu.roll(b_right_ref[g + ways - 1, at(i), :] * centre[g + ways - 1], 1, 1)
            for g in range(0, tiles, ways)
        }
        ahead = {g: pltpu.roll(centre[g], LANES - 1, 1) for g in range(0, tiles, ways)}
        pushed = None
        below = []
        for j in range(tiles):
            g = j // ways * ways
            b_right = b_right_ref[j, at(i), :]
            b_down = b_down_ref[j, at(i), :]
            below.append(z_ref[j, at(i + 1), :] if i + 1 < steps else wrapped[j])
            if j == g:
                from_left = jnp.where(first, pushed_out[(g - ways) % tiles], pushed_out[g])
            else:
                from_left = pushed
            if j + 1 < g + ways:
                to_right = centre[j + 1]
                pushed = b_right * centre[j]
            else:
                to_right = jnp.where(last, ahead[(g + ways) % tiles], ahead[g])
            moved = (b_right * to_right + from_left) + (b_down * below[j] + from_above[j])
            from_above[j] = b_down * centre[j]
            emit(i, j, centre[j], moved)
        centre = below


def precondition(b_right_ref, b_down_ref, g_ref, z_ref, work_ref):
    poly = chebyshev_polynomial()
    degree = SWEEPS - 1

    def at(i):
        return pl.ds(i * SUBS, SUBS)

    def first(i, j, centre, moved):
        z_ref[j, at(i), :] = poly[degree] * moved + poly[degree - 1] * centre

    spread(b_right_ref, b_down_ref, g_ref, first)

    def pair(k, carry):
        adds = []
        for half in range(2):
            value = jnp.float32(poly[half])
            for later in range(1, (degree - 1) // 2):
                value = jnp.where(k == (degree - 1) // 2 - 1 - later, jnp.float32(poly[2 * later + half]), value)
            adds.append(value)

        def one(target, add):
            def emit(i, j, centre, moved):
                target[j, at(i), :] = moved + add * g_ref[j, at(i), :]

            return emit

        spread(b_right_ref, b_down_ref, z_ref, one(work_ref, adds[1]))
        spread(b_right_ref, b_down_ref, work_ref, one(z_ref, adds[0]))
        return carry

    lax.fori_loop(0, (degree - 1) // 2, pair, 0)


def next_residual(b_right_ref, b_down_ref, g_ref, z_ref, next_ref, own_of):
    height = g_ref.shape[1]
    steps = height // SUBS
    sums = {}

    def emit(i, j, centre, moved):
        at = pl.ds(i * SUBS, SUBS)
        g = g_ref[j, at, :]
        following = g - MIX * (centre - moved)
        next_ref[j, at, :] = following
        key = own_of(i, j)
        now = (g * centre, following * centre)
        before = sums.get(key)
        sums[key] = now if before is None else (before[0] + now[0], before[1] + now[1])

    spread(b_right_ref, b_down_ref, z_ref, emit)
    sub = lax.broadcasted_iota(jnp.int32, (SUBS, LANES), 0)
    lane = lane_index()
    total = [jnp.zeros((SUBS, LANES), jnp.float32)] * 2
    for (low, high, lanes), parts in sums.items():
        inside = jnp.logical_and(jnp.logical_and(sub >= low, sub <= high), lane < lanes)
        total = [t + jnp.where(inside, p, 0.0) for t, p in zip(total, parts)]
    return total


def first_kernel(
    place_ref, inner_ref, outer_ref, first_rows_ref, second_rows_ref, first_corners_ref, second_corners_ref,
    b_right_ref, b_down_ref, scale_ref, root_ref, g0_ref, z0_ref, g1_ref, f1_ref, g2_ref, sums_ref,
    first_late_ref, second_late_ref,
    natural, work_ref,
):
    planes, inner, rows = inner_ref.shape[:3]
    tiles = inner + outer_ref.shape[1]
    chans = planes - 3
    own_tiles = tiles - 1
    height = rows + 2 * HALO
    steps = height // SUBS

    for p in range(planes):
        for j in range(tiles):
            natural[p, j, HALO:HALO + rows, :] = inner_ref[p, j] if j < inner else outer_ref[p, j - inner]
    odd = place_ref[4] == 1

    def edge_tile(j):
        if j < own_tiles:
            first, second = [ref[:, j].reshape(planes * HALO, LANES) for ref in (first_rows_ref, second_rows_ref)]
        else:
            first, second = [
                jnp.concatenate([unpack(p, ref[0, p // SLOTS], ref[1, p // SLOTS]) for p in range(planes)], axis=0)
                for ref in (first_corners_ref, second_corners_ref)
            ]
        return jnp.concatenate([jnp.where(odd, first, second), jnp.where(odd, second, first)], axis=0)

    def put_edge(j, value):
        value = value.reshape(2, planes, HALO, LANES)
        natural[:, j, 0:HALO, :] = value[0]
        natural[:, j, HALO + rows:height, :] = value[1]

    deal(edge_tile, 0, tiles, ways_of(tiles), put_edge)

    def at(i):
        return pl.ds(i * SUBS, SUBS)

    def interleaved(p, i, j):
        return natural[p, j, pl.ds(i, SUBS, stride=steps), :]

    sub = lax.broadcasted_iota(jnp.int32, (SUBS, LANES), 0)
    to_up = [
        jnp.where(sub == 0, 0.0, pltpu.roll(interleaved(chans + 2, steps - 1, j), 1, 0)) for j in range(tiles)
    ]
    for i in range(steps):
        to_right = [interleaved(chans + 1, i, j) for j in range(tiles)]
        to_left = leftward(to_right)
        for j in range(tiles):
            to_down = interleaved(chans + 2, i, j)
            diag = interleaved(chans, i, j) + to_right[j] + to_left[j] + to_down + to_up[j]
            inside = diag > 0.0
            safe = jnp.where(inside, diag, 1.0)
            guess = lax.rsqrt(safe)
            scale = guess * (1.5 - 0.5 * safe * guess * guess)
            scale_ref[j, at(i), :] = jnp.where(inside, scale, 0.0)
            root_ref[j, at(i), :] = safe * scale
            to_up[j] = to_down
    wrapped = [pltpu.roll(scale_ref[j, at(0), :], SUBS - 1, 0) for j in range(tiles)]
    for i in range(steps):
        scale = [scale_ref[j, at(i), :] for j in range(tiles)]
        right_scale = rightward(scale)
        for j in range(tiles):
            b_right_ref[j, at(i), :] = interleaved(chans + 1, i, j) * scale[j] * right_scale[j]
            down_scale = scale_ref[j, at(i + 1), :] if i + 1 < steps else wrapped[j]
            b_down_ref[j, at(i), :] = interleaved(chans + 2, i, j) * scale[j] * down_scale
            for c in range(chans):
                g0_ref[c, j, at(i), :] = interleaved(c, i, j) * scale[j]

    ways = ways_of(tiles)

    def own_of(i, j):
        low, high = -(-(HALO - i) // steps), (HALO + rows - 1 - i) // steps
        left = own_tiles * LANES - j // ways * ways * LANES - j % ways
        return low, high, min(LANES, max(0, -(-left // ways)))

    def channel(c, carry):
        g0, z0, g1, f1, g2 = [ref.at[c] for ref in (g0_ref, z0_ref, g1_ref, f1_ref, g2_ref)]
        precondition(b_right_ref, b_down_ref, g0, z0, work_ref)
        sum0, sum1 = next_residual(b_right_ref, b_down_ref, g0, z0, g1, own_of)
        precondition(b_right_ref, b_down_ref, g1, f1, work_ref)
        sum2, sum3 = next_residual(b_right_ref, b_down_ref, g1, f1, g2, own_of)
        return tuple(a + b for a, b in zip(carry, (sum0, sum1, sum2, sum3)))

    zero = jnp.zeros((SUBS, LANES), jnp.float32)
    parts = lax.fori_loop(0, chans, channel, (zero,) * 4)
    sums = zero
    for k, part in enumerate(parts):
        sums = jnp.where(sub == k, jnp.sum(part), sums)
    sums_ref[...] = sums

    def edge(c, j, at):
        s, i = divmod(HALO + at, steps)
        return g2_ref[c, j, pl.ds(i * SUBS + s, LATE, stride=SUBS), :]

    for c in range(chans):
        for j in range(tiles):
            low, high = edge(c, j, 0), edge(c, j, rows - LATE)
            first_late_ref[c, j] = jnp.where(odd, low, high)
            second_late_ref[c, j] = jnp.where(odd, high, low)


def second_kernel(
    c, place_ref, first_late_ref, second_late_ref, b_right_ref, b_down_ref, g2_ref, f2_ref, g_ref, work_ref
):
    tiles, height = b_right_ref.shape[:2]
    rows = height - 2 * HALO
    steps = height // SUBS
    odd = place_ref[4] == 1
    for j in range(tiles):
        g_ref[j] = g2_ref[c, j]
        first, second = first_late_ref[c, j], second_late_ref[c, j]
        for value, at in ((jnp.where(odd, first, second), HALO - LATE), (jnp.where(odd, second, first), HALO + rows)):
            done = 0
            while done < LATE:
                s, i = divmod(at + done, steps)
                count = min(LATE - done, steps - i)
                g_ref[j, pl.ds(i * SUBS + s, count, stride=SUBS), :] = value[done:done + count]
                done += count
    precondition(b_right_ref, b_down_ref, g_ref, f2_ref, work_ref)


def combine(n0, n1, n2, n3):
    gap = n0 - n1
    keep = -n1 / gap
    step = n0 / gap
    beta = (n0 * n2 - n1 * n1) / (gap * gap)
    along = keep + beta
    curvature = along * along * gap + 2.0 * along * step * (n1 - n2) + step * step * (n2 - n3)
    scaled = n0 * beta / curvature
    first_size = step * MIX
    second_size = scaled * MIX
    x0 = first_size + second_size * along
    x1 = second_size * step
    r0 = keep - scaled * along
    r1 = step + scaled * (along - step)
    r2 = scaled * step
    return x0, x1, r0, r1, r2


def third_kernel(
    sums_ref, scale_ref, root_ref, g0_ref, z0_ref, g1_ref, f1_ref, g2_ref, *refs
):
    *f2_refs, solution_hbm, residual_hbm, smoothed_hbm, natural, done, sems = refs
    rows, cols = solution_hbm.shape[1:]
    own_tiles = cols // LANES
    tiles, height = scale_ref.shape[:2]
    steps = height // SUBS
    ways = ways_of(tiles)
    x0, x1, r0, r1, r2 = combine(*[jnp.broadcast_to(sums_ref[k:k + 1, :], (SUBS, LANES)) for k in range(4)])
    matrix = undealing(ways) if ways > 1 else None
    outs = (solution_hbm, residual_hbm, smoothed_hbm)
    copies = []
    for c, f2_ref in enumerate(f2_refs):
        for j in range(tiles):
            for i in range(steps):
                at = pl.ds(i * SUBS, SUBS)
                scale = scale_ref[j, at, :]
                root = root_ref[j, at, :]
                g0, g1, g2, z0, f1 = [ref[c, j, at, :] for ref in (g0_ref, g1_ref, g2_ref, z0_ref, f1_ref)]
                f2 = f2_ref[j, at, :]
                there = pl.ds(i, SUBS, stride=steps)
                natural[c, 0, j, there, :] = scale * (x0 * z0 + x1 * f1)
                natural[c, 1, j, there, :] = root * (r0 * g0 + r1 * g1 + r2 * g2)
                natural[c, 2, j, there, :] = scale * (r0 * z0 + r1 * f1 + r2 * f2)
        for g in range(0, own_tiles, ways):
            value = jnp.concatenate(
                [natural[c, :, g + m, HALO:HALO + rows, :].reshape(3 * rows, LANES) for m in range(ways)], axis=1
            )
            width = min(ways, own_tiles - g) * LANES
            if ways > 1:
                value = permuted(value, matrix[:, :width], 2)
            for k in range(len(outs)):
                done[c, k, :, g * LANES:g * LANES + width] = value[k * rows:(k + 1) * rows]
        for k, ref in enumerate(outs):
            copies.append(pltpu.make_async_copy(done.at[c, k], ref.at[c], sems.at[c, k]))
            copies[-1].start()
    for copy in copies:
        copy.wait()


def sum_over(value, axes, beside):
    steps = []
    for axis in axes:
        size = lax.axis_size(axis)
        if size & (size - 1):
            value = lax.psum(value, axis)
            continue
        steps += [(axis, [(i, i ^ (1 << k)) for i in range(size)]) for k in range(size.bit_length() - 1)]
    done = []
    for k, (axis, pairs) in enumerate(steps):
        other = lax.ppermute(value, axis, pairs)
        if len(steps) - k <= len(beside):
            value, array = lax.optimization_barrier((value, beside[len(done)]))
            done.append(array)
        value = value + other
    return value, done + list(beside[len(done):])


def per_device(source, weight, seam_right, seam_down, offsets):
    chans, rows, cols = source.shape
    row_axis, col_axis = lax.axis_size("row"), lax.axis_size("col")
    row_at, col_at = lax.axis_index("row"), lax.axis_index("col")
    odd_row, odd_col = lax.rem(row_at, 2), lax.rem(col_at, 2)
    place = jnp.stack(
        [
            jnp.where(row_at == row_axis - 1, rows - 1, -1),
            jnp.where(col_at == col_axis - 1, LANES - 1, -1),
            lax.div(row_at * rows, TILE),
            col_at * (cols // TILE),
            odd_row,
            odd_col,
        ]
    ).astype(jnp.int32)

    in_vmem = pl.BlockSpec(memory_space=pltpu.VMEM)
    in_smem = pl.BlockSpec(memory_space=pltpu.SMEM)
    in_hbm = pl.BlockSpec(memory_space=pltpu.HBM)
    params = pltpu.CompilerParams(vmem_limit_bytes=VMEM_LIMIT)

    def shaped(*shape):
        return jax.ShapeDtypeStruct(shape, jnp.float32)

    def scratch(*shape):
        return pltpu.VMEM(shape, jnp.float32)

    planes = chans + 3
    own_tiles = cols // LANES
    tiles = own_tiles + 1
    packs = -(-planes // SLOTS)
    own, first_rows, second_rows, first_cols, second_cols = pl.pallas_call(
        own_kernel,
        out_shape=[shaped(planes, own_tiles, rows, LANES)]
        + [shaped(planes, own_tiles, HALO, LANES)] * 2
        + [shaped(packs, rows, LANES)] * 2,
        in_specs=[in_smem] + [in_hbm] * 5,
        out_specs=[in_vmem] * 5,
        scratch_shapes=[
            pltpu.SMEM((chans,) + offsets.shape[:2], jnp.int32),
            scratch(*source.shape),
            scratch(*weight.shape),
            pltpu.VMEM(weight.shape, jnp.int32),
            pltpu.VMEM(weight.shape, jnp.int32),
            pltpu.SemaphoreType.DMA((planes + 1,)),
        ],
        compiler_params=params,
    )(
        place,
        *[
            pltpu.with_memory_space_constraint(v, pltpu.HBM)
            for v in (offsets.transpose(2, 0, 1), source, weight, seam_right, seam_down)
        ],
    )

    def swap(first, second, axis):
        size = lax.axis_size(axis)
        received = []
        for start, value in enumerate((first, second)):
            pairs = [(i, i + 1) for i in range(start, size - 1, 2)]
            pairs += [(j, i) for i, j in pairs]
            received.append(None if value is None else lax.ppermute(value, axis, pairs))
        return received

    ways = ways_of(tiles)
    inner = pl.pallas_call(
        inner_dealt_kernel,
        out_shape=shaped(planes, tiles - ways, rows, LANES),
        in_specs=[in_vmem],
        out_specs=in_vmem,
        compiler_params=params,
        cost_estimate=pl.CostEstimate(flops=10**8, bytes_accessed=4 * 10**6, transcendentals=0),
    )(own)
    first_rows, _ = swap(first_rows, None, "row")
    first_cols, second_cols = swap(first_cols, second_cols, "col")
    first_cols, second_cols, second_rows, inner = lax.optimization_barrier(
        (first_cols, second_cols, second_rows, inner)
    )
    _, second_rows = swap(None, second_rows, "row")
    corners = pl.pallas_call(
        functools.partial(corners_kernel, chans),
        out_shape=[shaped(2, packs, HALO, LANES)] * 2,
        in_specs=[in_smem] + [in_vmem] * 2,
        out_specs=[in_vmem] * 2,
        compiler_params=params,
    )(place, first_cols, second_cols)
    first_corners, second_corners = swap(*corners, "row")
    outer = pl.pallas_call(
        outer_dealt_kernel,
        out_shape=shaped(planes, ways, rows, LANES),
        in_specs=[in_smem] + [in_vmem] * 3,
        out_specs=in_vmem,
        compiler_params=params,
        cost_estimate=pl.CostEstimate(flops=10**8, bytes_accessed=2 * 10**6, transcendentals=0),
    )(place, own, first_cols, second_cols)

    height = rows + 2 * HALO
    plane = shaped(tiles, height, LANES)
    field = shaped(chans, tiles, height, LANES)
    late = shaped(chans, tiles, LATE, LANES)
    *basis, sums, first_late, second_late = pl.pallas_call(
        first_kernel,
        out_shape=[plane] * 4 + [field] * 5 + [shaped(SUBS, LANES)] + [late] * 2,
        in_specs=[in_smem] + [in_vmem] * 6,
        out_specs=[in_vmem] * 12,
        scratch_shapes=[scratch(planes, tiles, height, LANES), scratch(*plane.shape)],
        compiler_params=params,
    )(place, inner, outer, first_rows, second_rows, first_corners, second_corners)

    first_late, second_late = swap(first_late, second_late, "row")

    b_right, b_down, scale, root, g0, z0, g1, f1, g2 = basis
    f2 = [
        pl.pallas_call(
            functools.partial(second_kernel, c),
            out_shape=plane,
            in_specs=[in_smem] + [in_vmem] * 5,
            out_specs=in_vmem,
            scratch_shapes=[scratch(*plane.shape)] * 2,
            compiler_params=params,
            cost_estimate=pl.CostEstimate(flops=10**8, bytes_accessed=10**7, transcendentals=0),
        )(place, first_late, second_late, b_right, b_down, g2)
        for c in range(chans)
    ]
    total, f2 = sum_over(sums, ("col", "row"), f2)
    return pl.pallas_call(
        third_kernel,
        out_shape=[shaped(chans, rows, cols)] * 3,
        in_specs=[in_vmem] * (8 + chans),
        out_specs=[pl.BlockSpec(memory_space=pltpu.HBM)] * 3,
        scratch_shapes=[
            scratch(chans, 3, tiles, height, LANES),
            scratch(chans, 3, rows, cols),
            pltpu.SemaphoreType.DMA((chans, 3)),
        ],
        compiler_params=params,
    )(total, scale, root, g0, z0, g1, f1, g2, *f2)


def solution(mesh):
    placed = (
        P(None, ("band", "row"), "col"),
        P(("band", "row"), "col"),
        P(("band", "row"), "col"),
        P(("band", "row"), "col"),
        P("band", None, None),
    )
    return jax.shard_map(
        per_device,
        mesh=mesh,
        in_specs=placed,
        out_specs=(
            P(None, ("band", "row"), "col"),
            P(None, ("band", "row"), "col"),
            P(None, ("band", "row"), "col"),
        ),
        check_vma=False,
    )
```

```python
import functools

import jax
import jax.numpy as jnp
from jax import lax
from jax.experimental import pallas as pl
from jax.experimental.pallas import tpu as pltpu
from jax.sharding import PartitionSpec as P

TILE = 256
SWEEPS = 8
SUBS = 8
LANES = 128
HALO = 16
LATE = 8
SLOT = 32
SLOTS = LANES // SLOT
WAYS = 3

seam_damping = 0.8
offset_unit = 32.0
spectrum_low = 0.08
spectrum_high = 2.0
MIX = 2.4

VMEM_LIMIT = 28 * 1024 * 1024


def chebyshev_polynomial():
    centre = (spectrum_high + spectrum_low) / 2.0
    radius = (spectrum_high - spectrum_low) / 2.0
    sigma = centre / radius
    size = SWEEPS
    update = [1.0 / centre] + [0.0] * (size - 1)
    smoothed = list(update)
    rho = 1.0 / sigma
    for _ in range(SWEEPS - 1):
        remainder = [-s for s in smoothed]
        remainder[0] += 1.0
        for k in range(size - 1):
            remainder[k + 1] += smoothed[k]
        following = 1.0 / (2.0 * sigma - rho)
        update = [following * rho * u + 2.0 * following / radius * r for u, r in zip(update, remainder)]
        smoothed = [s + u for s, u in zip(smoothed, update)]
        rho = following
    return smoothed


def lane_index():
    return lax.broadcasted_iota(jnp.int32, (SUBS, LANES), 1)


def odd(axis):
    return lax.rem(lax.axis_index(axis), 2) == 1


def pack(planes, start):
    lane = lax.broadcasted_iota(jnp.int32, planes[0].shape, 1)
    packed = [None] * (-(-len(planes) // SLOTS))
    for p, plane in enumerate(planes):
        slot = p % SLOTS
        by = (slot * SLOT - start) % LANES
        moved = pltpu.roll(plane, by, 1) if by else plane
        k = p // SLOTS
        packed[k] = moved if slot == 0 else jnp.where(lane < slot * SLOT, packed[k], moved)
    return packed


def own_kernel(
    offsets_hbm, src_hbm, weight_hbm, seam_right_hbm, seam_down_hbm,
    own_ref, first_rows_ref, second_rows_ref, first_cols_ref, second_cols_ref,
    offsets_ref, src_ref, weight_ref, seam_right_ref, seam_down_ref, sems,
):
    chans, rows, cols = src_ref.shape
    own_tiles = cols // LANES
    moves = [(weight_hbm, weight_ref), (seam_right_hbm, seam_right_ref), (seam_down_hbm, seam_down_ref)]
    moves += [(src_hbm.at[c], src_ref.at[c]) for c in range(chans)] + [(offsets_hbm, offsets_ref)]
    copies = [pltpu.make_async_copy(there, here, sems.at[k]) for k, (there, here) in enumerate(moves)]
    for copy in copies:
        copy.start()
    row = lax.broadcasted_iota(jnp.int32, (rows, LANES), 0)
    lane = lax.broadcasted_iota(jnp.int32, (rows, LANES), 1)
    sub = lax.broadcasted_iota(jnp.int32, (SUBS, LANES), 0)
    row_at, col_at = lax.axis_index("row"), lax.axis_index("col")
    last_row = jnp.where(row_at == lax.axis_size("row") - 1, rows - 1, -1)
    last_lane = jnp.where(col_at == lax.axis_size("col") - 1, LANES - 1, -1)
    tile_row, tile_at = lax.div(row_at * rows, TILE), col_at * (cols // TILE)
    odd_row, odd_col = odd("row"), odd("col")

    def tile(ref, j):
        return ref[:, j * LANES:(j + 1) * LANES]

    copies[0].wait()
    for j in range(own_tiles):
        own_ref[chans, j] = tile(weight_ref, j)
    copies[1].wait()
    for j in range(own_tiles):
        value = 1.0 - seam_damping * tile(seam_right_ref, j).astype(jnp.float32)
        own_ref[chans + 1, j] = jnp.where(lane == last_lane, 0.0, value) if j == own_tiles - 1 else value
    copies[2].wait()
    for j in range(own_tiles):
        value = 1.0 - seam_damping * tile(seam_down_ref, j).astype(jnp.float32)
        own_ref[chans + 2, j] = jnp.where(row == last_row, 0.0, value)
    copies[-1].wait()
    for c in range(chans):
        shift = [
            jnp.broadcast_to(offsets_ref[c, tile_row, tile_at + k], (rows, LANES)).astype(jnp.float32) / offset_unit
            for k in range(cols // TILE)
        ]
        copies[3 + c].wait()
        for j in range(own_tiles):
            own_ref[c, j] = tile(src_ref.at[c], j) + shift[j * LANES // TILE]

    planes = range(chans + 3)

    def low_rows(ref):
        for p in planes:
            ref[p] = own_ref[p, :, 0:HALO, :]

    def high_rows(ref):
        at = rows - HALO
        for p in planes:
            ref[p] = own_ref[p, :, at:rows, :]
        for j in range(own_tiles):
            above = jnp.where(sub == 0, own_ref[chans + 2, j, at - 1:at, :], 0.0)
            ref[chans, j, 0:SUBS, :] = own_ref[chans, j, at:at + SUBS, :] + above

    @pl.when(odd_row)
    def _():
        low_rows(first_rows_ref)
        high_rows(second_rows_ref)

    @pl.when(jnp.logical_not(odd_row))
    def _():
        high_rows(first_rows_ref)
        low_rows(second_rows_ref)

    left = pack([own_ref[p, 0] for p in planes], 0)
    right = pack([own_ref[p, own_tiles - 1] for p in planes], LANES - SLOT)
    for k, (a, b) in enumerate(zip(left, right)):
        first_cols_ref[k] = jnp.where(odd_col, a, b)
        second_cols_ref[k] = jnp.where(odd_col, b, a)


def corners_kernel(chans, first_ref, second_ref, first_out, second_out):
    rows = first_ref.shape[1]
    odd_row, odd_col = odd("row"), odd("col")
    sub = lax.broadcasted_iota(jnp.int32, (SUBS, LANES), 0)
    lane = lane_index()
    weight, down = chans, chans + 2
    slot = weight % SLOTS
    at = rows - HALO
    for side, (in_odd, in_even) in enumerate(((first_ref, second_ref), (second_ref, first_ref))):

        def tile(k, low, count=SUBS, in_odd=in_odd, in_even=in_even):
            return jnp.where(odd_col, in_odd[k, low:low + count, :], in_even[k, low:low + count, :])

        above = jnp.broadcast_to(tile(down // SLOTS, at - 1, 1), (SUBS, LANES))
        above = pltpu.roll(above, (slot - down % SLOTS) % SLOTS * SLOT, 1)
        own_slot = jnp.logical_and(lane >= slot * SLOT, lane < (slot + 1) * SLOT)
        above = jnp.where(jnp.logical_and(sub == 0, own_slot), above, 0.0)
        for k in range(first_ref.shape[0]):
            for low in range(0, HALO, SUBS):
                near = tile(k, low)
                far = tile(k, at + low)
                if low == 0 and k == weight // SLOTS:
                    far = far + above
                first_out[side, k, low:low + SUBS, :] = jnp.where(odd_row, near, far)
                second_out[side, k, low:low + SUBS, :] = jnp.where(odd_row, far, near)


def unpack(p, lefts, rights):
    lane = lax.broadcasted_iota(jnp.int32, lefts.shape, 1)
    slot = p % SLOTS
    if slot != SLOTS - 1:
        lefts = pltpu.roll(lefts, LANES - SLOT - slot * SLOT, 1)
    if slot:
        rights = pltpu.roll(rights, LANES - slot * SLOT, 1)
    return jnp.where(lane < SLOT, rights, jnp.where(lane >= LANES - SLOT, lefts, 0.0))


def ways_of(tiles):
    return WAYS if tiles % WAYS == 0 else 1


def split(value, count):
    parts = []
    for k in range(count):
        part = value.astype(jnp.bfloat16)
        parts.append(part)
        if k + 1 < count:
            value = value - part.astype(jnp.float32)
    return jnp.concatenate(parts, axis=0)


def permuted(value, index, count):
    rows = value.shape[0]
    out = jnp.dot(split(value, count), index, preferred_element_type=jnp.float32)
    total = out[:rows]
    for k in range(1, count):
        total = total + out[k * rows:(k + 1) * rows]
    return total


def dealing(ways):
    size = ways * LANES
    column = lax.broadcasted_iota(jnp.int32, (size, size), 0)
    place = lax.broadcasted_iota(jnp.int32, (size, size), 1)
    return jnp.where(column == ways * (place % LANES) + place // LANES, 1.0, 0.0).astype(jnp.bfloat16)


def undealing(ways):
    size = ways * LANES
    column = lax.broadcasted_iota(jnp.int32, (size, size), 1)
    place = lax.broadcasted_iota(jnp.int32, (size, size), 0)
    return jnp.where(column == ways * (place % LANES) + place // LANES, 1.0, 0.0).astype(jnp.bfloat16)


def deal(tile_of, low, high, ways, emit):
    matrix = dealing(ways) if ways > 1 else None
    for g in range(low, high, ways):
        if ways == 1:
            emit(g, tile_of(g))
            continue
        value = permuted(jnp.concatenate([tile_of(g + m) for m in range(ways)], axis=1), matrix, 3)
        for m in range(ways):
            emit(g + m, value[:, m * LANES:(m + 1) * LANES])


def inner_dealt_kernel(own_ref, dealt_ref):
    planes, own_tiles, rows = own_ref.shape[:3]

    def emit(j, value):
        dealt_ref[:, j] = value.reshape(planes, rows, LANES)

    deal(lambda j: own_ref[:, j].reshape(planes * rows, LANES), 0, dealt_ref.shape[1], ways_of(own_tiles + 1), emit)


def outer_dealt_kernel(own_ref, first_ref, second_ref, dealt_ref):
    planes, own_tiles, rows = own_ref.shape[:3]
    tiles = own_tiles + 1
    low = tiles - dealt_ref.shape[1]
    odd_col = odd("col")

    def tile_of(j):
        if j < own_tiles:
            return own_ref[:, j].reshape(planes * rows, LANES)
        parts = []
        for p in range(planes):
            first, second = first_ref[p // SLOTS], second_ref[p // SLOTS]
            parts.append(unpack(p, jnp.where(odd_col, first, second), jnp.where(odd_col, second, first)))
        return jnp.concatenate(parts, axis=0)

    def emit(j, value):
        dealt_ref[:, j - low] = value.reshape(planes, rows, LANES)

    deal(tile_of, low, tiles, ways_of(tiles), emit)


def rightward(values):
    tiles = len(values)
    ways = ways_of(tiles)
    last = lane_index() == LANES - 1
    ahead = {g: pltpu.roll(values[g], LANES - 1, 1) for g in range(0, tiles, ways)}
    out = []
    for j in range(tiles):
        if j % ways + 1 < ways:
            out.append(values[j + 1])
        else:
            g = j - ways + 1
            out.append(jnp.where(last, ahead[(g + ways) % tiles], ahead[g]))
    return out


def leftward(values):
    tiles = len(values)
    ways = ways_of(tiles)
    first = lane_index() == 0
    behind = {g: pltpu.roll(values[g + ways - 1], 1, 1) for g in range(0, tiles, ways)}
    out = []
    for j in range(tiles):
        if j % ways:
            out.append(values[j - 1])
        else:
            out.append(jnp.where(first, behind[(j - ways) % tiles], behind[j]))
    return out


def spread(b_right_ref, b_down_ref, z_ref, emit):
    tiles, height = z_ref.shape[:2]
    steps = height // SUBS
    ways = ways_of(tiles)
    lane = lane_index()
    first, last = (lane == 0, lane == LANES - 1)

    def at(i):
        return pl.ds(i * SUBS, SUBS)

    from_above = [pltpu.roll(b_down_ref[j, at(steps - 1), :] * z_ref[j, at(steps - 1), :], 1, 0) for j in range(tiles)]
    centre = [z_ref[j, at(0), :] for j in range(tiles)]
    wrapped = [pltpu.roll(v, SUBS - 1, 0) for v in centre]
    for i in range(steps):
        pushed_out = {
            g: pltpu.roll(b_right_ref[g + ways - 1, at(i), :] * centre[g + ways - 1], 1, 1)
            for g in range(0, tiles, ways)
        }
        ahead = {g: pltpu.roll(centre[g], LANES - 1, 1) for g in range(0, tiles, ways)}
        pushed = None
        below = []
        for j in range(tiles):
            g = j // ways * ways
            b_right = b_right_ref[j, at(i), :]
            b_down = b_down_ref[j, at(i), :]
            below.append(z_ref[j, at(i + 1), :] if i + 1 < steps else wrapped[j])
            if j == g:
                from_left = jnp.where(first, pushed_out[(g - ways) % tiles], pushed_out[g])
            else:
                from_left = pushed
            if j + 1 < g + ways:
                to_right = centre[j + 1]
                pushed = b_right * centre[j]
            else:
                to_right = jnp.where(last, ahead[(g + ways) % tiles], ahead[g])
            moved = (b_right * to_right + from_left) + (b_down * below[j] + from_above[j])
            from_above[j] = b_down * centre[j]
            emit(i, j, centre[j], moved)
        centre = below


def precondition(b_right_ref, b_down_ref, g_ref, z_ref, work_ref):
    poly = chebyshev_polynomial()
    degree = SWEEPS - 1

    def at(i):
        return pl.ds(i * SUBS, SUBS)

    def first(i, j, centre, moved):
        z_ref[j, at(i), :] = poly[degree] * moved + poly[degree - 1] * centre

    spread(b_right_ref, b_down_ref, g_ref, first)

    def pair(k, carry):
        adds = []
        for half in range(2):
            value = jnp.float32(poly[half])
            for later in range(1, (degree - 1) // 2):
                value = jnp.where(k == (degree - 1) // 2 - 1 - later, jnp.float32(poly[2 * later + half]), value)
            adds.append(value)

        def one(target, add):
            def emit(i, j, centre, moved):
                target[j, at(i), :] = moved + add * g_ref[j, at(i), :]

            return emit

        spread(b_right_ref, b_down_ref, z_ref, one(work_ref, adds[1]))
        spread(b_right_ref, b_down_ref, work_ref, one(z_ref, adds[0]))
        return carry

    lax.fori_loop(0, (degree - 1) // 2, pair, 0)


def next_residual(b_right_ref, b_down_ref, g_ref, z_ref, next_ref, own_of):
    height = g_ref.shape[1]
    steps = height // SUBS
    sums = {}

    def emit(i, j, centre, moved):
        at = pl.ds(i * SUBS, SUBS)
        g = g_ref[j, at, :]
        following = g - MIX * (centre - moved)
        next_ref[j, at, :] = following
        key = own_of(i, j)
        now = (g * centre, following * centre)
        before = sums.get(key)
        sums[key] = now if before is None else (before[0] + now[0], before[1] + now[1])

    spread(b_right_ref, b_down_ref, z_ref, emit)
    sub = lax.broadcasted_iota(jnp.int32, (SUBS, LANES), 0)
    lane = lane_index()
    total = [jnp.zeros((SUBS, LANES), jnp.float32)] * 2
    for (low, high, lanes), parts in sums.items():
        inside = jnp.logical_and(jnp.logical_and(sub >= low, sub <= high), lane < lanes)
        total = [t + jnp.where(inside, p, 0.0) for t, p in zip(total, parts)]
    return total


def first_kernel(
    inner_ref, outer_ref, first_rows_ref, second_rows_ref, first_corners_ref, second_corners_ref,
    b_right_ref, b_down_ref, scale_ref, root_ref, g0_ref, z0_ref, g1_ref, f1_ref, g2_ref, sums_ref,
    first_late_ref, second_late_ref,
    natural, work_ref,
):
    planes, inner, rows = inner_ref.shape[:3]
    tiles = inner + outer_ref.shape[1]
    chans = planes - 3
    own_tiles = tiles - 1
    height = rows + 2 * HALO
    steps = height // SUBS

    for p in range(planes):
        for j in range(tiles):
            natural[p, j, HALO:HALO + rows, :] = inner_ref[p, j] if j < inner else outer_ref[p, j - inner]
    odd_row = odd("row")

    def edge_tile(j):
        if j < own_tiles:
            first, second = [ref[:, j].reshape(planes * HALO, LANES) for ref in (first_rows_ref, second_rows_ref)]
        else:
            first, second = [
                jnp.concatenate([unpack(p, ref[0, p // SLOTS], ref[1, p // SLOTS]) for p in range(planes)], axis=0)
                for ref in (first_corners_ref, second_corners_ref)
            ]
        return jnp.concatenate([jnp.where(odd_row, first, second), jnp.where(odd_row, second, first)], axis=0)

    def put_edge(j, value):
        value = value.reshape(2, planes, HALO, LANES)
        natural[:, j, 0:HALO, :] = value[0]
        natural[:, j, HALO + rows:height, :] = value[1]

    deal(edge_tile, 0, tiles, ways_of(tiles), put_edge)

    def at(i):
        return pl.ds(i * SUBS, SUBS)

    def interleaved(p, i, j):
        return natural[p, j, pl.ds(i, SUBS, stride=steps), :]

    sub = lax.broadcasted_iota(jnp.int32, (SUBS, LANES), 0)
    to_up = [
        jnp.where(sub == 0, 0.0, pltpu.roll(interleaved(chans + 2, steps - 1, j), 1, 0)) for j in range(tiles)
    ]
    for i in range(steps):
        to_right = [interleaved(chans + 1, i, j) for j in range(tiles)]
        to_left = leftward(to_right)
        for j in range(tiles):
            to_down = interleaved(chans + 2, i, j)
            diag = interleaved(chans, i, j) + to_right[j] + to_left[j] + to_down + to_up[j]
            inside = diag > 0.0
            safe = jnp.where(inside, diag, 1.0)
            guess = lax.rsqrt(safe)
            scale = guess * (1.5 - 0.5 * safe * guess * guess)
            scale_ref[j, at(i), :] = jnp.where(inside, scale, 0.0)
            root_ref[j, at(i), :] = safe * scale
            to_up[j] = to_down
    wrapped = [pltpu.roll(scale_ref[j, at(0), :], SUBS - 1, 0) for j in range(tiles)]
    for i in range(steps):
        scale = [scale_ref[j, at(i), :] for j in range(tiles)]
        right_scale = rightward(scale)
        for j in range(tiles):
            b_right_ref[j, at(i), :] = interleaved(chans + 1, i, j) * scale[j] * right_scale[j]
            down_scale = scale_ref[j, at(i + 1), :] if i + 1 < steps else wrapped[j]
            b_down_ref[j, at(i), :] = interleaved(chans + 2, i, j) * scale[j] * down_scale
            for c in range(chans):
                g0_ref[c, j, at(i), :] = interleaved(c, i, j) * scale[j]

    ways = ways_of(tiles)

    def own_of(i, j):
        low, high = -(-(HALO - i) // steps), (HALO + rows - 1 - i) // steps
        left = own_tiles * LANES - j // ways * ways * LANES - j % ways
        return low, high, min(LANES, max(0, -(-left // ways)))

    def channel(c, carry):
        g0, z0, g1, f1, g2 = [ref.at[c] for ref in (g0_ref, z0_ref, g1_ref, f1_ref, g2_ref)]
        precondition(b_right_ref, b_down_ref, g0, z0, work_ref)
        sum0, sum1 = next_residual(b_right_ref, b_down_ref, g0, z0, g1, own_of)
        precondition(b_right_ref, b_down_ref, g1, f1, work_ref)
        sum2, sum3 = next_residual(b_right_ref, b_down_ref, g1, f1, g2, own_of)
        return tuple(a + b for a, b in zip(carry, (sum0, sum1, sum2, sum3)))

    zero = jnp.zeros((SUBS, LANES), jnp.float32)
    parts = lax.fori_loop(0, chans, channel, (zero,) * 4)
    sums = zero
    for k, part in enumerate(parts):
        sums = jnp.where(sub == k, jnp.sum(part), sums)
    sums_ref[...] = sums

    def edge(c, j, at):
        s, i = divmod(HALO + at, steps)
        return g2_ref[c, j, pl.ds(i * SUBS + s, LATE, stride=SUBS), :]

    for c in range(chans):
        for j in range(tiles):
            low, high = edge(c, j, 0), edge(c, j, rows - LATE)
            first_late_ref[c, j] = jnp.where(odd_row, low, high)
            second_late_ref[c, j] = jnp.where(odd_row, high, low)


def second_kernel(
    c, first_late_ref, second_late_ref, b_right_ref, b_down_ref, g2_ref, f2_ref, g_ref, work_ref
):
    tiles, height = b_right_ref.shape[:2]
    rows = height - 2 * HALO
    steps = height // SUBS
    odd_row = odd("row")
    for j in range(tiles):
        g_ref[j] = g2_ref[c, j]
        first, second = first_late_ref[c, j], second_late_ref[c, j]
        for value, at in ((jnp.where(odd_row, first, second), HALO - LATE), (jnp.where(odd_row, second, first), HALO + rows)):
            done = 0
            while done < LATE:
                s, i = divmod(at + done, steps)
                count = min(LATE - done, steps - i)
                g_ref[j, pl.ds(i * SUBS + s, count, stride=SUBS), :] = value[done:done + count]
                done += count
    precondition(b_right_ref, b_down_ref, g_ref, f2_ref, work_ref)


def combine(n0, n1, n2, n3):
    gap = n0 - n1
    keep = -n1 / gap
    step = n0 / gap
    beta = (n0 * n2 - n1 * n1) / (gap * gap)
    along = keep + beta
    curvature = along * along * gap + 2.0 * along * step * (n1 - n2) + step * step * (n2 - n3)
    scaled = n0 * beta / curvature
    first_size = step * MIX
    second_size = scaled * MIX
    x0 = first_size + second_size * along
    x1 = second_size * step
    r0 = keep - scaled * along
    r1 = step + scaled * (along - step)
    r2 = scaled * step
    return x0, x1, r0, r1, r2


def third_kernel(
    sums_ref, scale_ref, root_ref, g0_ref, z0_ref, g1_ref, f1_ref, g2_ref, *refs
):
    *f2_refs, solution_hbm, residual_hbm, smoothed_hbm, natural, done, sems = refs
    rows, cols = solution_hbm.shape[1:]
    own_tiles = cols // LANES
    tiles, height = scale_ref.shape[:2]
    steps = height // SUBS
    ways = ways_of(tiles)
    x0, x1, r0, r1, r2 = combine(*[jnp.broadcast_to(sums_ref[k:k + 1, :], (SUBS, LANES)) for k in range(4)])
    matrix = undealing(ways) if ways > 1 else None
    outs = (solution_hbm, residual_hbm, smoothed_hbm)
    copies = []
    for c, f2_ref in enumerate(f2_refs):
        for j in range(tiles):
            for i in range(steps):
                at = pl.ds(i * SUBS, SUBS)
                scale = scale_ref[j, at, :]
                root = root_ref[j, at, :]
                g0, g1, g2, z0, f1 = [ref[c, j, at, :] for ref in (g0_ref, g1_ref, g2_ref, z0_ref, f1_ref)]
                f2 = f2_ref[j, at, :]
                there = pl.ds(i, SUBS, stride=steps)
                natural[c, 0, j, there, :] = scale * (x0 * z0 + x1 * f1)
                natural[c, 1, j, there, :] = root * (r0 * g0 + r1 * g1 + r2 * g2)
                natural[c, 2, j, there, :] = scale * (r0 * z0 + r1 * f1 + r2 * f2)
        for g in range(0, own_tiles, ways):
            value = jnp.concatenate(
                [natural[c, :, g + m, HALO:HALO + rows, :].reshape(3 * rows, LANES) for m in range(ways)], axis=1
            )
            width = min(ways, own_tiles - g) * LANES
            if ways > 1:
                value = permuted(value, matrix[:, :width], 2)
            for k in range(len(outs)):
                done[c, k, :, g * LANES:g * LANES + width] = value[k * rows:(k + 1) * rows]
        for k, ref in enumerate(outs):
            copies.append(pltpu.make_async_copy(done.at[c, k], ref.at[c], sems.at[c, k]))
            copies[-1].start()
    for copy in copies:
        copy.wait()


def sum_over(value, axes, beside):
    steps = []
    for axis in axes:
        size = lax.axis_size(axis)
        if size & (size - 1):
            value = lax.psum(value, axis)
            continue
        steps += [(axis, [(i, i ^ (1 << k)) for i in range(size)]) for k in range(size.bit_length() - 1)]
    done = []
    for k, (axis, pairs) in enumerate(steps):
        other = lax.ppermute(value, axis, pairs)
        if len(steps) - k <= len(beside):
            value, array = lax.optimization_barrier((value, beside[len(done)]))
            done.append(array)
        value = value + other
    return value, done + list(beside[len(done):])


def per_device(source, weight, seam_right, seam_down, offsets):
    chans, rows, cols = source.shape
    in_vmem = pl.BlockSpec(memory_space=pltpu.VMEM)
    in_hbm = pl.BlockSpec(memory_space=pltpu.HBM)
    params = pltpu.CompilerParams(vmem_limit_bytes=VMEM_LIMIT)

    def shaped(*shape):
        return jax.ShapeDtypeStruct(shape, jnp.float32)

    def scratch(*shape):
        return pltpu.VMEM(shape, jnp.float32)

    planes = chans + 3
    own_tiles = cols // LANES
    tiles = own_tiles + 1
    packs = -(-planes // SLOTS)
    own, first_rows, second_rows, first_cols, second_cols = pl.pallas_call(
        own_kernel,
        out_shape=[shaped(planes, own_tiles, rows, LANES)]
        + [shaped(planes, own_tiles, HALO, LANES)] * 2
        + [shaped(packs, rows, LANES)] * 2,
        in_specs=[in_hbm] * 5,
        out_specs=[in_vmem] * 5,
        scratch_shapes=[
            pltpu.SMEM((chans,) + offsets.shape[:2], jnp.int32),
            scratch(*source.shape),
            scratch(*weight.shape),
            pltpu.VMEM(weight.shape, jnp.int32),
            pltpu.VMEM(weight.shape, jnp.int32),
            pltpu.SemaphoreType.DMA((planes + 1,)),
        ],
        compiler_params=params,
    )(
        *[
            pltpu.with_memory_space_constraint(v, pltpu.HBM)
            for v in (offsets.transpose(2, 0, 1), source, weight, seam_right, seam_down)
        ],
    )

    def swap(first, second, axis):
        size = lax.axis_size(axis)
        pairs = [[(i, i + 1) for i in range(start, size - 1, 2)] for start in range(2)]
        pairs = [some + [(j, i) for i, j in some] for some in pairs]
        return [lax.ppermute(value, axis, some) for value, some in zip((first, second), pairs)]

    ways = ways_of(tiles)
    inner = pl.pallas_call(
        inner_dealt_kernel,
        out_shape=shaped(planes, tiles - ways, rows, LANES),
        in_specs=[in_vmem],
        out_specs=in_vmem,
        compiler_params=params,
        cost_estimate=pl.CostEstimate(flops=10**8, bytes_accessed=4 * 10**6, transcendentals=0),
    )(own)
    first_rows, second_rows = swap(first_rows, second_rows, "row")
    first_cols, second_cols = swap(first_cols, second_cols, "col")
    first_cols, second_cols, inner = lax.optimization_barrier((first_cols, second_cols, inner))
    corners = pl.pallas_call(
        functools.partial(corners_kernel, chans),
        out_shape=[shaped(2, packs, HALO, LANES)] * 2,
        in_specs=[in_vmem] * 2,
        out_specs=[in_vmem] * 2,
        compiler_params=params,
    )(first_cols, second_cols)
    first_corners, second_corners = swap(*corners, "row")
    outer = pl.pallas_call(
        outer_dealt_kernel,
        out_shape=shaped(planes, ways, rows, LANES),
        in_specs=[in_vmem] * 3,
        out_specs=in_vmem,
        compiler_params=params,
        cost_estimate=pl.CostEstimate(flops=10**8, bytes_accessed=2 * 10**6, transcendentals=0),
    )(own, first_cols, second_cols)

    height = rows + 2 * HALO
    plane = shaped(tiles, height, LANES)
    field = shaped(chans, tiles, height, LANES)
    late = shaped(chans, tiles, LATE, LANES)
    *basis, sums, first_late, second_late = pl.pallas_call(
        first_kernel,
        out_shape=[plane] * 4 + [field] * 5 + [shaped(SUBS, LANES)] + [late] * 2,
        in_specs=[in_vmem] * 6,
        out_specs=[in_vmem] * 12,
        scratch_shapes=[scratch(planes, tiles, height, LANES), scratch(*plane.shape)],
        compiler_params=params,
    )(inner, outer, first_rows, second_rows, first_corners, second_corners)

    first_late, second_late = swap(first_late, second_late, "row")

    b_right, b_down, scale, root, g0, z0, g1, f1, g2 = basis
    f2 = [
        pl.pallas_call(
            functools.partial(second_kernel, c),
            out_shape=plane,
            in_specs=[in_vmem] * 5,
            out_specs=in_vmem,
            scratch_shapes=[scratch(*plane.shape)] * 2,
            compiler_params=params,
            cost_estimate=pl.CostEstimate(flops=10**8, bytes_accessed=10**7, transcendentals=0),
        )(first_late, second_late, b_right, b_down, g2)
        for c in range(chans)
    ]
    total, f2 = sum_over(sums, ("col", "row"), f2)
    return pl.pallas_call(
        third_kernel,
        out_shape=[shaped(chans, rows, cols)] * 3,
        in_specs=[in_vmem] * (8 + chans),
        out_specs=[pl.BlockSpec(memory_space=pltpu.HBM)] * 3,
        scratch_shapes=[
            scratch(chans, 3, tiles, height, LANES),
            scratch(chans, 3, rows, cols),
            pltpu.SemaphoreType.DMA((chans, 3)),
        ],
        compiler_params=params,
    )(total, scale, root, g0, z0, g1, f1, g2, *f2)


def solution(mesh):
    placed = (
        P(None, ("band", "row"), "col"),
        P(("band", "row"), "col"),
        P(("band", "row"), "col"),
        P(("band", "row"), "col"),
        P("band", None, None),
    )
    return jax.shard_map(
        per_device,
        mesh=mesh,
        in_specs=placed,
        out_specs=(
            P(None, ("band", "row"), "col"),
            P(None, ("band", "row"), "col"),
            P(None, ("band", "row"), "col"),
        ),
        check_vma=False,
    )
```

```python
import functools

import jax
import jax.numpy as jnp
from jax import lax
from jax.experimental import pallas as pl
from jax.experimental.pallas import tpu as pltpu
from jax.sharding import PartitionSpec as P

TILE = 256
SWEEPS = 8
SUBS = 8
LANES = 128
HALO = 16
LATE = 8
SLOT = 32
SLOTS = LANES // SLOT
WAYS = 3

seam_damping = 0.8
offset_unit = 32.0
spectrum_low = 0.08
spectrum_high = 2.0
MIX = 2.4

VMEM_LIMIT = 28 * 1024 * 1024


def chebyshev_polynomial():
    centre = (spectrum_high + spectrum_low) / 2.0
    radius = (spectrum_high - spectrum_low) / 2.0
    sigma = centre / radius
    size = SWEEPS
    update = [1.0 / centre] + [0.0] * (size - 1)
    smoothed = list(update)
    rho = 1.0 / sigma
    for _ in range(SWEEPS - 1):
        remainder = [-s for s in smoothed]
        remainder[0] += 1.0
        for k in range(size - 1):
            remainder[k + 1] += smoothed[k]
        following = 1.0 / (2.0 * sigma - rho)
        update = [following * rho * u + 2.0 * following / radius * r for u, r in zip(update, remainder)]
        smoothed = [s + u for s, u in zip(smoothed, update)]
        rho = following
    return smoothed


def lane_index():
    return lax.broadcasted_iota(jnp.int32, (SUBS, LANES), 1)


def odd(axis):
    return lax.rem(lax.axis_index(axis), 2) == 1


def pack(planes, start):
    lane = lax.broadcasted_iota(jnp.int32, planes[0].shape, 1)
    packed = [None] * (-(-len(planes) // SLOTS))
    for p, plane in enumerate(planes):
        slot = p % SLOTS
        by = (slot * SLOT - start) % LANES
        moved = pltpu.roll(plane, by, 1) if by else plane
        k = p // SLOTS
        packed[k] = moved if slot == 0 else jnp.where(lane < slot * SLOT, packed[k], moved)
    return packed


def own_kernel(
    offsets_hbm, src_hbm, weight_hbm, seam_right_hbm, seam_down_hbm,
    own_ref, first_rows_ref, second_rows_ref, first_cols_ref, second_cols_ref,
    offsets_ref, src_ref, weight_ref, seam_right_ref, seam_down_ref, sems,
):
    chans, rows, cols = src_ref.shape
    own_tiles = cols // LANES
    moves = [(weight_hbm, weight_ref), (seam_right_hbm, seam_right_ref), (seam_down_hbm, seam_down_ref)]
    moves += [(src_hbm.at[c], src_ref.at[c]) for c in range(chans)] + [(offsets_hbm, offsets_ref)]
    copies = [pltpu.make_async_copy(there, here, sems.at[k]) for k, (there, here) in enumerate(moves)]
    for copy in copies:
        copy.start()
    row = lax.broadcasted_iota(jnp.int32, (rows, LANES), 0)
    lane = lax.broadcasted_iota(jnp.int32, (rows, LANES), 1)
    sub = lax.broadcasted_iota(jnp.int32, (SUBS, LANES), 0)
    row_at, col_at = lax.axis_index("row"), lax.axis_index("col")
    last_row = jnp.where(row_at == lax.axis_size("row") - 1, rows - 1, -1)
    last_lane = jnp.where(col_at == lax.axis_size("col") - 1, LANES - 1, -1)
    tile_row, tile_at = lax.div(row_at * rows, TILE), col_at * (cols // TILE)
    odd_row, odd_col = odd("row"), odd("col")

    def tile(ref, j):
        return ref[:, j * LANES:(j + 1) * LANES]

    copies[0].wait()
    for j in range(own_tiles):
        own_ref[chans, j] = tile(weight_ref, j)
    copies[1].wait()
    for j in range(own_tiles):
        value = 1.0 - seam_damping * tile(seam_right_ref, j).astype(jnp.float32)
        own_ref[chans + 1, j] = jnp.where(lane == last_lane, 0.0, value) if j == own_tiles - 1 else value
    copies[2].wait()
    for j in range(own_tiles):
        value = 1.0 - seam_damping * tile(seam_down_ref, j).astype(jnp.float32)
        own_ref[chans + 2, j] = jnp.where(row == last_row, 0.0, value)
    copies[-1].wait()
    for c in range(chans):
        shift = [
            jnp.broadcast_to(offsets_ref[c, tile_row, tile_at + k], (rows, LANES)).astype(jnp.float32) / offset_unit
            for k in range(cols // TILE)
        ]
        copies[3 + c].wait()
        for j in range(own_tiles):
            own_ref[c, j] = tile(src_ref.at[c], j) + shift[j * LANES // TILE]

    planes = range(chans + 3)

    def low_rows(ref):
        for p in planes:
            ref[p] = own_ref[p, :, 0:HALO, :]

    def high_rows(ref):
        at = rows - HALO
        for p in planes:
            ref[p] = own_ref[p, :, at:rows, :]
        for j in range(own_tiles):
            above = jnp.where(sub == 0, own_ref[chans + 2, j, at - 1:at, :], 0.0)
            ref[chans, j, 0:SUBS, :] = own_ref[chans, j, at:at + SUBS, :] + above

    @pl.when(odd_row)
    def _():
        low_rows(first_rows_ref)
        high_rows(second_rows_ref)

    @pl.when(jnp.logical_not(odd_row))
    def _():
        high_rows(first_rows_ref)
        low_rows(second_rows_ref)

    left = pack([own_ref[p, 0] for p in planes], 0)
    right = pack([own_ref[p, own_tiles - 1] for p in planes], LANES - SLOT)
    for k, (a, b) in enumerate(zip(left, right)):
        first_cols_ref[k] = jnp.where(odd_col, a, b)
        second_cols_ref[k] = jnp.where(odd_col, b, a)


def corners_kernel(chans, first_ref, second_ref, first_out, second_out):
    rows = first_ref.shape[1]
    odd_row, odd_col = odd("row"), odd("col")
    sub = lax.broadcasted_iota(jnp.int32, (SUBS, LANES), 0)
    lane = lane_index()
    weight, down = chans, chans + 2
    slot = weight % SLOTS
    at = rows - HALO
    for side, (in_odd, in_even) in enumerate(((first_ref, second_ref), (second_ref, first_ref))):

        def tile(k, low, count=SUBS, in_odd=in_odd, in_even=in_even):
            return jnp.where(odd_col, in_odd[k, low:low + count, :], in_even[k, low:low + count, :])

        above = jnp.broadcast_to(tile(down // SLOTS, at - 1, 1), (SUBS, LANES))
        above = pltpu.roll(above, (slot - down % SLOTS) % SLOTS * SLOT, 1)
        own_slot = jnp.logical_and(lane >= slot * SLOT, lane < (slot + 1) * SLOT)
        above = jnp.where(jnp.logical_and(sub == 0, own_slot), above, 0.0)
        for k in range(first_ref.shape[0]):
            for low in range(0, HALO, SUBS):
                near = tile(k, low)
                far = tile(k, at + low)
                if low == 0 and k == weight // SLOTS:
                    far = far + above
                first_out[side, k, low:low + SUBS, :] = jnp.where(odd_row, near, far)
                second_out[side, k, low:low + SUBS, :] = jnp.where(odd_row, far, near)


def unpack(p, lefts, rights):
    lane = lax.broadcasted_iota(jnp.int32, lefts.shape, 1)
    slot = p % SLOTS
    if slot != SLOTS - 1:
        lefts = pltpu.roll(lefts, LANES - SLOT - slot * SLOT, 1)
    if slot:
        rights = pltpu.roll(rights, LANES - slot * SLOT, 1)
    return jnp.where(lane < SLOT, rights, jnp.where(lane >= LANES - SLOT, lefts, 0.0))


def ways_of(tiles):
    return WAYS if tiles % WAYS == 0 else 1


def split(value, count):
    parts = []
    for k in range(count):
        part = value.astype(jnp.bfloat16)
        parts.append(part)
        if k + 1 < count:
            value = value - part.astype(jnp.float32)
    return jnp.concatenate(parts, axis=0)


def permuted(value, index, count):
    rows = value.shape[0]
    out = jnp.dot(split(value, count), index, preferred_element_type=jnp.float32)
    total = out[:rows]
    for k in range(1, count):
        total = total + out[k * rows:(k + 1) * rows]
    return total


def dealing(ways):
    size = ways * LANES
    column = lax.broadcasted_iota(jnp.int32, (size, size), 0)
    place = lax.broadcasted_iota(jnp.int32, (size, size), 1)
    return jnp.where(column == ways * (place % LANES) + place // LANES, 1.0, 0.0).astype(jnp.bfloat16)


def undealing(ways):
    size = ways * LANES
    column = lax.broadcasted_iota(jnp.int32, (size, size), 1)
    place = lax.broadcasted_iota(jnp.int32, (size, size), 0)
    return jnp.where(column == ways * (place % LANES) + place // LANES, 1.0, 0.0).astype(jnp.bfloat16)


def deal(tile_of, low, high, ways, emit):
    matrix = dealing(ways) if ways > 1 else None
    for g in range(low, high, ways):
        if ways == 1:
            emit(g, tile_of(g))
            continue
        value = permuted(jnp.concatenate([tile_of(g + m) for m in range(ways)], axis=1), matrix, 3)
        for m in range(ways):
            emit(g + m, value[:, m * LANES:(m + 1) * LANES])


def inner_dealt_kernel(own_ref, dealt_ref):
    planes, own_tiles, rows = own_ref.shape[:3]

    def emit(j, value):
        dealt_ref[:, j] = value.reshape(planes, rows, LANES)

    deal(lambda j: own_ref[:, j].reshape(planes * rows, LANES), 0, dealt_ref.shape[1], ways_of(own_tiles + 1), emit)


def outer_dealt_kernel(own_ref, first_ref, second_ref, dealt_ref):
    planes, own_tiles, rows = own_ref.shape[:3]
    tiles = own_tiles + 1
    low = tiles - dealt_ref.shape[1]
    odd_col = odd("col")

    def tile_of(j):
        if j < own_tiles:
            return own_ref[:, j].reshape(planes * rows, LANES)
        parts = []
        for p in range(planes):
            first, second = first_ref[p // SLOTS], second_ref[p // SLOTS]
            parts.append(unpack(p, jnp.where(odd_col, first, second), jnp.where(odd_col, second, first)))
        return jnp.concatenate(parts, axis=0)

    def emit(j, value):
        dealt_ref[:, j - low] = value.reshape(planes, rows, LANES)

    deal(tile_of, low, tiles, ways_of(tiles), emit)


def rightward(values):
    tiles = len(values)
    ways = ways_of(tiles)
    last = lane_index() == LANES - 1
    ahead = {g: pltpu.roll(values[g], LANES - 1, 1) for g in range(0, tiles, ways)}
    out = []
    for j in range(tiles):
        if j % ways + 1 < ways:
            out.append(values[j + 1])
        else:
            g = j - ways + 1
            out.append(jnp.where(last, ahead[(g + ways) % tiles], ahead[g]))
    return out


def leftward(values):
    tiles = len(values)
    ways = ways_of(tiles)
    first = lane_index() == 0
    behind = {g: pltpu.roll(values[g + ways - 1], 1, 1) for g in range(0, tiles, ways)}
    out = []
    for j in range(tiles):
        if j % ways:
            out.append(values[j - 1])
        else:
            out.append(jnp.where(first, behind[(j - ways) % tiles], behind[j]))
    return out


def spread(b_right_ref, b_down_ref, z_ref, emit):
    tiles, height = z_ref.shape[:2]
    steps = height // SUBS
    ways = ways_of(tiles)
    lane = lane_index()
    first, last = (lane == 0, lane == LANES - 1)

    def at(i):
        return pl.ds(i * SUBS, SUBS)

    from_above = [pltpu.roll(b_down_ref[j, at(steps - 1), :] * z_ref[j, at(steps - 1), :], 1, 0) for j in range(tiles)]
    centre = [z_ref[j, at(0), :] for j in range(tiles)]
    wrapped = [pltpu.roll(v, SUBS - 1, 0) for v in centre]
    for i in range(steps):
        pushed_out = {
            g: pltpu.roll(b_right_ref[g + ways - 1, at(i), :] * centre[g + ways - 1], 1, 1)
            for g in range(0, tiles, ways)
        }
        ahead = {g: pltpu.roll(centre[g], LANES - 1, 1) for g in range(0, tiles, ways)}
        pushed = None
        below = []
        for j in range(tiles):
            g = j // ways * ways
            b_right = b_right_ref[j, at(i), :]
            b_down = b_down_ref[j, at(i), :]
            below.append(z_ref[j, at(i + 1), :] if i + 1 < steps else wrapped[j])
            if j == g:
                from_left = jnp.where(first, pushed_out[(g - ways) % tiles], pushed_out[g])
            else:
                from_left = pushed
            if j + 1 < g + ways:
                to_right = centre[j + 1]
                pushed = b_right * centre[j]
            else:
                to_right = jnp.where(last, ahead[(g + ways) % tiles], ahead[g])
            moved = (b_right * to_right + from_left) + (b_down * below[j] + from_above[j])
            from_above[j] = b_down * centre[j]
            emit(i, j, centre[j], moved)
        centre = below


def precondition(b_right_ref, b_down_ref, g_ref, z_ref, work_ref):
    poly = chebyshev_polynomial()
    degree = SWEEPS - 1

    def at(i):
        return pl.ds(i * SUBS, SUBS)

    def first(i, j, centre, moved):
        z_ref[j, at(i), :] = poly[degree] * moved + poly[degree - 1] * centre

    spread(b_right_ref, b_down_ref, g_ref, first)

    def pair(k, carry):
        adds = []
        for half in range(2):
            value = jnp.float32(poly[half])
            for later in range(1, (degree - 1) // 2):
                value = jnp.where(k == (degree - 1) // 2 - 1 - later, jnp.float32(poly[2 * later + half]), value)
            adds.append(value)

        def one(target, add):
            def emit(i, j, centre, moved):
                target[j, at(i), :] = moved + add * g_ref[j, at(i), :]

            return emit

        spread(b_right_ref, b_down_ref, z_ref, one(work_ref, adds[1]))
        spread(b_right_ref, b_down_ref, work_ref, one(z_ref, adds[0]))
        return carry

    lax.fori_loop(0, (degree - 1) // 2, pair, 0)


def next_residual(b_right_ref, b_down_ref, g_ref, z_ref, next_ref, own_of):
    height = g_ref.shape[1]
    steps = height // SUBS
    sums = {}

    def emit(i, j, centre, moved):
        at = pl.ds(i * SUBS, SUBS)
        g = g_ref[j, at, :]
        following = g - MIX * (centre - moved)
        next_ref[j, at, :] = following
        key = own_of(i, j)
        now = (g * centre, following * centre)
        before = sums.get(key)
        sums[key] = now if before is None else (before[0] + now[0], before[1] + now[1])

    spread(b_right_ref, b_down_ref, z_ref, emit)
    sub = lax.broadcasted_iota(jnp.int32, (SUBS, LANES), 0)
    lane = lane_index()
    total = [jnp.zeros((SUBS, LANES), jnp.float32)] * 2
    for (low, high, lanes), parts in sums.items():
        inside = jnp.logical_and(jnp.logical_and(sub >= low, sub <= high), lane < lanes)
        total = [t + jnp.where(inside, p, 0.0) for t, p in zip(total, parts)]
    return total


def first_kernel(
    inner_ref, outer_ref, first_rows_ref, second_rows_ref, first_corners_ref, second_corners_ref,
    b_right_ref, b_down_ref, scale_ref, root_ref, g0_ref, z0_ref, g1_ref, f1_ref, g2_ref, sums_ref,
    first_late_ref, second_late_ref,
    natural, work_ref,
):
    planes, inner, rows = inner_ref.shape[:3]
    tiles = inner + outer_ref.shape[1]
    chans = planes - 3
    own_tiles = tiles - 1
    height = rows + 2 * HALO
    steps = height // SUBS

    for p in range(planes):
        for j in range(tiles):
            natural[p, j, HALO:HALO + rows, :] = inner_ref[p, j] if j < inner else outer_ref[p, j - inner]
    odd_row = odd("row")

    def edge_tile(j):
        if j < own_tiles:
            first, second = [ref[:, j].reshape(planes * HALO, LANES) for ref in (first_rows_ref, second_rows_ref)]
        else:
            first, second = [
                jnp.concatenate([unpack(p, ref[0, p // SLOTS], ref[1, p // SLOTS]) for p in range(planes)], axis=0)
                for ref in (first_corners_ref, second_corners_ref)
            ]
        return jnp.concatenate([jnp.where(odd_row, first, second), jnp.where(odd_row, second, first)], axis=0)

    def put_edge(j, value):
        value = value.reshape(2, planes, HALO, LANES)
        natural[:, j, 0:HALO, :] = value[0]
        natural[:, j, HALO + rows:height, :] = value[1]

    deal(edge_tile, 0, tiles, ways_of(tiles), put_edge)

    def at(i):
        return pl.ds(i * SUBS, SUBS)

    def interleaved(p, i, j):
        return natural[p, j, pl.ds(i, SUBS, stride=steps), :]

    sub = lax.broadcasted_iota(jnp.int32, (SUBS, LANES), 0)
    to_up = [
        jnp.where(sub == 0, 0.0, pltpu.roll(interleaved(chans + 2, steps - 1, j), 1, 0)) for j in range(tiles)
    ]
    for i in range(steps):
        to_right = [interleaved(chans + 1, i, j) for j in range(tiles)]
        to_left = leftward(to_right)
        for j in range(tiles):
            to_down = interleaved(chans + 2, i, j)
            diag = interleaved(chans, i, j) + to_right[j] + to_left[j] + to_down + to_up[j]
            inside = diag > 0.0
            safe = jnp.where(inside, diag, 1.0)
            guess = lax.rsqrt(safe)
            scale = guess * (1.5 - 0.5 * safe * guess * guess)
            scale_ref[j, at(i), :] = jnp.where(inside, scale, 0.0)
            root_ref[j, at(i), :] = safe * scale
            to_up[j] = to_down
    wrapped = [pltpu.roll(scale_ref[j, at(0), :], SUBS - 1, 0) for j in range(tiles)]
    for i in range(steps):
        scale = [scale_ref[j, at(i), :] for j in range(tiles)]
        right_scale = rightward(scale)
        for j in range(tiles):
            b_right_ref[j, at(i), :] = interleaved(chans + 1, i, j) * scale[j] * right_scale[j]
            down_scale = scale_ref[j, at(i + 1), :] if i + 1 < steps else wrapped[j]
            b_down_ref[j, at(i), :] = interleaved(chans + 2, i, j) * scale[j] * down_scale
            for c in range(chans):
                g0_ref[c, j, at(i), :] = interleaved(c, i, j) * scale[j]

    ways = ways_of(tiles)

    def own_of(i, j):
        low, high = -(-(HALO - i) // steps), (HALO + rows - 1 - i) // steps
        left = own_tiles * LANES - j // ways * ways * LANES - j % ways
        return low, high, min(LANES, max(0, -(-left // ways)))

    def channel(c, carry):
        g0, z0, g1, f1, g2 = [ref.at[c] for ref in (g0_ref, z0_ref, g1_ref, f1_ref, g2_ref)]
        precondition(b_right_ref, b_down_ref, g0, z0, work_ref)
        sum0, sum1 = next_residual(b_right_ref, b_down_ref, g0, z0, g1, own_of)
        precondition(b_right_ref, b_down_ref, g1, f1, work_ref)
        sum2, sum3 = next_residual(b_right_ref, b_down_ref, g1, f1, g2, own_of)
        return tuple(a + b for a, b in zip(carry, (sum0, sum1, sum2, sum3)))

    zero = jnp.zeros((SUBS, LANES), jnp.float32)
    parts = lax.fori_loop(0, chans, channel, (zero,) * 4)
    sums = zero
    for k, part in enumerate(parts):
        sums = jnp.where(sub == k, jnp.sum(part), sums)
    sums_ref[...] = sums
    first_late_ref[chans * tiles] = sums

    def edge(c, j, at):
        s, i = divmod(HALO + at, steps)
        return g2_ref[c, j, pl.ds(i * SUBS + s, LATE, stride=SUBS), :]

    for c in range(chans):
        for j in range(tiles):
            low, high = edge(c, j, 0), edge(c, j, rows - LATE)
            first_late_ref[c * tiles + j] = jnp.where(odd_row, low, high)
            second_late_ref[c * tiles + j] = jnp.where(odd_row, high, low)


def second_kernel(
    c, first_late_ref, second_late_ref, b_right_ref, b_down_ref, g2_ref, f2_ref, g_ref, work_ref
):
    tiles, height = b_right_ref.shape[:2]
    rows = height - 2 * HALO
    steps = height // SUBS
    odd_row = odd("row")
    for j in range(tiles):
        g_ref[j] = g2_ref[c, j]
        first, second = first_late_ref[c * tiles + j], second_late_ref[c * tiles + j]
        for value, at in ((jnp.where(odd_row, first, second), HALO - LATE), (jnp.where(odd_row, second, first), HALO + rows)):
            done = 0
            while done < LATE:
                s, i = divmod(at + done, steps)
                count = min(LATE - done, steps - i)
                g_ref[j, pl.ds(i * SUBS + s, count, stride=SUBS), :] = value[done:done + count]
                done += count
    precondition(b_right_ref, b_down_ref, g_ref, f2_ref, work_ref)


def combine(n0, n1, n2, n3):
    gap = n0 - n1
    keep = -n1 / gap
    step = n0 / gap
    beta = (n0 * n2 - n1 * n1) / (gap * gap)
    along = keep + beta
    curvature = along * along * gap + 2.0 * along * step * (n1 - n2) + step * step * (n2 - n3)
    scaled = n0 * beta / curvature
    first_size = step * MIX
    second_size = scaled * MIX
    x0 = first_size + second_size * along
    x1 = second_size * step
    r0 = keep - scaled * along
    r1 = step + scaled * (along - step)
    r2 = scaled * step
    return x0, x1, r0, r1, r2


def third_kernel(
    sums_ref, scale_ref, root_ref, g0_ref, z0_ref, g1_ref, f1_ref, g2_ref, *refs
):
    *f2_refs, solution_hbm, residual_hbm, smoothed_hbm, natural, done, sems = refs
    rows, cols = solution_hbm.shape[1:]
    own_tiles = cols // LANES
    tiles, height = scale_ref.shape[:2]
    steps = height // SUBS
    ways = ways_of(tiles)
    x0, x1, r0, r1, r2 = combine(*[jnp.broadcast_to(sums_ref[k:k + 1, :], (SUBS, LANES)) for k in range(4)])
    matrix = undealing(ways) if ways > 1 else None
    outs = (solution_hbm, residual_hbm, smoothed_hbm)
    copies = []
    for c, f2_ref in enumerate(f2_refs):
        for j in range(tiles):
            for i in range(steps):
                at = pl.ds(i * SUBS, SUBS)
                scale = scale_ref[j, at, :]
                root = root_ref[j, at, :]
                g0, g1, g2, z0, f1 = [ref[c, j, at, :] for ref in (g0_ref, g1_ref, g2_ref, z0_ref, f1_ref)]
                f2 = f2_ref[j, at, :]
                there = pl.ds(i, SUBS, stride=steps)
                natural[c, 0, j, there, :] = scale * (x0 * z0 + x1 * f1)
                natural[c, 1, j, there, :] = root * (r0 * g0 + r1 * g1 + r2 * g2)
                natural[c, 2, j, there, :] = scale * (r0 * z0 + r1 * f1 + r2 * f2)
        for g in range(0, own_tiles, ways):
            value = jnp.concatenate(
                [natural[c, :, g + m, HALO:HALO + rows, :].reshape(3 * rows, LANES) for m in range(ways)], axis=1
            )
            width = min(ways, own_tiles - g) * LANES
            if ways > 1:
                value = permuted(value, matrix[:, :width], 2)
            for k in range(len(outs)):
                done[c, k, :, g * LANES:g * LANES + width] = value[k * rows:(k + 1) * rows]
        for k, ref in enumerate(outs):
            copies.append(pltpu.make_async_copy(done.at[c, k], ref.at[c], sems.at[c, k]))
            copies[-1].start()
    for copy in copies:
        copy.wait()


def sum_over(value, steps, beside):
    done = []
    for k, (axis, pairs) in enumerate(steps):
        other = lax.ppermute(value, axis, pairs)
        if len(steps) - k <= len(beside):
            value, array = lax.optimization_barrier((value, beside[len(done)]))
            done.append(array)
        value = value + other
    return value, done + list(beside[len(done):])


def per_device(source, weight, seam_right, seam_down, offsets):
    chans, rows, cols = source.shape
    row_axis, col_axis = lax.axis_size("row"), lax.axis_size("col")
    in_vmem = pl.BlockSpec(memory_space=pltpu.VMEM)
    in_hbm = pl.BlockSpec(memory_space=pltpu.HBM)
    params = pltpu.CompilerParams(vmem_limit_bytes=VMEM_LIMIT)

    def shaped(*shape):
        return jax.ShapeDtypeStruct(shape, jnp.float32)

    def scratch(*shape):
        return pltpu.VMEM(shape, jnp.float32)

    planes = chans + 3
    own_tiles = cols // LANES
    tiles = own_tiles + 1
    packs = -(-planes // SLOTS)
    own, first_rows, second_rows, first_cols, second_cols = pl.pallas_call(
        own_kernel,
        out_shape=[shaped(planes, own_tiles, rows, LANES)]
        + [shaped(planes, own_tiles, HALO, LANES)] * 2
        + [shaped(packs, rows, LANES)] * 2,
        in_specs=[in_hbm] * 5,
        out_specs=[in_vmem] * 5,
        scratch_shapes=[
            pltpu.SMEM((chans,) + offsets.shape[:2], jnp.int32),
            scratch(*source.shape),
            scratch(*weight.shape),
            pltpu.VMEM(weight.shape, jnp.int32),
            pltpu.VMEM(weight.shape, jnp.int32),
            pltpu.SemaphoreType.DMA((planes + 1,)),
        ],
        compiler_params=params,
    )(
        *[
            pltpu.with_memory_space_constraint(v, pltpu.HBM)
            for v in (offsets.transpose(2, 0, 1), source, weight, seam_right, seam_down)
        ],
    )

    def swap(first, second, axis):
        size = lax.axis_size(axis)
        pairs = [[(i, i + 1) for i in range(start, size - 1, 2)] for start in range(2)]
        pairs = [some + [(j, i) for i, j in some] for some in pairs]
        return [lax.ppermute(value, axis, some) for value, some in zip((first, second), pairs)]

    ways = ways_of(tiles)
    inner = pl.pallas_call(
        inner_dealt_kernel,
        out_shape=shaped(planes, tiles - ways, rows, LANES),
        in_specs=[in_vmem],
        out_specs=in_vmem,
        compiler_params=params,
        cost_estimate=pl.CostEstimate(flops=10**8, bytes_accessed=4 * 10**6, transcendentals=0),
    )(own)
    first_rows, second_rows = swap(first_rows, second_rows, "row")
    first_cols, second_cols = swap(first_cols, second_cols, "col")
    first_cols, second_cols, inner = lax.optimization_barrier((first_cols, second_cols, inner))
    corners = pl.pallas_call(
        functools.partial(corners_kernel, chans),
        out_shape=[shaped(2, packs, HALO, LANES)] * 2,
        in_specs=[in_vmem] * 2,
        out_specs=[in_vmem] * 2,
        compiler_params=params,
    )(first_cols, second_cols)
    first_corners, second_corners = swap(*corners, "row")
    outer = pl.pallas_call(
        outer_dealt_kernel,
        out_shape=shaped(planes, ways, rows, LANES),
        in_specs=[in_vmem] * 3,
        out_specs=in_vmem,
        compiler_params=params,
        cost_estimate=pl.CostEstimate(flops=10**8, bytes_accessed=2 * 10**6, transcendentals=0),
    )(own, first_cols, second_cols)

    height = rows + 2 * HALO
    plane = shaped(tiles, height, LANES)
    field = shaped(chans, tiles, height, LANES)
    lates = [shaped(chans * tiles + extra, LATE, LANES) for extra in (1, 0)]
    *basis, sums, first_late, second_late = pl.pallas_call(
        first_kernel,
        out_shape=[plane] * 4 + [field] * 5 + [shaped(SUBS, LANES)] + lates,
        in_specs=[in_vmem] * 6,
        out_specs=[in_vmem] * 12,
        scratch_shapes=[scratch(planes, tiles, height, LANES), scratch(*plane.shape)],
        compiler_params=params,
    )(inner, outer, first_rows, second_rows, first_corners, second_corners)

    first_late, second_late = swap(first_late, second_late, "row")

    b_right, b_down, scale, root, g0, z0, g1, f1, g2 = basis
    f2 = [
        pl.pallas_call(
            functools.partial(second_kernel, c),
            out_shape=plane,
            in_specs=[in_vmem] * 5,
            out_specs=in_vmem,
            scratch_shapes=[scratch(*plane.shape)] * 2,
            compiler_params=params,
            cost_estimate=pl.CostEstimate(flops=10**8, bytes_accessed=10**7, transcendentals=0),
        )(first_late, second_late, b_right, b_down, g2)
        for c in range(chans)
    ]
    if row_axis & (row_axis - 1) or col_axis & (col_axis - 1):
        total = lax.psum(sums, ("row", "col"))
    else:
        steps = [
            (axis, [(i, i ^ (1 << k)) for i in range(size)])
            for axis, size, low in (("row", row_axis, 1), ("col", col_axis, 0))
            for k in range(low, size.bit_length() - 1)
        ]
        if row_axis > 1:
            sums = sums + first_late[chans * tiles]
        total, f2 = sum_over(sums, steps, f2)
    return pl.pallas_call(
        third_kernel,
        out_shape=[shaped(chans, rows, cols)] * 3,
        in_specs=[in_vmem] * (8 + chans),
        out_specs=[pl.BlockSpec(memory_space=pltpu.HBM)] * 3,
        scratch_shapes=[
            scratch(chans, 3, tiles, height, LANES),
            scratch(chans, 3, rows, cols),
            pltpu.SemaphoreType.DMA((chans, 3)),
        ],
        compiler_params=params,
    )(total, scale, root, g0, z0, g1, f1, g2, *f2)


def solution(mesh):
    placed = (
        P(None, ("band", "row"), "col"),
        P(("band", "row"), "col"),
        P(("band", "row"), "col"),
        P(("band", "row"), "col"),
        P("band", None, None),
    )
    return jax.shard_map(
        per_device,
        mesh=mesh,
        in_specs=placed,
        out_specs=(
            P(None, ("band", "row"), "col"),
            P(None, ("band", "row"), "col"),
            P(None, ("band", "row"), "col"),
        ),
        check_vma=False,
    )
```

```python
import functools

import jax
import jax.numpy as jnp
from jax import lax
from jax.experimental import pallas as pl
from jax.experimental.pallas import tpu as pltpu
from jax.sharding import PartitionSpec as P

TILE = 256
SWEEPS = 8
SUBS = 8
LANES = 128
HALO = 16
LATE = 8
SLOT = 32
SLOTS = LANES // SLOT
WAYS = 3

seam_damping = 0.8
offset_unit = 32.0
spectrum_low = 0.08
spectrum_high = 2.0
MIX = 2.4

VMEM_LIMIT = 28 * 1024 * 1024


def chebyshev_polynomial():
    centre = (spectrum_high + spectrum_low) / 2.0
    radius = (spectrum_high - spectrum_low) / 2.0
    sigma = centre / radius
    size = SWEEPS
    update = [1.0 / centre] + [0.0] * (size - 1)
    smoothed = list(update)
    rho = 1.0 / sigma
    for _ in range(SWEEPS - 1):
        remainder = [-s for s in smoothed]
        remainder[0] += 1.0
        for k in range(size - 1):
            remainder[k + 1] += smoothed[k]
        following = 1.0 / (2.0 * sigma - rho)
        update = [following * rho * u + 2.0 * following / radius * r for u, r in zip(update, remainder)]
        smoothed = [s + u for s, u in zip(smoothed, update)]
        rho = following
    return smoothed


def lane_index():
    return lax.broadcasted_iota(jnp.int32, (SUBS, LANES), 1)


def odd(axis):
    return lax.rem(lax.axis_index(axis), 2) == 1


def pack(planes, start):
    lane = lax.broadcasted_iota(jnp.int32, planes[0].shape, 1)
    packed = [None] * (-(-len(planes) // SLOTS))
    for p, plane in enumerate(planes):
        slot = p % SLOTS
        by = (slot * SLOT - start) % LANES
        moved = pltpu.roll(plane, by, 1) if by else plane
        k = p // SLOTS
        packed[k] = moved if slot == 0 else jnp.where(lane < slot * SLOT, packed[k], moved)
    return packed


def own_kernel(
    offsets_hbm, src_hbm, weight_hbm, seam_right_hbm, seam_down_hbm,
    own_ref, first_rows_ref, second_rows_ref, first_cols_ref, second_cols_ref,
    offsets_ref, src_ref, weight_ref, seam_right_ref, seam_down_ref, sems,
):
    chans, rows, cols = src_ref.shape
    own_tiles = cols // LANES
    moves = [(weight_hbm, weight_ref), (seam_right_hbm, seam_right_ref), (seam_down_hbm, seam_down_ref)]
    moves += [(src_hbm.at[c], src_ref.at[c]) for c in range(chans)] + [(offsets_hbm, offsets_ref)]
    copies = [pltpu.make_async_copy(there, here, sems.at[k]) for k, (there, here) in enumerate(moves)]
    for copy in copies:
        copy.start()
    row = lax.broadcasted_iota(jnp.int32, (rows, LANES), 0)
    lane = lax.broadcasted_iota(jnp.int32, (rows, LANES), 1)
    sub = lax.broadcasted_iota(jnp.int32, (SUBS, LANES), 0)
    row_at, col_at = lax.axis_index("row"), lax.axis_index("col")
    last_row = jnp.where(row_at == lax.axis_size("row") - 1, rows - 1, -1)
    last_lane = jnp.where(col_at == lax.axis_size("col") - 1, LANES - 1, -1)
    tile_row, tile_at = lax.div(row_at * rows, TILE), col_at * (cols // TILE)
    odd_row, odd_col = odd("row"), odd("col")

    def tile(ref, j):
        return ref[:, j * LANES:(j + 1) * LANES]

    copies[0].wait()
    for j in range(own_tiles):
        own_ref[chans, j] = tile(weight_ref, j)
    copies[1].wait()
    for j in range(own_tiles):
        value = 1.0 - seam_damping * tile(seam_right_ref, j).astype(jnp.float32)
        own_ref[chans + 1, j] = jnp.where(lane == last_lane, 0.0, value) if j == own_tiles - 1 else value
    copies[2].wait()
    for j in range(own_tiles):
        value = 1.0 - seam_damping * tile(seam_down_ref, j).astype(jnp.float32)
        own_ref[chans + 2, j] = jnp.where(row == last_row, 0.0, value)
    copies[-1].wait()
    for c in range(chans):
        shift = [
            jnp.broadcast_to(offsets_ref[c, tile_row, tile_at + k], (rows, LANES)).astype(jnp.float32) / offset_unit
            for k in range(cols // TILE)
        ]
        copies[3 + c].wait()
        for j in range(own_tiles):
            own_ref[c, j] = tile(src_ref.at[c], j) + shift[j * LANES // TILE]

    planes = range(chans + 3)

    def low_rows(ref):
        for p in planes:
            ref[p] = own_ref[p, :, 0:HALO, :]

    def high_rows(ref):
        at = rows - HALO
        for p in planes:
            ref[p] = own_ref[p, :, at:rows, :]
        for j in range(own_tiles):
            above = jnp.where(sub == 0, own_ref[chans + 2, j, at - 1:at, :], 0.0)
            ref[chans, j, 0:SUBS, :] = own_ref[chans, j, at:at + SUBS, :] + above

    @pl.when(odd_row)
    def _():
        low_rows(first_rows_ref)
        high_rows(second_rows_ref)

    @pl.when(jnp.logical_not(odd_row))
    def _():
        high_rows(first_rows_ref)
        low_rows(second_rows_ref)

    left = pack([own_ref[p, 0] for p in planes], 0)
    right = pack([own_ref[p, own_tiles - 1] for p in planes], LANES - SLOT)
    for k, (a, b) in enumerate(zip(left, right)):
        first_cols_ref[k] = jnp.where(odd_col, a, b)
        second_cols_ref[k] = jnp.where(odd_col, b, a)


def corners_kernel(chans, first_ref, second_ref, first_out, second_out):
    rows = first_ref.shape[1]
    odd_row, odd_col = odd("row"), odd("col")
    sub = lax.broadcasted_iota(jnp.int32, (SUBS, LANES), 0)
    lane = lane_index()
    weight, down = chans, chans + 2
    slot = weight % SLOTS
    at = rows - HALO
    for side, (in_odd, in_even) in enumerate(((first_ref, second_ref), (second_ref, first_ref))):

        def tile(k, low, count=SUBS, in_odd=in_odd, in_even=in_even):
            return jnp.where(odd_col, in_odd[k, low:low + count, :], in_even[k, low:low + count, :])

        above = jnp.broadcast_to(tile(down // SLOTS, at - 1, 1), (SUBS, LANES))
        above = pltpu.roll(above, (slot - down % SLOTS) % SLOTS * SLOT, 1)
        own_slot = jnp.logical_and(lane >= slot * SLOT, lane < (slot + 1) * SLOT)
        above = jnp.where(jnp.logical_and(sub == 0, own_slot), above, 0.0)
        for k in range(first_ref.shape[0]):
            for low in range(0, HALO, SUBS):
                near = tile(k, low)
                far = tile(k, at + low)
                if low == 0 and k == weight // SLOTS:
                    far = far + above
                first_out[side, k, low:low + SUBS, :] = jnp.where(odd_row, near, far)
                second_out[side, k, low:low + SUBS, :] = jnp.where(odd_row, far, near)


def unpack(p, lefts, rights):
    lane = lax.broadcasted_iota(jnp.int32, lefts.shape, 1)
    slot = p % SLOTS
    if slot != SLOTS - 1:
        lefts = pltpu.roll(lefts, LANES - SLOT - slot * SLOT, 1)
    if slot:
        rights = pltpu.roll(rights, LANES - slot * SLOT, 1)
    return jnp.where(lane < SLOT, rights, jnp.where(lane >= LANES - SLOT, lefts, 0.0))


def ways_of(tiles):
    return WAYS if tiles % WAYS == 0 else 1


def split(value, count):
    parts = []
    for k in range(count):
        part = value.astype(jnp.bfloat16)
        parts.append(part)
        if k + 1 < count:
            value = value - part.astype(jnp.float32)
    return jnp.concatenate(parts, axis=0)


def permuted(value, index, count):
    rows = value.shape[0]
    out = jnp.dot(split(value, count), index, preferred_element_type=jnp.float32)
    total = out[:rows]
    for k in range(1, count):
        total = total + out[k * rows:(k + 1) * rows]
    return total


def dealing(ways):
    size = ways * LANES
    column = lax.broadcasted_iota(jnp.int32, (size, size), 0)
    place = lax.broadcasted_iota(jnp.int32, (size, size), 1)
    return jnp.where(column == ways * (place % LANES) + place // LANES, 1.0, 0.0).astype(jnp.bfloat16)


def undealing(ways):
    size = ways * LANES
    column = lax.broadcasted_iota(jnp.int32, (size, size), 1)
    place = lax.broadcasted_iota(jnp.int32, (size, size), 0)
    return jnp.where(column == ways * (place % LANES) + place // LANES, 1.0, 0.0).astype(jnp.bfloat16)


def deal(tile_of, low, high, ways, emit):
    matrix = dealing(ways) if ways > 1 else None
    for g in range(low, high, ways):
        if ways == 1:
            emit(g, tile_of(g))
            continue
        value = permuted(jnp.concatenate([tile_of(g + m) for m in range(ways)], axis=1), matrix, 3)
        for m in range(ways):
            emit(g + m, value[:, m * LANES:(m + 1) * LANES])


def inner_dealt_kernel(own_ref, dealt_ref):
    planes, own_tiles, rows = own_ref.shape[:3]

    def emit(j, value):
        dealt_ref[:, j] = value.reshape(planes, rows, LANES)

    deal(lambda j: own_ref[:, j].reshape(planes * rows, LANES), 0, dealt_ref.shape[1], ways_of(own_tiles + 1), emit)


def outer_dealt_kernel(own_ref, first_ref, second_ref, dealt_ref):
    planes, own_tiles, rows = own_ref.shape[:3]
    tiles = own_tiles + 1
    low = tiles - dealt_ref.shape[1]
    odd_col = odd("col")

    def tile_of(j):
        if j < own_tiles:
            return own_ref[:, j].reshape(planes * rows, LANES)
        parts = []
        for p in range(planes):
            first, second = first_ref[p // SLOTS], second_ref[p // SLOTS]
            parts.append(unpack(p, jnp.where(odd_col, first, second), jnp.where(odd_col, second, first)))
        return jnp.concatenate(parts, axis=0)

    def emit(j, value):
        dealt_ref[:, j - low] = value.reshape(planes, rows, LANES)

    deal(tile_of, low, tiles, ways_of(tiles), emit)


def rightward(values):
    tiles = len(values)
    ways = ways_of(tiles)
    last = lane_index() == LANES - 1
    ahead = {g: pltpu.roll(values[g], LANES - 1, 1) for g in range(0, tiles, ways)}
    out = []
    for j in range(tiles):
        if j % ways + 1 < ways:
            out.append(values[j + 1])
        else:
            g = j - ways + 1
            out.append(jnp.where(last, ahead[(g + ways) % tiles], ahead[g]))
    return out


def leftward(values):
    tiles = len(values)
    ways = ways_of(tiles)
    first = lane_index() == 0
    behind = {g: pltpu.roll(values[g + ways - 1], 1, 1) for g in range(0, tiles, ways)}
    out = []
    for j in range(tiles):
        if j % ways:
            out.append(values[j - 1])
        else:
            out.append(jnp.where(first, behind[(j - ways) % tiles], behind[j]))
    return out


def spread(b_right_ref, b_down_ref, z_ref, emit):
    tiles, height = z_ref.shape[:2]
    steps = height // SUBS
    ways = ways_of(tiles)
    lane = lane_index()
    first, last = (lane == 0, lane == LANES - 1)

    def at(i):
        return pl.ds(i * SUBS, SUBS)

    from_above = [pltpu.roll(b_down_ref[j, at(steps - 1), :] * z_ref[j, at(steps - 1), :], 1, 0) for j in range(tiles)]
    centre = [z_ref[j, at(0), :] for j in range(tiles)]
    wrapped = [pltpu.roll(v, SUBS - 1, 0) for v in centre]
    for i in range(steps):
        pushed_out = {
            g: pltpu.roll(b_right_ref[g + ways - 1, at(i), :] * centre[g + ways - 1], 1, 1)
            for g in range(0, tiles, ways)
        }
        ahead = {g: pltpu.roll(centre[g], LANES - 1, 1) for g in range(0, tiles, ways)}
        pushed = None
        below = []
        for j in range(tiles):
            g = j // ways * ways
            b_right = b_right_ref[j, at(i), :]
            b_down = b_down_ref[j, at(i), :]
            below.append(z_ref[j, at(i + 1), :] if i + 1 < steps else wrapped[j])
            if j == g:
                from_left = jnp.where(first, pushed_out[(g - ways) % tiles], pushed_out[g])
            else:
                from_left = pushed
            if j + 1 < g + ways:
                to_right = centre[j + 1]
                pushed = b_right * centre[j]
            else:
                to_right = jnp.where(last, ahead[(g + ways) % tiles], ahead[g])
            moved = (b_right * to_right + from_left) + (b_down * below[j] + from_above[j])
            from_above[j] = b_down * centre[j]
            emit(i, j, centre[j], moved)
        centre = below


def precondition(b_right_ref, b_down_ref, g_ref, z_ref, work_ref):
    poly = chebyshev_polynomial()
    degree = SWEEPS - 1

    def at(i):
        return pl.ds(i * SUBS, SUBS)

    def first(i, j, centre, moved):
        z_ref[j, at(i), :] = poly[degree] * moved + poly[degree - 1] * centre

    spread(b_right_ref, b_down_ref, g_ref, first)

    def pair(k, carry):
        adds = []
        for half in range(2):
            value = jnp.float32(poly[half])
            for later in range(1, (degree - 1) // 2):
                value = jnp.where(k == (degree - 1) // 2 - 1 - later, jnp.float32(poly[2 * later + half]), value)
            adds.append(value)

        def one(target, add):
            def emit(i, j, centre, moved):
                target[j, at(i), :] = moved + add * g_ref[j, at(i), :]

            return emit

        spread(b_right_ref, b_down_ref, z_ref, one(work_ref, adds[1]))
        spread(b_right_ref, b_down_ref, work_ref, one(z_ref, adds[0]))
        return carry

    lax.fori_loop(0, (degree - 1) // 2, pair, 0)


def next_residual(b_right_ref, b_down_ref, g_ref, z_ref, next_ref, own_of):
    height = g_ref.shape[1]
    steps = height // SUBS
    sums = {}

    def emit(i, j, centre, moved):
        at = pl.ds(i * SUBS, SUBS)
        g = g_ref[j, at, :]
        following = g - MIX * (centre - moved)
        next_ref[j, at, :] = following
        key = own_of(i, j)
        now = (g * centre, following * centre)
        before = sums.get(key)
        sums[key] = now if before is None else (before[0] + now[0], before[1] + now[1])

    spread(b_right_ref, b_down_ref, z_ref, emit)
    sub = lax.broadcasted_iota(jnp.int32, (SUBS, LANES), 0)
    lane = lane_index()
    total = [jnp.zeros((SUBS, LANES), jnp.float32)] * 2
    for (low, high, lanes), parts in sums.items():
        inside = jnp.logical_and(jnp.logical_and(sub >= low, sub <= high), lane < lanes)
        total = [t + jnp.where(inside, p, 0.0) for t, p in zip(total, parts)]
    return total


def first_kernel(
    inner_ref, outer_ref, second_rows_ref, first_rows_ref, second_corners_ref, first_corners_ref,
    b_right_ref, b_down_ref, scale_ref, root_ref, g0_ref, z0_ref, g1_ref, f1_ref, g2_ref, sums_ref,
    first_late_ref, second_late_ref,
    natural, work_ref,
):
    planes, inner, rows = inner_ref.shape[:3]
    tiles = inner + outer_ref.shape[1]
    chans = planes - 3
    own_tiles = tiles - 1
    height = rows + 2 * HALO
    steps = height // SUBS

    for p in range(planes):
        for j in range(tiles):
            natural[p, j, HALO:HALO + rows, :] = inner_ref[p, j] if j < inner else outer_ref[p, j - inner]
    odd_row = odd("row")

    def edge_tile(j):
        if j < own_tiles:
            first, second = [ref[:, j].reshape(planes * HALO, LANES) for ref in (first_rows_ref, second_rows_ref)]
        else:
            first, second = [
                jnp.concatenate([unpack(p, ref[0, p // SLOTS], ref[1, p // SLOTS]) for p in range(planes)], axis=0)
                for ref in (first_corners_ref, second_corners_ref)
            ]
        return jnp.concatenate([jnp.where(odd_row, first, second), jnp.where(odd_row, second, first)], axis=0)

    def put_edge(j, value):
        value = value.reshape(2, planes, HALO, LANES)
        natural[:, j, 0:HALO, :] = value[0]
        natural[:, j, HALO + rows:height, :] = value[1]

    deal(edge_tile, 0, tiles, ways_of(tiles), put_edge)

    def at(i):
        return pl.ds(i * SUBS, SUBS)

    def interleaved(p, i, j):
        return natural[p, j, pl.ds(i, SUBS, stride=steps), :]

    sub = lax.broadcasted_iota(jnp.int32, (SUBS, LANES), 0)
    to_up = [
        jnp.where(sub == 0, 0.0, pltpu.roll(interleaved(chans + 2, steps - 1, j), 1, 0)) for j in range(tiles)
    ]
    for i in range(steps):
        to_right = [interleaved(chans + 1, i, j) for j in range(tiles)]
        to_left = leftward(to_right)
        for j in range(tiles):
            to_down = interleaved(chans + 2, i, j)
            diag = interleaved(chans, i, j) + to_right[j] + to_left[j] + to_down + to_up[j]
            inside = diag > 0.0
            safe = jnp.where(inside, diag, 1.0)
            guess = lax.rsqrt(safe)
            scale = guess * (1.5 - 0.5 * safe * guess * guess)
            scale_ref[j, at(i), :] = jnp.where(inside, scale, 0.0)
            root_ref[j, at(i), :] = safe * scale
            to_up[j] = to_down
    wrapped = [pltpu.roll(scale_ref[j, at(0), :], SUBS - 1, 0) for j in range(tiles)]
    for i in range(steps):
        scale = [scale_ref[j, at(i), :] for j in range(tiles)]
        right_scale = rightward(scale)
        for j in range(tiles):
            b_right_ref[j, at(i), :] = interleaved(chans + 1, i, j) * scale[j] * right_scale[j]
            down_scale = scale_ref[j, at(i + 1), :] if i + 1 < steps else wrapped[j]
            b_down_ref[j, at(i), :] = interleaved(chans + 2, i, j) * scale[j] * down_scale
            for c in range(chans):
                g0_ref[c, j, at(i), :] = interleaved(c, i, j) * scale[j]

    ways = ways_of(tiles)

    def own_of(i, j):
        low, high = -(-(HALO - i) // steps), (HALO + rows - 1 - i) // steps
        left = own_tiles * LANES - j // ways * ways * LANES - j % ways
        return low, high, min(LANES, max(0, -(-left // ways)))

    def channel(c, carry):
        g0, z0, g1, f1, g2 = [ref.at[c] for ref in (g0_ref, z0_ref, g1_ref, f1_ref, g2_ref)]
        precondition(b_right_ref, b_down_ref, g0, z0, work_ref)
        sum0, sum1 = next_residual(b_right_ref, b_down_ref, g0, z0, g1, own_of)
        precondition(b_right_ref, b_down_ref, g1, f1, work_ref)
        sum2, sum3 = next_residual(b_right_ref, b_down_ref, g1, f1, g2, own_of)
        return tuple(a + b for a, b in zip(carry, (sum0, sum1, sum2, sum3)))

    zero = jnp.zeros((SUBS, LANES), jnp.float32)
    parts = lax.fori_loop(0, chans, channel, (zero,) * 4)
    sums = zero
    for k, part in enumerate(parts):
        sums = jnp.where(sub == k, jnp.sum(part), sums)
    sums_ref[...] = sums

    def edge(c, j, at):
        s, i = divmod(HALO + at, steps)
        return g2_ref[c, j, pl.ds(i * SUBS + s, LATE, stride=SUBS), :]

    for c in range(chans):
        for j in range(tiles):
            low, high = edge(c, j, 0), edge(c, j, rows - LATE)
            first_late_ref[c * tiles + j] = jnp.where(odd_row, low, high)
            second_late_ref[c * tiles + j] = jnp.where(odd_row, high, low)


def second_kernel(
    c, first_late_ref, second_late_ref, b_right_ref, b_down_ref, g2_ref, f2_ref, g_ref, work_ref
):
    tiles, height = b_right_ref.shape[:2]
    rows = height - 2 * HALO
    steps = height // SUBS
    odd_row = odd("row")
    for j in range(tiles):
        g_ref[j] = g2_ref[c, j]
        first, second = first_late_ref[c * tiles + j], second_late_ref[c * tiles + j]
        for value, at in ((jnp.where(odd_row, first, second), HALO - LATE), (jnp.where(odd_row, second, first), HALO + rows)):
            done = 0
            while done < LATE:
                s, i = divmod(at + done, steps)
                count = min(LATE - done, steps - i)
                g_ref[j, pl.ds(i * SUBS + s, count, stride=SUBS), :] = value[done:done + count]
                done += count
    precondition(b_right_ref, b_down_ref, g_ref, f2_ref, work_ref)


def combine(n0, n1, n2, n3):
    gap = n0 - n1
    keep = -n1 / gap
    step = n0 / gap
    beta = (n0 * n2 - n1 * n1) / (gap * gap)
    along = keep + beta
    curvature = along * along * gap + 2.0 * along * step * (n1 - n2) + step * step * (n2 - n3)
    scaled = n0 * beta / curvature
    first_size = step * MIX
    second_size = scaled * MIX
    x0 = first_size + second_size * along
    x1 = second_size * step
    r0 = keep - scaled * along
    r1 = step + scaled * (along - step)
    r2 = scaled * step
    return x0, x1, r0, r1, r2


def third_kernel(
    sums_ref, scale_ref, root_ref, g0_ref, z0_ref, g1_ref, f1_ref, g2_ref, *refs
):
    *f2_refs, solution_hbm, residual_hbm, smoothed_hbm, natural, done, sems = refs
    rows, cols = solution_hbm.shape[1:]
    own_tiles = cols // LANES
    tiles, height = scale_ref.shape[:2]
    steps = height // SUBS
    ways = ways_of(tiles)
    x0, x1, r0, r1, r2 = combine(*[jnp.broadcast_to(sums_ref[k:k + 1, :], (SUBS, LANES)) for k in range(4)])
    matrix = undealing(ways) if ways > 1 else None
    outs = (solution_hbm, residual_hbm, smoothed_hbm)
    copies = []
    chans = len(f2_refs)
    for g in range(0, own_tiles, ways):
        width = min(ways, own_tiles - g) * LANES
        for c, f2_ref in enumerate(f2_refs):
            for j in range(g, g + ways):
                for i in range(steps):
                    at = pl.ds(i * SUBS, SUBS)
                    scale = scale_ref[j, at, :]
                    root = root_ref[j, at, :]
                    g0, g1, g2, z0, f1 = [ref[c, j, at, :] for ref in (g0_ref, g1_ref, g2_ref, z0_ref, f1_ref)]
                    f2 = f2_ref[j, at, :]
                    there = pl.ds(i, SUBS, stride=steps)
                    natural[c, 0, j, there, :] = scale * (x0 * z0 + x1 * f1)
                    natural[c, 1, j, there, :] = root * (r0 * g0 + r1 * g1 + r2 * g2)
                    natural[c, 2, j, there, :] = scale * (r0 * z0 + r1 * f1 + r2 * f2)
        value = jnp.concatenate(
            [natural[:, :, g + m, HALO:HALO + rows, :].reshape(3 * chans * rows, LANES) for m in range(ways)], axis=1
        )
        if ways > 1:
            value = permuted(value, matrix[:, :width], 2)
        columns = pl.ds(g * LANES, width)
        for c in range(chans):
            for k, ref in enumerate(outs):
                at = (c * 3 + k) * rows
                done[c, k, :, columns] = value[at:at + rows]
                copy = pltpu.make_async_copy(
                    done.at[c, k, :, columns], ref.at[c, :, columns], sems.at[g // ways, c * 3 + k]
                )
                copy.start()
                copies.append(copy)
    for copy in copies:
        copy.wait()


def sum_over(value, steps):
    done = []
    for axis, pairs, beside in steps:
        other = lax.ppermute(value, axis, pairs)
        if beside:
            value, *arrays = lax.optimization_barrier((value, *beside))
            done += arrays
        value = value + other
    return value, done


def per_device(source, weight, seam_right, seam_down, offsets):
    chans, rows, cols = source.shape
    row_axis, col_axis = lax.axis_size("row"), lax.axis_size("col")
    in_vmem = pl.BlockSpec(memory_space=pltpu.VMEM)
    in_hbm = pl.BlockSpec(memory_space=pltpu.HBM)
    params = pltpu.CompilerParams(vmem_limit_bytes=VMEM_LIMIT)

    def shaped(*shape):
        return jax.ShapeDtypeStruct(shape, jnp.float32)

    def scratch(*shape):
        return pltpu.VMEM(shape, jnp.float32)

    planes = chans + 3
    own_tiles = cols // LANES
    tiles = own_tiles + 1
    packs = -(-planes // SLOTS)
    own, first_rows, second_rows, first_cols, second_cols = pl.pallas_call(
        own_kernel,
        out_shape=[shaped(planes, own_tiles, rows, LANES)]
        + [shaped(planes, own_tiles, HALO, LANES)] * 2
        + [shaped(packs, rows, LANES)] * 2,
        in_specs=[in_hbm] * 5,
        out_specs=[in_vmem] * 5,
        scratch_shapes=[
            pltpu.SMEM((chans,) + offsets.shape[:2], jnp.int32),
            scratch(*source.shape),
            scratch(*weight.shape),
            pltpu.VMEM(weight.shape, jnp.int32),
            pltpu.VMEM(weight.shape, jnp.int32),
            pltpu.SemaphoreType.DMA((planes + 1,)),
        ],
        compiler_params=params,
    )(
        *[
            pltpu.with_memory_space_constraint(v, pltpu.HBM)
            for v in (offsets.transpose(2, 0, 1), source, weight, seam_right, seam_down)
        ],
    )

    def swap(first, second, axis, order):
        size = lax.axis_size(axis)
        pairs = [[(i, i + 1) for i in range(start, size - 1, 2)] for start in range(2)]
        pairs = [some + [(j, i) for i, j in some] for some in pairs]
        received = {k: lax.ppermute((first, second)[k], axis, pairs[k]) for k in order}
        return received[0], received[1]

    ways = ways_of(tiles)
    inner = pl.pallas_call(
        inner_dealt_kernel,
        out_shape=shaped(planes, tiles - ways, rows, LANES),
        in_specs=[in_vmem],
        out_specs=in_vmem,
        compiler_params=params,
        cost_estimate=pl.CostEstimate(flops=10**8, bytes_accessed=4 * 10**6, transcendentals=0),
    )(own)
    first_rows, second_rows = swap(first_rows, second_rows, "row", (1, 0))
    first_cols, second_cols = swap(first_cols, second_cols, "col", (0, 1))
    first_cols, second_cols, inner = lax.optimization_barrier((first_cols, second_cols, inner))
    corners = pl.pallas_call(
        functools.partial(corners_kernel, chans),
        out_shape=[shaped(2, packs, HALO, LANES)] * 2,
        in_specs=[in_vmem] * 2,
        out_specs=[in_vmem] * 2,
        compiler_params=params,
    )(first_cols, second_cols)
    first_corners, second_corners = swap(*corners, "row", (1, 0))
    outer = pl.pallas_call(
        outer_dealt_kernel,
        out_shape=shaped(planes, ways, rows, LANES),
        in_specs=[in_vmem] * 3,
        out_specs=in_vmem,
        compiler_params=params,
        cost_estimate=pl.CostEstimate(flops=10**8, bytes_accessed=2 * 10**6, transcendentals=0),
    )(own, first_cols, second_cols)

    height = rows + 2 * HALO
    plane = shaped(tiles, height, LANES)
    field = shaped(chans, tiles, height, LANES)
    late = shaped(chans * tiles, LATE, LANES)
    *basis, sums, first_late, second_late = pl.pallas_call(
        first_kernel,
        out_shape=[plane] * 4 + [field] * 5 + [shaped(SUBS, LANES)] + [late] * 2,
        in_specs=[in_vmem] * 6,
        out_specs=[in_vmem] * 12,
        scratch_shapes=[scratch(planes, tiles, height, LANES), scratch(*plane.shape)],
        compiler_params=params,
    )(inner, outer, second_rows, first_rows, second_corners, first_corners)

    first_late, second_late = swap(first_late, second_late, "row", (0, 1))

    b_right, b_down, scale, root, g0, z0, g1, f1, g2 = basis
    f2 = [
        pl.pallas_call(
            functools.partial(second_kernel, c),
            out_shape=plane,
            in_specs=[in_vmem] * 5,
            out_specs=in_vmem,
            scratch_shapes=[scratch(*plane.shape)] * 2,
            compiler_params=params,
            cost_estimate=pl.CostEstimate(flops=10**8, bytes_accessed=10**7, transcendentals=0),
        )(first_late, second_late, b_right, b_down, g2)
        for c in range(chans)
    ]
    if row_axis & (row_axis - 1) or col_axis & (col_axis - 1):
        total = lax.psum(sums, ("row", "col"))
    else:
        steps = [
            [axis, [(i, i ^ (1 << k)) for i in range(size)], []]
            for axis, size in (("col", col_axis), ("row", row_axis))
            for k in range(size.bit_length() - 1)
        ]
        if len(steps) > 1:
            steps[-2][2], steps[-1][2] = f2[:1], f2[1:]
            total, f2 = sum_over(sums, steps)
        else:
            total, _ = sum_over(sums, steps)
    return pl.pallas_call(
        third_kernel,
        out_shape=[shaped(chans, rows, cols)] * 3,
        in_specs=[in_vmem] * (8 + chans),
        out_specs=[pl.BlockSpec(memory_space=pltpu.HBM)] * 3,
        scratch_shapes=[
            scratch(chans, 3, tiles, height, LANES),
            scratch(chans, 3, rows, cols),
            pltpu.SemaphoreType.DMA((-(-own_tiles // ways), chans * 3)),
        ],
        compiler_params=params,
    )(total, scale, root, g0, z0, g1, f1, g2, *f2)


def solution(mesh):
    placed = (
        P(None, ("band", "row"), "col"),
        P(("band", "row"), "col"),
        P(("band", "row"), "col"),
        P(("band", "row"), "col"),
        P("band", None, None),
    )
    return jax.shard_map(
        per_device,
        mesh=mesh,
        in_specs=placed,
        out_specs=(
            P(None, ("band", "row"), "col"),
            P(None, ("band", "row"), "col"),
            P(None, ("band", "row"), "col"),
        ),
        check_vma=False,
    )
```

```python
import functools

import jax
import jax.numpy as jnp
from jax import lax
from jax.experimental import pallas as pl
from jax.experimental.pallas import tpu as pltpu
from jax.sharding import PartitionSpec as P

TILE = 256
SWEEPS = 8
SUBS = 8
LANES = 128
HALO = 16
LATE = 8
SLOT = 32
SLOTS = LANES // SLOT
SPARE = 8
WAYS = 3

seam_damping = 0.8
offset_unit = 32.0
spectrum_low = 0.08
spectrum_high = 2.0
MIX = 2.4

VMEM_LIMIT = 28 * 1024 * 1024


def chebyshev_polynomial():
    centre = (spectrum_high + spectrum_low) / 2.0
    radius = (spectrum_high - spectrum_low) / 2.0
    sigma = centre / radius
    size = SWEEPS
    update = [1.0 / centre] + [0.0] * (size - 1)
    smoothed = list(update)
    rho = 1.0 / sigma
    for _ in range(SWEEPS - 1):
        remainder = [-s for s in smoothed]
        remainder[0] += 1.0
        for k in range(size - 1):
            remainder[k + 1] += smoothed[k]
        following = 1.0 / (2.0 * sigma - rho)
        update = [following * rho * u + 2.0 * following / radius * r for u, r in zip(update, remainder)]
        smoothed = [s + u for s, u in zip(smoothed, update)]
        rho = following
    return smoothed


def lane_index():
    return lax.broadcasted_iota(jnp.int32, (SUBS, LANES), 1)


def odd(axis):
    return lax.rem(lax.axis_index(axis), 2) == 1


def pack(planes, start):
    lane = lax.broadcasted_iota(jnp.int32, planes[0].shape, 1)
    packed = [None] * (-(-len(planes) // SLOTS))
    for p, plane in enumerate(planes):
        slot = p % SLOTS
        by = (slot * SLOT - start) % LANES
        moved = pltpu.roll(plane, by, 1) if by else plane
        k = p // SLOTS
        packed[k] = moved if slot == 0 else jnp.where(lane < slot * SLOT, packed[k], moved)
    return packed


def own_kernel(
    offsets_hbm, src_hbm, weight_hbm, seam_right_hbm, seam_down_hbm,
    own_ref, first_rows_ref, second_rows_ref, first_cols_ref, second_cols_ref,
    offsets_ref, src_ref, weight_ref, seam_right_ref, seam_down_ref, sems,
):
    chans, rows, cols = src_ref.shape
    own_tiles = cols // LANES
    moves = [(weight_hbm, weight_ref), (seam_right_hbm, seam_right_ref), (seam_down_hbm, seam_down_ref)]
    moves += [(src_hbm.at[c], src_ref.at[c]) for c in range(chans)] + [(offsets_hbm, offsets_ref)]
    copies = [pltpu.make_async_copy(there, here, sems.at[k]) for k, (there, here) in enumerate(moves)]
    for copy in copies:
        copy.start()
    row = lax.broadcasted_iota(jnp.int32, (rows, LANES), 0)
    lane = lax.broadcasted_iota(jnp.int32, (rows, LANES), 1)
    sub = lax.broadcasted_iota(jnp.int32, (SUBS, LANES), 0)
    row_at, col_at = lax.axis_index("row"), lax.axis_index("col")
    last_row = jnp.where(row_at == lax.axis_size("row") - 1, rows - 1, -1)
    last_lane = jnp.where(col_at == lax.axis_size("col") - 1, LANES - 1, -1)
    tile_row, tile_at = lax.div(row_at * rows, TILE), col_at * (cols // TILE)
    odd_row, odd_col = odd("row"), odd("col")

    def tile(ref, j):
        return ref[:, j * LANES:(j + 1) * LANES]

    copies[0].wait()
    for j in range(own_tiles):
        own_ref[chans, j] = tile(weight_ref, j)
    copies[1].wait()
    for j in range(own_tiles):
        value = 1.0 - seam_damping * tile(seam_right_ref, j).astype(jnp.float32)
        own_ref[chans + 1, j] = jnp.where(lane == last_lane, 0.0, value) if j == own_tiles - 1 else value
    copies[2].wait()
    for j in range(own_tiles):
        value = 1.0 - seam_damping * tile(seam_down_ref, j).astype(jnp.float32)
        own_ref[chans + 2, j] = jnp.where(row == last_row, 0.0, value)
    copies[-1].wait()
    for c in range(chans):
        shift = [
            jnp.broadcast_to(offsets_ref[c, tile_row, tile_at + k], (rows, LANES)).astype(jnp.float32) / offset_unit
            for k in range(cols // TILE)
        ]
        copies[3 + c].wait()
        for j in range(own_tiles):
            own_ref[c, j] = tile(src_ref.at[c], j) + shift[j * LANES // TILE]

    planes = range(chans + 3)

    def low_rows(ref):
        for p in planes:
            ref[p] = own_ref[p, :, 0:HALO, :]

    def high_rows(ref):
        at = rows - HALO
        for p in planes:
            ref[p] = own_ref[p, :, at:rows, :]
        for j in range(own_tiles):
            above = jnp.where(sub == 0, own_ref[chans + 2, j, at - 1:at, :], 0.0)
            ref[chans, j, 0:SUBS, :] = own_ref[chans, j, at:at + SUBS, :] + above

    @pl.when(odd_row)
    def _():
        low_rows(first_rows_ref)
        high_rows(second_rows_ref)

    @pl.when(jnp.logical_not(odd_row))
    def _():
        high_rows(first_rows_ref)
        low_rows(second_rows_ref)

    left = pack([own_ref[p, 0] for p in planes], 0)
    right = pack([own_ref[p, own_tiles - 1] for p in planes], LANES - SLOT)
    for k, (a, b) in enumerate(zip(left, right)):
        first_cols_ref[k] = jnp.where(odd_col, a, b)
        second_cols_ref[k] = jnp.where(odd_col, b, a)


def corners_kernel(chans, first_ref, second_ref, first_out, second_out):
    rows = first_ref.shape[1]
    odd_row, odd_col = odd("row"), odd("col")
    sub = lax.broadcasted_iota(jnp.int32, (SUBS, LANES), 0)
    lane = lane_index()
    weight, down = chans, chans + 2
    slot = weight % SLOTS
    at = rows - HALO
    for side, (in_odd, in_even) in enumerate(((first_ref, second_ref), (second_ref, first_ref))):

        def tile(k, low, count=SUBS, in_odd=in_odd, in_even=in_even):
            return jnp.where(odd_col, in_odd[k, low:low + count, :], in_even[k, low:low + count, :])

        above = jnp.broadcast_to(tile(down // SLOTS, at - 1, 1), (SUBS, LANES))
        above = pltpu.roll(above, (slot - down % SLOTS) % SLOTS * SLOT, 1)
        own_slot = jnp.logical_and(lane >= slot * SLOT, lane < (slot + 1) * SLOT)
        above = jnp.where(jnp.logical_and(sub == 0, own_slot), above, 0.0)
        for k in range(first_ref.shape[0]):
            for low in range(0, HALO, SUBS):
                near = tile(k, low)
                far = tile(k, at + low)
                if low == 0 and k == weight // SLOTS:
                    far = far + above
                first_out[side, k, low:low + SUBS, :] = jnp.where(odd_row, near, far)
                second_out[side, k, low:low + SUBS, :] = jnp.where(odd_row, far, near)


def unpack(p, lefts, rights):
    lane = lax.broadcasted_iota(jnp.int32, lefts.shape, 1)
    slot = p % SLOTS
    if slot != SLOTS - 1:
        lefts = pltpu.roll(lefts, LANES - SLOT - slot * SLOT, 1)
    if slot:
        rights = pltpu.roll(rights, LANES - slot * SLOT, 1)
    return jnp.where(lane < SLOT, rights, jnp.where(lane >= LANES - SLOT, lefts, 0.0))


def ways_of(tiles):
    return WAYS if tiles % WAYS == 0 else 1


def split(value, count):
    parts = []
    for k in range(count):
        part = value.astype(jnp.bfloat16)
        parts.append(part)
        if k + 1 < count:
            value = value - part.astype(jnp.float32)
    return jnp.concatenate(parts, axis=0)


def permuted(value, index, count):
    rows = value.shape[0]
    out = jnp.dot(split(value, count), index, preferred_element_type=jnp.float32)
    total = out[:rows]
    for k in range(1, count):
        total = total + out[k * rows:(k + 1) * rows]
    return total


def dealing(ways):
    size = ways * LANES
    column = lax.broadcasted_iota(jnp.int32, (size, size), 0)
    place = lax.broadcasted_iota(jnp.int32, (size, size), 1)
    return jnp.where(column == ways * (place % LANES) + place // LANES, 1.0, 0.0).astype(jnp.bfloat16)


def undealing(ways):
    size = ways * LANES
    column = lax.broadcasted_iota(jnp.int32, (size, size), 1)
    place = lax.broadcasted_iota(jnp.int32, (size, size), 0)
    return jnp.where(column == ways * (place % LANES) + place // LANES, 1.0, 0.0).astype(jnp.bfloat16)


def deal(tile_of, low, high, ways, emit):
    matrix = dealing(ways) if ways > 1 else None
    for g in range(low, high, ways):
        if ways == 1:
            emit(g, tile_of(g))
            continue
        value = permuted(jnp.concatenate([tile_of(g + m) for m in range(ways)], axis=1), matrix, 3)
        for m in range(ways):
            emit(g + m, value[:, m * LANES:(m + 1) * LANES])


def inner_dealt_kernel(own_ref, dealt_ref):
    planes, own_tiles, rows = own_ref.shape[:3]

    def emit(j, value):
        dealt_ref[:, j] = value.reshape(planes, rows, LANES)

    deal(lambda j: own_ref[:, j].reshape(planes * rows, LANES), 0, dealt_ref.shape[1], ways_of(own_tiles + 1), emit)


def outer_dealt_kernel(own_ref, first_ref, second_ref, dealt_ref):
    planes, own_tiles, rows = own_ref.shape[:3]
    tiles = own_tiles + 1
    low = tiles - dealt_ref.shape[1]
    odd_col = odd("col")

    def tile_of(j):
        if j < own_tiles:
            return own_ref[:, j].reshape(planes * rows, LANES)
        parts = []
        for p in range(planes):
            first, second = first_ref[p // SLOTS], second_ref[p // SLOTS]
            parts.append(unpack(p, jnp.where(odd_col, first, second), jnp.where(odd_col, second, first)))
        return jnp.concatenate(parts, axis=0)

    def emit(j, value):
        dealt_ref[:, j - low] = value.reshape(planes, rows, LANES)

    deal(tile_of, low, tiles, ways_of(tiles), emit)


def rightward(values):
    tiles = len(values)
    ways = ways_of(tiles)
    last = lane_index() == LANES - 1
    ahead = {g: pltpu.roll(values[g], LANES - 1, 1) for g in range(0, tiles, ways)}
    out = []
    for j in range(tiles):
        if j % ways + 1 < ways:
            out.append(values[j + 1])
        else:
            g = j - ways + 1
            out.append(jnp.where(last, ahead[(g + ways) % tiles], ahead[g]))
    return out


def leftward(values):
    tiles = len(values)
    ways = ways_of(tiles)
    first = lane_index() == 0
    behind = {g: pltpu.roll(values[g + ways - 1], 1, 1) for g in range(0, tiles, ways)}
    out = []
    for j in range(tiles):
        if j % ways:
            out.append(values[j - 1])
        else:
            out.append(jnp.where(first, behind[(j - ways) % tiles], behind[j]))
    return out


def spread(b_right_ref, b_down_ref, z_ref, emit):
    tiles, height = z_ref.shape[:2]
    steps = (height - SPARE) // SUBS
    ways = ways_of(tiles)
    lane = lane_index()
    first, last = (lane == 0, lane == LANES - 1)

    def at(i):
        return pl.ds(i * SUBS, SUBS)

    from_above = [pltpu.roll(b_down_ref[j, at(steps - 1), :] * z_ref[j, at(steps - 1), :], 1, 0) for j in range(tiles)]
    centre = [z_ref[j, at(0), :] for j in range(tiles)]
    wrapped = [pltpu.roll(v, SUBS - 1, 0) for v in centre]
    for i in range(steps):
        pushed_out = {
            g: pltpu.roll(b_right_ref[g + ways - 1, at(i), :] * centre[g + ways - 1], 1, 1)
            for g in range(0, tiles, ways)
        }
        ahead = {g: pltpu.roll(centre[g], LANES - 1, 1) for g in range(0, tiles, ways)}
        pushed = None
        below = []
        for j in range(tiles):
            g = j // ways * ways
            b_right = b_right_ref[j, at(i), :]
            b_down = b_down_ref[j, at(i), :]
            below.append(z_ref[j, at(i + 1), :] if i + 1 < steps else wrapped[j])
            if j == g:
                from_left = jnp.where(first, pushed_out[(g - ways) % tiles], pushed_out[g])
            else:
                from_left = pushed
            if j + 1 < g + ways:
                to_right = centre[j + 1]
                pushed = b_right * centre[j]
            else:
                to_right = jnp.where(last, ahead[(g + ways) % tiles], ahead[g])
            moved = (b_right * to_right + from_left) + (b_down * below[j] + from_above[j])
            from_above[j] = b_down * centre[j]
            emit(i, j, centre[j], moved)
        centre = below


def precondition(b_right_ref, b_down_ref, g_ref, z_ref, work_ref):
    poly = chebyshev_polynomial()
    degree = SWEEPS - 1

    def at(i):
        return pl.ds(i * SUBS, SUBS)

    def first(i, j, centre, moved):
        z_ref[j, at(i), :] = poly[degree] * moved + poly[degree - 1] * centre

    spread(b_right_ref, b_down_ref, g_ref, first)

    def pair(k, carry):
        adds = []
        for half in range(2):
            value = jnp.float32(poly[half])
            for later in range(1, (degree - 1) // 2):
                value = jnp.where(k == (degree - 1) // 2 - 1 - later, jnp.float32(poly[2 * later + half]), value)
            adds.append(value)

        def one(target, add):
            def emit(i, j, centre, moved):
                target[j, at(i), :] = moved + add * g_ref[j, at(i), :]

            return emit

        spread(b_right_ref, b_down_ref, z_ref, one(work_ref, adds[1]))
        spread(b_right_ref, b_down_ref, work_ref, one(z_ref, adds[0]))
        return carry

    lax.fori_loop(0, (degree - 1) // 2, pair, 0)


def next_residual(b_right_ref, b_down_ref, g_ref, z_ref, next_ref, own_of):
    height = g_ref.shape[1]
    steps = (height - SPARE) // SUBS
    sums = {}

    def emit(i, j, centre, moved):
        at = pl.ds(i * SUBS, SUBS)
        g = g_ref[j, at, :]
        following = g - MIX * (centre - moved)
        next_ref[j, at, :] = following
        key = own_of(i, j)
        now = (g * centre, following * centre)
        before = sums.get(key)
        sums[key] = now if before is None else (before[0] + now[0], before[1] + now[1])

    spread(b_right_ref, b_down_ref, z_ref, emit)
    sub = lax.broadcasted_iota(jnp.int32, (SUBS, LANES), 0)
    lane = lane_index()
    total = [jnp.zeros((SUBS, LANES), jnp.float32)] * 2
    for (low, high, lanes), parts in sums.items():
        inside = jnp.logical_and(jnp.logical_and(sub >= low, sub <= high), lane < lanes)
        total = [t + jnp.where(inside, p, 0.0) for t, p in zip(total, parts)]
    return total


def first_kernel(
    inner_ref, outer_ref, second_rows_ref, first_rows_ref, second_corners_ref, first_corners_ref,
    b_right_ref, b_down_ref, scale_ref, root_ref, g0_ref, z0_ref, g1_ref, f1_ref, g2_ref, sums_ref,
    first_late_ref, second_late_ref,
    natural, work_ref,
):
    planes, inner, rows = inner_ref.shape[:3]
    tiles = inner + outer_ref.shape[1]
    chans = planes - 3
    own_tiles = tiles - 1
    height = rows + 2 * HALO
    steps = height // SUBS

    for p in range(planes):
        for j in range(tiles):
            natural[p, j, HALO:HALO + rows, :] = inner_ref[p, j] if j < inner else outer_ref[p, j - inner]
    odd_row = odd("row")

    def edge_tile(j):
        if j < own_tiles:
            first, second = [ref[:, j].reshape(planes * HALO, LANES) for ref in (first_rows_ref, second_rows_ref)]
        else:
            first, second = [
                jnp.concatenate([unpack(p, ref[0, p // SLOTS], ref[1, p // SLOTS]) for p in range(planes)], axis=0)
                for ref in (first_corners_ref, second_corners_ref)
            ]
        return jnp.concatenate([jnp.where(odd_row, first, second), jnp.where(odd_row, second, first)], axis=0)

    def put_edge(j, value):
        value = value.reshape(2, planes, HALO, LANES)
        natural[:, j, 0:HALO, :] = value[0]
        natural[:, j, HALO + rows:height, :] = value[1]

    deal(edge_tile, 0, tiles, ways_of(tiles), put_edge)

    def at(i):
        return pl.ds(i * SUBS, SUBS)

    def interleaved(p, i, j):
        return natural[p, j, pl.ds(i, SUBS, stride=steps), :]

    sub = lax.broadcasted_iota(jnp.int32, (SUBS, LANES), 0)
    to_up = [
        jnp.where(sub == 0, 0.0, pltpu.roll(interleaved(chans + 2, steps - 1, j), 1, 0)) for j in range(tiles)
    ]
    for i in range(steps):
        to_right = [interleaved(chans + 1, i, j) for j in range(tiles)]
        to_left = leftward(to_right)
        for j in range(tiles):
            to_down = interleaved(chans + 2, i, j)
            diag = interleaved(chans, i, j) + to_right[j] + to_left[j] + to_down + to_up[j]
            inside = diag > 0.0
            safe = jnp.where(inside, diag, 1.0)
            guess = lax.rsqrt(safe)
            scale = guess * (1.5 - 0.5 * safe * guess * guess)
            scale_ref[j, at(i), :] = jnp.where(inside, scale, 0.0)
            root_ref[j, at(i), :] = safe * scale
            to_up[j] = to_down
    wrapped = [pltpu.roll(scale_ref[j, at(0), :], SUBS - 1, 0) for j in range(tiles)]
    for i in range(steps):
        scale = [scale_ref[j, at(i), :] for j in range(tiles)]
        right_scale = rightward(scale)
        for j in range(tiles):
            b_right_ref[j, at(i), :] = interleaved(chans + 1, i, j) * scale[j] * right_scale[j]
            down_scale = scale_ref[j, at(i + 1), :] if i + 1 < steps else wrapped[j]
            b_down_ref[j, at(i), :] = interleaved(chans + 2, i, j) * scale[j] * down_scale
            for c in range(chans):
                g0_ref[c, j, at(i), :] = interleaved(c, i, j) * scale[j]

    ways = ways_of(tiles)

    def own_of(i, j):
        low, high = -(-(HALO - i) // steps), (HALO + rows - 1 - i) // steps
        left = own_tiles * LANES - j // ways * ways * LANES - j % ways
        return low, high, min(LANES, max(0, -(-left // ways)))

    def channel(c, carry):
        g0, z0, g1, f1, g2 = [ref.at[c] for ref in (g0_ref, z0_ref, g1_ref, f1_ref, g2_ref)]
        precondition(b_right_ref, b_down_ref, g0, z0, work_ref)
        sum0, sum1 = next_residual(b_right_ref, b_down_ref, g0, z0, g1, own_of)
        precondition(b_right_ref, b_down_ref, g1, f1, work_ref)
        sum2, sum3 = next_residual(b_right_ref, b_down_ref, g1, f1, g2, own_of)
        return tuple(a + b for a, b in zip(carry, (sum0, sum1, sum2, sum3)))

    zero = jnp.zeros((SUBS, LANES), jnp.float32)
    parts = lax.fori_loop(0, chans, channel, (zero,) * 4)
    sums = zero
    for k, part in enumerate(parts):
        sums = jnp.where(sub == k, jnp.sum(part), sums)
    sums_ref[...] = sums
    first_late_ref[chans * tiles] = sums

    def edge(c, j, at):
        s, i = divmod(HALO + at, steps)
        return g2_ref[c, j, pl.ds(i * SUBS + s, LATE, stride=SUBS), :]

    for c in range(chans):
        for j in range(tiles):
            low, high = edge(c, j, 0), edge(c, j, rows - LATE)
            first_late_ref[c * tiles + j] = jnp.where(odd_row, low, high)
            second_late_ref[c * tiles + j] = jnp.where(odd_row, high, low)


def second_kernel(
    c, first_late_ref, second_late_ref, b_right_ref, b_down_ref, g2_ref, f2_ref, g_ref, work_ref
):
    tiles, height = b_right_ref.shape[:2]
    rows = height - SPARE - 2 * HALO
    steps = (height - SPARE) // SUBS
    odd_row = odd("row")
    for j in range(tiles):
        g_ref[j] = g2_ref[c, j]
        first, second = first_late_ref[c * tiles + j], second_late_ref[c * tiles + j]
        for value, at in ((jnp.where(odd_row, first, second), HALO - LATE), (jnp.where(odd_row, second, first), HALO + rows)):
            done = 0
            while done < LATE:
                s, i = divmod(at + done, steps)
                count = min(LATE - done, steps - i)
                g_ref[j, pl.ds(i * SUBS + s, count, stride=SUBS), :] = value[done:done + count]
                done += count
    precondition(b_right_ref, b_down_ref, g_ref, f2_ref, work_ref)


def combine(n0, n1, n2, n3):
    gap = n0 - n1
    keep = -n1 / gap
    step = n0 / gap
    beta = (n0 * n2 - n1 * n1) / (gap * gap)
    along = keep + beta
    curvature = along * along * gap + 2.0 * along * step * (n1 - n2) + step * step * (n2 - n3)
    scaled = n0 * beta / curvature
    first_size = step * MIX
    second_size = scaled * MIX
    x0 = first_size + second_size * along
    x1 = second_size * step
    r0 = keep - scaled * along
    r1 = step + scaled * (along - step)
    r2 = scaled * step
    return x0, x1, r0, r1, r2


def third_kernel(
    sums_ref, scale_ref, root_ref, g0_ref, z0_ref, g1_ref, f1_ref, g2_ref, *refs
):
    *f2_refs, solution_hbm, residual_hbm, smoothed_hbm, natural, done, sems = refs
    rows, cols = solution_hbm.shape[1:]
    own_tiles = cols // LANES
    tiles, height = scale_ref.shape[:2]
    steps = (height - SPARE) // SUBS
    ways = ways_of(tiles)
    x0, x1, r0, r1, r2 = combine(*[jnp.broadcast_to(sums_ref[k:k + 1, :], (SUBS, LANES)) for k in range(4)])
    matrix = undealing(ways) if ways > 1 else None
    outs = (solution_hbm, residual_hbm, smoothed_hbm)
    copies = []
    for c, f2_ref in enumerate(f2_refs):
        for j in range(tiles):
            for i in range(steps):
                at = pl.ds(i * SUBS, SUBS)
                scale = scale_ref[j, at, :]
                root = root_ref[j, at, :]
                g0, g1, g2, z0, f1 = [ref[c, j, at, :] for ref in (g0_ref, g1_ref, g2_ref, z0_ref, f1_ref)]
                f2 = f2_ref[j, at, :]
                there = pl.ds(i, SUBS, stride=steps)
                natural[c, 0, j, there, :] = scale * (x0 * z0 + x1 * f1)
                natural[c, 1, j, there, :] = root * (r0 * g0 + r1 * g1 + r2 * g2)
                natural[c, 2, j, there, :] = scale * (r0 * z0 + r1 * f1 + r2 * f2)
        for g in range(0, own_tiles, ways):
            value = jnp.concatenate(
                [natural[c, :, g + m, HALO:HALO + rows, :].reshape(3 * rows, LANES) for m in range(ways)], axis=1
            )
            width = min(ways, own_tiles - g) * LANES
            if ways > 1:
                value = permuted(value, matrix[:, :width], 2)
            for k in range(len(outs)):
                done[c, k, :, g * LANES:g * LANES + width] = value[k * rows:(k + 1) * rows]
        for k, ref in enumerate(outs):
            copies.append(pltpu.make_async_copy(done.at[c, k], ref.at[c], sems.at[c, k]))
            copies[-1].start()
    for copy in copies:
        copy.wait()


def sum_over(value, steps, beside):
    done = []
    for k, (axis, pairs) in enumerate(steps):
        other = lax.ppermute(value, axis, pairs)
        if len(steps) - k <= len(beside):
            value, array = lax.optimization_barrier((value, beside[len(done)]))
            done.append(array)
        value = value + other
    return value, done + list(beside[len(done):])


def per_device(source, weight, seam_right, seam_down, offsets):
    chans, rows, cols = source.shape
    row_axis, col_axis = lax.axis_size("row"), lax.axis_size("col")
    in_vmem = pl.BlockSpec(memory_space=pltpu.VMEM)
    in_hbm = pl.BlockSpec(memory_space=pltpu.HBM)
    params = pltpu.CompilerParams(vmem_limit_bytes=VMEM_LIMIT)

    def shaped(*shape):
        return jax.ShapeDtypeStruct(shape, jnp.float32)

    def scratch(*shape):
        return pltpu.VMEM(shape, jnp.float32)

    planes = chans + 3
    own_tiles = cols // LANES
    tiles = own_tiles + 1
    packs = -(-planes // SLOTS)
    own, first_rows, second_rows, first_cols, second_cols = pl.pallas_call(
        own_kernel,
        out_shape=[shaped(planes, own_tiles, rows, LANES)]
        + [shaped(planes, own_tiles, HALO, LANES)] * 2
        + [shaped(packs, rows, LANES)] * 2,
        in_specs=[in_hbm] * 5,
        out_specs=[in_vmem] * 5,
        scratch_shapes=[
            pltpu.SMEM((chans,) + offsets.shape[:2], jnp.int32),
            scratch(*source.shape),
            scratch(*weight.shape),
            pltpu.VMEM(weight.shape, jnp.int32),
            pltpu.VMEM(weight.shape, jnp.int32),
            pltpu.SemaphoreType.DMA((planes + 1,)),
        ],
        compiler_params=params,
    )(
        *[
            pltpu.with_memory_space_constraint(v, pltpu.HBM)
            for v in (offsets.transpose(2, 0, 1), source, weight, seam_right, seam_down)
        ],
    )

    def swap(first, second, axis, order):
        size = lax.axis_size(axis)
        pairs = [[(i, i + 1) for i in range(start, size - 1, 2)] for start in range(2)]
        pairs = [some + [(j, i) for i, j in some] for some in pairs]
        received = {k: lax.ppermute((first, second)[k], axis, pairs[k]) for k in order}
        return received[0], received[1]

    ways = ways_of(tiles)
    inner = pl.pallas_call(
        inner_dealt_kernel,
        out_shape=shaped(planes, tiles - ways, rows, LANES),
        in_specs=[in_vmem],
        out_specs=in_vmem,
        compiler_params=params,
        cost_estimate=pl.CostEstimate(flops=10**8, bytes_accessed=4 * 10**6, transcendentals=0),
    )(own)
    first_rows, second_rows = swap(first_rows, second_rows, "row", (1, 0))
    first_cols, second_cols = swap(first_cols, second_cols, "col", (0, 1))
    first_cols, second_cols, inner = lax.optimization_barrier((first_cols, second_cols, inner))
    corners = pl.pallas_call(
        functools.partial(corners_kernel, chans),
        out_shape=[shaped(2, packs, HALO, LANES)] * 2,
        in_specs=[in_vmem] * 2,
        out_specs=[in_vmem] * 2,
        compiler_params=params,
    )(first_cols, second_cols)
    first_corners, second_corners = swap(*corners, "row", (1, 0))
    outer = pl.pallas_call(
        outer_dealt_kernel,
        out_shape=shaped(planes, ways, rows, LANES),
        in_specs=[in_vmem] * 3,
        out_specs=in_vmem,
        compiler_params=params,
        cost_estimate=pl.CostEstimate(flops=10**8, bytes_accessed=2 * 10**6, transcendentals=0),
    )(own, first_cols, second_cols)

    height = rows + 2 * HALO
    plane = shaped(tiles, height + SPARE, LANES)
    field = shaped(chans, tiles, height + SPARE, LANES)
    lates = [shaped(chans * tiles + extra, LATE, LANES) for extra in (1, 0)]
    *basis, sums, first_late, second_late = pl.pallas_call(
        first_kernel,
        out_shape=[plane] * 4 + [field] * 5 + [shaped(SUBS, LANES)] + lates,
        in_specs=[in_vmem] * 6,
        out_specs=[in_vmem] * 12,
        scratch_shapes=[scratch(planes, tiles, height, LANES), scratch(*plane.shape)],
        compiler_params=params,
    )(inner, outer, second_rows, first_rows, second_corners, first_corners)

    first_late, second_late = swap(first_late, second_late, "row", (0, 1))

    b_right, b_down, scale, root, g0, z0, g1, f1, g2 = basis
    f2 = [
        pl.pallas_call(
            functools.partial(second_kernel, c),
            out_shape=plane,
            in_specs=[in_vmem] * 5,
            out_specs=in_vmem,
            scratch_shapes=[scratch(*plane.shape)] * 2,
            compiler_params=params,
            cost_estimate=pl.CostEstimate(flops=10**8, bytes_accessed=10**7, transcendentals=0),
        )(first_late, second_late, b_right, b_down, g2)
        for c in range(chans)
    ]
    if row_axis & (row_axis - 1) or col_axis & (col_axis - 1):
        total = lax.psum(sums, ("row", "col"))
    else:
        steps = [
            (axis, [(i, i ^ (1 << k)) for i in range(size)])
            for axis, size, low in (("row", row_axis, 1), ("col", col_axis, 0))
            for k in range(low, size.bit_length() - 1)
        ]
        if row_axis > 1:
            sums = sums + first_late[chans * tiles]
        total, f2 = sum_over(sums, steps, f2)
    return pl.pallas_call(
        third_kernel,
        out_shape=[shaped(chans, rows, cols)] * 3,
        in_specs=[in_vmem] * (8 + chans),
        out_specs=[pl.BlockSpec(memory_space=pltpu.HBM)] * 3,
        scratch_shapes=[
            scratch(chans, 3, tiles, height, LANES),
            scratch(chans, 3, rows, cols),
            pltpu.SemaphoreType.DMA((chans, 3)),
        ],
        compiler_params=params,
    )(total, scale, root, g0, z0, g1, f1, g2, *f2)


def solution(mesh):
    placed = (
        P(None, ("band", "row"), "col"),
        P(("band", "row"), "col"),
        P(("band", "row"), "col"),
        P(("band", "row"), "col"),
        P("band", None, None),
    )
    return jax.shard_map(
        per_device,
        mesh=mesh,
        in_specs=placed,
        out_specs=(
            P(None, ("band", "row"), "col"),
            P(None, ("band", "row"), "col"),
            P(None, ("band", "row"), "col"),
        ),
        check_vma=False,
    )
```

```python
import functools

import jax
import jax.numpy as jnp
from jax import lax
from jax.experimental import pallas as pl
from jax.experimental.pallas import tpu as pltpu
from jax.sharding import PartitionSpec as P

TILE = 256
SWEEPS = 8
SUBS = 8
LANES = 128
HALO = 16
LATE = 8
SLOT = 32
SLOTS = LANES // SLOT
WAYS = 3

seam_damping = 0.8
offset_unit = 32.0
spectrum_low = 0.08
spectrum_high = 2.0
MIX = 2.4

VMEM_LIMIT = 28 * 1024 * 1024


def chebyshev_polynomial():
    centre = (spectrum_high + spectrum_low) / 2.0
    radius = (spectrum_high - spectrum_low) / 2.0
    sigma = centre / radius
    size = SWEEPS
    update = [1.0 / centre] + [0.0] * (size - 1)
    smoothed = list(update)
    rho = 1.0 / sigma
    for _ in range(SWEEPS - 1):
        remainder = [-s for s in smoothed]
        remainder[0] += 1.0
        for k in range(size - 1):
            remainder[k + 1] += smoothed[k]
        following = 1.0 / (2.0 * sigma - rho)
        update = [following * rho * u + 2.0 * following / radius * r for u, r in zip(update, remainder)]
        smoothed = [s + u for s, u in zip(smoothed, update)]
        rho = following
    return smoothed


def lane_index():
    return lax.broadcasted_iota(jnp.int32, (SUBS, LANES), 1)


def odd(axis):
    return lax.rem(lax.axis_index(axis), 2) == 1


def pack(planes, start):
    lane = lax.broadcasted_iota(jnp.int32, planes[0].shape, 1)
    packed = [None] * (-(-len(planes) // SLOTS))
    for p, plane in enumerate(planes):
        slot = p % SLOTS
        by = (slot * SLOT - start) % LANES
        moved = pltpu.roll(plane, by, 1) if by else plane
        k = p // SLOTS
        packed[k] = moved if slot == 0 else jnp.where(lane < slot * SLOT, packed[k], moved)
    return packed


def own_kernel(
    offsets_hbm, src_hbm, weight_hbm, seam_right_hbm, seam_down_hbm,
    own_ref, first_rows_ref, second_rows_ref, first_cols_ref, second_cols_ref,
    offsets_ref, src_ref, weight_ref, seam_right_ref, seam_down_ref, sems,
):
    chans, rows, cols = src_ref.shape
    own_tiles = cols // LANES
    moves = [(weight_hbm, weight_ref), (seam_right_hbm, seam_right_ref), (seam_down_hbm, seam_down_ref)]
    moves += [(src_hbm.at[c], src_ref.at[c]) for c in range(chans)] + [(offsets_hbm, offsets_ref)]
    copies = [pltpu.make_async_copy(there, here, sems.at[k]) for k, (there, here) in enumerate(moves)]
    for copy in copies:
        copy.start()
    row = lax.broadcasted_iota(jnp.int32, (rows, LANES), 0)
    lane = lax.broadcasted_iota(jnp.int32, (rows, LANES), 1)
    sub = lax.broadcasted_iota(jnp.int32, (SUBS, LANES), 0)
    row_at, col_at = lax.axis_index("row"), lax.axis_index("col")
    last_row = jnp.where(row_at == lax.axis_size("row") - 1, rows - 1, -1)
    last_lane = jnp.where(col_at == lax.axis_size("col") - 1, LANES - 1, -1)
    tile_row, tile_at = lax.div(row_at * rows, TILE), col_at * (cols // TILE)
    odd_row, odd_col = odd("row"), odd("col")

    def tile(ref, j):
        return ref[:, j * LANES:(j + 1) * LANES]

    copies[0].wait()
    for j in range(own_tiles):
        own_ref[chans, j] = tile(weight_ref, j)
    copies[1].wait()
    for j in range(own_tiles):
        value = 1.0 - seam_damping * tile(seam_right_ref, j).astype(jnp.float32)
        own_ref[chans + 1, j] = jnp.where(lane == last_lane, 0.0, value) if j == own_tiles - 1 else value
    copies[2].wait()
    for j in range(own_tiles):
        value = 1.0 - seam_damping * tile(seam_down_ref, j).astype(jnp.float32)
        own_ref[chans + 2, j] = jnp.where(row == last_row, 0.0, value)
    copies[-1].wait()
    for c in range(chans):
        shift = [
            jnp.broadcast_to(offsets_ref[c, tile_row, tile_at + k], (rows, LANES)).astype(jnp.float32) / offset_unit
            for k in range(cols // TILE)
        ]
        copies[3 + c].wait()
        for j in range(own_tiles):
            own_ref[c, j] = tile(src_ref.at[c], j) + shift[j * LANES // TILE]

    planes = range(chans + 3)

    def low_rows(ref):
        for p in planes:
            ref[p] = own_ref[p, :, 0:HALO, :]

    def high_rows(ref):
        at = rows - HALO
        for p in planes:
            ref[p] = own_ref[p, :, at:rows, :]
        for j in range(own_tiles):
            above = jnp.where(sub == 0, own_ref[chans + 2, j, at - 1:at, :], 0.0)
            ref[chans, j, 0:SUBS, :] = own_ref[chans, j, at:at + SUBS, :] + above

    @pl.when(odd_row)
    def _():
        low_rows(first_rows_ref)
        high_rows(second_rows_ref)

    @pl.when(jnp.logical_not(odd_row))
    def _():
        high_rows(first_rows_ref)
        low_rows(second_rows_ref)

    left = pack([own_ref[p, 0] for p in planes], 0)
    right = pack([own_ref[p, own_tiles - 1] for p in planes], LANES - SLOT)
    for k, (a, b) in enumerate(zip(left, right)):
        first_cols_ref[k] = jnp.where(odd_col, a, b)
        second_cols_ref[k] = jnp.where(odd_col, b, a)


def corners_kernel(chans, first_ref, second_ref, first_out, second_out):
    rows = first_ref.shape[1]
    odd_row, odd_col = odd("row"), odd("col")
    sub = lax.broadcasted_iota(jnp.int32, (SUBS, LANES), 0)
    lane = lane_index()
    weight, down = chans, chans + 2
    slot = weight % SLOTS
    at = rows - HALO
    for side, (in_odd, in_even) in enumerate(((first_ref, second_ref), (second_ref, first_ref))):

        def tile(k, low, count=SUBS, in_odd=in_odd, in_even=in_even):
            return jnp.where(odd_col, in_odd[k, low:low + count, :], in_even[k, low:low + count, :])

        above = jnp.broadcast_to(tile(down // SLOTS, at - 1, 1), (SUBS, LANES))
        above = pltpu.roll(above, (slot - down % SLOTS) % SLOTS * SLOT, 1)
        own_slot = jnp.logical_and(lane >= slot * SLOT, lane < (slot + 1) * SLOT)
        above = jnp.where(jnp.logical_and(sub == 0, own_slot), above, 0.0)
        for k in range(first_ref.shape[0]):
            for low in range(0, HALO, SUBS):
                near = tile(k, low)
                far = tile(k, at + low)
                if low == 0 and k == weight // SLOTS:
                    far = far + above
                first_out[side, k, low:low + SUBS, :] = jnp.where(odd_row, near, far)
                second_out[side, k, low:low + SUBS, :] = jnp.where(odd_row, far, near)


def unpack(p, lefts, rights):
    lane = lax.broadcasted_iota(jnp.int32, lefts.shape, 1)
    slot = p % SLOTS
    if slot != SLOTS - 1:
        lefts = pltpu.roll(lefts, LANES - SLOT - slot * SLOT, 1)
    if slot:
        rights = pltpu.roll(rights, LANES - slot * SLOT, 1)
    return jnp.where(lane < SLOT, rights, jnp.where(lane >= LANES - SLOT, lefts, 0.0))


def ways_of(tiles):
    return WAYS if tiles % WAYS == 0 else 1


def split(value, count):
    parts = []
    for k in range(count):
        part = value.astype(jnp.bfloat16)
        parts.append(part)
        if k + 1 < count:
            value = value - part.astype(jnp.float32)
    return jnp.concatenate(parts, axis=0)


def permuted(value, index, count):
    rows = value.shape[0]
    out = jnp.dot(split(value, count), index, preferred_element_type=jnp.float32)
    total = out[:rows]
    for k in range(1, count):
        total = total + out[k * rows:(k + 1) * rows]
    return total


def dealing(ways):
    size = ways * LANES
    column = lax.broadcasted_iota(jnp.int32, (size, size), 0)
    place = lax.broadcasted_iota(jnp.int32, (size, size), 1)
    return jnp.where(column == ways * (place % LANES) + place // LANES, 1.0, 0.0).astype(jnp.bfloat16)


def undealing(ways):
    size = ways * LANES
    column = lax.broadcasted_iota(jnp.int32, (size, size), 1)
    place = lax.broadcasted_iota(jnp.int32, (size, size), 0)
    return jnp.where(column == ways * (place % LANES) + place // LANES, 1.0, 0.0).astype(jnp.bfloat16)


def deal(tile_of, low, high, ways, emit):
    matrix = dealing(ways) if ways > 1 else None
    for g in range(low, high, ways):
        if ways == 1:
            emit(g, tile_of(g))
            continue
        value = permuted(jnp.concatenate([tile_of(g + m) for m in range(ways)], axis=1), matrix, 3)
        for m in range(ways):
            emit(g + m, value[:, m * LANES:(m + 1) * LANES])


def inner_dealt_kernel(own_ref, dealt_ref):
    planes, own_tiles, rows = own_ref.shape[:3]

    def emit(j, value):
        dealt_ref[:, j] = value.reshape(planes, rows, LANES)

    deal(lambda j: own_ref[:, j].reshape(planes * rows, LANES), 0, dealt_ref.shape[1], ways_of(own_tiles + 1), emit)


def outer_dealt_kernel(own_ref, first_ref, second_ref, dealt_ref):
    planes, own_tiles, rows = own_ref.shape[:3]
    tiles = own_tiles + 1
    low = tiles - dealt_ref.shape[1]
    odd_col = odd("col")

    def tile_of(j):
        if j < own_tiles:
            return own_ref[:, j].reshape(planes * rows, LANES)
        parts = []
        for p in range(planes):
            first, second = first_ref[p // SLOTS], second_ref[p // SLOTS]
            parts.append(unpack(p, jnp.where(odd_col, first, second), jnp.where(odd_col, second, first)))
        return jnp.concatenate(parts, axis=0)

    def emit(j, value):
        dealt_ref[:, j - low] = value.reshape(planes, rows, LANES)

    deal(tile_of, low, tiles, ways_of(tiles), emit)


def rightward(values):
    tiles = len(values)
    ways = ways_of(tiles)
    last = lane_index() == LANES - 1
    ahead = {g: pltpu.roll(values[g], LANES - 1, 1) for g in range(0, tiles, ways)}
    out = []
    for j in range(tiles):
        if j % ways + 1 < ways:
            out.append(values[j + 1])
        else:
            g = j - ways + 1
            out.append(jnp.where(last, ahead[(g + ways) % tiles], ahead[g]))
    return out


def leftward(values):
    tiles = len(values)
    ways = ways_of(tiles)
    first = lane_index() == 0
    behind = {g: pltpu.roll(values[g + ways - 1], 1, 1) for g in range(0, tiles, ways)}
    out = []
    for j in range(tiles):
        if j % ways:
            out.append(values[j - 1])
        else:
            out.append(jnp.where(first, behind[(j - ways) % tiles], behind[j]))
    return out


SLOTTED = 8


class Vectors:
    def __init__(self, ref, slot=None):
        self.ref, self.slots, self.slot = ref, 1 if slot is None else SLOTTED, slot or 0
        self.tiles, self.steps = ref.shape[0], ref.shape[1] // (SUBS * self.slots)

    def row(self, i):
        return (i * self.slots + self.slot) * SUBS

    def get(self, i, j):
        return self.ref[j, self.row(i):self.row(i) + SUBS, :]

    def put(self, i, j, value):
        self.ref[j, self.row(i):self.row(i) + SUBS, :] = value


def shared(ref):
    return [Vectors(ref, slot) for slot in (0, 1, 2, 3, 7)]


def spread(b_right, b_down, z, emit):
    tiles, steps = z.tiles, z.steps
    ways = ways_of(tiles)
    lane = lane_index()
    first, last = (lane == 0, lane == LANES - 1)
    from_above = [pltpu.roll(b_down.get(steps - 1, j) * z.get(steps - 1, j), 1, 0) for j in range(tiles)]
    centre = [z.get(0, j) for j in range(tiles)]
    wrapped = [pltpu.roll(v, SUBS - 1, 0) for v in centre]
    for i in range(steps):
        pushed_out = {
            g: pltpu.roll(b_right.get(i, g + ways - 1) * centre[g + ways - 1], 1, 1) for g in range(0, tiles, ways)
        }
        ahead = {g: pltpu.roll(centre[g], LANES - 1, 1) for g in range(0, tiles, ways)}
        pushed = None
        below = []
        for j in range(tiles):
            g = j // ways * ways
            right = b_right.get(i, j)
            down = b_down.get(i, j)
            below.append(z.get(i + 1, j) if i + 1 < steps else wrapped[j])
            if j == g:
                from_left = jnp.where(first, pushed_out[(g - ways) % tiles], pushed_out[g])
            else:
                from_left = pushed
            if j + 1 < g + ways:
                to_right = centre[j + 1]
                pushed = right * centre[j]
            else:
                to_right = jnp.where(last, ahead[(g + ways) % tiles], ahead[g])
            moved = (right * to_right + from_left) + (down * below[j] + from_above[j])
            from_above[j] = down * centre[j]
            emit(i, j, centre[j], moved)
        centre = below


def precondition(b_right, b_down, g, z, work, out):
    poly = chebyshev_polynomial()
    degree = SWEEPS - 1

    def first(i, j, centre, moved):
        z.put(i, j, poly[degree] * moved + poly[degree - 1] * centre)

    spread(b_right, b_down, g, first)

    def pair(k, carry):
        adds = []
        for half in range(2):
            value = jnp.float32(poly[half])
            for later in range(1, (degree - 1) // 2):
                value = jnp.where(k == (degree - 1) // 2 - 1 - later, jnp.float32(poly[2 * later + half]), value)
            adds.append(value)

        def to_work(i, j, centre, moved):
            work.put(i, j, moved + adds[1] * g.get(i, j))

        def to_z(i, j, centre, moved):
            value = moved + adds[0] * g.get(i, j)
            z.put(i, j, value)
            out.put(i, j, value)

        spread(b_right, b_down, z, to_work)
        spread(b_right, b_down, work, to_z)
        return carry

    lax.fori_loop(0, (degree - 1) // 2, pair, 0)


def next_residual(b_right, b_down, g, z, out, own_of):
    sums = {}

    def emit(i, j, centre, moved):
        old = g.get(i, j)
        following = old - MIX * (centre - moved)
        g.put(i, j, following)
        out.put(i, j, following)
        key = own_of(i, j)
        now = (old * centre, following * centre)
        before = sums.get(key)
        sums[key] = now if before is None else (before[0] + now[0], before[1] + now[1])

    spread(b_right, b_down, z, emit)
    sub = lax.broadcasted_iota(jnp.int32, (SUBS, LANES), 0)
    lane = lane_index()
    total = [jnp.zeros((SUBS, LANES), jnp.float32)] * 2
    for (low, high, lanes), parts in sums.items():
        inside = jnp.logical_and(jnp.logical_and(sub >= low, sub <= high), lane < lanes)
        total = [t + jnp.where(inside, p, 0.0) for t, p in zip(total, parts)]
    return total


def first_kernel(
    inner_ref, outer_ref, second_rows_ref, first_rows_ref, second_corners_ref, first_corners_ref,
    b_right_ref, b_down_ref, scale_ref, root_ref, g0_ref, z0_ref, g1_ref, f1_ref, g2_ref, sums_ref,
    first_late_ref, second_late_ref,
    natural, hot_ref,
):
    planes, inner, rows = inner_ref.shape[:3]
    tiles = inner + outer_ref.shape[1]
    chans = planes - 3
    own_tiles = tiles - 1
    height = rows + 2 * HALO
    steps = height // SUBS

    for p in range(planes):
        for j in range(tiles):
            natural[p, j, HALO:HALO + rows, :] = inner_ref[p, j] if j < inner else outer_ref[p, j - inner]
    odd_row = odd("row")

    def edge_tile(j):
        if j < own_tiles:
            first, second = [ref[:, j].reshape(planes * HALO, LANES) for ref in (first_rows_ref, second_rows_ref)]
        else:
            first, second = [
                jnp.concatenate([unpack(p, ref[0, p // SLOTS], ref[1, p // SLOTS]) for p in range(planes)], axis=0)
                for ref in (first_corners_ref, second_corners_ref)
            ]
        return jnp.concatenate([jnp.where(odd_row, first, second), jnp.where(odd_row, second, first)], axis=0)

    def put_edge(j, value):
        value = value.reshape(2, planes, HALO, LANES)
        natural[:, j, 0:HALO, :] = value[0]
        natural[:, j, HALO + rows:height, :] = value[1]

    deal(edge_tile, 0, tiles, ways_of(tiles), put_edge)

    def at(i):
        return pl.ds(i * SUBS, SUBS)

    def interleaved(p, i, j):
        return natural[p, j, pl.ds(i, SUBS, stride=steps), :]

    sub = lax.broadcasted_iota(jnp.int32, (SUBS, LANES), 0)
    to_up = [
        jnp.where(sub == 0, 0.0, pltpu.roll(interleaved(chans + 2, steps - 1, j), 1, 0)) for j in range(tiles)
    ]
    for i in range(steps):
        to_right = [interleaved(chans + 1, i, j) for j in range(tiles)]
        to_left = leftward(to_right)
        for j in range(tiles):
            to_down = interleaved(chans + 2, i, j)
            diag = interleaved(chans, i, j) + to_right[j] + to_left[j] + to_down + to_up[j]
            inside = diag > 0.0
            safe = jnp.where(inside, diag, 1.0)
            guess = lax.rsqrt(safe)
            scale = guess * (1.5 - 0.5 * safe * guess * guess)
            scale_ref[j, at(i), :] = jnp.where(inside, scale, 0.0)
            root_ref[j, at(i), :] = safe * scale
            to_up[j] = to_down
    b_right, b_down, g, z, work = shared(hot_ref)
    wrapped = [pltpu.roll(scale_ref[j, at(0), :], SUBS - 1, 0) for j in range(tiles)]
    for i in range(steps):
        scale = [scale_ref[j, at(i), :] for j in range(tiles)]
        right_scale = rightward(scale)
        for j in range(tiles):
            value = interleaved(chans + 1, i, j) * scale[j] * right_scale[j]
            b_right_ref[j, at(i), :] = value
            b_right.put(i, j, value)
            down_scale = scale_ref[j, at(i + 1), :] if i + 1 < steps else wrapped[j]
            value = interleaved(chans + 2, i, j) * scale[j] * down_scale
            b_down_ref[j, at(i), :] = value
            b_down.put(i, j, value)
            for c in range(chans):
                g0_ref[c, j, at(i), :] = interleaved(c, i, j) * scale[j]

    ways = ways_of(tiles)

    def own_of(i, j):
        low, high = -(-(HALO - i) // steps), (HALO + rows - 1 - i) // steps
        left = own_tiles * LANES - j // ways * ways * LANES - j % ways
        return low, high, min(LANES, max(0, -(-left // ways)))

    def channel(c, carry):
        g0, z0, g1, f1, g2 = [Vectors(ref.at[c]) for ref in (g0_ref, z0_ref, g1_ref, f1_ref, g2_ref)]
        for j in range(tiles):
            for i in range(steps):
                g.put(i, j, g0.get(i, j))
        precondition(b_right, b_down, g, z, work, z0)
        sum0, sum1 = next_residual(b_right, b_down, g, z, g1, own_of)
        precondition(b_right, b_down, g, z, work, f1)
        sum2, sum3 = next_residual(b_right, b_down, g, z, g2, own_of)
        return tuple(a + b for a, b in zip(carry, (sum0, sum1, sum2, sum3)))

    zero = jnp.zeros((SUBS, LANES), jnp.float32)
    parts = lax.fori_loop(0, chans, channel, (zero,) * 4)
    sums = zero
    for k, part in enumerate(parts):
        sums = jnp.where(sub == k, jnp.sum(part), sums)
    sums_ref[...] = sums
    first_late_ref[chans * tiles] = sums

    def edge(c, j, at):
        s, i = divmod(HALO + at, steps)
        return g2_ref[c, j, pl.ds(i * SUBS + s, LATE, stride=SUBS), :]

    for c in range(chans):
        for j in range(tiles):
            low, high = edge(c, j, 0), edge(c, j, rows - LATE)
            first_late_ref[c * tiles + j] = jnp.where(odd_row, low, high)
            second_late_ref[c * tiles + j] = jnp.where(odd_row, high, low)


def second_kernel(
    c, first_late_ref, second_late_ref, b_right_ref, b_down_ref, g2_ref, f2_ref, hot_ref
):
    tiles, height = b_right_ref.shape[:2]
    rows = height - 2 * HALO
    steps = height // SUBS
    odd_row = odd("row")
    b_right, b_down, g, z, work = shared(hot_ref)
    for j in range(tiles):
        for target, source in ((b_right, b_right_ref), (b_down, b_down_ref), (g, g2_ref.at[c])):
            for i in range(steps):
                target.put(i, j, source[j, i * SUBS:(i + 1) * SUBS, :])
        first, second = first_late_ref[c * tiles + j], second_late_ref[c * tiles + j]
        for value, at in ((jnp.where(odd_row, first, second), HALO - LATE), (jnp.where(odd_row, second, first), HALO + rows)):
            done = 0
            while done < LATE:
                s, i = divmod(at + done, steps)
                count = min(LATE - done, steps - i)
                hot_ref[j, pl.ds(g.row(i) + s, count, stride=SLOTTED * SUBS), :] = value[done:done + count]
                done += count
    precondition(b_right, b_down, g, z, work, Vectors(f2_ref))


def combine(n0, n1, n2, n3):
    gap = n0 - n1
    keep = -n1 / gap
    step = n0 / gap
    beta = (n0 * n2 - n1 * n1) / (gap * gap)
    along = keep + beta
    curvature = along * along * gap + 2.0 * along * step * (n1 - n2) + step * step * (n2 - n3)
    scaled = n0 * beta / curvature
    first_size = step * MIX
    second_size = scaled * MIX
    x0 = first_size + second_size * along
    x1 = second_size * step
    r0 = keep - scaled * along
    r1 = step + scaled * (along - step)
    r2 = scaled * step
    return x0, x1, r0, r1, r2


def third_kernel(
    sums_ref, scale_ref, root_ref, g0_ref, z0_ref, g1_ref, f1_ref, g2_ref, *refs
):
    *f2_refs, solution_hbm, residual_hbm, smoothed_hbm, natural, done, sems = refs
    rows, cols = solution_hbm.shape[1:]
    own_tiles = cols // LANES
    tiles, height = scale_ref.shape[:2]
    steps = height // SUBS
    ways = ways_of(tiles)
    x0, x1, r0, r1, r2 = combine(*[jnp.broadcast_to(sums_ref[k:k + 1, :], (SUBS, LANES)) for k in range(4)])
    matrix = undealing(ways) if ways > 1 else None
    outs = (solution_hbm, residual_hbm, smoothed_hbm)
    copies = []
    for c, f2_ref in enumerate(f2_refs):
        for j in range(tiles):
            for i in range(steps):
                at = pl.ds(i * SUBS, SUBS)
                scale = scale_ref[j, at, :]
                root = root_ref[j, at, :]
                g0, g1, g2, z0, f1 = [ref[c, j, at, :] for ref in (g0_ref, g1_ref, g2_ref, z0_ref, f1_ref)]
                f2 = f2_ref[j, at, :]
                there = pl.ds(i, SUBS, stride=steps)
                natural[c, 0, j, there, :] = scale * (x0 * z0 + x1 * f1)
                natural[c, 1, j, there, :] = root * (r0 * g0 + r1 * g1 + r2 * g2)
                natural[c, 2, j, there, :] = scale * (r0 * z0 + r1 * f1 + r2 * f2)
        for g in range(0, own_tiles, ways):
            value = jnp.concatenate(
                [natural[c, :, g + m, HALO:HALO + rows, :].reshape(3 * rows, LANES) for m in range(ways)], axis=1
            )
            width = min(ways, own_tiles - g) * LANES
            if ways > 1:
                value = permuted(value, matrix[:, :width], 2)
            for k in range(len(outs)):
                done[c, k, :, g * LANES:g * LANES + width] = value[k * rows:(k + 1) * rows]
        for k, ref in enumerate(outs):
            copies.append(pltpu.make_async_copy(done.at[c, k], ref.at[c], sems.at[c, k]))
            copies[-1].start()
    for copy in copies:
        copy.wait()


def sum_over(value, steps, beside):
    done = []
    for k, (axis, pairs) in enumerate(steps):
        other = lax.ppermute(value, axis, pairs)
        if len(steps) - k <= len(beside):
            value, array = lax.optimization_barrier((value, beside[len(done)]))
            done.append(array)
        value = value + other
    return value, done + list(beside[len(done):])


def per_device(source, weight, seam_right, seam_down, offsets):
    chans, rows, cols = source.shape
    row_axis, col_axis = lax.axis_size("row"), lax.axis_size("col")
    in_vmem = pl.BlockSpec(memory_space=pltpu.VMEM)
    in_hbm = pl.BlockSpec(memory_space=pltpu.HBM)
    params = pltpu.CompilerParams(vmem_limit_bytes=VMEM_LIMIT)

    def shaped(*shape):
        return jax.ShapeDtypeStruct(shape, jnp.float32)

    def scratch(*shape):
        return pltpu.VMEM(shape, jnp.float32)

    planes = chans + 3
    own_tiles = cols // LANES
    tiles = own_tiles + 1
    packs = -(-planes // SLOTS)
    own, first_rows, second_rows, first_cols, second_cols = pl.pallas_call(
        own_kernel,
        out_shape=[shaped(planes, own_tiles, rows, LANES)]
        + [shaped(planes, own_tiles, HALO, LANES)] * 2
        + [shaped(packs, rows, LANES)] * 2,
        in_specs=[in_hbm] * 5,
        out_specs=[in_vmem] * 5,
        scratch_shapes=[
            pltpu.SMEM((chans,) + offsets.shape[:2], jnp.int32),
            scratch(*source.shape),
            scratch(*weight.shape),
            pltpu.VMEM(weight.shape, jnp.int32),
            pltpu.VMEM(weight.shape, jnp.int32),
            pltpu.SemaphoreType.DMA((planes + 1,)),
        ],
        compiler_params=params,
    )(
        *[
            pltpu.with_memory_space_constraint(v, pltpu.HBM)
            for v in (offsets.transpose(2, 0, 1), source, weight, seam_right, seam_down)
        ],
    )

    def swap(first, second, axis, order):
        size = lax.axis_size(axis)
        pairs = [[(i, i + 1) for i in range(start, size - 1, 2)] for start in range(2)]
        pairs = [some + [(j, i) for i, j in some] for some in pairs]
        received = {k: lax.ppermute((first, second)[k], axis, pairs[k]) for k in order}
        return received[0], received[1]

    ways = ways_of(tiles)
    inner = pl.pallas_call(
        inner_dealt_kernel,
        out_shape=shaped(planes, tiles - ways, rows, LANES),
        in_specs=[in_vmem],
        out_specs=in_vmem,
        compiler_params=params,
        cost_estimate=pl.CostEstimate(flops=10**8, bytes_accessed=4 * 10**6, transcendentals=0),
    )(own)
    first_rows, second_rows = swap(first_rows, second_rows, "row", (1, 0))
    first_cols, second_cols = swap(first_cols, second_cols, "col", (0, 1))
    first_cols, second_cols, inner = lax.optimization_barrier((first_cols, second_cols, inner))
    corners = pl.pallas_call(
        functools.partial(corners_kernel, chans),
        out_shape=[shaped(2, packs, HALO, LANES)] * 2,
        in_specs=[in_vmem] * 2,
        out_specs=[in_vmem] * 2,
        compiler_params=params,
    )(first_cols, second_cols)
    first_corners, second_corners = swap(*corners, "row", (1, 0))
    outer = pl.pallas_call(
        outer_dealt_kernel,
        out_shape=shaped(planes, ways, rows, LANES),
        in_specs=[in_vmem] * 3,
        out_specs=in_vmem,
        compiler_params=params,
        cost_estimate=pl.CostEstimate(flops=10**8, bytes_accessed=2 * 10**6, transcendentals=0),
    )(own, first_cols, second_cols)

    height = rows + 2 * HALO
    plane = shaped(tiles, height, LANES)
    field = shaped(chans, tiles, height, LANES)
    hot = scratch(tiles, height * SLOTTED, LANES)
    lates = [shaped(chans * tiles + extra, LATE, LANES) for extra in (1, 0)]
    *basis, sums, first_late, second_late = pl.pallas_call(
        first_kernel,
        out_shape=[plane] * 4 + [field] * 5 + [shaped(SUBS, LANES)] + lates,
        in_specs=[in_vmem] * 6,
        out_specs=[in_vmem] * 12,
        scratch_shapes=[scratch(planes, tiles, height, LANES), hot],
        compiler_params=params,
    )(inner, outer, second_rows, first_rows, second_corners, first_corners)

    first_late, second_late = swap(first_late, second_late, "row", (0, 1))

    b_right, b_down, scale, root, g0, z0, g1, f1, g2 = basis
    f2 = [
        pl.pallas_call(
            functools.partial(second_kernel, c),
            out_shape=plane,
            in_specs=[in_vmem] * 5,
            out_specs=in_vmem,
            scratch_shapes=[hot],
            compiler_params=params,
            cost_estimate=pl.CostEstimate(flops=10**8, bytes_accessed=10**7, transcendentals=0),
        )(first_late, second_late, b_right, b_down, g2)
        for c in range(chans)
    ]
    if row_axis & (row_axis - 1) or col_axis & (col_axis - 1):
        total = lax.psum(sums, ("row", "col"))
    else:
        steps = [
            (axis, [(i, i ^ (1 << k)) for i in range(size)])
            for axis, size, low in (("row", row_axis, 1), ("col", col_axis, 0))
            for k in range(low, size.bit_length() - 1)
        ]
        if row_axis > 1:
            sums = sums + first_late[chans * tiles]
        total, f2 = sum_over(sums, steps, f2)
    return pl.pallas_call(
        third_kernel,
        out_shape=[shaped(chans, rows, cols)] * 3,
        in_specs=[in_vmem] * (8 + chans),
        out_specs=[pl.BlockSpec(memory_space=pltpu.HBM)] * 3,
        scratch_shapes=[
            scratch(chans, 3, tiles, height, LANES),
            scratch(chans, 3, rows, cols),
            pltpu.SemaphoreType.DMA((chans, 3)),
        ],
        compiler_params=params,
    )(total, scale, root, g0, z0, g1, f1, g2, *f2)


def solution(mesh):
    placed = (
        P(None, ("band", "row"), "col"),
        P(("band", "row"), "col"),
        P(("band", "row"), "col"),
        P(("band", "row"), "col"),
        P("band", None, None),
    )
    return jax.shard_map(
        per_device,
        mesh=mesh,
        in_specs=placed,
        out_specs=(
            P(None, ("band", "row"), "col"),
            P(None, ("band", "row"), "col"),
            P(None, ("band", "row"), "col"),
        ),
        check_vma=False,
    )
```

```python
import functools

import jax
import jax.numpy as jnp
from jax import lax
from jax.experimental import pallas as pl
from jax.experimental.pallas import tpu as pltpu
from jax.sharding import PartitionSpec as P

TILE = 256
SWEEPS = 8
SUBS = 8
LANES = 128
HALO = 16
LATE = 8
SLOT = 32
SLOTS = LANES // SLOT
WAYS = 3

seam_damping = 0.8
offset_unit = 32.0
spectrum_low = 0.08
spectrum_high = 2.0
MIX = 2.4

VMEM_LIMIT = 28 * 1024 * 1024


def chebyshev_polynomial():
    centre = (spectrum_high + spectrum_low) / 2.0
    radius = (spectrum_high - spectrum_low) / 2.0
    sigma = centre / radius
    size = SWEEPS
    update = [1.0 / centre] + [0.0] * (size - 1)
    smoothed = list(update)
    rho = 1.0 / sigma
    for _ in range(SWEEPS - 1):
        remainder = [-s for s in smoothed]
        remainder[0] += 1.0
        for k in range(size - 1):
            remainder[k + 1] += smoothed[k]
        following = 1.0 / (2.0 * sigma - rho)
        update = [following * rho * u + 2.0 * following / radius * r for u, r in zip(update, remainder)]
        smoothed = [s + u for s, u in zip(smoothed, update)]
        rho = following
    return smoothed


def lane_index():
    return lax.broadcasted_iota(jnp.int32, (SUBS, LANES), 1)


def odd(axis):
    return lax.rem(lax.axis_index(axis), 2) == 1


def pack(planes, start):
    lane = lax.broadcasted_iota(jnp.int32, planes[0].shape, 1)
    packed = [None] * (-(-len(planes) // SLOTS))
    for p, plane in enumerate(planes):
        slot = p % SLOTS
        by = (slot * SLOT - start) % LANES
        moved = pltpu.roll(plane, by, 1) if by else plane
        k = p // SLOTS
        packed[k] = moved if slot == 0 else jnp.where(lane < slot * SLOT, packed[k], moved)
    return packed


def own_kernel(
    offsets_hbm, src_hbm, weight_hbm, seam_right_hbm, seam_down_hbm,
    own_ref, first_rows_ref, second_rows_ref, first_cols_ref, second_cols_ref,
    offsets_ref, src_ref, weight_ref, seam_right_ref, seam_down_ref, sems,
):
    chans, rows, cols = src_ref.shape
    own_tiles = cols // LANES
    moves = [(weight_hbm, weight_ref), (seam_right_hbm, seam_right_ref), (seam_down_hbm, seam_down_ref)]
    moves += [(src_hbm.at[c], src_ref.at[c]) for c in range(chans)] + [(offsets_hbm, offsets_ref)]
    copies = [pltpu.make_async_copy(there, here, sems.at[k]) for k, (there, here) in enumerate(moves)]
    for copy in copies:
        copy.start()
    row = lax.broadcasted_iota(jnp.int32, (rows, LANES), 0)
    lane = lax.broadcasted_iota(jnp.int32, (rows, LANES), 1)
    sub = lax.broadcasted_iota(jnp.int32, (SUBS, LANES), 0)
    row_at, col_at = lax.axis_index("row"), lax.axis_index("col")
    last_row = jnp.where(row_at == lax.axis_size("row") - 1, rows - 1, -1)
    last_lane = jnp.where(col_at == lax.axis_size("col") - 1, LANES - 1, -1)
    tile_row, tile_at = lax.div(row_at * rows, TILE), col_at * (cols // TILE)
    odd_row, odd_col = odd("row"), odd("col")

    def tile(ref, j):
        return ref[:, j * LANES:(j + 1) * LANES]

    copies[0].wait()
    for j in range(own_tiles):
        own_ref[chans, j] = tile(weight_ref, j)
    copies[1].wait()
    for j in range(own_tiles):
        value = 1.0 - seam_damping * tile(seam_right_ref, j).astype(jnp.float32)
        own_ref[chans + 1, j] = jnp.where(lane == last_lane, 0.0, value) if j == own_tiles - 1 else value
    copies[2].wait()
    for j in range(own_tiles):
        value = 1.0 - seam_damping * tile(seam_down_ref, j).astype(jnp.float32)
        own_ref[chans + 2, j] = jnp.where(row == last_row, 0.0, value)
    copies[-1].wait()
    for c in range(chans):
        shift = [
            jnp.broadcast_to(offsets_ref[c, tile_row, tile_at + k], (rows, LANES)).astype(jnp.float32) / offset_unit
            for k in range(cols // TILE)
        ]
        copies[3 + c].wait()
        for j in range(own_tiles):
            own_ref[c, j] = tile(src_ref.at[c], j) + shift[j * LANES // TILE]

    planes = range(chans + 3)

    def low_rows(ref):
        for p in planes:
            ref[p] = own_ref[p, :, 0:HALO, :]

    def high_rows(ref):
        at = rows - HALO
        for p in planes:
            ref[p] = own_ref[p, :, at:rows, :]
        for j in range(own_tiles):
            above = jnp.where(sub == 0, own_ref[chans + 2, j, at - 1:at, :], 0.0)
            ref[chans, j, 0:SUBS, :] = own_ref[chans, j, at:at + SUBS, :] + above

    @pl.when(odd_row)
    def _():
        low_rows(first_rows_ref)
        high_rows(second_rows_ref)

    @pl.when(jnp.logical_not(odd_row))
    def _():
        high_rows(first_rows_ref)
        low_rows(second_rows_ref)

    left = pack([own_ref[p, 0] for p in planes], 0)
    right = pack([own_ref[p, own_tiles - 1] for p in planes], LANES - SLOT)
    for k, (a, b) in enumerate(zip(left, right)):
        first_cols_ref[k] = jnp.where(odd_col, a, b)
        second_cols_ref[k] = jnp.where(odd_col, b, a)


def corners_kernel(chans, first_ref, second_ref, first_out, second_out):
    rows = first_ref.shape[1]
    odd_row, odd_col = odd("row"), odd("col")
    sub = lax.broadcasted_iota(jnp.int32, (SUBS, LANES), 0)
    lane = lane_index()
    weight, down = chans, chans + 2
    slot = weight % SLOTS
    at = rows - HALO
    for side, (in_odd, in_even) in enumerate(((first_ref, second_ref), (second_ref, first_ref))):

        def tile(k, low, count=SUBS, in_odd=in_odd, in_even=in_even):
            return jnp.where(odd_col, in_odd[k, low:low + count, :], in_even[k, low:low + count, :])

        above = jnp.broadcast_to(tile(down // SLOTS, at - 1, 1), (SUBS, LANES))
        above = pltpu.roll(above, (slot - down % SLOTS) % SLOTS * SLOT, 1)
        own_slot = jnp.logical_and(lane >= slot * SLOT, lane < (slot + 1) * SLOT)
        above = jnp.where(jnp.logical_and(sub == 0, own_slot), above, 0.0)
        for k in range(first_ref.shape[0]):
            for low in range(0, HALO, SUBS):
                near = tile(k, low)
                far = tile(k, at + low)
                if low == 0 and k == weight // SLOTS:
                    far = far + above
                first_out[side, k, low:low + SUBS, :] = jnp.where(odd_row, near, far)
                second_out[side, k, low:low + SUBS, :] = jnp.where(odd_row, far, near)


def unpack(p, lefts, rights):
    lane = lax.broadcasted_iota(jnp.int32, lefts.shape, 1)
    slot = p % SLOTS
    if slot != SLOTS - 1:
        lefts = pltpu.roll(lefts, LANES - SLOT - slot * SLOT, 1)
    if slot:
        rights = pltpu.roll(rights, LANES - slot * SLOT, 1)
    return jnp.where(lane < SLOT, rights, jnp.where(lane >= LANES - SLOT, lefts, 0.0))


def ways_of(tiles):
    return WAYS if tiles % WAYS == 0 else 1


def split(value, count):
    parts = []
    for k in range(count):
        part = value.astype(jnp.bfloat16)
        parts.append(part)
        if k + 1 < count:
            value = value - part.astype(jnp.float32)
    return jnp.concatenate(parts, axis=0)


def permuted(value, index, count):
    rows = value.shape[0]
    out = jnp.dot(split(value, count), index, preferred_element_type=jnp.float32)
    total = out[:rows]
    for k in range(1, count):
        total = total + out[k * rows:(k + 1) * rows]
    return total


def dealing(ways):
    size = ways * LANES
    column = lax.broadcasted_iota(jnp.int32, (size, size), 0)
    place = lax.broadcasted_iota(jnp.int32, (size, size), 1)
    return jnp.where(column == ways * (place % LANES) + place // LANES, 1.0, 0.0).astype(jnp.bfloat16)


def undealing(ways):
    size = ways * LANES
    column = lax.broadcasted_iota(jnp.int32, (size, size), 1)
    place = lax.broadcasted_iota(jnp.int32, (size, size), 0)
    return jnp.where(column == ways * (place % LANES) + place // LANES, 1.0, 0.0).astype(jnp.bfloat16)


def deal(tile_of, low, high, ways, emit):
    matrix = dealing(ways) if ways > 1 else None
    for g in range(low, high, ways):
        if ways == 1:
            emit(g, tile_of(g))
            continue
        value = permuted(jnp.concatenate([tile_of(g + m) for m in range(ways)], axis=1), matrix, 3)
        for m in range(ways):
            emit(g + m, value[:, m * LANES:(m + 1) * LANES])


def inner_dealt_kernel(own_ref, dealt_ref):
    planes, own_tiles, rows = own_ref.shape[:3]

    def emit(j, value):
        dealt_ref[:, j] = value.reshape(planes, rows, LANES)

    deal(lambda j: own_ref[:, j].reshape(planes * rows, LANES), 0, dealt_ref.shape[1], ways_of(own_tiles + 1), emit)


def outer_dealt_kernel(own_ref, first_ref, second_ref, dealt_ref):
    planes, own_tiles, rows = own_ref.shape[:3]
    tiles = own_tiles + 1
    low = tiles - dealt_ref.shape[1]
    odd_col = odd("col")

    def tile_of(j):
        if j < own_tiles:
            return own_ref[:, j].reshape(planes * rows, LANES)
        parts = []
        for p in range(planes):
            first, second = first_ref[p // SLOTS], second_ref[p // SLOTS]
            parts.append(unpack(p, jnp.where(odd_col, first, second), jnp.where(odd_col, second, first)))
        return jnp.concatenate(parts, axis=0)

    def emit(j, value):
        dealt_ref[:, j - low] = value.reshape(planes, rows, LANES)

    deal(tile_of, low, tiles, ways_of(tiles), emit)


def rightward(values):
    tiles = len(values)
    ways = ways_of(tiles)
    last = lane_index() == LANES - 1
    ahead = {g: pltpu.roll(values[g], LANES - 1, 1) for g in range(0, tiles, ways)}
    out = []
    for j in range(tiles):
        if j % ways + 1 < ways:
            out.append(values[j + 1])
        else:
            g = j - ways + 1
            out.append(jnp.where(last, ahead[(g + ways) % tiles], ahead[g]))
    return out


def leftward(values):
    tiles = len(values)
    ways = ways_of(tiles)
    first = lane_index() == 0
    behind = {g: pltpu.roll(values[g + ways - 1], 1, 1) for g in range(0, tiles, ways)}
    out = []
    for j in range(tiles):
        if j % ways:
            out.append(values[j - 1])
        else:
            out.append(jnp.where(first, behind[(j - ways) % tiles], behind[j]))
    return out


def spread(b_right_ref, b_down_ref, z_ref, emit):
    tiles, height = z_ref.shape[:2]
    steps = height // SUBS
    ways = ways_of(tiles)
    lane = lane_index()
    first, last = (lane == 0, lane == LANES - 1)

    def at(i):
        return pl.ds(i * SUBS, SUBS)

    from_above = [pltpu.roll(b_down_ref[j, at(steps - 1), :] * z_ref[j, at(steps - 1), :], 1, 0) for j in range(tiles)]
    centre = [z_ref[j, at(0), :] for j in range(tiles)]
    wrapped = [pltpu.roll(v, SUBS - 1, 0) for v in centre]
    for i in range(steps):
        pushed_out = {
            g: pltpu.roll(b_right_ref[g + ways - 1, at(i), :] * centre[g + ways - 1], 1, 1)
            for g in range(0, tiles, ways)
        }
        ahead = {g: pltpu.roll(centre[g], LANES - 1, 1) for g in range(0, tiles, ways)}
        pushed = None
        below = []
        for j in range(tiles):
            g = j // ways * ways
            b_right = b_right_ref[j, at(i), :]
            b_down = b_down_ref[j, at(i), :]
            below.append(z_ref[j, at(i + 1), :] if i + 1 < steps else wrapped[j])
            if j == g:
                from_left = jnp.where(first, pushed_out[(g - ways) % tiles], pushed_out[g])
            else:
                from_left = pushed
            if j + 1 < g + ways:
                to_right = centre[j + 1]
                pushed = b_right * centre[j]
            else:
                to_right = jnp.where(last, ahead[(g + ways) % tiles], ahead[g])
            moved = (b_right * to_right + from_left) + (b_down * below[j] + from_above[j])
            from_above[j] = b_down * centre[j]
            emit(i, j, centre[j], moved)
        centre = below


def precondition(b_right_ref, b_down_ref, g_ref, z_ref, work_ref):
    poly = chebyshev_polynomial()
    degree = SWEEPS - 1

    def at(i):
        return pl.ds(i * SUBS, SUBS)

    def first(i, j, centre, moved):
        z_ref[j, at(i), :] = poly[degree] * moved + poly[degree - 1] * centre

    spread(b_right_ref, b_down_ref, g_ref, first)

    def pair(k, carry):
        adds = []
        for half in range(2):
            value = jnp.float32(poly[half])
            for later in range(1, (degree - 1) // 2):
                value = jnp.where(k == (degree - 1) // 2 - 1 - later, jnp.float32(poly[2 * later + half]), value)
            adds.append(value)

        def one(target, add):
            def emit(i, j, centre, moved):
                target[j, at(i), :] = moved + add * g_ref[j, at(i), :]

            return emit

        spread(b_right_ref, b_down_ref, z_ref, one(work_ref, adds[1]))
        spread(b_right_ref, b_down_ref, work_ref, one(z_ref, adds[0]))
        return carry

    lax.fori_loop(0, (degree - 1) // 2, pair, 0)


def next_residual(b_right_ref, b_down_ref, g_ref, z_ref, next_ref, own_of):
    height = g_ref.shape[1]
    steps = height // SUBS
    sums = {}

    def emit(i, j, centre, moved):
        at = pl.ds(i * SUBS, SUBS)
        g = g_ref[j, at, :]
        following = g - MIX * (centre - moved)
        next_ref[j, at, :] = following
        key = own_of(i, j)
        now = (g * centre, following * centre)
        before = sums.get(key)
        sums[key] = now if before is None else (before[0] + now[0], before[1] + now[1])

    spread(b_right_ref, b_down_ref, z_ref, emit)
    sub = lax.broadcasted_iota(jnp.int32, (SUBS, LANES), 0)
    lane = lane_index()
    total = [jnp.zeros((SUBS, LANES), jnp.float32)] * 2
    for (low, high, lanes), parts in sums.items():
        inside = jnp.logical_and(jnp.logical_and(sub >= low, sub <= high), lane < lanes)
        total = [t + jnp.where(inside, p, 0.0) for t, p in zip(total, parts)]
    return total


def first_kernel(
    inner_ref, outer_ref, second_rows_ref, first_rows_ref, second_corners_ref, first_corners_ref,
    b_right_ref, b_down_ref, scale_ref, root_ref, g0_ref, z0_ref, g1_ref, f1_ref, g2_ref, sums_ref,
    first_late_ref, second_late_ref,
    natural, work_ref,
):
    planes, inner, rows = inner_ref.shape[:3]
    tiles = inner + outer_ref.shape[1]
    chans = planes - 3
    own_tiles = tiles - 1
    height = rows + 2 * HALO
    steps = height // SUBS

    for p in range(planes):
        for j in range(tiles):
            natural[p, j, HALO:HALO + rows, :] = inner_ref[p, j] if j < inner else outer_ref[p, j - inner]
    odd_row = odd("row")

    def edge_tile(j):
        if j < own_tiles:
            first, second = [ref[:, j].reshape(planes * HALO, LANES) for ref in (first_rows_ref, second_rows_ref)]
        else:
            first, second = [
                jnp.concatenate([unpack(p, ref[0, p // SLOTS], ref[1, p // SLOTS]) for p in range(planes)], axis=0)
                for ref in (first_corners_ref, second_corners_ref)
            ]
        return jnp.concatenate([jnp.where(odd_row, first, second), jnp.where(odd_row, second, first)], axis=0)

    def put_edge(j, value):
        value = value.reshape(2, planes, HALO, LANES)
        natural[:, j, 0:HALO, :] = value[0]
        natural[:, j, HALO + rows:height, :] = value[1]

    deal(edge_tile, 0, tiles, ways_of(tiles), put_edge)

    def at(i):
        return pl.ds(i * SUBS, SUBS)

    def interleaved(p, i, j):
        return natural[p, j, pl.ds(i, SUBS, stride=steps), :]

    sub = lax.broadcasted_iota(jnp.int32, (SUBS, LANES), 0)
    to_up = [
        jnp.where(sub == 0, 0.0, pltpu.roll(interleaved(chans + 2, steps - 1, j), 1, 0)) for j in range(tiles)
    ]
    for i in range(steps):
        to_right = [interleaved(chans + 1, i, j) for j in range(tiles)]
        to_left = leftward(to_right)
        for j in range(tiles):
            to_down = interleaved(chans + 2, i, j)
            diag = interleaved(chans, i, j) + to_right[j] + to_left[j] + to_down + to_up[j]
            inside = diag > 0.0
            safe = jnp.where(inside, diag, 1.0)
            guess = lax.rsqrt(safe)
            scale = guess * (1.5 - 0.5 * safe * guess * guess)
            scale_ref[j, at(i), :] = jnp.where(inside, scale, 0.0)
            root_ref[j, at(i), :] = safe * scale
            to_up[j] = to_down
    wrapped = [pltpu.roll(scale_ref[j, at(0), :], SUBS - 1, 0) for j in range(tiles)]
    for i in range(steps):
        scale = [scale_ref[j, at(i), :] for j in range(tiles)]
        right_scale = rightward(scale)
        for j in range(tiles):
            b_right_ref[j, at(i), :] = interleaved(chans + 1, i, j) * scale[j] * right_scale[j]
            down_scale = scale_ref[j, at(i + 1), :] if i + 1 < steps else wrapped[j]
            b_down_ref[j, at(i), :] = interleaved(chans + 2, i, j) * scale[j] * down_scale
            for c in range(chans):
                g0_ref[c, j, at(i), :] = interleaved(c, i, j) * scale[j]

    ways = ways_of(tiles)

    def own_of(i, j):
        low, high = -(-(HALO - i) // steps), (HALO + rows - 1 - i) // steps
        left = own_tiles * LANES - j // ways * ways * LANES - j % ways
        return low, high, min(LANES, max(0, -(-left // ways)))

    def channel(c, carry):
        g0, z0, g1, f1, g2 = [ref.at[c] for ref in (g0_ref, z0_ref, g1_ref, f1_ref, g2_ref)]
        precondition(b_right_ref, b_down_ref, g0, z0, work_ref)
        sum0, sum1 = next_residual(b_right_ref, b_down_ref, g0, z0, g1, own_of)
        precondition(b_right_ref, b_down_ref, g1, f1, work_ref)
        sum2, sum3 = next_residual(b_right_ref, b_down_ref, g1, f1, g2, own_of)
        return tuple(a + b for a, b in zip(carry, (sum0, sum1, sum2, sum3)))

    zero = jnp.zeros((SUBS, LANES), jnp.float32)
    parts = lax.fori_loop(0, chans, channel, (zero,) * 4)
    sums = zero
    for k, part in enumerate(parts):
        sums = jnp.where(sub == k, jnp.sum(part), sums)
    sums_ref[...] = sums
    first_late_ref[chans * tiles] = sums

    def edge(c, j, at):
        s, i = divmod(HALO + at, steps)
        return g2_ref[c, j, pl.ds(i * SUBS + s, LATE, stride=SUBS), :]

    for c in range(chans):
        for j in range(tiles):
            low, high = edge(c, j, 0), edge(c, j, rows - LATE)
            first_late_ref[c * tiles + j] = jnp.where(odd_row, low, high)
            second_late_ref[c * tiles + j] = jnp.where(odd_row, high, low)


def second_kernel(
    c, first_late_ref, second_late_ref, b_right_ref, b_down_ref, g2_ref, f2_ref, g_ref, work_ref
):
    tiles, height = b_right_ref.shape[:2]
    rows = height - 2 * HALO
    steps = height // SUBS
    odd_row = odd("row")
    for j in range(tiles):
        g_ref[j] = g2_ref[c, j]
        first, second = first_late_ref[c * tiles + j], second_late_ref[c * tiles + j]
        for value, at in ((jnp.where(odd_row, first, second), HALO - LATE), (jnp.where(odd_row, second, first), HALO + rows)):
            done = 0
            while done < LATE:
                s, i = divmod(at + done, steps)
                count = min(LATE - done, steps - i)
                g_ref[j, pl.ds(i * SUBS + s, count, stride=SUBS), :] = value[done:done + count]
                done += count
    precondition(b_right_ref, b_down_ref, g_ref, f2_ref, work_ref)


def combine(n0, n1, n2, n3):
    gap = n0 - n1
    keep = -n1 / gap
    step = n0 / gap
    beta = (n0 * n2 - n1 * n1) / (gap * gap)
    along = keep + beta
    curvature = along * along * gap + 2.0 * along * step * (n1 - n2) + step * step * (n2 - n3)
    scaled = n0 * beta / curvature
    first_size = step * MIX
    second_size = scaled * MIX
    x0 = first_size + second_size * along
    x1 = second_size * step
    r0 = keep - scaled * along
    r1 = step + scaled * (along - step)
    r2 = scaled * step
    return x0, x1, r0, r1, r2


def third_kernel(
    sums_ref, scale_ref, root_ref, g0_ref, z0_ref, g1_ref, f1_ref, g2_ref, *refs
):
    *f2_refs, solution_hbm, residual_hbm, smoothed_hbm, natural, done, sems = refs
    rows, cols = solution_hbm.shape[1:]
    own_tiles = cols // LANES
    tiles, height = scale_ref.shape[:2]
    steps = height // SUBS
    ways = ways_of(tiles)
    x0, x1, r0, r1, r2 = combine(*[jnp.broadcast_to(sums_ref[k:k + 1, :], (SUBS, LANES)) for k in range(4)])
    matrix = undealing(ways) if ways > 1 else None
    outs = (solution_hbm, residual_hbm, smoothed_hbm)
    copies = []
    for c, f2_ref in enumerate(f2_refs):
        for j in range(tiles):
            for i in range(steps):
                at = pl.ds(i * SUBS, SUBS)
                scale = scale_ref[j, at, :]
                root = root_ref[j, at, :]
                g0, g1, g2, z0, f1 = [ref[c, j, at, :] for ref in (g0_ref, g1_ref, g2_ref, z0_ref, f1_ref)]
                f2 = f2_ref[j, at, :]
                there = pl.ds(i, SUBS, stride=steps)
                natural[c, 0, j, there, :] = scale * (x0 * z0 + x1 * f1)
                natural[c, 1, j, there, :] = root * (r0 * g0 + r1 * g1 + r2 * g2)
                natural[c, 2, j, there, :] = scale * (r0 * z0 + r1 * f1 + r2 * f2)
        for g in range(0, own_tiles, ways):
            value = jnp.concatenate(
                [natural[c, :, g + m, HALO:HALO + rows, :].reshape(3 * rows, LANES) for m in range(ways)], axis=1
            )
            width = min(ways, own_tiles - g) * LANES
            if ways > 1:
                value = permuted(value, matrix[:, :width], 2)
            for k in range(len(outs)):
                done[c, k, :, g * LANES:g * LANES + width] = value[k * rows:(k + 1) * rows]
        for k, ref in enumerate(outs):
            copies.append(pltpu.make_async_copy(done.at[c, k], ref.at[c], sems.at[c, k]))
            copies[-1].start()
    for copy in copies:
        copy.wait()


def sum_over(value, steps, beside):
    done = []
    for k, (axis, pairs) in enumerate(steps):
        other = lax.ppermute(value, axis, pairs)
        if len(steps) - k <= len(beside):
            value, array = lax.optimization_barrier((value, beside[len(done)]))
            done.append(array)
        value = value + other
    return value, done + list(beside[len(done):])


def per_device(source, weight, seam_right, seam_down, offsets):
    chans, rows, cols = source.shape
    row_axis, col_axis = lax.axis_size("row"), lax.axis_size("col")
    in_vmem = pl.BlockSpec(memory_space=pltpu.VMEM)
    in_hbm = pl.BlockSpec(memory_space=pltpu.HBM)
    params = pltpu.CompilerParams(vmem_limit_bytes=VMEM_LIMIT)

    def shaped(*shape):
        return jax.ShapeDtypeStruct(shape, jnp.float32)

    def scratch(*shape):
        return pltpu.VMEM(shape, jnp.float32)

    planes = chans + 3
    own_tiles = cols // LANES
    tiles = own_tiles + 1
    packs = -(-planes // SLOTS)
    own, first_rows, second_rows, first_cols, second_cols = pl.pallas_call(
        own_kernel,
        out_shape=[shaped(planes, own_tiles, rows, LANES)]
        + [shaped(planes, own_tiles, HALO, LANES)] * 2
        + [shaped(packs, rows, LANES)] * 2,
        in_specs=[in_hbm] * 5,
        out_specs=[in_vmem] * 5,
        scratch_shapes=[
            pltpu.SMEM((chans,) + offsets.shape[:2], jnp.int32),
            scratch(*source.shape),
            scratch(*weight.shape),
            pltpu.VMEM(weight.shape, jnp.int32),
            pltpu.VMEM(weight.shape, jnp.int32),
            pltpu.SemaphoreType.DMA((planes + 1,)),
        ],
        compiler_params=params,
    )(
        *[
            pltpu.with_memory_space_constraint(v, pltpu.HBM)
            for v in (offsets.transpose(2, 0, 1), source, weight, seam_right, seam_down)
        ],
    )

    def swap(first, second, axis, order):
        size = lax.axis_size(axis)
        pairs = [[(i, i + 1) for i in range(start, size - 1, 2)] for start in range(2)]
        pairs = [some + [(j, i) for i, j in some] for some in pairs]
        received = {k: lax.ppermute((first, second)[k], axis, pairs[k]) for k in order}
        return received[0], received[1]

    ways = ways_of(tiles)
    inner = pl.pallas_call(
        inner_dealt_kernel,
        out_shape=shaped(planes, tiles - ways, rows, LANES),
        in_specs=[in_vmem],
        out_specs=in_vmem,
        compiler_params=params,
        cost_estimate=pl.CostEstimate(flops=10**8, bytes_accessed=4 * 10**6, transcendentals=0),
    )(own)
    first_rows, second_rows = swap(first_rows, second_rows, "row", (1, 0))
    first_cols, second_cols = swap(first_cols, second_cols, "col", (0, 1))
    first_cols, second_cols, inner = lax.optimization_barrier((first_cols, second_cols, inner))
    corners = pl.pallas_call(
        functools.partial(corners_kernel, chans),
        out_shape=[shaped(2, packs, HALO, LANES)] * 2,
        in_specs=[in_vmem] * 2,
        out_specs=[in_vmem] * 2,
        compiler_params=params,
    )(first_cols, second_cols)
    first_corners, second_corners = swap(*corners, "row", (1, 0))
    outer = pl.pallas_call(
        outer_dealt_kernel,
        out_shape=shaped(planes, ways, rows, LANES),
        in_specs=[in_vmem] * 3,
        out_specs=in_vmem,
        compiler_params=params,
        cost_estimate=pl.CostEstimate(flops=10**8, bytes_accessed=2 * 10**6, transcendentals=0),
    )(own, first_cols, second_cols)

    height = rows + 2 * HALO
    plane = shaped(tiles, height, LANES)
    field = shaped(chans, tiles, height, LANES)
    lates = [shaped(chans * tiles + extra, LATE, LANES) for extra in (1, 0)]
    *basis, sums, first_late, second_late = pl.pallas_call(
        first_kernel,
        out_shape=[plane] * 4 + [field] * 5 + [shaped(SUBS, LANES)] + lates,
        in_specs=[in_vmem] * 6,
        out_specs=[in_vmem] * 12,
        scratch_shapes=[scratch(planes, tiles, height, LANES), scratch(*plane.shape)],
        compiler_params=params,
    )(inner, outer, second_rows, first_rows, second_corners, first_corners)

    first_late, second_late = swap(first_late, second_late, "row", (0, 1))

    b_right, b_down, scale, root, g0, z0, g1, f1, g2 = basis
    f2 = [
        pl.pallas_call(
            functools.partial(second_kernel, c),
            out_shape=plane,
            in_specs=[in_vmem] * 5,
            out_specs=in_vmem,
            scratch_shapes=[scratch(*plane.shape)] * 2,
            compiler_params=params,
            cost_estimate=pl.CostEstimate(flops=10**8, bytes_accessed=10**7, transcendentals=0),
        )(first_late, second_late, b_right, b_down, g2)
        for c in range(chans)
    ]
    if row_axis & (row_axis - 1) or col_axis & (col_axis - 1):
        total = lax.psum(sums, ("row", "col"))
    else:
        steps = [
            (axis, [(i, i ^ (1 << k)) for i in range(size)])
            for axis, size, low in (("row", row_axis, 1), ("col", col_axis, 0))
            for k in range(low, size.bit_length() - 1)
        ]
        if row_axis > 1:
            sums = sums + first_late[chans * tiles]
        total, f2 = sum_over(sums, steps, f2)
    return pl.pallas_call(
        third_kernel,
        out_shape=[shaped(chans, rows, cols)] * 3,
        in_specs=[in_vmem] * (8 + chans),
        out_specs=[pl.BlockSpec(memory_space=pltpu.HBM)] * 3,
        scratch_shapes=[
            scratch(chans, 3, tiles, height, LANES),
            scratch(chans, 3, rows, cols),
            pltpu.SemaphoreType.DMA((chans, 3)),
        ],
        compiler_params=params,
    )(total, scale, root, g0, z0, g1, f1, g2, *f2)


def solution(mesh):
    placed = (
        P(None, ("band", "row"), "col"),
        P(("band", "row"), "col"),
        P(("band", "row"), "col"),
        P(("band", "row"), "col"),
        P("band", None, None),
    )
    return jax.shard_map(
        per_device,
        mesh=mesh,
        in_specs=placed,
        out_specs=(
            P(None, ("band", "row"), "col"),
            P(None, ("band", "row"), "col"),
            P(None, ("band", "row"), "col"),
        ),
        check_vma=False,
    )
```

```python
import functools

import jax
import jax.numpy as jnp
from jax import lax
from jax.experimental import pallas as pl
from jax.experimental.pallas import tpu as pltpu
from jax.sharding import PartitionSpec as P

TILE = 256
SWEEPS = 8
SUBS = 8
LANES = 128
HALO = 16
LATE = 8
SLOT = 32
SLOTS = LANES // SLOT
WAYS = 3

seam_damping = 0.8
offset_unit = 32.0
spectrum_low = 0.08
spectrum_high = 2.0
MIX = 2.4

VMEM_LIMIT = 28 * 1024 * 1024


def chebyshev_polynomial():
    centre = (spectrum_high + spectrum_low) / 2.0
    radius = (spectrum_high - spectrum_low) / 2.0
    sigma = centre / radius
    size = SWEEPS
    update = [1.0 / centre] + [0.0] * (size - 1)
    smoothed = list(update)
    rho = 1.0 / sigma
    for _ in range(SWEEPS - 1):
        remainder = [-s for s in smoothed]
        remainder[0] += 1.0
        for k in range(size - 1):
            remainder[k + 1] += smoothed[k]
        following = 1.0 / (2.0 * sigma - rho)
        update = [following * rho * u + 2.0 * following / radius * r for u, r in zip(update, remainder)]
        smoothed = [s + u for s, u in zip(smoothed, update)]
        rho = following
    return smoothed


def lane_index():
    return lax.broadcasted_iota(jnp.int32, (SUBS, LANES), 1)


def odd(axis):
    return lax.rem(lax.axis_index(axis), 2) == 1


def pack(planes, start):
    lane = lax.broadcasted_iota(jnp.int32, planes[0].shape, 1)
    packed = [None] * (-(-len(planes) // SLOTS))
    for p, plane in enumerate(planes):
        slot = p % SLOTS
        by = (slot * SLOT - start) % LANES
        moved = pltpu.roll(plane, by, 1) if by else plane
        k = p // SLOTS
        packed[k] = moved if slot == 0 else jnp.where(lane < slot * SLOT, packed[k], moved)
    return packed


def own_kernel(
    offsets_hbm, src_hbm, weight_hbm, seam_right_hbm, seam_down_hbm,
    own_ref, first_rows_ref, second_rows_ref, first_cols_ref, second_cols_ref,
    offsets_ref, src_ref, weight_ref, seam_right_ref, seam_down_ref, sems,
):
    chans, rows, cols = src_ref.shape
    own_tiles = cols // LANES
    moves = [(weight_hbm, weight_ref), (seam_right_hbm, seam_right_ref), (seam_down_hbm, seam_down_ref)]
    moves += [(src_hbm.at[c], src_ref.at[c]) for c in range(chans)] + [(offsets_hbm, offsets_ref)]
    copies = [pltpu.make_async_copy(there, here, sems.at[k]) for k, (there, here) in enumerate(moves)]
    for copy in copies:
        copy.start()
    row = lax.broadcasted_iota(jnp.int32, (rows, LANES), 0)
    lane = lax.broadcasted_iota(jnp.int32, (rows, LANES), 1)
    sub = lax.broadcasted_iota(jnp.int32, (SUBS, LANES), 0)
    row_at, col_at = lax.axis_index("row"), lax.axis_index("col")
    last_row = jnp.where(row_at == lax.axis_size("row") - 1, rows - 1, -1)
    last_lane = jnp.where(col_at == lax.axis_size("col") - 1, LANES - 1, -1)
    tile_row, tile_at = lax.div(row_at * rows, TILE), col_at * (cols // TILE)
    odd_row, odd_col = odd("row"), odd("col")

    def tile(ref, j):
        return ref[:, j * LANES:(j + 1) * LANES]

    copies[0].wait()
    for j in range(own_tiles):
        own_ref[chans, j] = tile(weight_ref, j)
    copies[1].wait()
    for j in range(own_tiles):
        value = 1.0 - seam_damping * tile(seam_right_ref, j).astype(jnp.float32)
        own_ref[chans + 1, j] = jnp.where(lane == last_lane, 0.0, value) if j == own_tiles - 1 else value
    copies[2].wait()
    for j in range(own_tiles):
        value = 1.0 - seam_damping * tile(seam_down_ref, j).astype(jnp.float32)
        own_ref[chans + 2, j] = jnp.where(row == last_row, 0.0, value)
    copies[-1].wait()
    for c in range(chans):
        shift = [
            jnp.broadcast_to(offsets_ref[c, tile_row, tile_at + k], (rows, LANES)).astype(jnp.float32) / offset_unit
            for k in range(cols // TILE)
        ]
        copies[3 + c].wait()
        for j in range(own_tiles):
            own_ref[c, j] = tile(src_ref.at[c], j) + shift[j * LANES // TILE]

    planes = range(chans + 3)

    def low_rows(ref):
        for p in planes:
            ref[p] = own_ref[p, :, 0:HALO, :]

    def high_rows(ref):
        at = rows - HALO
        for p in planes:
            ref[p] = own_ref[p, :, at:rows, :]
        for j in range(own_tiles):
            above = jnp.where(sub == 0, own_ref[chans + 2, j, at - 1:at, :], 0.0)
            ref[chans, j, 0:SUBS, :] = own_ref[chans, j, at:at + SUBS, :] + above

    @pl.when(odd_row)
    def _():
        low_rows(first_rows_ref)
        high_rows(second_rows_ref)

    @pl.when(jnp.logical_not(odd_row))
    def _():
        high_rows(first_rows_ref)
        low_rows(second_rows_ref)

    left = pack([own_ref[p, 0] for p in planes], 0)
    right = pack([own_ref[p, own_tiles - 1] for p in planes], LANES - SLOT)
    for k, (a, b) in enumerate(zip(left, right)):
        first_cols_ref[k] = jnp.where(odd_col, a, b)
        second_cols_ref[k] = jnp.where(odd_col, b, a)


def corners_kernel(chans, first_ref, second_ref, first_out, second_out):
    rows = first_ref.shape[1]
    odd_row, odd_col = odd("row"), odd("col")
    sub = lax.broadcasted_iota(jnp.int32, (SUBS, LANES), 0)
    lane = lane_index()
    weight, down = chans, chans + 2
    slot = weight % SLOTS
    at = rows - HALO
    for side, (in_odd, in_even) in enumerate(((first_ref, second_ref), (second_ref, first_ref))):

        def tile(k, low, count=SUBS, in_odd=in_odd, in_even=in_even):
            return jnp.where(odd_col, in_odd[k, low:low + count, :], in_even[k, low:low + count, :])

        above = jnp.broadcast_to(tile(down // SLOTS, at - 1, 1), (SUBS, LANES))
        above = pltpu.roll(above, (slot - down % SLOTS) % SLOTS * SLOT, 1)
        own_slot = jnp.logical_and(lane >= slot * SLOT, lane < (slot + 1) * SLOT)
        above = jnp.where(jnp.logical_and(sub == 0, own_slot), above, 0.0)
        for k in range(first_ref.shape[0]):
            for low in range(0, HALO, SUBS):
                near = tile(k, low)
                far = tile(k, at + low)
                if low == 0 and k == weight // SLOTS:
                    far = far + above
                first_out[side, k, low:low + SUBS, :] = jnp.where(odd_row, near, far)
                second_out[side, k, low:low + SUBS, :] = jnp.where(odd_row, far, near)


def unpack(p, lefts, rights):
    lane = lax.broadcasted_iota(jnp.int32, lefts.shape, 1)
    slot = p % SLOTS
    if slot != SLOTS - 1:
        lefts = pltpu.roll(lefts, LANES - SLOT - slot * SLOT, 1)
    if slot:
        rights = pltpu.roll(rights, LANES - slot * SLOT, 1)
    return jnp.where(lane < SLOT, rights, jnp.where(lane >= LANES - SLOT, lefts, 0.0))


def ways_of(tiles):
    return WAYS if tiles % WAYS == 0 else 1


def split(value, count):
    parts = []
    for k in range(count):
        part = value.astype(jnp.bfloat16)
        parts.append(part)
        if k + 1 < count:
            value = value - part.astype(jnp.float32)
    return jnp.concatenate(parts, axis=0)


def permuted(value, index, count):
    rows = value.shape[0]
    out = jnp.dot(split(value, count), index, preferred_element_type=jnp.float32)
    total = out[:rows]
    for k in range(1, count):
        total = total + out[k * rows:(k + 1) * rows]
    return total


def dealing(ways):
    size = ways * LANES
    column = lax.broadcasted_iota(jnp.int32, (size, size), 0)
    place = lax.broadcasted_iota(jnp.int32, (size, size), 1)
    return jnp.where(column == ways * (place % LANES) + place // LANES, 1.0, 0.0).astype(jnp.bfloat16)


def undealing(ways):
    size = ways * LANES
    column = lax.broadcasted_iota(jnp.int32, (size, size), 1)
    place = lax.broadcasted_iota(jnp.int32, (size, size), 0)
    return jnp.where(column == ways * (place % LANES) + place // LANES, 1.0, 0.0).astype(jnp.bfloat16)


def deal(tile_of, low, high, ways, emit):
    matrix = dealing(ways) if ways > 1 else None
    for g in range(low, high, ways):
        if ways == 1:
            emit(g, tile_of(g))
            continue
        value = permuted(jnp.concatenate([tile_of(g + m) for m in range(ways)], axis=1), matrix, 3)
        for m in range(ways):
            emit(g + m, value[:, m * LANES:(m + 1) * LANES])


def inner_dealt_kernel(own_ref, dealt_ref):
    planes, own_tiles, rows = own_ref.shape[:3]

    def emit(j, value):
        dealt_ref[:, j] = value.reshape(planes, rows, LANES)

    deal(lambda j: own_ref[:, j].reshape(planes * rows, LANES), 0, dealt_ref.shape[1], ways_of(own_tiles + 1), emit)


def outer_dealt_kernel(own_ref, first_ref, second_ref, dealt_ref):
    planes, own_tiles, rows = own_ref.shape[:3]
    tiles = own_tiles + 1
    low = tiles - dealt_ref.shape[1]
    odd_col = odd("col")

    def tile_of(j):
        if j < own_tiles:
            return own_ref[:, j].reshape(planes * rows, LANES)
        parts = []
        for p in range(planes):
            first, second = first_ref[p // SLOTS], second_ref[p // SLOTS]
            parts.append(unpack(p, jnp.where(odd_col, first, second), jnp.where(odd_col, second, first)))
        return jnp.concatenate(parts, axis=0)

    def emit(j, value):
        dealt_ref[:, j - low] = value.reshape(planes, rows, LANES)

    deal(tile_of, low, tiles, ways_of(tiles), emit)


def rightward(values):
    tiles = len(values)
    ways = ways_of(tiles)
    last = lane_index() == LANES - 1
    ahead = {g: pltpu.roll(values[g], LANES - 1, 1) for g in range(0, tiles, ways)}
    out = []
    for j in range(tiles):
        if j % ways + 1 < ways:
            out.append(values[j + 1])
        else:
            g = j - ways + 1
            out.append(jnp.where(last, ahead[(g + ways) % tiles], ahead[g]))
    return out


def leftward(values):
    tiles = len(values)
    ways = ways_of(tiles)
    first = lane_index() == 0
    behind = {g: pltpu.roll(values[g + ways - 1], 1, 1) for g in range(0, tiles, ways)}
    out = []
    for j in range(tiles):
        if j % ways:
            out.append(values[j - 1])
        else:
            out.append(jnp.where(first, behind[(j - ways) % tiles], behind[j]))
    return out


def spread(b_right_ref, b_down_ref, z_ref, emit):
    tiles, height = z_ref.shape[:2]
    steps = height // SUBS
    ways = ways_of(tiles)
    lane = lane_index()
    first, last = (lane == 0, lane == LANES - 1)

    def at(i):
        return pl.ds(i * SUBS, SUBS)

    from_above = [pltpu.roll(b_down_ref[j, at(steps - 1), :] * z_ref[j, at(steps - 1), :], 1, 0) for j in range(tiles)]
    centre = [z_ref[j, at(0), :] for j in range(tiles)]
    wrapped = [pltpu.roll(v, SUBS - 1, 0) for v in centre]
    for i in range(steps):
        pushed_out = {
            g: pltpu.roll(b_right_ref[g + ways - 1, at(i), :] * centre[g + ways - 1], 1, 1)
            for g in range(0, tiles, ways)
        }
        ahead = {g: pltpu.roll(centre[g], LANES - 1, 1) for g in range(0, tiles, ways)}
        pushed = None
        below = []
        for j in range(tiles):
            g = j // ways * ways
            b_right = b_right_ref[j, at(i), :]
            b_down = b_down_ref[j, at(i), :]
            below.append(z_ref[j, at(i + 1), :] if i + 1 < steps else wrapped[j])
            if j == g:
                from_left = jnp.where(first, pushed_out[(g - ways) % tiles], pushed_out[g])
            else:
                from_left = pushed
            if j + 1 < g + ways:
                to_right = centre[j + 1]
                pushed = b_right * centre[j]
            else:
                to_right = jnp.where(last, ahead[(g + ways) % tiles], ahead[g])
            moved = (b_right * to_right + from_left) + (b_down * below[j] + from_above[j])
            from_above[j] = b_down * centre[j]
            emit(i, j, centre[j], moved)
        centre = below


def precondition(b_right_ref, b_down_ref, g_ref, z_ref, work_ref):
    poly = chebyshev_polynomial()
    degree = SWEEPS - 1

    def at(i):
        return pl.ds(i * SUBS, SUBS)

    def first(i, j, centre, moved):
        z_ref[j, at(i), :] = poly[degree] * moved + poly[degree - 1] * centre

    spread(b_right_ref, b_down_ref, g_ref, first)

    def pair(k, carry):
        adds = []
        for half in range(2):
            value = jnp.float32(poly[half])
            for later in range(1, (degree - 1) // 2):
                value = jnp.where(k == (degree - 1) // 2 - 1 - later, jnp.float32(poly[2 * later + half]), value)
            adds.append(value)

        def one(target, add):
            def emit(i, j, centre, moved):
                target[j, at(i), :] = moved + add * g_ref[j, at(i), :]

            return emit

        spread(b_right_ref, b_down_ref, z_ref, one(work_ref, adds[1]))
        spread(b_right_ref, b_down_ref, work_ref, one(z_ref, adds[0]))
        return carry

    lax.fori_loop(0, (degree - 1) // 2, pair, 0)


def next_residual(b_right_ref, b_down_ref, g_ref, z_ref, next_ref, own_of):
    height = g_ref.shape[1]
    steps = height // SUBS
    sums = {}

    def emit(i, j, centre, moved):
        at = pl.ds(i * SUBS, SUBS)
        g = g_ref[j, at, :]
        following = g - MIX * (centre - moved)
        next_ref[j, at, :] = following
        key = own_of(i, j)
        now = (g * centre, following * centre)
        before = sums.get(key)
        sums[key] = now if before is None else (before[0] + now[0], before[1] + now[1])

    spread(b_right_ref, b_down_ref, z_ref, emit)
    sub = lax.broadcasted_iota(jnp.int32, (SUBS, LANES), 0)
    lane = lane_index()
    total = [jnp.zeros((SUBS, LANES), jnp.float32)] * 2
    for (low, high, lanes), parts in sums.items():
        inside = jnp.logical_and(jnp.logical_and(sub >= low, sub <= high), lane < lanes)
        total = [t + jnp.where(inside, p, 0.0) for t, p in zip(total, parts)]
    return total


def first_kernel(
    inner_ref, outer_ref, second_rows_ref, first_rows_ref, second_corners_ref, first_corners_ref,
    b_right_ref, b_down_ref, scale_ref, root_ref, g0_ref, z0_ref, g1_ref, f1_ref, g2_ref, sums_ref,
    first_late_ref, second_late_ref,
    natural, work_ref,
):
    planes, inner, rows = inner_ref.shape[:3]
    tiles = inner + outer_ref.shape[1]
    chans = planes - 3
    own_tiles = tiles - 1
    height = rows + 2 * HALO
    steps = height // SUBS

    for p in range(planes):
        for j in range(tiles):
            natural[p, j, HALO:HALO + rows, :] = inner_ref[p, j] if j < inner else outer_ref[p, j - inner]
    odd_row = odd("row")

    def edge_tile(j):
        if j < own_tiles:
            first, second = [ref[:, j].reshape(planes * HALO, LANES) for ref in (first_rows_ref, second_rows_ref)]
        else:
            first, second = [
                jnp.concatenate([unpack(p, ref[0, p // SLOTS], ref[1, p // SLOTS]) for p in range(planes)], axis=0)
                for ref in (first_corners_ref, second_corners_ref)
            ]
        return jnp.concatenate([jnp.where(odd_row, first, second), jnp.where(odd_row, second, first)], axis=0)

    def put_edge(j, value):
        value = value.reshape(2, planes, HALO, LANES)
        natural[:, j, 0:HALO, :] = value[0]
        natural[:, j, HALO + rows:height, :] = value[1]

    deal(edge_tile, 0, tiles, ways_of(tiles), put_edge)

    def at(i):
        return pl.ds(i * SUBS, SUBS)

    def interleaved(p, i, j):
        return natural[p, j, pl.ds(i, SUBS, stride=steps), :]

    sub = lax.broadcasted_iota(jnp.int32, (SUBS, LANES), 0)
    to_up = [
        jnp.where(sub == 0, 0.0, pltpu.roll(interleaved(chans + 2, steps - 1, j), 1, 0)) for j in range(tiles)
    ]
    for i in range(steps):
        to_right = [interleaved(chans + 1, i, j) for j in range(tiles)]
        to_left = leftward(to_right)
        for j in range(tiles):
            to_down = interleaved(chans + 2, i, j)
            diag = interleaved(chans, i, j) + to_right[j] + to_left[j] + to_down + to_up[j]
            inside = diag > 0.0
            safe = jnp.where(inside, diag, 1.0)
            guess = lax.rsqrt(safe)
            scale = guess * (1.5 - 0.5 * safe * guess * guess)
            scale_ref[j, at(i), :] = jnp.where(inside, scale, 0.0)
            root_ref[j, at(i), :] = safe * scale
            to_up[j] = to_down
    wrapped = [pltpu.roll(scale_ref[j, at(0), :], SUBS - 1, 0) for j in range(tiles)]
    for i in range(steps):
        scale = [scale_ref[j, at(i), :] for j in range(tiles)]
        right_scale = rightward(scale)
        for j in range(tiles):
            b_right_ref[j, at(i), :] = interleaved(chans + 1, i, j) * scale[j] * right_scale[j]
            down_scale = scale_ref[j, at(i + 1), :] if i + 1 < steps else wrapped[j]
            b_down_ref[j, at(i), :] = interleaved(chans + 2, i, j) * scale[j] * down_scale
            for c in range(chans):
                g0_ref[c, j, at(i), :] = interleaved(c, i, j) * scale[j]

    ways = ways_of(tiles)

    def own_of(i, j):
        low, high = -(-(HALO - i) // steps), (HALO + rows - 1 - i) // steps
        left = own_tiles * LANES - j // ways * ways * LANES - j % ways
        return low, high, min(LANES, max(0, -(-left // ways)))

    def channel(c, carry):
        g0, z0, g1, f1, g2 = [ref.at[c] for ref in (g0_ref, z0_ref, g1_ref, f1_ref, g2_ref)]
        precondition(b_right_ref, b_down_ref, g0, z0, work_ref)
        sum0, sum1 = next_residual(b_right_ref, b_down_ref, g0, z0, g1, own_of)
        precondition(b_right_ref, b_down_ref, g1, f1, work_ref)
        sum2, sum3 = next_residual(b_right_ref, b_down_ref, g1, f1, g2, own_of)
        return tuple(a + b for a, b in zip(carry, (sum0, sum1, sum2, sum3)))

    zero = jnp.zeros((SUBS, LANES), jnp.float32)
    parts = lax.fori_loop(0, chans, channel, (zero,) * 4)
    sums = zero
    for k, part in enumerate(parts):
        sums = jnp.where(sub == k, jnp.sum(part), sums)
    sums_ref[...] = sums
    first_late_ref[chans * tiles] = sums

    def edge(c, j, at):
        s, i = divmod(HALO + at, steps)
        return g2_ref[c, j, pl.ds(i * SUBS + s, LATE, stride=SUBS), :]

    for c in range(chans):
        for j in range(tiles):
            low, high = edge(c, j, 0), edge(c, j, rows - LATE)
            first_late_ref[c * tiles + j] = jnp.where(odd_row, low, high)
            second_late_ref[c * tiles + j] = jnp.where(odd_row, high, low)


def second_kernel(
    c, first_late_ref, second_late_ref, b_right_ref, b_down_ref, g2_ref, f2_ref, g_ref, work_ref
):
    tiles, height = b_right_ref.shape[:2]
    rows = height - 2 * HALO
    steps = height // SUBS
    odd_row = odd("row")
    for j in range(tiles):
        g_ref[j] = g2_ref[c, j]
        first, second = first_late_ref[c * tiles + j], second_late_ref[c * tiles + j]
        for value, at in ((jnp.where(odd_row, first, second), HALO - LATE), (jnp.where(odd_row, second, first), HALO + rows)):
            done = 0
            while done < LATE:
                s, i = divmod(at + done, steps)
                count = min(LATE - done, steps - i)
                g_ref[j, pl.ds(i * SUBS + s, count, stride=SUBS), :] = value[done:done + count]
                done += count
    precondition(b_right_ref, b_down_ref, g_ref, f2_ref, work_ref)


def combine(n0, n1, n2, n3):
    gap = n0 - n1
    keep = -n1 / gap
    step = n0 / gap
    beta = (n0 * n2 - n1 * n1) / (gap * gap)
    along = keep + beta
    curvature = along * along * gap + 2.0 * along * step * (n1 - n2) + step * step * (n2 - n3)
    scaled = n0 * beta / curvature
    first_size = step * MIX
    second_size = scaled * MIX
    x0 = first_size + second_size * along
    x1 = second_size * step
    r0 = keep - scaled * along
    r1 = step + scaled * (along - step)
    r2 = scaled * step
    return x0, x1, r0, r1, r2


def third_kernel(
    sums_ref, scale_ref, root_ref, g0_ref, z0_ref, g1_ref, f1_ref, g2_ref, *refs
):
    *f2_refs, solution_hbm, residual_hbm, smoothed_hbm, natural, done, sems = refs
    rows, cols = solution_hbm.shape[1:]
    own_tiles = cols // LANES
    tiles, height = scale_ref.shape[:2]
    steps = height // SUBS
    ways = ways_of(tiles)
    x0, x1, r0, r1, r2 = combine(*[jnp.broadcast_to(sums_ref[k:k + 1, :], (SUBS, LANES)) for k in range(4)])
    matrix = undealing(ways) if ways > 1 else None
    outs = (solution_hbm, residual_hbm, smoothed_hbm)
    copies = []
    for c, f2_ref in enumerate(f2_refs):
        for j in range(tiles):
            for i in range(steps):
                at = pl.ds(i * SUBS, SUBS)
                scale = scale_ref[j, at, :]
                root = root_ref[j, at, :]
                g0, g1, g2, z0, f1 = [ref[c, j, at, :] for ref in (g0_ref, g1_ref, g2_ref, z0_ref, f1_ref)]
                f2 = f2_ref[j, at, :]
                there = pl.ds(i, SUBS, stride=steps)
                natural[c, 0, j, there, :] = scale * (x0 * z0 + x1 * f1)
                natural[c, 1, j, there, :] = root * (r0 * g0 + r1 * g1 + r2 * g2)
                natural[c, 2, j, there, :] = scale * (r0 * z0 + r1 * f1 + r2 * f2)
        for g in range(0, own_tiles, ways):
            value = jnp.concatenate(
                [natural[c, :, g + m, HALO:HALO + rows, :].reshape(3 * rows, LANES) for m in range(ways)], axis=1
            )
            width = min(ways, own_tiles - g) * LANES
            if ways > 1:
                value = permuted(value, matrix[:, :width], 2)
            for k in range(len(outs)):
                done[c, k, :, g * LANES:g * LANES + width] = value[k * rows:(k + 1) * rows]
        for k, ref in enumerate(outs):
            copies.append(pltpu.make_async_copy(done.at[c, k], ref.at[c], sems.at[c, k]))
            copies[-1].start()
    for copy in copies:
        copy.wait()


def sum_over(value, rounds, beside):
    done = []
    for k, (axis, bits) in enumerate(rounds):
        size = lax.axis_size(axis)
        others = [
            lax.ppermute(value, axis, [(i, i ^ mask) for i in range(size)])
            for mask in ((bits[0],) if len(bits) == 1 else (bits[0], bits[1], bits[0] | bits[1]))
        ]
        left = len(rounds) - k
        if left <= len(beside):
            now = beside[len(done):] if left == 1 else beside[len(done):len(done) + 1]
            value, *arrays = lax.optimization_barrier((value, *now))
            done += arrays
        value = value + others[0]
        if len(others) > 1:
            value = value + (others[1] + others[2])
    return value, done + list(beside[len(done):])


def per_device(source, weight, seam_right, seam_down, offsets):
    chans, rows, cols = source.shape
    row_axis, col_axis = lax.axis_size("row"), lax.axis_size("col")
    in_vmem = pl.BlockSpec(memory_space=pltpu.VMEM)
    in_hbm = pl.BlockSpec(memory_space=pltpu.HBM)
    params = pltpu.CompilerParams(vmem_limit_bytes=VMEM_LIMIT)

    def shaped(*shape):
        return jax.ShapeDtypeStruct(shape, jnp.float32)

    def scratch(*shape):
        return pltpu.VMEM(shape, jnp.float32)

    planes = chans + 3
    own_tiles = cols // LANES
    tiles = own_tiles + 1
    packs = -(-planes // SLOTS)
    own, first_rows, second_rows, first_cols, second_cols = pl.pallas_call(
        own_kernel,
        out_shape=[shaped(planes, own_tiles, rows, LANES)]
        + [shaped(planes, own_tiles, HALO, LANES)] * 2
        + [shaped(packs, rows, LANES)] * 2,
        in_specs=[in_hbm] * 5,
        out_specs=[in_vmem] * 5,
        scratch_shapes=[
            pltpu.SMEM((chans,) + offsets.shape[:2], jnp.int32),
            scratch(*source.shape),
            scratch(*weight.shape),
            pltpu.VMEM(weight.shape, jnp.int32),
            pltpu.VMEM(weight.shape, jnp.int32),
            pltpu.SemaphoreType.DMA((planes + 1,)),
        ],
        compiler_params=params,
    )(
        *[
            pltpu.with_memory_space_constraint(v, pltpu.HBM)
            for v in (offsets.transpose(2, 0, 1), source, weight, seam_right, seam_down)
        ],
    )

    def swap(first, second, axis, order):
        size = lax.axis_size(axis)
        pairs = [[(i, i + 1) for i in range(start, size - 1, 2)] for start in range(2)]
        pairs = [some + [(j, i) for i, j in some] for some in pairs]
        received = {k: lax.ppermute((first, second)[k], axis, pairs[k]) for k in order}
        return received[0], received[1]

    ways = ways_of(tiles)
    inner = pl.pallas_call(
        inner_dealt_kernel,
        out_shape=shaped(planes, tiles - ways, rows, LANES),
        in_specs=[in_vmem],
        out_specs=in_vmem,
        compiler_params=params,
        cost_estimate=pl.CostEstimate(flops=10**8, bytes_accessed=4 * 10**6, transcendentals=0),
    )(own)
    first_rows, second_rows = swap(first_rows, second_rows, "row", (1, 0))
    first_cols, second_cols = swap(first_cols, second_cols, "col", (0, 1))
    first_cols, second_cols, inner = lax.optimization_barrier((first_cols, second_cols, inner))
    corners = pl.pallas_call(
        functools.partial(corners_kernel, chans),
        out_shape=[shaped(2, packs, HALO, LANES)] * 2,
        in_specs=[in_vmem] * 2,
        out_specs=[in_vmem] * 2,
        compiler_params=params,
    )(first_cols, second_cols)
    first_corners, second_corners = swap(*corners, "row", (1, 0))
    outer = pl.pallas_call(
        outer_dealt_kernel,
        out_shape=shaped(planes, ways, rows, LANES),
        in_specs=[in_vmem] * 3,
        out_specs=in_vmem,
        compiler_params=params,
        cost_estimate=pl.CostEstimate(flops=10**8, bytes_accessed=2 * 10**6, transcendentals=0),
    )(own, first_cols, second_cols)

    height = rows + 2 * HALO
    plane = shaped(tiles, height, LANES)
    field = shaped(chans, tiles, height, LANES)
    lates = [shaped(chans * tiles + extra, LATE, LANES) for extra in (1, 0)]
    *basis, sums, first_late, second_late = pl.pallas_call(
        first_kernel,
        out_shape=[plane] * 4 + [field] * 5 + [shaped(SUBS, LANES)] + lates,
        in_specs=[in_vmem] * 6,
        out_specs=[in_vmem] * 12,
        scratch_shapes=[scratch(planes, tiles, height, LANES), scratch(*plane.shape)],
        compiler_params=params,
    )(inner, outer, second_rows, first_rows, second_corners, first_corners)

    first_late, second_late = swap(first_late, second_late, "row", (0, 1))

    b_right, b_down, scale, root, g0, z0, g1, f1, g2 = basis
    f2 = [
        pl.pallas_call(
            functools.partial(second_kernel, c),
            out_shape=plane,
            in_specs=[in_vmem] * 5,
            out_specs=in_vmem,
            scratch_shapes=[scratch(*plane.shape)] * 2,
            compiler_params=params,
            cost_estimate=pl.CostEstimate(flops=10**8, bytes_accessed=10**7, transcendentals=0),
        )(first_late, second_late, b_right, b_down, g2)
        for c in range(chans)
    ]
    if row_axis & (row_axis - 1) or col_axis & (col_axis - 1):
        total = lax.psum(sums, ("row", "col"))
    else:
        rounds = []
        for axis, size, low in (("row", row_axis, 1), ("col", col_axis, 0)):
            bits = [1 << k for k in range(low, size.bit_length() - 1)]
            rounds += [(axis, bits[k:k + 2]) for k in range(0, len(bits), 2)]
        if row_axis > 1:
            sums = sums + first_late[chans * tiles]
        total, f2 = sum_over(sums, rounds, f2)
    return pl.pallas_call(
        third_kernel,
        out_shape=[shaped(chans, rows, cols)] * 3,
        in_specs=[in_vmem] * (8 + chans),
        out_specs=[pl.BlockSpec(memory_space=pltpu.HBM)] * 3,
        scratch_shapes=[
            scratch(chans, 3, tiles, height, LANES),
            scratch(chans, 3, rows, cols),
            pltpu.SemaphoreType.DMA((chans, 3)),
        ],
        compiler_params=params,
    )(total, scale, root, g0, z0, g1, f1, g2, *f2)


def solution(mesh):
    placed = (
        P(None, ("band", "row"), "col"),
        P(("band", "row"), "col"),
        P(("band", "row"), "col"),
        P(("band", "row"), "col"),
        P("band", None, None),
    )
    return jax.shard_map(
        per_device,
        mesh=mesh,
        in_specs=placed,
        out_specs=(
            P(None, ("band", "row"), "col"),
            P(None, ("band", "row"), "col"),
            P(None, ("band", "row"), "col"),
        ),
        check_vma=False,
    )
```

```python
import functools

import jax
import jax.numpy as jnp
from jax import lax
from jax.experimental import pallas as pl
from jax.experimental.pallas import tpu as pltpu
from jax.sharding import PartitionSpec as P

TILE = 256
SWEEPS = 8
SUBS = 8
LANES = 128
HALO = 16
LATE = 8
SLOT = 32
SLOTS = LANES // SLOT
WAYS = 3

seam_damping = 0.8
offset_unit = 32.0
spectrum_low = 0.08
spectrum_high = 2.0
MIX = 2.4

VMEM_LIMIT = 28 * 1024 * 1024


def chebyshev_polynomial():
    centre = (spectrum_high + spectrum_low) / 2.0
    radius = (spectrum_high - spectrum_low) / 2.0
    sigma = centre / radius
    size = SWEEPS
    update = [1.0 / centre] + [0.0] * (size - 1)
    smoothed = list(update)
    rho = 1.0 / sigma
    for _ in range(SWEEPS - 1):
        remainder = [-s for s in smoothed]
        remainder[0] += 1.0
        for k in range(size - 1):
            remainder[k + 1] += smoothed[k]
        following = 1.0 / (2.0 * sigma - rho)
        update = [following * rho * u + 2.0 * following / radius * r for u, r in zip(update, remainder)]
        smoothed = [s + u for s, u in zip(smoothed, update)]
        rho = following
    return smoothed


def lane_index():
    return lax.broadcasted_iota(jnp.int32, (SUBS, LANES), 1)


def odd(axis):
    return lax.rem(lax.axis_index(axis), 2) == 1


def pack(planes, start):
    lane = lax.broadcasted_iota(jnp.int32, planes[0].shape, 1)
    packed = [None] * (-(-len(planes) // SLOTS))
    for p, plane in enumerate(planes):
        slot = p % SLOTS
        by = (slot * SLOT - start) % LANES
        moved = pltpu.roll(plane, by, 1) if by else plane
        k = p // SLOTS
        packed[k] = moved if slot == 0 else jnp.where(lane < slot * SLOT, packed[k], moved)
    return packed


def own_kernel(
    offsets_hbm, src_hbm, weight_hbm, seam_right_hbm, seam_down_hbm,
    own_ref, first_rows_ref, second_rows_ref, first_cols_ref, second_cols_ref,
    offsets_ref, src_ref, weight_ref, seam_right_ref, seam_down_ref, sems,
):
    chans, rows, cols = src_ref.shape
    own_tiles = cols // LANES
    moves = [(weight_hbm, weight_ref), (seam_right_hbm, seam_right_ref), (seam_down_hbm, seam_down_ref)]
    moves += [(src_hbm.at[c], src_ref.at[c]) for c in range(chans)] + [(offsets_hbm, offsets_ref)]
    copies = [pltpu.make_async_copy(there, here, sems.at[k]) for k, (there, here) in enumerate(moves)]
    for copy in copies:
        copy.start()
    row = lax.broadcasted_iota(jnp.int32, (rows, LANES), 0)
    lane = lax.broadcasted_iota(jnp.int32, (rows, LANES), 1)
    sub = lax.broadcasted_iota(jnp.int32, (SUBS, LANES), 0)
    row_at, col_at = lax.axis_index("row"), lax.axis_index("col")
    last_row = jnp.where(row_at == lax.axis_size("row") - 1, rows - 1, -1)
    last_lane = jnp.where(col_at == lax.axis_size("col") - 1, LANES - 1, -1)
    tile_row, tile_at = lax.div(row_at * rows, TILE), col_at * (cols // TILE)
    odd_row, odd_col = odd("row"), odd("col")

    def tile(ref, j):
        return ref[:, j * LANES:(j + 1) * LANES]

    copies[0].wait()
    for j in range(own_tiles):
        own_ref[chans, j] = tile(weight_ref, j)
    copies[1].wait()
    for j in range(own_tiles):
        value = 1.0 - seam_damping * tile(seam_right_ref, j).astype(jnp.float32)
        own_ref[chans + 1, j] = jnp.where(lane == last_lane, 0.0, value) if j == own_tiles - 1 else value
    copies[2].wait()
    for j in range(own_tiles):
        value = 1.0 - seam_damping * tile(seam_down_ref, j).astype(jnp.float32)
        own_ref[chans + 2, j] = jnp.where(row == last_row, 0.0, value)
    copies[-1].wait()
    for c in range(chans):
        shift = [
            jnp.broadcast_to(offsets_ref[c, tile_row, tile_at + k], (rows, LANES)).astype(jnp.float32) / offset_unit
            for k in range(cols // TILE)
        ]
        copies[3 + c].wait()
        for j in range(own_tiles):
            own_ref[c, j] = tile(src_ref.at[c], j) + shift[j * LANES // TILE]

    planes = range(chans + 3)

    def low_rows(ref):
        for p in planes:
            ref[p] = own_ref[p, :, 0:HALO, :]

    def high_rows(ref):
        at = rows - HALO
        for p in planes:
            ref[p] = own_ref[p, :, at:rows, :]
        for j in range(own_tiles):
            above = jnp.where(sub == 0, own_ref[chans + 2, j, at - 1:at, :], 0.0)
            ref[chans, j, 0:SUBS, :] = own_ref[chans, j, at:at + SUBS, :] + above

    @pl.when(odd_row)
    def _():
        low_rows(first_rows_ref)
        high_rows(second_rows_ref)

    @pl.when(jnp.logical_not(odd_row))
    def _():
        high_rows(first_rows_ref)
        low_rows(second_rows_ref)

    left = pack([own_ref[p, 0] for p in planes], 0)
    right = pack([own_ref[p, own_tiles - 1] for p in planes], LANES - SLOT)
    for k, (a, b) in enumerate(zip(left, right)):
        first_cols_ref[k] = jnp.where(odd_col, a, b)
        second_cols_ref[k] = jnp.where(odd_col, b, a)


def corners_kernel(chans, first_ref, second_ref, first_out, second_out):
    rows = first_ref.shape[1]
    odd_row, odd_col = odd("row"), odd("col")
    sub = lax.broadcasted_iota(jnp.int32, (SUBS, LANES), 0)
    lane = lane_index()
    weight, down = chans, chans + 2
    slot = weight % SLOTS
    at = rows - HALO
    for side, (in_odd, in_even) in enumerate(((first_ref, second_ref), (second_ref, first_ref))):

        def tile(k, low, count=SUBS, in_odd=in_odd, in_even=in_even):
            return jnp.where(odd_col, in_odd[k, low:low + count, :], in_even[k, low:low + count, :])

        above = jnp.broadcast_to(tile(down // SLOTS, at - 1, 1), (SUBS, LANES))
        above = pltpu.roll(above, (slot - down % SLOTS) % SLOTS * SLOT, 1)
        own_slot = jnp.logical_and(lane >= slot * SLOT, lane < (slot + 1) * SLOT)
        above = jnp.where(jnp.logical_and(sub == 0, own_slot), above, 0.0)
        for k in range(first_ref.shape[0]):
            for low in range(0, HALO, SUBS):
                near = tile(k, low)
                far = tile(k, at + low)
                if low == 0 and k == weight // SLOTS:
                    far = far + above
                first_out[side, k, low:low + SUBS, :] = jnp.where(odd_row, near, far)
                second_out[side, k, low:low + SUBS, :] = jnp.where(odd_row, far, near)


def unpack(p, lefts, rights):
    lane = lax.broadcasted_iota(jnp.int32, lefts.shape, 1)
    slot = p % SLOTS
    if slot != SLOTS - 1:
        lefts = pltpu.roll(lefts, LANES - SLOT - slot * SLOT, 1)
    if slot:
        rights = pltpu.roll(rights, LANES - slot * SLOT, 1)
    return jnp.where(lane < SLOT, rights, jnp.where(lane >= LANES - SLOT, lefts, 0.0))


def ways_of(tiles):
    return WAYS if tiles % WAYS == 0 else 1


def split(value, count):
    parts = []
    for k in range(count):
        part = value.astype(jnp.bfloat16)
        parts.append(part)
        if k + 1 < count:
            value = value - part.astype(jnp.float32)
    return jnp.concatenate(parts, axis=0)


def permuted(value, index, count):
    rows = value.shape[0]
    out = jnp.dot(split(value, count), index, preferred_element_type=jnp.float32)
    total = out[:rows]
    for k in range(1, count):
        total = total + out[k * rows:(k + 1) * rows]
    return total


def dealing(ways):
    size = ways * LANES
    column = lax.broadcasted_iota(jnp.int32, (size, size), 0)
    place = lax.broadcasted_iota(jnp.int32, (size, size), 1)
    return jnp.where(column == ways * (place % LANES) + place // LANES, 1.0, 0.0).astype(jnp.bfloat16)


def undealing(ways):
    size = ways * LANES
    column = lax.broadcasted_iota(jnp.int32, (size, size), 1)
    place = lax.broadcasted_iota(jnp.int32, (size, size), 0)
    return jnp.where(column == ways * (place % LANES) + place // LANES, 1.0, 0.0).astype(jnp.bfloat16)


def deal(tile_of, low, high, ways, emit):
    matrix = dealing(ways) if ways > 1 else None
    for g in range(low, high, ways):
        if ways == 1:
            emit(g, tile_of(g))
            continue
        value = permuted(jnp.concatenate([tile_of(g + m) for m in range(ways)], axis=1), matrix, 3)
        for m in range(ways):
            emit(g + m, value[:, m * LANES:(m + 1) * LANES])


def inner_dealt_kernel(own_ref, dealt_ref):
    planes, own_tiles, rows = own_ref.shape[:3]

    def emit(j, value):
        dealt_ref[:, j] = value.reshape(planes, rows, LANES)

    deal(lambda j: own_ref[:, j].reshape(planes * rows, LANES), 0, dealt_ref.shape[1], ways_of(own_tiles + 1), emit)


def outer_dealt_kernel(own_ref, first_ref, second_ref, dealt_ref):
    planes, own_tiles, rows = own_ref.shape[:3]
    tiles = own_tiles + 1
    low = tiles - dealt_ref.shape[1]
    odd_col = odd("col")

    def tile_of(j):
        if j < own_tiles:
            return own_ref[:, j].reshape(planes * rows, LANES)
        parts = []
        for p in range(planes):
            first, second = first_ref[p // SLOTS], second_ref[p // SLOTS]
            parts.append(unpack(p, jnp.where(odd_col, first, second), jnp.where(odd_col, second, first)))
        return jnp.concatenate(parts, axis=0)

    def emit(j, value):
        dealt_ref[:, j - low] = value.reshape(planes, rows, LANES)

    deal(tile_of, low, tiles, ways_of(tiles), emit)


def rightward(values):
    tiles = len(values)
    ways = ways_of(tiles)
    last = lane_index() == LANES - 1
    ahead = {g: pltpu.roll(values[g], LANES - 1, 1) for g in range(0, tiles, ways)}
    out = []
    for j in range(tiles):
        if j % ways + 1 < ways:
            out.append(values[j + 1])
        else:
            g = j - ways + 1
            out.append(jnp.where(last, ahead[(g + ways) % tiles], ahead[g]))
    return out


def leftward(values):
    tiles = len(values)
    ways = ways_of(tiles)
    first = lane_index() == 0
    behind = {g: pltpu.roll(values[g + ways - 1], 1, 1) for g in range(0, tiles, ways)}
    out = []
    for j in range(tiles):
        if j % ways:
            out.append(values[j - 1])
        else:
            out.append(jnp.where(first, behind[(j - ways) % tiles], behind[j]))
    return out


def spread(b_right_ref, b_down_ref, z_ref, emit):
    tiles, height = z_ref.shape[:2]
    steps = height // SUBS
    ways = ways_of(tiles)
    lane = lane_index()
    first, last = (lane == 0, lane == LANES - 1)

    def at(i):
        return pl.ds(i * SUBS, SUBS)

    from_above = [pltpu.roll(b_down_ref[j, at(steps - 1), :] * z_ref[j, at(steps - 1), :], 1, 0) for j in range(tiles)]
    centre = [z_ref[j, at(0), :] for j in range(tiles)]
    wrapped = [pltpu.roll(v, SUBS - 1, 0) for v in centre]
    for i in range(steps):
        pushed_out = {
            g: pltpu.roll(b_right_ref[g + ways - 1, at(i), :] * centre[g + ways - 1], 1, 1)
            for g in range(0, tiles, ways)
        }
        ahead = {g: pltpu.roll(centre[g], LANES - 1, 1) for g in range(0, tiles, ways)}
        pushed = None
        below = []
        for j in range(tiles):
            g = j // ways * ways
            b_right = b_right_ref[j, at(i), :]
            b_down = b_down_ref[j, at(i), :]
            below.append(z_ref[j, at(i + 1), :] if i + 1 < steps else wrapped[j])
            if j == g:
                from_left = jnp.where(first, pushed_out[(g - ways) % tiles], pushed_out[g])
            else:
                from_left = pushed
            if j + 1 < g + ways:
                to_right = centre[j + 1]
                pushed = b_right * centre[j]
            else:
                to_right = jnp.where(last, ahead[(g + ways) % tiles], ahead[g])
            moved = (b_right * to_right + from_left) + (b_down * below[j] + from_above[j])
            from_above[j] = b_down * centre[j]
            emit(i, j, centre[j], moved)
        centre = below


def precondition(b_right_ref, b_down_ref, g_ref, z_ref, work_ref):
    poly = chebyshev_polynomial()
    degree = SWEEPS - 1

    def at(i):
        return pl.ds(i * SUBS, SUBS)

    def first(i, j, centre, moved):
        z_ref[j, at(i), :] = poly[degree] * moved + poly[degree - 1] * centre

    spread(b_right_ref, b_down_ref, g_ref, first)

    def pair(k, carry):
        adds = []
        for half in range(2):
            value = jnp.float32(poly[half])
            for later in range(1, (degree - 1) // 2):
                value = jnp.where(k == (degree - 1) // 2 - 1 - later, jnp.float32(poly[2 * later + half]), value)
            adds.append(value)

        def one(target, add):
            def emit(i, j, centre, moved):
                target[j, at(i), :] = moved + add * g_ref[j, at(i), :]

            return emit

        spread(b_right_ref, b_down_ref, z_ref, one(work_ref, adds[1]))
        spread(b_right_ref, b_down_ref, work_ref, one(z_ref, adds[0]))
        return carry

    lax.fori_loop(0, (degree - 1) // 2, pair, 0)


def next_residual(b_right_ref, b_down_ref, g_ref, z_ref, next_ref, own_of):
    height = g_ref.shape[1]
    steps = height // SUBS
    sums = {}

    def emit(i, j, centre, moved):
        at = pl.ds(i * SUBS, SUBS)
        g = g_ref[j, at, :]
        following = g - MIX * (centre - moved)
        next_ref[j, at, :] = following
        key = own_of(i, j)
        now = (g * centre, following * centre)
        before = sums.get(key)
        sums[key] = now if before is None else (before[0] + now[0], before[1] + now[1])

    spread(b_right_ref, b_down_ref, z_ref, emit)
    sub = lax.broadcasted_iota(jnp.int32, (SUBS, LANES), 0)
    lane = lane_index()
    total = [jnp.zeros((SUBS, LANES), jnp.float32)] * 2
    for (low, high, lanes), parts in sums.items():
        inside = jnp.logical_and(jnp.logical_and(sub >= low, sub <= high), lane < lanes)
        total = [t + jnp.where(inside, p, 0.0) for t, p in zip(total, parts)]
    return total


def first_kernel(
    inner_ref, outer_ref, second_rows_ref, first_rows_ref, second_corners_ref, first_corners_ref,
    b_right_ref, b_down_ref, scale_ref, root_ref, g0_ref, z0_ref, g1_ref, f1_ref, g2_ref, sums_ref,
    first_late_ref, second_late_ref,
    natural, work_ref,
):
    planes, inner, rows = inner_ref.shape[:3]
    tiles = inner + outer_ref.shape[1]
    chans = planes - 3
    own_tiles = tiles - 1
    height = rows + 2 * HALO
    steps = height // SUBS

    for p in range(planes):
        for j in range(tiles):
            natural[p, j, HALO:HALO + rows, :] = inner_ref[p, j] if j < inner else outer_ref[p, j - inner]
    odd_row = odd("row")

    def edge_tile(j):
        if j < own_tiles:
            first, second = [ref[:, j].reshape(planes * HALO, LANES) for ref in (first_rows_ref, second_rows_ref)]
        else:
            first, second = [
                jnp.concatenate([unpack(p, ref[0, p // SLOTS], ref[1, p // SLOTS]) for p in range(planes)], axis=0)
                for ref in (first_corners_ref, second_corners_ref)
            ]
        return jnp.concatenate([jnp.where(odd_row, first, second), jnp.where(odd_row, second, first)], axis=0)

    def put_edge(j, value):
        value = value.reshape(2, planes, HALO, LANES)
        natural[:, j, 0:HALO, :] = value[0]
        natural[:, j, HALO + rows:height, :] = value[1]

    deal(edge_tile, 0, tiles, ways_of(tiles), put_edge)

    def at(i):
        return pl.ds(i * SUBS, SUBS)

    def interleaved(p, i, j):
        return natural[p, j, pl.ds(i, SUBS, stride=steps), :]

    sub = lax.broadcasted_iota(jnp.int32, (SUBS, LANES), 0)
    to_up = [
        jnp.where(sub == 0, 0.0, pltpu.roll(interleaved(chans + 2, steps - 1, j), 1, 0)) for j in range(tiles)
    ]
    for i in range(steps):
        to_right = [interleaved(chans + 1, i, j) for j in range(tiles)]
        to_left = leftward(to_right)
        for j in range(tiles):
            to_down = interleaved(chans + 2, i, j)
            diag = interleaved(chans, i, j) + to_right[j] + to_left[j] + to_down + to_up[j]
            inside = diag > 0.0
            safe = jnp.where(inside, diag, 1.0)
            guess = lax.rsqrt(safe)
            scale = guess * (1.5 - 0.5 * safe * guess * guess)
            scale_ref[j, at(i), :] = jnp.where(inside, scale, 0.0)
            root_ref[j, at(i), :] = safe * scale
            to_up[j] = to_down
    wrapped = [pltpu.roll(scale_ref[j, at(0), :], SUBS - 1, 0) for j in range(tiles)]
    for i in range(steps):
        scale = [scale_ref[j, at(i), :] for j in range(tiles)]
        right_scale = rightward(scale)
        for j in range(tiles):
            b_right_ref[j, at(i), :] = interleaved(chans + 1, i, j) * scale[j] * right_scale[j]
            down_scale = scale_ref[j, at(i + 1), :] if i + 1 < steps else wrapped[j]
            b_down_ref[j, at(i), :] = interleaved(chans + 2, i, j) * scale[j] * down_scale
            for c in range(chans):
                g0_ref[c, j, at(i), :] = interleaved(c, i, j) * scale[j]

    ways = ways_of(tiles)

    def own_of(i, j):
        low, high = -(-(HALO - i) // steps), (HALO + rows - 1 - i) // steps
        left = own_tiles * LANES - j // ways * ways * LANES - j % ways
        return low, high, min(LANES, max(0, -(-left // ways)))

    def channel(c, carry):
        g0, z0, g1, f1, g2 = [ref.at[c] for ref in (g0_ref, z0_ref, g1_ref, f1_ref, g2_ref)]
        precondition(b_right_ref, b_down_ref, g0, z0, work_ref)
        sum0, sum1 = next_residual(b_right_ref, b_down_ref, g0, z0, g1, own_of)
        precondition(b_right_ref, b_down_ref, g1, f1, work_ref)
        sum2, sum3 = next_residual(b_right_ref, b_down_ref, g1, f1, g2, own_of)
        return tuple(a + b for a, b in zip(carry, (sum0, sum1, sum2, sum3)))

    zero = jnp.zeros((SUBS, LANES), jnp.float32)
    parts = lax.fori_loop(0, chans, channel, (zero,) * 4)
    sums = zero
    for k, part in enumerate(parts):
        sums = jnp.where(sub == k, jnp.sum(part), sums)
    sums_ref[...] = sums
    first_late_ref[chans * tiles] = sums

    def edge(c, j, at):
        s, i = divmod(HALO + at, steps)
        return g2_ref[c, j, pl.ds(i * SUBS + s, LATE, stride=SUBS), :]

    for c in range(chans):
        for j in range(tiles):
            low, high = edge(c, j, 0), edge(c, j, rows - LATE)
            first_late_ref[c * tiles + j] = jnp.where(odd_row, low, high)
            second_late_ref[c * tiles + j] = jnp.where(odd_row, high, low)


def second_kernel(
    c, first_late_ref, second_late_ref, b_right_ref, b_down_ref, g2_ref, f2_ref, g_ref, work_ref
):
    tiles, height = b_right_ref.shape[:2]
    rows = height - 2 * HALO
    steps = height // SUBS
    odd_row = odd("row")
    for j in range(tiles):
        g_ref[j] = g2_ref[c, j]
        first, second = first_late_ref[c * tiles + j], second_late_ref[c * tiles + j]
        for value, at in ((jnp.where(odd_row, first, second), HALO - LATE), (jnp.where(odd_row, second, first), HALO + rows)):
            done = 0
            while done < LATE:
                s, i = divmod(at + done, steps)
                count = min(LATE - done, steps - i)
                g_ref[j, pl.ds(i * SUBS + s, count, stride=SUBS), :] = value[done:done + count]
                done += count
    precondition(b_right_ref, b_down_ref, g_ref, f2_ref, work_ref)


def combine(n0, n1, n2, n3):
    gap = n0 - n1
    keep = -n1 / gap
    step = n0 / gap
    beta = (n0 * n2 - n1 * n1) / (gap * gap)
    along = keep + beta
    curvature = along * along * gap + 2.0 * along * step * (n1 - n2) + step * step * (n2 - n3)
    scaled = n0 * beta / curvature
    first_size = step * MIX
    second_size = scaled * MIX
    x0 = first_size + second_size * along
    x1 = second_size * step
    r0 = keep - scaled * along
    r1 = step + scaled * (along - step)
    r2 = scaled * step
    return x0, x1, r0, r1, r2


def third_kernel(
    sums_ref, scale_ref, root_ref, g0_ref, z0_ref, g1_ref, f1_ref, g2_ref, *refs
):
    *f2_refs, solution_hbm, residual_hbm, smoothed_hbm, natural, done, sems = refs
    rows, cols = solution_hbm.shape[1:]
    own_tiles = cols // LANES
    tiles, height = scale_ref.shape[:2]
    steps = height // SUBS
    ways = ways_of(tiles)
    x0, x1, r0, r1, r2 = combine(*[jnp.broadcast_to(sums_ref[k:k + 1, :], (SUBS, LANES)) for k in range(4)])
    matrix = undealing(ways) if ways > 1 else None
    outs = (solution_hbm, residual_hbm, smoothed_hbm)
    copies = []
    for c, f2_ref in enumerate(f2_refs):
        for j in range(tiles):
            for i in range(steps):
                at = pl.ds(i * SUBS, SUBS)
                scale = scale_ref[j, at, :]
                root = root_ref[j, at, :]
                g0, g1, g2, z0, f1 = [ref[c, j, at, :] for ref in (g0_ref, g1_ref, g2_ref, z0_ref, f1_ref)]
                f2 = f2_ref[j, at, :]
                there = pl.ds(i, SUBS, stride=steps)
                natural[c, 0, j, there, :] = scale * (x0 * z0 + x1 * f1)
                natural[c, 1, j, there, :] = root * (r0 * g0 + r1 * g1 + r2 * g2)
                natural[c, 2, j, there, :] = scale * (r0 * z0 + r1 * f1 + r2 * f2)
        for g in range(0, own_tiles, ways):
            value = jnp.concatenate(
                [natural[c, :, g + m, HALO:HALO + rows, :].reshape(3 * rows, LANES) for m in range(ways)], axis=1
            )
            width = min(ways, own_tiles - g) * LANES
            if ways > 1:
                value = permuted(value, matrix[:, :width], 2)
            for k in range(len(outs)):
                columns = pl.ds(g * LANES, width)
                done[c, k, :, columns] = value[k * rows:(k + 1) * rows]
                there = outs[k].at[c, :, columns]
                copies.append(pltpu.make_async_copy(done.at[c, k, :, columns], there, sems.at[c, k, g // ways]))
                copies[-1].start()
    for copy in copies:
        copy.wait()


def sum_over(value, rounds, beside):
    done = []
    for k, (axis, bits) in enumerate(rounds):
        size = lax.axis_size(axis)
        others = [
            lax.ppermute(value, axis, [(i, i ^ mask) for i in range(size)])
            for mask in ((bits[0],) if len(bits) == 1 else (bits[0], bits[1], bits[0] | bits[1]))
        ]
        left = len(rounds) - k
        if left <= len(beside):
            now = beside[len(done):] if left == 1 else beside[len(done):len(done) + 1]
            value, *arrays = lax.optimization_barrier((value, *now))
            done += arrays
        value = value + others[0]
        if len(others) > 1:
            value = value + (others[1] + others[2])
    return value, done + list(beside[len(done):])


def per_device(source, weight, seam_right, seam_down, offsets):
    chans, rows, cols = source.shape
    row_axis, col_axis = lax.axis_size("row"), lax.axis_size("col")
    in_vmem = pl.BlockSpec(memory_space=pltpu.VMEM)
    in_hbm = pl.BlockSpec(memory_space=pltpu.HBM)
    params = pltpu.CompilerParams(vmem_limit_bytes=VMEM_LIMIT)

    def shaped(*shape):
        return jax.ShapeDtypeStruct(shape, jnp.float32)

    def scratch(*shape):
        return pltpu.VMEM(shape, jnp.float32)

    planes = chans + 3
    own_tiles = cols // LANES
    tiles = own_tiles + 1
    packs = -(-planes // SLOTS)
    own, first_rows, second_rows, first_cols, second_cols = pl.pallas_call(
        own_kernel,
        out_shape=[shaped(planes, own_tiles, rows, LANES)]
        + [shaped(planes, own_tiles, HALO, LANES)] * 2
        + [shaped(packs, rows, LANES)] * 2,
        in_specs=[in_hbm] * 5,
        out_specs=[in_vmem] * 5,
        scratch_shapes=[
            pltpu.SMEM((chans,) + offsets.shape[:2], jnp.int32),
            scratch(*source.shape),
            scratch(*weight.shape),
            pltpu.VMEM(weight.shape, jnp.int32),
            pltpu.VMEM(weight.shape, jnp.int32),
            pltpu.SemaphoreType.DMA((planes + 1,)),
        ],
        compiler_params=params,
    )(
        *[
            pltpu.with_memory_space_constraint(v, pltpu.HBM)
            for v in (offsets.transpose(2, 0, 1), source, weight, seam_right, seam_down)
        ],
    )

    def swap(first, second, axis, order):
        size = lax.axis_size(axis)
        pairs = [[(i, i + 1) for i in range(start, size - 1, 2)] for start in range(2)]
        pairs = [some + [(j, i) for i, j in some] for some in pairs]
        received = {k: lax.ppermute((first, second)[k], axis, pairs[k]) for k in order}
        return received[0], received[1]

    ways = ways_of(tiles)
    inner = pl.pallas_call(
        inner_dealt_kernel,
        out_shape=shaped(planes, tiles - ways, rows, LANES),
        in_specs=[in_vmem],
        out_specs=in_vmem,
        compiler_params=params,
        cost_estimate=pl.CostEstimate(flops=10**8, bytes_accessed=4 * 10**6, transcendentals=0),
    )(own)
    first_rows, second_rows = swap(first_rows, second_rows, "row", (1, 0))
    first_cols, second_cols = swap(first_cols, second_cols, "col", (0, 1))
    first_cols, second_cols, inner = lax.optimization_barrier((first_cols, second_cols, inner))
    corners = pl.pallas_call(
        functools.partial(corners_kernel, chans),
        out_shape=[shaped(2, packs, HALO, LANES)] * 2,
        in_specs=[in_vmem] * 2,
        out_specs=[in_vmem] * 2,
        compiler_params=params,
    )(first_cols, second_cols)
    first_corners, second_corners = swap(*corners, "row", (1, 0))
    outer = pl.pallas_call(
        outer_dealt_kernel,
        out_shape=shaped(planes, ways, rows, LANES),
        in_specs=[in_vmem] * 3,
        out_specs=in_vmem,
        compiler_params=params,
        cost_estimate=pl.CostEstimate(flops=10**8, bytes_accessed=2 * 10**6, transcendentals=0),
    )(own, first_cols, second_cols)

    height = rows + 2 * HALO
    plane = shaped(tiles, height, LANES)
    field = shaped(chans, tiles, height, LANES)
    lates = [shaped(chans * tiles + extra, LATE, LANES) for extra in (1, 0)]
    *basis, sums, first_late, second_late = pl.pallas_call(
        first_kernel,
        out_shape=[plane] * 4 + [field] * 5 + [shaped(SUBS, LANES)] + lates,
        in_specs=[in_vmem] * 6,
        out_specs=[in_vmem] * 12,
        scratch_shapes=[scratch(planes, tiles, height, LANES), scratch(*plane.shape)],
        compiler_params=params,
    )(inner, outer, second_rows, first_rows, second_corners, first_corners)

    first_late, second_late = swap(first_late, second_late, "row", (0, 1))

    b_right, b_down, scale, root, g0, z0, g1, f1, g2 = basis
    f2 = [
        pl.pallas_call(
            functools.partial(second_kernel, c),
            out_shape=plane,
            in_specs=[in_vmem] * 5,
            out_specs=in_vmem,
            scratch_shapes=[scratch(*plane.shape)] * 2,
            compiler_params=params,
            cost_estimate=pl.CostEstimate(flops=10**8, bytes_accessed=10**7, transcendentals=0),
        )(first_late, second_late, b_right, b_down, g2)
        for c in range(chans)
    ]
    if row_axis & (row_axis - 1) or col_axis & (col_axis - 1):
        total = lax.psum(sums, ("row", "col"))
    else:
        rounds = []
        for axis, size, low in (("row", row_axis, 1), ("col", col_axis, 0)):
            bits = [1 << k for k in range(low, size.bit_length() - 1)]
            rounds += [(axis, bits[k:k + 2]) for k in range(0, len(bits), 2)]
        if row_axis > 1:
            sums = sums + first_late[chans * tiles]
        total, f2 = sum_over(sums, rounds, f2)
    return pl.pallas_call(
        third_kernel,
        out_shape=[shaped(chans, rows, cols)] * 3,
        in_specs=[in_vmem] * (8 + chans),
        out_specs=[pl.BlockSpec(memory_space=pltpu.HBM)] * 3,
        scratch_shapes=[
            scratch(chans, 3, tiles, height, LANES),
            scratch(chans, 3, rows, cols),
            pltpu.SemaphoreType.DMA((chans, 3, -(-own_tiles // ways_of(tiles)))),
        ],
        compiler_params=params,
    )(total, scale, root, g0, z0, g1, f1, g2, *f2)


def solution(mesh):
    placed = (
        P(None, ("band", "row"), "col"),
        P(("band", "row"), "col"),
        P(("band", "row"), "col"),
        P(("band", "row"), "col"),
        P("band", None, None),
    )
    return jax.shard_map(
        per_device,
        mesh=mesh,
        in_specs=placed,
        out_specs=(
            P(None, ("band", "row"), "col"),
            P(None, ("band", "row"), "col"),
            P(None, ("band", "row"), "col"),
        ),
        check_vma=False,
    )
```
